32 devices in a mesh: dp: 8 (over y, x, core), col: 4 (over z).
Axes of the slice: x: 2, y: 2, z: 4, core: 2. Of those that a mesh axis runs over, the one named last changes fastest.
Arguments:
- item_ids: int32 [256, 32], P('dp'), may hold values from 0 to 37482
- target_ids: int32 [256, 32], P('dp'), may hold values from 0 to 37482
- negative_ids: int32 [2048], replicated, may hold values from 0 to 37482
- reset_mask: int32 [256, 32], P('dp'), may hold values 0 or 1
- carry_flags: int32 [256], P('dp'), may hold values 0 or 1
- carried_state: float32 [256, 1000], P('dp', 'col'), may hold values from -3 to 3
- embed_table: float32 [1000, 37888], P('col'), may hold values from -6 to 6
- input_weight: float32 [3, 1000, 1000], P(None, 'col'), may hold values from -0.1875 to 0.1875
- hidden_weight: float32 [3, 1000, 1000], P(None, 'col'), may hold values from -0.1875 to 0.1875
- gate_bias: float32 [3, 1000], P(None, 'col'), may hold values from -3 to 3
- hidden_bias: float32 [1000], P('col'), may hold values from -3 to 3
- out_table: float32 [1000, 37888], P('col'), may hold values from -0.5 to 0.5
- out_bias: float32 [37888], replicated, may hold values from -3 to 3
Outputs:
- loss: float32 [256, 32], P('dp')
- grad_embed: float32 [1000, 37888], P('col', 'dp')
- grad_input_weight: float32 [3, 1000, 1000], P(None, 'col')
- grad_hidden_weight: float32 [3, 1000, 1000], P(None, 'col')
- grad_gate_bias: float32 [3, 1000], P(None, 'col')
- grad_hidden_bias: float32 [1000], P('col')
- grad_out_table: float32 [1000, 37888], P('col', 'dp')
- grad_out_bias: float32 [37888], P('dp')
- grad_carried: float32 [256, 1000], P('dp', 'col')
The draws below stay inside these ranges and needn't reach their ends.
All inputs are finite; a program needn't handle non-finite values. No bound on the sum of `reset_mask` or of `carry_flags` on one device may be relied on, other than what follows from the above.
Results may differ from the reference program's by a relative error of at most 0.0003.
Values sent between devices are 32-bit elements; how exact they have to be, the bound alone decides.
A program may use at most 384 MiB of HBM per device.

```python
import math
import jax
import jax.numpy as jnp
import numpy as np
from jax import lax

D = 1000
H = 1000
V = 37483
NEG = 2048
STEPS = 32
SESSIONS = 256
ROWS = 37888


def set_ends(result, stream_key, low, largest):
    spot = [jax.random.randint(jax.random.fold_in(stream_key, axis), (), 0, length) for axis, length in enumerate(result.shape)]
    longest = result.shape.index(max(result.shape))
    next_to = spot[:longest] + [(spot[longest] + 1) % result.shape[longest]] + spot[longest + 1:]
    return result.at[tuple(spot)].set(low).at[tuple(next_to)].set(largest)


def levels(stream_key, dims, pieces, low, top_value):
    loudness = 1.0
    for axis_at, parts in pieces:
        heights = jax.random.uniform(jax.random.fold_in(jax.random.fold_in(stream_key, 6), axis_at), (parts,), jnp.float32, low / len(pieces), top_value / len(pieces))
        loudness = loudness * jnp.repeat(jnp.exp(heights), dims[axis_at] // parts).reshape((-1,) + (1,) * (len(dims) - 1 - axis_at))
    return loudness


def rank_bounds(count, slope):
    loads = [(1 << 20) // math.isqrt(grade ** slope) + 1 for grade in range(1, count + 1)]
    scale = 1 + sum(loads) // (1 << 30)
    return np.cumsum(np.array([max(1, weight // scale) for weight in loads]))


def ranked_ids(stream_key, shape, count, lean):
    grid = rank_bounds(count, lean)
    ticket = jax.random.randint(jax.random.fold_in(stream_key, 1), shape, 0, int(grid[count - 1]))
    grade = jnp.searchsorted(jnp.asarray(grid, jnp.int32), ticket, side="right")
    return jax.random.permutation(jax.random.fold_in(stream_key, 2), count)[grade].astype(jnp.int32)


def gaussian(stream_key, shape, scale, limit, shards=(), kind=jnp.bfloat16):
    drawn = scale * jax.random.normal(stream_key, shape, jnp.float32)
    if shards:
        drawn = drawn * levels(stream_key, shape, shards, -0.22, 0.18)
    return jnp.clip(drawn, -limit, limit).astype(kind)


def setup_inputs(seed: int = 0) -> dict:
    key_list = jax.random.split(jax.random.key(seed), 14)
    item_ids = set_ends(ranked_ids(key_list[0], (SESSIONS, STEPS), V, 2), jax.random.fold_in(key_list[0], 3), 0, V - 1).astype(jnp.int32)
    target_ids = set_ends(ranked_ids(key_list[1], (SESSIONS, STEPS), V, 2), jax.random.fold_in(key_list[1], 3), 0, V - 1).astype(jnp.int32)
    negative_ids = set_ends(ranked_ids(key_list[2], (NEG,), V, 1), jax.random.fold_in(key_list[2], 3), 0, V - 1).astype(jnp.int32)
    reset_mask = set_ends((jax.random.randint(key_list[3], (SESSIONS, STEPS), 0, 16) < 1).astype(jnp.int32), jax.random.fold_in(key_list[3], 1), 0, 1)
    carry_flags = set_ends((jax.random.randint(key_list[4], (SESSIONS,), 0, 4) < 3).astype(jnp.int32), jax.random.fold_in(key_list[4], 1), 0, 1)
    carried_state = gaussian(key_list[5], (SESSIONS, H), 0.5, 3.0, ((0, 8), (1, 4)), jnp.float32)
    embed_table = gaussian(key_list[6], (D, ROWS), 1.0, 6.0, ((0, 4),), jnp.float32)
    input_weight = gaussian(key_list[7], (3, H, D), D ** -0.5, 0.1875, ((1, 4),), jnp.float32)
    hidden_weight = gaussian(key_list[8], (3, H, H), H ** -0.5, 0.1875, ((1, 4),), jnp.float32)
    gate_bias = gaussian(key_list[9], (3, H), 0.5, 3.0, ((1, 4),), jnp.float32)
    hidden_bias = gaussian(key_list[10], (H,), 0.5, 3.0, ((0, 4),), jnp.float32)
    out_table = gaussian(key_list[11], (H, ROWS), (H // 8) ** -0.5, 0.5, ((0, 4),), jnp.float32)
    out_bias = gaussian(key_list[12], (ROWS,), 0.5, 3.0, (), jnp.float32)
    return {"item_ids": item_ids, "target_ids": target_ids, "negative_ids": negative_ids, "reset_mask": reset_mask, "carry_flags": carry_flags, "carried_state": carried_state, "embed_table": embed_table, "input_weight": input_weight, "hidden_weight": hidden_weight, "gate_bias": gate_bias, "hidden_bias": hidden_bias, "out_table": out_table, "out_bias": out_bias}


bpr_weight = 1.0
precise = lax.Precision.HIGHEST

@jax.custom_vjp
def low(v):
    return lax.optimization_barrier(v.astype(jnp.bfloat16)).astype(jnp.float32)

@jax.custom_vjp
def low_back(v):
    return v

def low_keep(v):
    return (low(v), None)

def low_pass(kept, grad):
    return (grad,)

def back_keep(v):
    return (v, None)

def back_low(kept, grad):
    return (low(grad),)
low.defvjp(low_keep, low_pass)
low_back.defvjp(back_keep, back_low)

def forward(params, item_ids, target_ids, negative_ids, reset_mask, carry_flags):
    embed_table, input_weight, hidden_weight, gate_bias, hidden_bias, out_table, out_bias, carried_state = params
    embed_rows = embed_table.T
    out_rows = out_table.T
    inputs = embed_rows[item_ids.T]
    x_gates = jnp.einsum('tsd,ghd->tsgh', inputs, input_weight, precision=precise) + gate_bias
    keep_time = (1 - reset_mask.T).astype(jnp.float32)
    neg_rows = out_rows[negative_ids]
    neg_bias = out_bias[negative_ids]
    start = carry_flags.astype(jnp.float32)[:, None] * carried_state

    def step(state, slices):
        x_now, keep_now, target_now = slices
        prev = keep_now[:, None] * state
        h_gates = jnp.einsum('sk,ghk->sgh', prev, hidden_weight, precision=precise)
        reset_gate = jax.nn.sigmoid(x_now[:, 0] + h_gates[:, 0])
        update_gate = jax.nn.sigmoid(x_now[:, 1] + h_gates[:, 1])
        inner = h_gates[:, 2] + hidden_bias
        candidate = jnp.tanh(x_now[:, 2] + reset_gate * inner)
        new_state = (1.0 - update_gate) * candidate + update_gate * prev
        pos_score = lax.optimization_barrier(jnp.sum(new_state * out_rows[target_now], axis=-1)) + out_bias[target_now]
        neg_score = jnp.dot(new_state, neg_rows.T, precision=precise) + neg_bias
        top = lax.optimization_barrier(jnp.max(neg_score, axis=-1, keepdims=True))
        expd = jnp.exp(neg_score - top)
        weight = expd / lax.optimization_barrier(jnp.sum(expd, axis=-1, keepdims=True))
        sig = jax.nn.sigmoid(pos_score[:, None] - neg_score)
        ppos = lax.optimization_barrier(jnp.sum(weight * sig, axis=-1))
        quad = lax.optimization_barrier(jnp.sum(weight * neg_score * neg_score, axis=-1))
        return (new_state, -jnp.log(ppos) + bpr_weight * quad)
    final, losses = lax.scan(jax.checkpoint(step), start, (x_gates, keep_time, target_ids.T))
    return (jnp.sum(losses) / STEPS, losses.T)

def reference(item_ids, target_ids, negative_ids, reset_mask, carry_flags, carried_state, embed_table, input_weight, hidden_weight, gate_bias, hidden_bias, out_table, out_bias):
    params = (embed_table, input_weight, hidden_weight, gate_bias, hidden_bias, out_table, out_bias, carried_state)

    def objective(params_in):
        return forward(params_in, item_ids, target_ids, negative_ids, reset_mask, carry_flags)
    total, backward, losses = jax.vjp(objective, params, has_aux=True)
    grads = backward(jnp.ones_like(total))[0]
    g_embed, g_input, g_hidden, g_gate, g_hbias, g_out, g_obias, g_carried = grads
    return (losses, g_embed, g_input, g_hidden, g_gate, g_hbias, g_out, g_obias, g_carried)
```

```python
import functools

import jax
import jax.numpy as jnp
from jax import lax
from jax.experimental import pallas as pl
from jax.experimental.pallas import tpu as pltpu
from jax.sharding import PartitionSpec as P

LANES = 128
ROWS8 = 8
VMEM_BYTES = 60 << 20
f32 = jnp.float32
bf16 = jnp.bfloat16
high = lax.Precision.HIGH


def round_up(value, unit):
    return -(-value // unit) * unit


def params():
    return pltpu.CompilerParams(vmem_limit_bytes=VMEM_BYTES)


def in_vmem():
    return pl.BlockSpec(memory_space=pltpu.VMEM)


def in_smem():
    return pl.BlockSpec(memory_space=pltpu.SMEM)


def gather_kernel(chunk, count, width, ids, table, bias, out, padded, turned):
    step = pl.program_id(0)

    @pl.when(step == 0)
    def _():
        padded[...] = jnp.zeros_like(padded)

    padded[0:width, :] = table[...]
    padded[width : width + 1, :] = bias[...]
    turned[pl.ds(pl.multiple_of(step * chunk, chunk), chunk), :] = padded[...].T

    @pl.when(step == pl.num_programs(0) - 1)
    def _():
        def body(block, carry):
            for j in range(ROWS8):
                row = ids[block * ROWS8 + j]
                out[pl.ds(block * ROWS8 + j, 1), :] = turned[pl.ds(row, 1), :]
            return carry

        lax.fori_loop(0, count // ROWS8, body, 0)


def gather_rows(table, bias, ids, block):
    width, rows = table.shape
    count = ids.shape[0]
    chunk = LANES * max(k for k in range(1, 9) if rows % (LANES * k) == 0)
    return pl.pallas_call(
        functools.partial(gather_kernel, chunk, count, width),
        out_shape=jax.ShapeDtypeStruct((count, block), f32),
        grid_spec=pltpu.PrefetchScalarGridSpec(
            num_scalar_prefetch=1,
            grid=(rows // chunk,),
            in_specs=[
                pl.BlockSpec((width, chunk), lambda i, ids: (0, i)),
                pl.BlockSpec((1, chunk), lambda i, ids: (0, i)),
            ],
            out_specs=pl.BlockSpec((count, block), lambda i, ids: (0, 0)),
            scratch_shapes=[pltpu.VMEM((block, chunk), f32), pltpu.VMEM((rows, block), f32)],
        ),
        compiler_params=params(),
    )(ids, table, bias)


def scatter_kernel(width, n_lists, *refs):
    bounds = refs[0]
    lists = refs[1 : 1 + 3 * n_lists]
    out, bias_out, acc = refs[1 + 3 * n_lists :]
    acc[...] = jnp.zeros_like(acc)
    low = bounds[0]
    for k in range(n_lists):
        rows_of, ids, data = lists[3 * k : 3 * k + 3]

        def body(i, carry):
            spot = pl.ds(ids[i] - low, 1)
            acc[spot, :] = acc[spot, :] + data[pl.ds(rows_of[i], 1), :]
            return carry

        lax.fori_loop(bounds[1 + 2 * k], bounds[2 + 2 * k], body, 0)
    for j in range(acc.shape[0] // LANES):
        cols = slice(j * LANES, (j + 1) * LANES)
        turned = acc[cols, :].T
        out[:, cols] = turned[:width]
        bias_out[:, cols] = turned[width : width + 1]


def scatter_rows(lists, low, own_rows, width, block):
    ends = [low]
    operands, specs = [], []
    for order, ids, data in lists:
        ends += [jnp.sum(ids < low, dtype=jnp.int32), jnp.sum(ids < low + own_rows, dtype=jnp.int32)]
        operands += [order, ids, data]
        specs += [in_smem(), in_smem(), in_vmem()]
    return pl.pallas_call(
        functools.partial(scatter_kernel, width, len(lists)),
        out_shape=(
            jax.ShapeDtypeStruct((width, own_rows), f32),
            jax.ShapeDtypeStruct((1, own_rows), f32),
        ),
        in_specs=[in_smem()] + specs,
        out_specs=(in_vmem(), in_vmem()),
        scratch_shapes=[pltpu.VMEM((own_rows, block), f32)],
        compiler_params=params(),
    )(jnp.stack(ends), *operands)


def split_weight(weight, high_part, low_part):
    step = 128

    @pl.loop(0, weight.shape[0] // step)
    def _(i):
        rows = pl.ds(pl.multiple_of(i * step, step), step)
        value = weight[rows, :]
        top = value.astype(bf16)
        high_part[rows, :] = top
        low_part[rows, :] = (value - top.astype(f32)).astype(bf16)


def two_part(value):
    top = value.astype(bf16).astype(f32)
    return jnp.concatenate([top, value - top], axis=0).astype(bf16)


def forward_kernel(
    steps, width, weight, x_gates, keep, start, prevs, resets, updates, cands, inners, outs, w_high, w_low
):
    rows_per, units = start.shape
    split_weight(weight, w_high, w_low)
    lane = lax.broadcasted_iota(jnp.int32, (rows_per, units), 1)

    def step(t, state):
        rows = pl.ds(pl.multiple_of(t * rows_per, rows_per), rows_per)
        prev = jnp.where(lane == width, 1.0, keep[rows, :] * state)
        pair = two_part(prev)

        def gate(g):
            cols = slice(g * units, (g + 1) * units)
            first = jnp.dot(pair, w_high[:, cols], preferred_element_type=f32)
            second = jnp.dot(pair, w_low[:, cols], preferred_element_type=f32)
            return first[:rows_per] + first[rows_per:] + second[:rows_per], cols

        h_reset, cols = gate(0)
        reset = jax.nn.sigmoid(x_gates[rows, cols] + h_reset)
        h_update, cols = gate(1)
        update = jax.nn.sigmoid(x_gates[rows, cols] + h_update)
        inner, cols = gate(2)
        cand = jnp.tanh(x_gates[rows, cols] + reset * inner)
        new = (1.0 - update) * cand + update * prev
        prevs[rows, :] = prev
        resets[rows, :] = reset
        updates[rows, :] = update
        cands[rows, :] = cand
        inners[rows, :] = inner
        outs[rows, :] = new
        return new

    lax.fori_loop(0, steps, step, start[...])


def run_forward(weight_turned, x_gates, keep, start, steps, width):
    events, units = x_gates.shape[0], start.shape[1]
    saved = jax.ShapeDtypeStruct((events, units), f32)
    return pl.pallas_call(
        functools.partial(forward_kernel, steps, width),
        out_shape=(saved,) * 6,
        in_specs=[in_vmem()] * 4,
        out_specs=(in_vmem(),) * 6,
        scratch_shapes=[pltpu.VMEM(weight_turned.shape, bf16)] * 2,
        compiler_params=params(),
    )(weight_turned, x_gates, keep, start)


def backward_kernel(
    steps, weight, douts, keep, prevs, resets, updates, cands, inners, dgates, dstart, w_high, w_low
):
    rows_per, units = dstart.shape
    split_weight(weight, w_high, w_low)

    def step(i, dstate):
        t = steps - 1 - i
        rows = pl.ds(pl.multiple_of(t * rows_per, rows_per), rows_per)
        reset, update, cand = resets[rows, :], updates[rows, :], cands[rows, :]
        dh = douts[rows, :] + dstate
        dcand = dh * (1.0 - update) * (1.0 - cand * cand)
        dreset = dcand * inners[rows, :] * reset * (1.0 - reset)
        dupdate = dh * (prevs[rows, :] - cand) * update * (1.0 - update)
        dinner = dcand * reset
        dgates[rows, 0:units] = dreset
        dgates[rows, units : 2 * units] = dupdate
        dgates[rows, 2 * units : 3 * units] = dinner
        dgates[rows, 3 * units : 4 * units] = dcand
        total = dh * update
        for g, part in enumerate((dreset, dupdate, dinner)):
            pair = two_part(part)
            sect = slice(g * units, (g + 1) * units)
            first = jnp.dot(pair, w_high[sect, :], preferred_element_type=f32)
            second = jnp.dot(pair, w_low[sect, :], preferred_element_type=f32)
            total = total + (first[:rows_per] + first[rows_per:] + second[:rows_per])
        return keep[rows, :] * total

    dstart[...] = lax.fori_loop(0, steps, step, jnp.zeros((rows_per, units), f32))


def run_backward(weight, douts, keep, saved, rows_per, steps):
    events, units = douts.shape
    return pl.pallas_call(
        functools.partial(backward_kernel, steps),
        out_shape=(
            jax.ShapeDtypeStruct((events, 4 * units), f32),
            jax.ShapeDtypeStruct((rows_per, units), f32),
        ),
        in_specs=[in_vmem()] * 8,
        out_specs=(in_vmem(),) * 2,
        scratch_shapes=[pltpu.VMEM(weight.shape, bf16)] * 2,
        compiler_params=params(),
    )(weight, douts, keep, *saved)


def pad_units(weight, bias, n_col, block):
    gates, own, full = weight.shape
    part = full // n_col
    rows = weight.reshape(gates, own, n_col, part)
    rows = jnp.pad(rows, ((0, 0), (0, block - own), (0, 0), (0, block - part)))
    rows = rows.reshape(gates, block, n_col * block)
    return rows.at[:, :own, part].set(bias)


def gather_weight(own, n_dp):
    gates, block, units = own.shape
    flat = own.reshape(n_dp, gates * block // n_dp, units)
    piece = lax.dynamic_index_in_dim(flat, lax.axis_index("dp"), 0, keepdims=False)
    every = lax.all_gather(piece, ("col", "dp"))
    every = every.reshape(-1, gates, block, units)
    return jnp.moveaxis(every, 0, 1).reshape(gates, -1, units)


def reduce_weight(partial, n_dp, n_col):
    gates, rows, units = partial.shape
    block = rows // n_col
    parts = jnp.moveaxis(partial.reshape(gates, n_col, block, units), 1, 0)
    parts = jnp.moveaxis(parts.reshape(n_col, n_dp, gates * block // n_dp, units), 1, 0)
    mine = lax.psum_scatter(parts, "dp", scatter_dimension=0)
    mine = lax.psum_scatter(mine, "col", scatter_dimension=0)
    return lax.all_gather(mine, "dp").reshape(gates, block, units)


def swap_col(rows, n_col):
    return lax.all_to_all(rows, "col", split_axis=0, concat_axis=0, tiled=True)


def unpad_last(value, n_col, part):
    block = value.shape[-1] // n_col
    return value.reshape(value.shape[:-1] + (n_col, block))[..., :part].reshape(value.shape[:-1] + (n_col * part,))


def local(
    n_dp,
    n_col,
    item_ids,
    target_ids,
    negative_ids,
    reset_mask,
    carry_flags,
    carried_state,
    embed_table,
    input_weight,
    hidden_weight,
    gate_bias,
    hidden_bias,
    out_table,
    out_bias,
):
    sessions, steps = item_ids.shape
    own_sessions = sessions // n_col
    rows_per = round_up(own_sessions, ROWS8)
    width = embed_table.shape[0]
    table_rows = embed_table.shape[1]
    own_rows = table_rows // n_dp
    block = round_up(width + 1, LANES)
    units = n_col * block
    events = steps * rows_per
    factor = 1.0 / steps
    dp_at, col_at = lax.axis_index("dp"), lax.axis_index("col")

    def by_owner(value):
        value = jnp.moveaxis(value.reshape(n_col, own_sessions, steps), 1, 2)
        value = jnp.pad(value, ((0, 0), (0, 0), (0, rows_per - own_sessions)))
        return value.reshape(-1)

    item_flat, target_flat = by_owner(item_ids), by_owner(target_ids)
    own_keep = lax.dynamic_index_in_dim(
        by_owner(1 - reset_mask).reshape(n_col, events, 1), col_at, 0, keepdims=False
    ).astype(f32)
    valid = jnp.tile(jnp.arange(rows_per) < own_sessions, steps)
    lane = jnp.arange(units) % block
    first_pad = jnp.arange(units) == width

    own_in = pad_units(input_weight, gate_bias, n_col, block)
    no_bias = jnp.zeros_like(hidden_bias)
    own_hid = pad_units(hidden_weight, jnp.stack([no_bias, no_bias, hidden_bias]), n_col, block)
    all_hid = gather_weight(own_hid, n_dp).reshape(-1, units)
    all_in = gather_weight(own_in, n_dp).reshape(-1, units)

    all_items = lax.all_gather(item_flat, "dp", tiled=True)
    all_targets = lax.all_gather(target_flat, "dp", tiled=True)

    def ordered(ids):
        ids, order = lax.sort((ids, lax.iota(jnp.int32, ids.shape[0])), num_keys=1)
        return order, ids

    no_row = jnp.zeros((1, table_rows), f32)
    item_rows = gather_rows(embed_table, no_row, item_flat, block).reshape(n_col, events, block)
    carried = (carry_flags.astype(f32)[:, None] * carried_state).reshape(n_col, own_sessions, width)
    carried = jnp.pad(carried, ((0, 0), (0, rows_per - own_sessions), (0, block - width)))
    arrived = swap_col(jnp.concatenate([item_rows, carried], axis=1), n_col)
    arrived = jnp.moveaxis(arrived, 0, 1).reshape(events + rows_per, units)
    inputs = jnp.where(first_pad, 1.0, arrived[:events])
    start = arrived[events:]

    neg_count = negative_ids.shape[0]
    own_negs = lax.dynamic_slice_in_dim(negative_ids, dp_at * (neg_count // n_dp), neg_count // n_dp)
    out_rows = gather_rows(out_table, out_bias[None, :], jnp.concatenate([target_flat, own_negs]), block)
    targets = swap_col(out_rows[: n_col * events].reshape(n_col, events, block), n_col)
    targets = jnp.moveaxis(targets, 0, 1).reshape(events, units)
    negs = lax.all_gather(out_rows[n_col * events :], ("dp", "col")).reshape(n_dp, n_col, -1, block)
    negs = jnp.moveaxis(negs, 1, 2).reshape(neg_count, units)

    x_gates = lax.dot_general(inputs, all_in, (((1,), (1,)), ((), ())), precision=high)
    prevs, resets, updates, cands, inners, outs = run_forward(
        all_hid.T, x_gates, own_keep, start, steps, width
    )

    shares = jnp.where(lane == width, 1.0 / n_col, jnp.where(lane < width, outs, 0.0))
    pos_score = jnp.sum(shares * targets, axis=-1, keepdims=True)
    neg_score = lax.dot_general(shares, negs, (((1,), (1,)), ((), ())), precision=high)
    top = jnp.max(neg_score, axis=-1, keepdims=True)
    expd = jnp.exp(neg_score - top)
    weight = expd / jnp.sum(expd, axis=-1, keepdims=True)
    sig = jax.nn.sigmoid(pos_score - neg_score)
    ppos = jnp.sum(weight * sig, axis=-1, keepdims=True)
    quad = jnp.sum(weight * neg_score * neg_score, axis=-1, keepdims=True)
    slope = jnp.sum(weight * sig * (1.0 - sig), axis=-1, keepdims=True)
    own_loss = (-jnp.log(ppos) + quad).reshape(steps, rows_per)[:, :own_sessions]
    loss = lax.all_gather(own_loss.T, "col", tiled=True)
    dneg = factor * weight * (1.0 - sig * sig / ppos + neg_score * neg_score + 2.0 * neg_score - quad)
    dneg = jnp.where(valid[:, None], dneg, 0.0)
    dpos = jnp.where(valid[:, None], -factor * slope / ppos, 0.0)
    douts = jnp.dot(dneg, negs, precision=high) + dpos * targets
    douts = jnp.where(lane < width, douts, 0.0)
    neg_part = lax.dot_general(dneg, shares, (((0,), (0,)), ((), ())), precision=high)
    target_part = dpos * shares

    neg_own = lax.psum_scatter(neg_part.reshape(n_dp, -1, units), "dp", scatter_dimension=0)
    neg_own = jnp.moveaxis(neg_own.reshape(-1, n_col, block), 1, 0)
    neg_own = lax.psum_scatter(neg_own, "col", scatter_dimension=0)
    neg_all = lax.all_gather(neg_own, "dp", tiled=True)
    target_own = swap_col(jnp.moveaxis(target_part.reshape(events, n_col, block), 1, 0), n_col)
    target_all = lax.all_gather(target_own.reshape(-1, block), "dp", tiled=True)
    low = (dp_at * own_rows).astype(jnp.int32)
    grad_out, grad_obias = scatter_rows(
        [ordered(all_targets) + (target_all,), ordered(negative_ids) + (neg_all,)],
        low,
        own_rows,
        width,
        block,
    )
    grad_obias = grad_obias[0] * n_col

    dgates, dstart = run_backward(
        all_hid, douts, own_keep, (prevs, resets, updates, cands, inners), rows_per, steps
    )
    dx = jnp.concatenate([dgates[:, : 2 * units], dgates[:, 3 * units :]], axis=1)
    dh = dgates[:, : 3 * units]
    hid_part = lax.dot_general(dh, prevs, (((0,), (0,)), ((), ())), precision=high)
    in_part = lax.dot_general(dx, inputs, (((0,), (0,)), ((), ())), precision=high)
    dinputs = jnp.dot(dx, all_in, precision=high)
    gates = input_weight.shape[0]
    back = jnp.concatenate([dinputs, dstart], axis=0).reshape(events + rows_per, n_col, block)
    back = swap_col(jnp.moveaxis(back, 1, 0), n_col)
    grad_carried = carry_flags.astype(f32)[:, None] * back[:, events : events + own_sessions, :width].reshape(
        sessions, width
    )
    item_all = lax.all_gather(back[:, :events].reshape(-1, block), "dp", tiled=True)
    grad_embed, _ = scatter_rows([ordered(all_items) + (item_all,)], low, own_rows, width, block)
    grad_in = reduce_weight(in_part.reshape(gates, units, units), n_dp, n_col)
    grad_hid = reduce_weight(hid_part.reshape(gates, units, units), n_dp, n_col)
    grad_in, grad_hid = grad_in[:, :width], grad_hid[:, :width]
    return (
        loss,
        grad_embed,
        unpad_last(grad_in, n_col, width),
        unpad_last(grad_hid, n_col, width),
        grad_in[:, :, width],
        grad_hid[gates - 1, :, width],
        grad_out,
        grad_obias,
        grad_carried,
    )


def solution(mesh):
    in_specs = (
        P("dp", None),
        P("dp", None),
        P(),
        P("dp", None),
        P("dp"),
        P("dp", "col"),
        P("col", None),
        P(None, "col", None),
        P(None, "col", None),
        P(None, "col"),
        P("col"),
        P("col", None),
        P(),
    )
    out_specs = (
        P("dp", None),
        P("col", "dp"),
        P(None, "col", None),
        P(None, "col", None),
        P(None, "col"),
        P("col"),
        P("col", "dp"),
        P("dp"),
        P("dp", "col"),
    )
    body = functools.partial(local, mesh.shape["dp"], mesh.shape["col"])
    return jax.shard_map(body, mesh=mesh, in_specs=in_specs, out_specs=out_specs, check_vma=False)
```

```python
import functools

import jax
import jax.numpy as jnp
from jax import lax
from jax.experimental import pallas as pl
from jax.experimental.pallas import tpu as pltpu
from jax.sharding import PartitionSpec as P

LANES = 128
ROWS8 = 8
VMEM_BYTES = 60 << 20
f32 = jnp.float32
bf16 = jnp.bfloat16
high = lax.Precision.HIGH
MESH = pl.DeviceIdType.MESH


def round_up(value, unit):
    return -(-value // unit) * unit


def params():
    return pltpu.CompilerParams(vmem_limit_bytes=VMEM_BYTES)


def in_vmem():
    return pl.BlockSpec(memory_space=pltpu.VMEM)


def in_smem():
    return pl.BlockSpec(memory_space=pltpu.SMEM)


def gather_kernel(chunk, count, width, ids, table, bias, out, padded, turned):
    step = pl.program_id(0)

    @pl.when(step == 0)
    def _():
        padded[...] = jnp.zeros_like(padded)

    padded[0:width, :] = table[...]
    padded[width : width + 1, :] = bias[...]
    turned[pl.ds(pl.multiple_of(step * chunk, chunk), chunk), :] = padded[...].T

    @pl.when(step == pl.num_programs(0) - 1)
    def _():
        def body(block, carry):
            for j in range(ROWS8):
                row = ids[block * ROWS8 + j]
                out[pl.ds(block * ROWS8 + j, 1), :] = turned[pl.ds(row, 1), :]
            return carry

        lax.fori_loop(0, count // ROWS8, body, 0)


def gather_rows(table, bias, ids, block):
    width, rows = table.shape
    count = ids.shape[0]
    chunk = LANES * max(k for k in range(1, 9) if rows % (LANES * k) == 0)
    return pl.pallas_call(
        functools.partial(gather_kernel, chunk, count, width),
        out_shape=jax.ShapeDtypeStruct((count, block), f32),
        grid_spec=pltpu.PrefetchScalarGridSpec(
            num_scalar_prefetch=1,
            grid=(rows // chunk,),
            in_specs=[
                pl.BlockSpec((width, chunk), lambda i, ids: (0, i)),
                pl.BlockSpec((1, chunk), lambda i, ids: (0, i)),
            ],
            out_specs=pl.BlockSpec((count, block), lambda i, ids: (0, 0)),
            scratch_shapes=[pltpu.VMEM((block, chunk), f32), pltpu.VMEM((rows, block), f32)],
        ),
        compiler_params=params(),
    )(ids, table, bias)


def scatter_kernel(width, n_lists, *refs):
    bounds = refs[0]
    lists = refs[1 : 1 + 3 * n_lists]
    out, bias_out, acc = refs[1 + 3 * n_lists :]
    acc[...] = jnp.zeros_like(acc)
    low = bounds[0]
    for k in range(n_lists):
        rows_of, ids, data = lists[3 * k : 3 * k + 3]

        def body(i, carry):
            spot = pl.ds(ids[i] - low, 1)
            acc[spot, :] = acc[spot, :] + data[pl.ds(rows_of[i], 1), :]
            return carry

        lax.fori_loop(bounds[1 + 2 * k], bounds[2 + 2 * k], body, 0)
    for j in range(acc.shape[0] // LANES):
        cols = slice(j * LANES, (j + 1) * LANES)
        turned = acc[cols, :].T
        out[:, cols] = turned[:width]
        bias_out[:, cols] = turned[width : width + 1]


def scatter_rows(lists, low, own_rows, width, block):
    ends = [low]
    operands, specs = [], []
    for order, ids, data in lists:
        ends += [jnp.sum(ids < low, dtype=jnp.int32), jnp.sum(ids < low + own_rows, dtype=jnp.int32)]
        operands += [order, ids, data]
        specs += [in_smem(), in_smem(), in_vmem()]
    return pl.pallas_call(
        functools.partial(scatter_kernel, width, len(lists)),
        out_shape=(
            jax.ShapeDtypeStruct((width, own_rows), f32),
            jax.ShapeDtypeStruct((1, own_rows), f32),
        ),
        in_specs=[in_smem()] + specs,
        out_specs=(in_vmem(), in_vmem()),
        scratch_shapes=[pltpu.VMEM((own_rows, block), f32)],
        compiler_params=params(),
    )(jnp.stack(ends), *operands)


def split_weight(weight, high_part, low_part):
    step = 128

    @pl.loop(0, weight.shape[0] // step)
    def _(i):
        rows = pl.ds(pl.multiple_of(i * step, step), step)
        value = weight[rows, :]
        top = value.astype(bf16)
        high_part[rows, :] = top
        low_part[rows, :] = (value - top.astype(f32)).astype(bf16)


def two_part(value):
    top = value.astype(bf16).astype(f32)
    return jnp.concatenate([top, value - top], axis=0).astype(bf16)


def forward_kernel(
    steps, width, weight, x_gates, keep, start, prevs, resets, updates, cands, inners, outs, w_high, w_low
):
    rows_per, units = start.shape
    split_weight(weight, w_high, w_low)
    lane = lax.broadcasted_iota(jnp.int32, (rows_per, units), 1)

    def step(t, state):
        rows = pl.ds(pl.multiple_of(t * rows_per, rows_per), rows_per)
        prev = jnp.where(lane == width, 1.0, keep[rows, :] * state)
        pair = two_part(prev)

        def gate(g):
            cols = slice(g * units, (g + 1) * units)
            first = jnp.dot(pair, w_high[:, cols], preferred_element_type=f32)
            second = jnp.dot(pair, w_low[:, cols], preferred_element_type=f32)
            return first[:rows_per] + first[rows_per:] + second[:rows_per], cols

        h_reset, cols = gate(0)
        reset = jax.nn.sigmoid(x_gates[rows, cols] + h_reset)
        h_update, cols = gate(1)
        update = jax.nn.sigmoid(x_gates[rows, cols] + h_update)
        inner, cols = gate(2)
        cand = jnp.tanh(x_gates[rows, cols] + reset * inner)
        new = (1.0 - update) * cand + update * prev
        prevs[rows, :] = prev
        resets[rows, :] = reset
        updates[rows, :] = update
        cands[rows, :] = cand
        inners[rows, :] = inner
        outs[rows, :] = new
        return new

    lax.fori_loop(0, steps, step, start[...])


def run_forward(weight_turned, x_gates, keep, start, steps, width):
    events, units = x_gates.shape[0], start.shape[1]
    saved = jax.ShapeDtypeStruct((events, units), f32)
    return pl.pallas_call(
        functools.partial(forward_kernel, steps, width),
        out_shape=(saved,) * 6,
        in_specs=[in_vmem()] * 4,
        out_specs=(in_vmem(),) * 6,
        scratch_shapes=[pltpu.VMEM(weight_turned.shape, bf16)] * 2,
        compiler_params=params(),
    )(weight_turned, x_gates, keep, start)


def backward_kernel(
    steps, weight, douts, keep, prevs, resets, updates, cands, inners, dgates, dstart, w_high, w_low
):
    rows_per, units = dstart.shape
    split_weight(weight, w_high, w_low)

    def step(i, dstate):
        t = steps - 1 - i
        rows = pl.ds(pl.multiple_of(t * rows_per, rows_per), rows_per)
        reset, update, cand = resets[rows, :], updates[rows, :], cands[rows, :]
        dh = douts[rows, :] + dstate
        dcand = dh * (1.0 - update) * (1.0 - cand * cand)
        dreset = dcand * inners[rows, :] * reset * (1.0 - reset)
        dupdate = dh * (prevs[rows, :] - cand) * update * (1.0 - update)
        dinner = dcand * reset
        dgates[rows, 0:units] = dreset
        dgates[rows, units : 2 * units] = dupdate
        dgates[rows, 2 * units : 3 * units] = dinner
        dgates[rows, 3 * units : 4 * units] = dcand
        total = dh * update
        for g, part in enumerate((dreset, dupdate, dinner)):
            pair = two_part(part)
            sect = slice(g * units, (g + 1) * units)
            first = jnp.dot(pair, w_high[sect, :], preferred_element_type=f32)
            second = jnp.dot(pair, w_low[sect, :], preferred_element_type=f32)
            total = total + (first[:rows_per] + first[rows_per:] + second[:rows_per])
        return keep[rows, :] * total

    dstart[...] = lax.fori_loop(0, steps, step, jnp.zeros((rows_per, units), f32))


def run_backward(weight, douts, keep, saved, rows_per, steps):
    events, units = douts.shape
    return pl.pallas_call(
        functools.partial(backward_kernel, steps),
        out_shape=(
            jax.ShapeDtypeStruct((events, 4 * units), f32),
            jax.ShapeDtypeStruct((rows_per, units), f32),
        ),
        in_specs=[in_vmem()] * 8,
        out_specs=(in_vmem(),) * 2,
        scratch_shapes=[pltpu.VMEM(weight.shape, bf16)] * 2,
        compiler_params=params(),
    )(weight, douts, keep, *saved)


def place():
    d = lax.axis_index("dp")
    c = lax.axis_index("col")
    return d // 4, (d // 2) % 2, d % 2, c, d


def greet(partners):
    barrier = pltpu.get_barrier_semaphore()
    for partner in partners:
        pl.semaphore_signal(barrier, inc=1, device_id=partner, device_id_type=MESH)
    pl.semaphore_wait(barrier, len(partners))


def reduce_kernel(first, second, out, mine, core_in, x_in, y_in, xy_in, yx_in, z_in, total, local_sem, send_sem, recv_sem):
    y, x, k, c, d = place()
    half = mine.shape[4] // 2
    core_to, x_to, y_to, far_to = ((d + 1 - 2 * k, c), (d + 2 - 4 * x, c), (d + 4 - 8 * y, c), (d + 6 - 4 * x - 8 * y, c))
    z_to = [lax.rem(c + m, 4) for m in (1, 2, 3)]
    greet([core_to, x_to, y_to, far_to] + [(d, z) for z in z_to])
    partials = (first, second)
    gates = first.shape[0]
    jobs = 2 * gates

    def send(j, slot, source, target, to):
        copy = pltpu.make_async_remote_copy(
            src_ref=source,
            dst_ref=target,
            send_sem=send_sem.at[j, slot],
            recv_sem=recv_sem.at[j, slot],
            device_id=to,
            device_id_type=MESH,
        )
        copy.start()
        return copy

    started = [{} for _ in range(jobs)]
    loads = []
    for j in range(jobs):
        source = partials[j // gates].at[j % gates]
        load = pltpu.make_async_copy(source.at[:, :, :, k], mine.at[j], local_sem.at[j])
        load.start()
        loads.append(load)
        started[j]["core"] = send(j, 0, source.at[:, :, :, 1 - k], core_in.at[j], core_to)

    def stage_core(j):
        loads[j].wait()
        started[j]["core"].wait_recv()
        for a in range(4):
            for b in range(2):
                for e in range(2):
                    mine[j, a, b, e] = mine[j, a, b, e] + core_in[j, a, b, e]
        started[j]["x"] = send(j, 1, mine.at[j, :, :, 1 - x, 0:half], x_in.at[j], x_to)
        started[j]["y"] = send(j, 2, mine.at[j, :, 1 - y, :, half : 2 * half], y_in.at[j], y_to)

    def stage_first(j):
        started[j]["x"].wait_recv()
        for a in range(4):
            for b in range(2):
                mine[j, a, b, x, 0:half] = mine[j, a, b, x, 0:half] + x_in[j, a, b]
        started[j]["xy"] = send(j, 3, mine.at[j, :, 1 - y, x, 0:half], xy_in.at[j], y_to)
        started[j]["y"].wait_recv()
        for a in range(4):
            for e in range(2):
                mine[j, a, y, e, half : 2 * half] = mine[j, a, y, e, half : 2 * half] + y_in[j, a, e]
        started[j]["yx"] = send(j, 4, mine.at[j, :, y, 1 - x, half : 2 * half], yx_in.at[j], x_to)

    def stage_second(j):
        started[j]["xy"].wait_recv()
        started[j]["yx"].wait_recv()
        for a in range(4):
            mine[j, a, y, x, 0:half] = mine[j, a, y, x, 0:half] + xy_in[j, a]
            mine[j, a, y, x, half : 2 * half] = mine[j, a, y, x, half : 2 * half] + yx_in[j, a]
        for m in range(3):
            started[j]["z", m] = send(j, 5 + m, mine.at[j, z_to[m], y, x], z_in.at[j, m], (d, z_to[m]))

    def stage_z(j):
        for m in range(3):
            started[j]["z", m].wait_recv()
        total[j] = ((mine[j, c, y, x] + z_in[j, 0]) + z_in[j, 1]) + z_in[j, 2]
        spot = out.at[j // gates, j % gates, d]
        keep = pltpu.make_async_copy(total.at[j], spot, local_sem.at[j])
        keep.start()
        started[j]["keep"] = keep
        for slot, (name, to) in enumerate((("gx", x_to), ("gy", y_to), ("gf", far_to), ("gc", core_to))):
            started[j][name] = send(j, 8 + slot, total.at[j], spot, to)

    def stage_share(j):
        for slot, (name, to) in enumerate((("gx", x_to), ("gy", y_to), ("gf", far_to))):
            started[j][name].wait_recv()
            spot = out.at[j // gates, j % gates, to[0]]
            started[j]["c" + name] = send(j, 12 + slot, spot, spot, core_to)

    def stage_end(j):
        for name in ("gc", "cgx", "cgy", "cgf"):
            started[j][name].wait_recv()
        for name, copy in started[j].items():
            if name == "keep":
                copy.wait()
            else:
                copy.wait_send()

    stages = (stage_core, stage_first, stage_second, stage_z, stage_share, stage_end)
    for tick in range(jobs + len(stages) - 1):
        for depth, stage in enumerate(stages):
            if 0 <= tick - depth < jobs:
                stage(tick - depth)


def reduce_weights(first, second, collective_id):
    gates, units, _ = first.shape
    piece = units // 32
    shape = (gates, 4, 2, 2, 2, piece, units)
    jobs = 2 * gates
    half = piece // 2
    return pl.pallas_call(
        reduce_kernel,
        out_shape=jax.ShapeDtypeStruct((2, gates, 8, piece, units), f32),
        in_specs=[pl.BlockSpec(memory_space=pl.ANY)] * 2,
        out_specs=pl.BlockSpec(memory_space=pl.ANY),
        scratch_shapes=[
            pltpu.VMEM((jobs, 4, 2, 2, piece, units), f32),
            pltpu.VMEM((jobs, 4, 2, 2, piece, units), f32),
            pltpu.VMEM((jobs, 4, 2, half, units), f32),
            pltpu.VMEM((jobs, 4, 2, half, units), f32),
            pltpu.VMEM((jobs, 4, half, units), f32),
            pltpu.VMEM((jobs, 4, half, units), f32),
            pltpu.VMEM((jobs, 3, piece, units), f32),
            pltpu.VMEM((jobs, piece, units), f32),
            pltpu.SemaphoreType.DMA((jobs,)),
            pltpu.SemaphoreType.DMA((jobs, 15)),
            pltpu.SemaphoreType.DMA((jobs, 15)),
        ],
        compiler_params=pltpu.CompilerParams(
            collective_id=collective_id, has_side_effects=True, vmem_limit_bytes=VMEM_BYTES
        ),
    )(first.reshape(shape), second.reshape(shape)).reshape(2, gates, 8 * piece, units)


UNITS = ((0, 0), (0, 1), (1, 0), (0, 2), (1, 1), (1, 2))


def head_kernel(
    chunk,
    width,
    item_ids,
    out_ids,
    embed,
    table,
    bias,
    own_in,
    own_hid,
    carried,
    all_in,
    all_hid,
    arrived,
    out_rows,
    padded,
    turned,
    item_rows,
    held,
    local_sem,
    send_sem,
    recv_sem,
    row_send,
    row_recv,
):
    y, x, k, c, d = place()
    i = pl.program_id(0)
    n = pl.num_programs(0) // 2
    core_to, x_to, y_to = (d + 1 - 2 * k, c), (d + 2 - 4 * x, c), (d + 4 - 8 * y, c)
    z_all = (c + 1 - 2 * lax.rem(c, 2), lax.rem(c + 2, 4), 3 - c)
    owns, alls = (own_in, own_hid), (all_in, all_hid)
    piece = own_in.shape[4]
    half = piece // 2
    block = item_rows.shape[2]
    items = item_rows.shape[1]
    carried_rows = carried.shape[1]
    events = items - carried_rows

    def send(u, slot):
        w, m = UNITS[u]
        z = z_all[m]
        every = alls[w]
        if slot == 0:
            source, target, to = owns[w].at[:, y, x, k], every.at[:, c, y, x, k], (d, z)
        elif slot in (4, 6):
            spot = (
                every.at[:, z, y, 1 - x, k, 0:half] if slot == 4 else every.at[:, z, 1 - y, x, k, half : 2 * half]
            )
            source, target, to = spot, spot, (y_to if slot == 4 else x_to)
        else:
            py, px, to = {
                1: (y, x, x_to),
                2: (y, x, y_to),
                3: (y, x, core_to),
                5: (y, 1 - x, core_to),
                7: (1 - y, x, core_to),
                8: (1 - y, 1 - x, core_to),
            }[slot]
            spot = every.at[:, z, py, px, k]
            source, target = spot, spot
        return pltpu.make_async_remote_copy(
            src_ref=source,
            dst_ref=target,
            send_sem=send_sem.at[u, slot],
            recv_sem=recv_sem.at[u, slot],
            device_id=to,
            device_id_type=MESH,
        )

    def load(w):
        return pltpu.make_async_copy(owns[w], held.at[w], local_sem.at[w])

    def keep(w):
        return pltpu.make_async_copy(held.at[w], alls[w].at[:, c], local_sem.at[2 + w])

    def keep_own(_):
        for w in range(2):
            load(w).wait()
            keep(w).start()

    def item_send(m):
        return pltpu.make_async_remote_copy(
            src_ref=item_rows.at[z_all[m]],
            dst_ref=arrived.at[:, pl.ds(pl.multiple_of(c * block, block), block)],
            send_sem=row_send.at[m],
            recv_sem=row_recv.at[m],
            device_id=(d, z_all[m]),
            device_id_type=MESH,
        )

    def begin_items(_):
        for m in range(3):
            item_send(m).start()

    def item_keep():
        return pltpu.make_async_copy(
            item_rows.at[c], arrived.at[:, pl.ds(pl.multiple_of(c * block, block), block)], local_sem.at[4]
        )

    def begin():
        greet([core_to, x_to, y_to] + [(d, z) for z in z_all])
        begin_z(0)
        begin_z(1)
        load(0).start()
        load(1).start()

    def begin_z(u):
        send(u, 0).start()

    def spread(u):
        send(u, 0).wait_recv()
        for slot in (1, 2, 3):
            send(u, slot).start()

    def forward(u):
        send(u, 1).wait_recv()
        send(u, 4).start()
        send(u, 5).start()
        send(u, 2).wait_recv()
        send(u, 6).start()
        send(u, 7).start()

    def far(u):
        send(u, 4).wait_recv()
        send(u, 6).wait_recv()
        send(u, 8).start()

    def close(u):
        for slot in (3, 5, 7, 8):
            send(u, slot).wait_recv()
        for slot in range(9):
            send(u, slot).wait_send()

    timeline = [(-1, begin, None), (4, keep_own, 0), (64, begin_items, 0)]
    timeline += [(at, begin_z, 2 + j) for j, at in enumerate((10, 18, 34, 50))]
    for u, at in enumerate((11, 23, 34, 46, 58, 90)):
        timeline += [(at, spread, u), (at + 12, forward, u), (at + 20, far, u)]
    timeline.sort(key=lambda entry: entry[0])
    last = 2 * n - 1

    @pl.when(i == 0)
    def _():
        padded[...] = jnp.zeros_like(padded)

    for at, action, u in timeline:
        if at < last:

            @pl.when(i == max(at, 0))
            def _(action=action, u=u):
                action() if u is None else action(u)

    @pl.when(i < n)
    def _():
        padded[0:width, :] = embed[...]

    @pl.when(i >= n)
    def _():
        padded[0:width, :] = table[...]
        padded[width : width + 1, :] = bias[...]

    spot = lax.rem(i, n) * chunk
    turned[pl.ds(pl.multiple_of(spot, chunk), chunk), :] = padded[...].T

    @pl.when(i == n - 1)
    def _():
        for z in range(4):

            def body(b, carry, z=z):
                for j in range(8):
                    row = item_ids[z * events + b * 8 + j]
                    item_rows[z, pl.ds(b * 8 + j, 1), :] = turned[pl.ds(row, 1), :]
                return carry

            lax.fori_loop(0, events // 8, body, 0)
            item_rows[z, events:items, :] = carried[z]
        item_keep().start()

    @pl.when(i == last)
    def _():
        def body(b, carry):
            for j in range(8):
                row = out_ids[b * 8 + j]
                out_rows[pl.ds(b * 8 + j, 1), :] = turned[pl.ds(row, 1), :]
            return carry

        lax.fori_loop(0, out_rows.shape[0] // 8, body, 0)
        for at, action, u in timeline:
            if at >= last:
                action(u)
        for u in range(6):
            close(u)
        for m in range(3):
            item_send(m).wait()
        for w in range(2):
            keep(w).wait()
        item_keep().wait()


def gather_all(embed, table, bias, item_ids, out_ids, own_in, own_hid, carried, collective_id):
    width, rows = embed.shape
    gates, block, units = own_in.shape
    piece = block // 8
    chunk = 128 * max(k for k in range(1, 9) if rows % (128 * k) == 0)
    n = rows // chunk
    items = item_ids.shape[0] // 4 + carried.shape[1]
    own_shape = (gates, 2, 2, 2, piece, units)
    all_shape = (gates, 4, 2, 2, 2, piece, units)
    smem = pl.BlockSpec(memory_space=pltpu.SMEM)
    hbm = pl.BlockSpec(memory_space=pl.ANY)
    all_in, all_hid, arrived, out_rows = pl.pallas_call(
        functools.partial(head_kernel, chunk, width),
        out_shape=(
            jax.ShapeDtypeStruct(all_shape, f32),
            jax.ShapeDtypeStruct(all_shape, f32),
            jax.ShapeDtypeStruct((items, units), f32),
            jax.ShapeDtypeStruct((out_ids.shape[0], block), f32),
        ),
        grid=(2 * n,),
        in_specs=[
            smem,
            smem,
            pl.BlockSpec((width, chunk), lambda i: (0, jnp.minimum(i, n - 1))),
            pl.BlockSpec((width, chunk), lambda i: (0, jnp.maximum(i - n, 0))),
            pl.BlockSpec((1, chunk), lambda i: (0, jnp.maximum(i - n, 0))),
            hbm,
            hbm,
            pl.BlockSpec(carried.shape, lambda i: (0, 0, 0)),
        ],
        out_specs=(hbm, hbm, hbm, pl.BlockSpec((out_ids.shape[0], block), lambda i: (0, 0))),
        scratch_shapes=[
            pltpu.VMEM((block, chunk), f32),
            pltpu.VMEM((rows, block), f32),
            pltpu.VMEM((4, items, block), f32),
            pltpu.VMEM((2,) + own_shape, f32),
            pltpu.SemaphoreType.DMA((5,)),
            pltpu.SemaphoreType.DMA((6, 9)),
            pltpu.SemaphoreType.DMA((6, 9)),
            pltpu.SemaphoreType.DMA((3,)),
            pltpu.SemaphoreType.DMA((3,)),
        ],
        compiler_params=pltpu.CompilerParams(
            collective_id=collective_id, has_side_effects=True, vmem_limit_bytes=VMEM_BYTES
        ),
    )(item_ids, out_ids, embed, table, bias, own_in.reshape(own_shape), own_hid.reshape(own_shape), carried)
    return (
        all_in.reshape(gates, 4 * block, units),
        all_hid.reshape(gates, 4 * block, units),
        arrived,
        out_rows,
    )


def pad_units(weight, bias, n_col, block):
    gates, own, full = weight.shape
    part = full // n_col
    rows = weight.reshape(gates, own, n_col, part)
    rows = jnp.pad(rows, ((0, 0), (0, block - own), (0, 0), (0, block - part)))
    rows = rows.reshape(gates, block, n_col * block)
    return rows.at[:, :own, part].set(bias)


def gather_weight(own, n_dp):
    gates, block, units = own.shape
    flat = own.reshape(n_dp, gates * block // n_dp, units)
    piece = lax.dynamic_index_in_dim(flat, lax.axis_index("dp"), 0, keepdims=False)
    every = lax.all_gather(piece, ("col", "dp"))
    every = every.reshape(-1, gates, block, units)
    return jnp.moveaxis(every, 0, 1).reshape(gates, -1, units)


def reduce_weight(partial, n_dp, n_col):
    gates, rows, units = partial.shape
    block = rows // n_col
    parts = jnp.moveaxis(partial.reshape(gates, n_col, block, units), 1, 0)
    parts = jnp.moveaxis(parts.reshape(n_col, n_dp, gates * block // n_dp, units), 1, 0)
    mine = lax.psum_scatter(parts, "dp", scatter_dimension=0)
    mine = lax.psum_scatter(mine, "col", scatter_dimension=0)
    return lax.all_gather(mine, "dp").reshape(gates, block, units)


def swap_col(rows, n_col):
    return lax.all_to_all(rows, "col", split_axis=0, concat_axis=0, tiled=True)


def unpad_last(value, n_col, part):
    block = value.shape[-1] // n_col
    return value.reshape(value.shape[:-1] + (n_col, block))[..., :part].reshape(value.shape[:-1] + (n_col * part,))


def local(
    n_dp,
    n_col,
    item_ids,
    target_ids,
    negative_ids,
    reset_mask,
    carry_flags,
    carried_state,
    embed_table,
    input_weight,
    hidden_weight,
    gate_bias,
    hidden_bias,
    out_table,
    out_bias,
):
    sessions, steps = item_ids.shape
    own_sessions = sessions // n_col
    rows_per = round_up(own_sessions, ROWS8)
    width = embed_table.shape[0]
    table_rows = embed_table.shape[1]
    own_rows = table_rows // n_dp
    block = round_up(width + 1, LANES)
    units = n_col * block
    events = steps * rows_per
    direct = n_dp == 8 and n_col == 4 and block % 64 == 0
    factor = 1.0 / steps
    dp_at, col_at = lax.axis_index("dp"), lax.axis_index("col")

    def by_owner(value):
        value = jnp.moveaxis(value.reshape(n_col, own_sessions, steps), 1, 2)
        value = jnp.pad(value, ((0, 0), (0, 0), (0, rows_per - own_sessions)))
        return value.reshape(-1)

    item_flat, target_flat = by_owner(item_ids), by_owner(target_ids)
    own_keep = lax.dynamic_index_in_dim(
        by_owner(1 - reset_mask).reshape(n_col, events, 1), col_at, 0, keepdims=False
    ).astype(f32)
    valid = jnp.tile(jnp.arange(rows_per) < own_sessions, steps)
    lane = jnp.arange(units) % block
    first_pad = jnp.arange(units) == width

    own_in = pad_units(input_weight, gate_bias, n_col, block)
    no_bias = jnp.zeros_like(hidden_bias)
    own_hid = pad_units(hidden_weight, jnp.stack([no_bias, no_bias, hidden_bias]), n_col, block)

    all_items = lax.all_gather(item_flat, "dp", tiled=True)
    all_targets = lax.all_gather(target_flat, "dp", tiled=True)

    def ordered(ids):
        ids, order = lax.sort((ids, lax.iota(jnp.int32, ids.shape[0])), num_keys=1)
        return order, ids

    carried = (carry_flags.astype(f32)[:, None] * carried_state).reshape(n_col, own_sessions, width)
    carried = jnp.pad(carried, ((0, 0), (0, rows_per - own_sessions), (0, block - width)))
    neg_count = negative_ids.shape[0]
    own_negs = lax.dynamic_slice_in_dim(negative_ids, dp_at * (neg_count // n_dp), neg_count // n_dp)
    out_ids = jnp.concatenate([target_flat, own_negs])
    if direct:
        all_in, all_hid, arrived, out_rows = gather_all(
            embed_table, out_table, out_bias[None, :], item_flat, out_ids, own_in, own_hid, carried, 1
        )
    else:
        all_hid = gather_weight(own_hid, n_dp)
        all_in = gather_weight(own_in, n_dp)
        no_row = jnp.zeros((1, table_rows), f32)
        item_rows = gather_rows(embed_table, no_row, item_flat, block).reshape(n_col, events, block)
        arrived = swap_col(jnp.concatenate([item_rows, carried], axis=1), n_col)
        arrived = jnp.moveaxis(arrived, 0, 1).reshape(events + rows_per, units)
        out_rows = gather_rows(out_table, out_bias[None, :], out_ids, block)
    all_hid, all_in = all_hid.reshape(-1, units), all_in.reshape(-1, units)
    inputs = jnp.where(first_pad, 1.0, arrived[:events])
    start = arrived[events:]
    targets = swap_col(out_rows[: n_col * events].reshape(n_col, events, block), n_col)
    targets = jnp.moveaxis(targets, 0, 1).reshape(events, units)
    negs = lax.all_gather(out_rows[n_col * events :], ("dp", "col")).reshape(n_dp, n_col, -1, block)
    negs = jnp.moveaxis(negs, 1, 2).reshape(neg_count, units)

    x_gates = lax.dot_general(inputs, all_in, (((1,), (1,)), ((), ())), precision=high)
    prevs, resets, updates, cands, inners, outs = run_forward(
        all_hid.T, x_gates, own_keep, start, steps, width
    )

    shares = jnp.where(lane == width, 1.0 / n_col, jnp.where(lane < width, outs, 0.0))
    pos_score = jnp.sum(shares * targets, axis=-1, keepdims=True)
    neg_score = lax.dot_general(shares, negs, (((1,), (1,)), ((), ())), precision=high)
    top = jnp.max(neg_score, axis=-1, keepdims=True)
    expd = jnp.exp(neg_score - top)
    weight = expd / jnp.sum(expd, axis=-1, keepdims=True)
    sig = jax.nn.sigmoid(pos_score - neg_score)
    ppos = jnp.sum(weight * sig, axis=-1, keepdims=True)
    quad = jnp.sum(weight * neg_score * neg_score, axis=-1, keepdims=True)
    slope = jnp.sum(weight * sig * (1.0 - sig), axis=-1, keepdims=True)
    own_loss = (-jnp.log(ppos) + quad).reshape(steps, rows_per)[:, :own_sessions]
    loss = lax.all_gather(own_loss.T, "col", tiled=True)
    dneg = factor * weight * (1.0 - sig * sig / ppos + neg_score * neg_score + 2.0 * neg_score - quad)
    dneg = jnp.where(valid[:, None], dneg, 0.0)
    dpos = jnp.where(valid[:, None], -factor * slope / ppos, 0.0)
    douts = jnp.dot(dneg, negs, precision=high) + dpos * targets
    douts = jnp.where(lane < width, douts, 0.0)
    neg_part = lax.dot_general(dneg, shares, (((0,), (0,)), ((), ())), precision=high)
    target_part = dpos * shares

    neg_own = lax.psum_scatter(neg_part.reshape(n_dp, -1, units), "dp", scatter_dimension=0)
    neg_own = jnp.moveaxis(neg_own.reshape(-1, n_col, block), 1, 0)
    neg_own = lax.psum_scatter(neg_own, "col", scatter_dimension=0)
    neg_all = lax.all_gather(neg_own, "dp", tiled=True)
    target_own = swap_col(jnp.moveaxis(target_part.reshape(events, n_col, block), 1, 0), n_col)
    target_all = lax.all_gather(target_own.reshape(-1, block), "dp", tiled=True)
    low = (dp_at * own_rows).astype(jnp.int32)
    grad_out, grad_obias = scatter_rows(
        [ordered(all_targets) + (target_all,), ordered(negative_ids) + (neg_all,)],
        low,
        own_rows,
        width,
        block,
    )
    grad_obias = grad_obias[0] * n_col

    dgates, dstart = run_backward(
        all_hid, douts, own_keep, (prevs, resets, updates, cands, inners), rows_per, steps
    )
    dx = jnp.concatenate([dgates[:, : 2 * units], dgates[:, 3 * units :]], axis=1)
    dh = dgates[:, : 3 * units]
    hid_part = lax.dot_general(dh, prevs, (((0,), (0,)), ((), ())), precision=high)
    in_part = lax.dot_general(dx, inputs, (((0,), (0,)), ((), ())), precision=high)
    dinputs = jnp.dot(dx, all_in, precision=high)
    gates = input_weight.shape[0]
    back = jnp.concatenate([dinputs, dstart], axis=0).reshape(events + rows_per, n_col, block)
    back = swap_col(jnp.moveaxis(back, 1, 0), n_col)
    grad_carried = carry_flags.astype(f32)[:, None] * back[:, events : events + own_sessions, :width].reshape(
        sessions, width
    )
    item_all = lax.all_gather(back[:, :events].reshape(-1, block), "dp", tiled=True)
    grad_embed, _ = scatter_rows([ordered(all_items) + (item_all,)], low, own_rows, width, block)
    in_part, hid_part = in_part.reshape(gates, units, units), hid_part.reshape(gates, units, units)
    if direct:
        reduced = reduce_weights(in_part, hid_part, 2)
        grad_in, grad_hid = reduced[0], reduced[1]
    else:
        grad_in = reduce_weight(in_part, n_dp, n_col)
        grad_hid = reduce_weight(hid_part, n_dp, n_col)
    grad_in, grad_hid = grad_in[:, :width], grad_hid[:, :width]
    return (
        loss,
        grad_embed,
        unpad_last(grad_in, n_col, width),
        unpad_last(grad_hid, n_col, width),
        grad_in[:, :, width],
        grad_hid[gates - 1, :, width],
        grad_out,
        grad_obias,
        grad_carried,
    )


def solution(mesh):
    in_specs = (
        P("dp", None),
        P("dp", None),
        P(),
        P("dp", None),
        P("dp"),
        P("dp", "col"),
        P("col", None),
        P(None, "col", None),
        P(None, "col", None),
        P(None, "col"),
        P("col"),
        P("col", None),
        P(),
    )
    out_specs = (
        P("dp", None),
        P("col", "dp"),
        P(None, "col", None),
        P(None, "col", None),
        P(None, "col"),
        P("col"),
        P("col", "dp"),
        P("dp"),
        P("dp", "col"),
    )
    body = functools.partial(local, mesh.shape["dp"], mesh.shape["col"])
    return jax.shard_map(body, mesh=mesh, in_specs=in_specs, out_specs=out_specs, check_vma=False)
```

```python
import functools

import jax
import jax.numpy as jnp
from jax import lax
from jax.experimental import pallas as pl
from jax.experimental.pallas import tpu as pltpu
from jax.sharding import PartitionSpec as P

LANES = 128
ROWS8 = 8
VMEM_BYTES = 60 << 20
f32 = jnp.float32
bf16 = jnp.bfloat16
high = lax.Precision.HIGH
MESH = pl.DeviceIdType.MESH


def round_up(value, unit):
    return -(-value // unit) * unit


def params():
    return pltpu.CompilerParams(vmem_limit_bytes=VMEM_BYTES)


def takes(micros):
    return pl.CostEstimate(flops=int(micros * 1.1e9), bytes_accessed=1 << 20, transcendentals=0)


def in_vmem():
    return pl.BlockSpec(memory_space=pltpu.VMEM)


def in_smem():
    return pl.BlockSpec(memory_space=pltpu.SMEM)


def gather_kernel(chunk, count, width, ids, table, bias, out, padded, turned):
    step = pl.program_id(0)

    @pl.when(step == 0)
    def _():
        padded[...] = jnp.zeros_like(padded)

    padded[0:width, :] = table[...]
    padded[width : width + 1, :] = bias[...]
    turned[pl.ds(pl.multiple_of(step * chunk, chunk), chunk), :] = padded[...].T

    @pl.when(step == pl.num_programs(0) - 1)
    def _():
        def body(block, carry):
            for j in range(ROWS8):
                row = ids[block * ROWS8 + j]
                out[pl.ds(block * ROWS8 + j, 1), :] = turned[pl.ds(row, 1), :]
            return carry

        lax.fori_loop(0, count // ROWS8, body, 0)


def gather_rows(table, bias, ids, block):
    width, rows = table.shape
    count = ids.shape[0]
    chunk = LANES * max(k for k in range(1, 9) if rows % (LANES * k) == 0)
    return pl.pallas_call(
        functools.partial(gather_kernel, chunk, count, width),
        out_shape=jax.ShapeDtypeStruct((count, block), f32),
        grid_spec=pltpu.PrefetchScalarGridSpec(
            num_scalar_prefetch=1,
            grid=(rows // chunk,),
            in_specs=[
                pl.BlockSpec((width, chunk), lambda i, ids: (0, i)),
                pl.BlockSpec((1, chunk), lambda i, ids: (0, i)),
            ],
            out_specs=pl.BlockSpec((count, block), lambda i, ids: (0, 0)),
            scratch_shapes=[pltpu.VMEM((block, chunk), f32), pltpu.VMEM((rows, block), f32)],
        ),
        compiler_params=params(),
    )(ids, table, bias)


def scatter_kernel(width, n_lists, *refs):
    bounds = refs[0]
    lists = refs[1 : 1 + 3 * n_lists]
    out, bias_out, acc = refs[1 + 3 * n_lists :]
    acc[...] = jnp.zeros_like(acc)
    low = bounds[0]
    for k in range(n_lists):
        rows_of, ids, data = lists[3 * k : 3 * k + 3]

        def body(i, carry):
            spot = pl.ds(ids[i] - low, 1)
            acc[spot, :] = acc[spot, :] + data[pl.ds(rows_of[i], 1), :]
            return carry

        lax.fori_loop(bounds[1 + 2 * k], bounds[2 + 2 * k], body, 0)
    for j in range(acc.shape[0] // LANES):
        cols = slice(j * LANES, (j + 1) * LANES)
        turned = acc[cols, :].T
        out[:, cols] = turned[:width]
        bias_out[:, cols] = turned[width : width + 1]


def scatter_rows(lists, low, own_rows, width, block):
    ends = [low]
    operands, specs = [], []
    for order, ids, data in lists:
        ends += [jnp.sum(ids < low, dtype=jnp.int32), jnp.sum(ids < low + own_rows, dtype=jnp.int32)]
        operands += [order, ids, data]
        specs += [in_smem(), in_smem(), in_vmem()]
    return pl.pallas_call(
        functools.partial(scatter_kernel, width, len(lists)),
        out_shape=(
            jax.ShapeDtypeStruct((width, own_rows), f32),
            jax.ShapeDtypeStruct((1, own_rows), f32),
        ),
        in_specs=[in_smem()] + specs,
        out_specs=(in_vmem(), in_vmem()),
        scratch_shapes=[pltpu.VMEM((own_rows, block), f32)],
        cost_estimate=takes(20),
        compiler_params=params(),
    )(jnp.stack(ends), *operands)


def split_weight(weight, high_part, low_part):
    step = 128

    @pl.loop(0, weight.shape[0] // step)
    def _(i):
        rows = pl.ds(pl.multiple_of(i * step, step), step)
        value = weight[rows, :]
        top = value.astype(bf16)
        high_part[rows, :] = top
        low_part[rows, :] = (value - top.astype(f32)).astype(bf16)


def two_part(value):
    top = value.astype(bf16).astype(f32)
    return jnp.concatenate([top, value - top], axis=0).astype(bf16)


def forward_kernel(
    steps,
    width,
    hidden,
    entering,
    inputs,
    keep,
    start,
    prevs,
    resets,
    updates,
    cands,
    inners,
    outs,
    w_high,
    w_low,
    x_gates,
    hid_buf,
    in_buf,
    pair_buf,
    sem,
):
    rows_per, units = start.shape
    step_rows = hid_buf.shape[1]
    chunks = hidden.shape[0] // step_rows

    def load(i, slot):
        rows = pl.ds(pl.multiple_of(i * step_rows, step_rows), step_rows)
        return (
            pltpu.make_async_copy(hidden.at[rows], hid_buf.at[slot], sem.at[0, slot]),
            pltpu.make_async_copy(entering.at[rows], in_buf.at[slot], sem.at[1, slot]),
        )

    for copy in load(0, 0):
        copy.start()
    top = inputs[...].astype(bf16)
    pair_buf[0] = top
    pair_buf[1] = (inputs[...] - top.astype(f32)).astype(bf16)

    @pl.loop(0, chunks)
    def _(i):
        slot = lax.rem(i, 2)

        @pl.when(i + 1 < chunks)
        def _():
            for copy in load(i + 1, 1 - slot):
                copy.start()

        for copy in load(i, slot):
            copy.wait()
        cols = pl.ds(pl.multiple_of(i * step_rows, step_rows), step_rows)
        turned = hid_buf[slot].T
        first = turned.astype(bf16)
        w_high[:, cols] = first
        w_low[:, cols] = (turned - first.astype(f32)).astype(bf16)
        value = in_buf[slot]
        first = value.astype(bf16)
        second = (value - first.astype(f32)).astype(bf16)
        over = (((1,), (1,)), ((), ()))
        x_gates[:, cols] = (
            lax.dot_general(pair_buf[0], first, over, preferred_element_type=f32)
            + lax.dot_general(pair_buf[1], first, over, preferred_element_type=f32)
            + lax.dot_general(pair_buf[0], second, over, preferred_element_type=f32)
        )

    lane = lax.broadcasted_iota(jnp.int32, (rows_per, units), 1)

    def step(t, state):
        rows = pl.ds(pl.multiple_of(t * rows_per, rows_per), rows_per)
        prev = jnp.where(lane == width, 1.0, keep[rows, :] * state)
        pair = two_part(prev)

        def gate(g):
            cols = slice(g * units, (g + 1) * units)
            first = jnp.dot(pair, w_high[:, cols], preferred_element_type=f32)
            second = jnp.dot(pair, w_low[:, cols], preferred_element_type=f32)
            return first[:rows_per] + first[rows_per:] + second[:rows_per], cols

        h_reset, cols = gate(0)
        reset = jax.nn.sigmoid(x_gates[rows, cols] + h_reset)
        h_update, cols = gate(1)
        update = jax.nn.sigmoid(x_gates[rows, cols] + h_update)
        inner, cols = gate(2)
        cand = jnp.tanh(x_gates[rows, cols] + reset * inner)
        new = (1.0 - update) * cand + update * prev
        prevs[rows, :] = prev
        resets[rows, :] = reset
        updates[rows, :] = update
        cands[rows, :] = cand
        inners[rows, :] = inner
        outs[rows, :] = new
        return new

    lax.fori_loop(0, steps, step, start[...])


def run_forward(hidden, entering, inputs, keep, start, steps, width):
    events, units = inputs.shape
    saved = jax.ShapeDtypeStruct((events, units), f32)
    step_rows = units // 4
    hbm = pl.BlockSpec(memory_space=pl.ANY)
    return pl.pallas_call(
        functools.partial(forward_kernel, steps, width),
        out_shape=(saved,) * 6,
        in_specs=[hbm, hbm] + [in_vmem()] * 3,
        out_specs=(in_vmem(),) * 6,
        scratch_shapes=[
            pltpu.VMEM(hidden.shape[::-1], bf16),
            pltpu.VMEM(hidden.shape[::-1], bf16),
            pltpu.VMEM((events, hidden.shape[0]), f32),
            pltpu.VMEM((2, step_rows, units), f32),
            pltpu.VMEM((2, step_rows, units), f32),
            pltpu.VMEM((2, events, units), bf16),
            pltpu.SemaphoreType.DMA((2, 2)),
        ],
        cost_estimate=takes(75),
        compiler_params=params(),
    )(hidden, entering, inputs, keep, start)


def backward_kernel(
    steps, weight, douts, keep, prevs, resets, updates, cands, inners, dgates, dstart, w_high, w_low
):
    rows_per, units = dstart.shape
    split_weight(weight, w_high, w_low)

    def step(i, dstate):
        t = steps - 1 - i
        rows = pl.ds(pl.multiple_of(t * rows_per, rows_per), rows_per)
        reset, update, cand = resets[rows, :], updates[rows, :], cands[rows, :]
        dh = douts[rows, :] + dstate
        dcand = dh * (1.0 - update) * (1.0 - cand * cand)
        dreset = dcand * inners[rows, :] * reset * (1.0 - reset)
        dupdate = dh * (prevs[rows, :] - cand) * update * (1.0 - update)
        dinner = dcand * reset
        dgates[rows, 0:units] = dreset
        dgates[rows, units : 2 * units] = dupdate
        dgates[rows, 2 * units : 3 * units] = dinner
        dgates[rows, 3 * units : 4 * units] = dcand
        total = dh * update
        for g, part in enumerate((dreset, dupdate, dinner)):
            pair = two_part(part)
            sect = slice(g * units, (g + 1) * units)
            first = jnp.dot(pair, w_high[sect, :], preferred_element_type=f32)
            second = jnp.dot(pair, w_low[sect, :], preferred_element_type=f32)
            total = total + (first[:rows_per] + first[rows_per:] + second[:rows_per])
        return keep[rows, :] * total

    dstart[...] = lax.fori_loop(0, steps, step, jnp.zeros((rows_per, units), f32))


def run_backward(weight, douts, keep, saved, rows_per, steps):
    events, units = douts.shape
    return pl.pallas_call(
        functools.partial(backward_kernel, steps),
        out_shape=(
            jax.ShapeDtypeStruct((events, 4 * units), f32),
            jax.ShapeDtypeStruct((rows_per, units), f32),
        ),
        in_specs=[in_vmem()] * 8,
        out_specs=(in_vmem(),) * 2,
        scratch_shapes=[pltpu.VMEM(weight.shape, bf16)] * 2,
        cost_estimate=takes(67),
        compiler_params=params(),
    )(weight, douts, keep, *saved)


def place():
    d = lax.axis_index("dp")
    c = lax.axis_index("col")
    return d // 4, (d // 2) % 2, d % 2, c, d


def greet(partners):
    barrier = pltpu.get_barrier_semaphore()
    for partner in partners:
        pl.semaphore_signal(barrier, inc=1, device_id=partner, device_id_type=MESH)
    pl.semaphore_wait(barrier, len(partners))


class Spot:
    def __init__(self):
        self.y, self.x, self.k, self.c, self.d = place()
        y, x, k, c, d = self.y, self.x, self.k, self.c, self.d
        self.x_d, self.y_d, self.core_d = d + 2 - 4 * x, d + 4 - 8 * y, d + 1 - 2 * k
        self.far_d = d + 6 - 4 * x - 8 * y
        self.core_to, self.x_to, self.y_to, self.far_to = (self.core_d, c), (self.x_d, c), (self.y_d, c), (self.far_d, c)
        self.z_to = (c + 1 - 2 * lax.rem(c, 2), lax.rem(c + 2, 4), 3 - c)

    def greet_all(self):
        greet([self.core_to, self.x_to, self.y_to, self.far_to] + [(self.d, z) for z in self.z_to])


def remote(source, target, send, recv, to):
    copy = pltpu.make_async_remote_copy(
        src_ref=source, dst_ref=target, send_sem=send, recv_sem=recv, device_id=to, device_id_type=MESH
    )
    copy.start()
    return copy


class RowsFlow:
    def __init__(self, spot, outgoing, z_rows, every, local_sem, send_sem, recv_sem):
        self.spot, self.outgoing, self.z_rows, self.every = spot, outgoing, z_rows, every
        self.local_sem, self.send_sem, self.recv_sem = local_sem, send_sem, recv_sem
        self.started = {}
        self.rows = every.shape[2]
        self.sources = (spot.c,) + spot.z_to

    def send(self, u, slot, source, target, to):
        return remote(source, target, self.send_sem.at[u, slot], self.recv_sem.at[u, slot], to)

    def begin(self):
        spot = self.spot
        for m in range(3):
            z = spot.z_to[m]
            self.started["z", m] = self.send(1 + m, 0, self.outgoing.at[z], self.z_rows.at[spot.c], (spot.d, z))
        self.spread(0)

    def spread(self, u):
        spot, src = self.spot, self.sources[u]
        if u > 0:
            self.started["z", u - 1].wait_recv()
            source = self.z_rows.at[src, 0 : self.rows]
        else:
            source = self.outgoing.at[src, 0 : self.rows]
        target = self.every.at[spot.d, src]
        keep = pltpu.make_async_copy(source, target, self.local_sem.at[u])
        keep.start()
        self.started["keep", u] = keep
        for slot, (name, to) in enumerate((("x", spot.x_to), ("y", spot.y_to), ("c", spot.core_to))):
            self.started[name, u] = self.send(u, 1 + slot, source, target, to)

    def forward(self, u):
        spot, src, mid = self.spot, self.sources[u], self.rows // 2
        self.started["x", u].wait_recv()
        piece = self.every.at[spot.x_d, src, 0:mid]
        self.started["xy", u] = self.send(u, 4, piece, piece, spot.y_to)
        piece = self.every.at[spot.x_d, src]
        self.started["xc", u] = self.send(u, 5, piece, piece, spot.core_to)
        self.started["y", u].wait_recv()
        piece = self.every.at[spot.y_d, src, mid : self.rows]
        self.started["yx", u] = self.send(u, 6, piece, piece, spot.x_to)
        piece = self.every.at[spot.y_d, src]
        self.started["yc", u] = self.send(u, 7, piece, piece, spot.core_to)

    def far(self, u):
        spot, src = self.spot, self.sources[u]
        self.started["xy", u].wait_recv()
        self.started["yx", u].wait_recv()
        piece = self.every.at[spot.far_d, src]
        self.started["fc", u] = self.send(u, 8, piece, piece, spot.core_to)

    def close(self):
        for u in range(4):
            for name in ("c", "xc", "yc", "fc"):
                self.started[name, u].wait_recv()
            self.started["keep", u].wait()
        for (name, _), copy in self.started.items():
            if name != "keep":
                copy.wait_send()


class SumFlow:
    def __init__(self, spot, mine, core_in, x_in, y_in, xy_in, yx_in, z_in, total, out_at, local_sem, send_sem, recv_sem):
        self.spot, self.mine, self.core_in, self.out_at = spot, mine, core_in, out_at
        self.x_in, self.y_in, self.xy_in, self.yx_in, self.z_in, self.total = x_in, y_in, xy_in, yx_in, z_in, total
        self.local_sem, self.send_sem, self.recv_sem = local_sem, send_sem, recv_sem
        self.started = [{} for _ in range(mine.shape[0])]
        self.half = mine.shape[4] // 2

    def send(self, j, slot, source, target, to):
        return remote(source, target, self.send_sem.at[j, slot], self.recv_sem.at[j, slot], to)

    def over_core(self, j, source):
        self.started[j]["core"] = self.send(j, 0, source, self.core_in.at[j], self.spot.core_to)

    def core(self, j):
        spot, mine, half, started = self.spot, self.mine, self.half, self.started[j]
        started["core"].wait_recv()

        @pl.loop(0, 4)
        def _(a):
            for b in range(2):
                for e in range(2):
                    mine[j, a, b, e] = mine[j, a, b, e] + self.core_in[j, a, b, e]

        started["x"] = self.send(j, 1, mine.at[j, :, :, 1 - spot.x, 0:half], self.x_in.at[j], spot.x_to)
        started["y"] = self.send(j, 2, mine.at[j, :, 1 - spot.y, :, half : 2 * half], self.y_in.at[j], spot.y_to)

    def first(self, j):
        spot, mine, half, started = self.spot, self.mine, self.half, self.started[j]
        x, y = spot.x, spot.y
        started["x"].wait_recv()
        for a in range(4):
            for b in range(2):
                mine[j, a, b, x, 0:half] = mine[j, a, b, x, 0:half] + self.x_in[j, a, b]
        started["xy"] = self.send(j, 3, mine.at[j, :, 1 - y, x, 0:half], self.xy_in.at[j], spot.y_to)
        started["y"].wait_recv()
        for a in range(4):
            for e in range(2):
                mine[j, a, y, e, half : 2 * half] = mine[j, a, y, e, half : 2 * half] + self.y_in[j, a, e]
        started["yx"] = self.send(j, 4, mine.at[j, :, y, 1 - x, half : 2 * half], self.yx_in.at[j], spot.x_to)

    def second(self, j):
        spot, mine, half, started = self.spot, self.mine, self.half, self.started[j]
        x, y = spot.x, spot.y
        started["xy"].wait_recv()
        started["yx"].wait_recv()
        for a in range(4):
            mine[j, a, y, x, 0:half] = mine[j, a, y, x, 0:half] + self.xy_in[j, a]
            mine[j, a, y, x, half : 2 * half] = mine[j, a, y, x, half : 2 * half] + self.yx_in[j, a]
        for m in range(3):
            z = spot.z_to[m]
            started["z", m] = self.send(j, 5 + m, mine.at[j, z, y, x], self.z_in.at[j, m], (spot.d, z))

    def along(self, j):
        spot, started, total = self.spot, self.started[j], self.total
        for m in range(3):
            started["z", m].wait_recv()
        own = self.mine[j, spot.c, spot.y, spot.x]
        total[j] = ((own + self.z_in[j, 0]) + self.z_in[j, 1]) + self.z_in[j, 2]
        target = self.out_at(j, spot.d)
        started["keep"] = pltpu.make_async_copy(total.at[j], target, self.local_sem.at[j])
        started["keep"].start()
        pairs = (("gx", spot.x_to), ("gy", spot.y_to), ("gf", spot.far_to), ("gc", spot.core_to))
        for slot, (name, to) in enumerate(pairs):
            started[name] = self.send(j, 8 + slot, total.at[j], target, to)

    def share(self, j):
        spot, started = self.spot, self.started[j]
        for slot, (name, to) in enumerate((("gx", spot.x_to), ("gy", spot.y_to), ("gf", spot.far_to))):
            started[name].wait_recv()
            piece = self.out_at(j, to[0])
            started["c" + name] = self.send(j, 12 + slot, piece, piece, spot.core_to)

    def end(self, j, core_sent=False):
        started = self.started[j]
        for name in ("gc", "cgx", "cgy", "cgf"):
            started[name].wait_recv()
        for name, copy in started.items():
            if name == "keep":
                copy.wait()
            elif not (name == "core" and core_sent):
                copy.wait_send()


def sum_scratch(jobs, piece, lanes):
    half = piece // 2
    return [
        pltpu.VMEM((jobs, 4, 2, 2, piece, lanes), f32),
        pltpu.VMEM((jobs, 4, 2, 2, piece, lanes), f32),
        pltpu.VMEM((jobs, 4, 2, half, lanes), f32),
        pltpu.VMEM((jobs, 4, 2, half, lanes), f32),
        pltpu.VMEM((jobs, 4, half, lanes), f32),
        pltpu.VMEM((jobs, 4, half, lanes), f32),
        pltpu.VMEM((jobs, 3, piece, lanes), f32),
        pltpu.VMEM((jobs, piece, lanes), f32),
    ]


def flow_sems(jobs):
    dma = pltpu.SemaphoreType.DMA
    return [dma((jobs,)), dma((jobs, 15)), dma((jobs, 15)), dma((4,)), dma((4, 9)), dma((4, 9))]


GATE_OF = ((0, 1, 3), (0, 1, 2))


def split_two(value):
    top = value.astype(bf16)
    return top, (value - top.astype(f32)).astype(bf16)


def three_products(first, second, over):
    def product(a, b):
        return lax.dot_general(a, b, (over, ((), ())), preferred_element_type=f32)

    return product(first[0], second[0]) + product(first[1], second[0]) + product(first[0], second[1])


def tail_kernel(
    inputs,
    prevs,
    dgates,
    dstart,
    entering,
    out,
    item_all,
    start_all,
    mine,
    core_in,
    x_in,
    y_in,
    xy_in,
    yx_in,
    z_in,
    total,
    core_out,
    turned,
    acts,
    flow,
    w_flow,
    din,
    z_rows,
    flow_sem,
    start_sem,
    sum_local,
    sum_send,
    sum_recv,
    row_local,
    row_send,
    row_recv,
):
    spot = Spot()
    spot.greet_all()
    c, k = spot.c, spot.k
    jobs, _, _, _, piece, units = mine.shape
    block = din.shape[2]
    events = acts.shape[2]
    gates = jobs // 2
    sums = SumFlow(
        spot, mine, core_in, x_in, y_in, xy_in, yx_in, z_in, total,
        lambda j, d: out.at[j // gates, j % gates, d], sum_local, sum_send, sum_recv,
    )
    rows = RowsFlow(spot, din, z_rows, item_all, row_local, row_send, row_recv)

    def gate_cols(g):
        return dgates.at[:, pl.ds(g * units, units)]

    queue = [inputs, gate_cols(0), gate_cols(1), gate_cols(3), prevs, gate_cols(2)]

    def flow_copy(n):
        return pltpu.make_async_copy(queue[n], flow.at[n % 2], flow_sem.at[n % 2])

    def w_copy(n, slot):
        rows = pl.ds(pl.multiple_of(n * block, block), block)
        return pltpu.make_async_copy(entering.at[rows], w_flow.at[slot], flow_sem.at[2 + slot])

    flow_copy(0).start()
    flow_copy(1).start()
    w_copy(0, 0).start()

    def next_flow(n):
        if n + 2 < len(queue):
            flow_copy(n + 2).start()

    def take_act(n, w):
        flow_copy(n).wait()
        acts[w, 0], acts[w, 1] = split_two(flow[n % 2])
        next_flow(n)

    def take_gate(n, g, at):
        flow_copy(n).wait()

        @pl.loop(0, 4)
        def _(b):
            cols = pl.ds(pl.multiple_of(b * block, block), block)
            value = flow[n % 2, :, cols]
            turned[g, 0, b], turned[g, 1, b] = split_two(value.T)
            if at is not None:
                chunk = 4 * at + b
                slot = lax.rem(b, 2)

                @pl.when(chunk + 1 < 12)
                def _():
                    w_copy(chunk + 1, 1 - slot).start()

                w_copy(chunk, slot).wait()
                share = three_products(split_two(value), split_two(w_flow[slot]), ((1,), (0,)))
                for e in range(4):
                    part = share[:, e * block : (e + 1) * block]
                    if at == 0:
                        before = jnp.where(b == 0, 0.0, din[e, 0:events, :])
                    else:
                        before = din[e, 0:events, :]
                    din[e, 0:events, :] = before + part

        next_flow(n)

    def rows_begin():
        for e in range(4):
            din[e, events:, :] = dstart[:, e * block : (e + 1) * block]
        rows.begin()

    def rows_end():
        keeps = [
            pltpu.make_async_copy(din.at[c, events:], start_all.at[c], start_sem.at[0]),
        ] + [
            pltpu.make_async_copy(z_rows.at[z, events:], start_all.at[z], start_sem.at[1 + m])
            for m, z in enumerate(spot.z_to)
        ]
        for keep in keeps:
            keep.start()
        rows.close()
        for keep in keeps:
            keep.wait()

    def partial(j):
        w, g = j // gates, GATE_OF[j // gates][j % gates]
        slot = j % 2
        if j >= 2:
            sums.started[j - 2]["core"].wait_send()

        @pl.loop(0, 4)
        def _(b):
            value = three_products(
                (turned[g, 0, b], turned[g, 1, b]), (acts[w, 0], acts[w, 1]), ((1,), (0,))
            ).reshape(2, 2, 2, piece, units)
            for p in range(2):
                for q in range(2):
                    mine[j, b, p, q] = jnp.where(k == 0, value[p, q, 0], value[p, q, 1])
                    core_out[slot, b, p, q] = jnp.where(k == 0, value[p, q, 1], value[p, q, 0])

        sums.over_core(j, core_out.at[slot])

    A, B, C, Z, S = sums.core, sums.first, sums.second, sums.along, sums.share

    def E(j):
        sums.end(j, core_sent=j < jobs - 2)

    take_act(0, 0)
    take_gate(1, 0, 0)
    partial(0)
    take_gate(2, 1, 1)
    partial(1)
    A(0)
    take_gate(3, 3, 2)
    rows_begin()
    partial(2)
    A(1)
    take_act(4, 1)
    partial(3)
    A(2), B(0), rows.spread(1), rows.forward(0)
    partial(4)
    A(3), B(1), C(0), rows.spread(2), rows.forward(1), rows.far(0)
    take_gate(5, 2, None)
    partial(5)
    A(4), B(2), C(1), Z(0), rows.spread(3), rows.forward(2), rows.far(1)
    A(5), B(3), C(2), Z(1), S(0), rows.forward(3), rows.far(2)
    B(4), C(3), Z(2), S(1), E(0), rows.far(3)
    B(5), C(4), Z(3), S(2), E(1)
    C(5), Z(4), S(3), E(2)
    rows_end()
    Z(5), S(4), E(3)
    S(5), E(4), E(5)


def run_tail(inputs, prevs, dgates, dstart, entering, collective_id):
    events, units = inputs.shape
    gates, block = 3, units // 4
    piece = block // 8
    jobs = 2 * gates
    start_rows = dstart.shape[0]
    hbm = pl.BlockSpec(memory_space=pl.ANY)
    grads, item_all, start_all = pl.pallas_call(
        tail_kernel,
        out_shape=(
            jax.ShapeDtypeStruct((2, gates, 8, piece, units), f32),
            jax.ShapeDtypeStruct((8, 4, events, block), f32),
            jax.ShapeDtypeStruct((4, start_rows, block), f32),
        ),
        in_specs=[hbm, hbm, hbm, pl.BlockSpec(memory_space=pltpu.VMEM), hbm],
        out_specs=(hbm, hbm, hbm),
        scratch_shapes=sum_scratch(jobs, piece, units)
        + [
            pltpu.VMEM((2, 4, 2, 2, piece, units), f32),
            pltpu.VMEM((4, 2, 4, block, events), bf16),
            pltpu.VMEM((2, 2, events, units), bf16),
            pltpu.VMEM((2, events, units), f32),
            pltpu.VMEM((2, block, units), f32),
            pltpu.VMEM((4, events + start_rows, block), f32),
            pltpu.VMEM((4, events + start_rows, block), f32),
            pltpu.SemaphoreType.DMA((4,)),
            pltpu.SemaphoreType.DMA((4,)),
        ]
        + flow_sems(jobs),
        cost_estimate=takes(190),
        compiler_params=pltpu.CompilerParams(
            collective_id=collective_id, has_side_effects=True, vmem_limit_bytes=VMEM_BYTES
        ),
    )(inputs, prevs, dgates, dstart, entering)
    return grads.reshape(2, gates, 8 * piece, units), item_all, start_all


UNITS = ((0, 0), (0, 1), (1, 0), (0, 2), (1, 1), (1, 2))


def head_kernel(
    chunk,
    width,
    item_ids,
    out_ids,
    embed,
    table,
    bias,
    own_in,
    own_hid,
    carried,
    own_ids,
    all_in,
    all_hid,
    arrived,
    all_ids,
    out_rows,
    padded,
    turned,
    item_rows,
    held,
    local_sem,
    send_sem,
    recv_sem,
    row_send,
    row_recv,
    id_send,
    id_recv,
):
    y, x, k, c, d = place()
    i = pl.program_id(0)
    n = pl.num_programs(0) // 2
    core_to, x_to, y_to = (d + 1 - 2 * k, c), (d + 2 - 4 * x, c), (d + 4 - 8 * y, c)
    z_all = (c + 1 - 2 * lax.rem(c, 2), lax.rem(c + 2, 4), 3 - c)
    owns, alls = (own_in, own_hid), (all_in, all_hid)
    piece = own_in.shape[4]
    half = piece // 2
    block = item_rows.shape[2]
    items = item_rows.shape[1]
    carried_rows = carried.shape[1]
    events = items - carried_rows

    def send(u, slot):
        w, m = UNITS[u]
        z = z_all[m]
        every = alls[w]
        if slot == 0:
            source, target, to = owns[w].at[:, y, x, k], every.at[:, c, y, x, k], (d, z)
        elif slot in (4, 6):
            spot = (
                every.at[:, z, y, 1 - x, k, 0:half] if slot == 4 else every.at[:, z, 1 - y, x, k, half : 2 * half]
            )
            source, target, to = spot, spot, (y_to if slot == 4 else x_to)
        else:
            py, px, to = {
                1: (y, x, x_to),
                2: (y, x, y_to),
                3: (y, x, core_to),
                5: (y, 1 - x, core_to),
                7: (1 - y, x, core_to),
                8: (1 - y, 1 - x, core_to),
            }[slot]
            spot = every.at[:, z, py, px, k]
            source, target = spot, spot
        return pltpu.make_async_remote_copy(
            src_ref=source,
            dst_ref=target,
            send_sem=send_sem.at[u, slot],
            recv_sem=recv_sem.at[u, slot],
            device_id=to,
            device_id_type=MESH,
        )

    def load(w):
        return pltpu.make_async_copy(owns[w], held.at[w], local_sem.at[w])

    def keep(w):
        return pltpu.make_async_copy(held.at[w], alls[w].at[:, c], local_sem.at[2 + w])

    def keep_own(_):
        for w in range(2):
            load(w).wait()
            keep(w).start()

    def item_send(m):
        return pltpu.make_async_remote_copy(
            src_ref=item_rows.at[z_all[m]],
            dst_ref=arrived.at[:, pl.ds(pl.multiple_of(c * block, block), block)],
            send_sem=row_send.at[m],
            recv_sem=row_recv.at[m],
            device_id=(d, z_all[m]),
            device_id_type=MESH,
        )

    def begin_items(_):
        for m in range(3):
            item_send(m).start()

    def item_keep():
        return pltpu.make_async_copy(
            item_rows.at[c], arrived.at[:, pl.ds(pl.multiple_of(c * block, block), block)], local_sem.at[4]
        )

    def id_copy(m):
        to = lax.rem(d + 1 + m, 8)
        return pltpu.make_async_remote_copy(
            src_ref=own_ids,
            dst_ref=all_ids.at[d],
            send_sem=id_send.at[m],
            recv_sem=id_recv.at[m],
            device_id=(to, c),
            device_id_type=MESH,
        )

    def id_keep():
        return pltpu.make_async_copy(own_ids, all_ids.at[d], local_sem.at[5])

    def begin():
        greet([(lax.rem(d + 1 + m, 8), c) for m in range(7)] + [(d, z) for z in z_all])
        id_keep().start()
        for m in range(7):
            id_copy(m).start()
        begin_z(0)
        begin_z(1)
        load(0).start()
        load(1).start()

    def begin_z(u):
        send(u, 0).start()

    def spread(u):
        send(u, 0).wait_recv()
        for slot in (1, 2, 3):
            send(u, slot).start()

    def forward(u):
        send(u, 1).wait_recv()
        send(u, 4).start()
        send(u, 5).start()
        send(u, 2).wait_recv()
        send(u, 6).start()
        send(u, 7).start()

    def far(u):
        send(u, 4).wait_recv()
        send(u, 6).wait_recv()
        send(u, 8).start()

    def close(u):
        for slot in (3, 5, 7, 8):
            send(u, slot).wait_recv()
        for slot in range(9):
            send(u, slot).wait_send()

    timeline = [(-1, begin, None), (4, keep_own, 0), (64, begin_items, 0)]
    timeline += [(at, begin_z, 2 + j) for j, at in enumerate((10, 18, 34, 50))]
    for u, at in enumerate((11, 23, 34, 46, 58, 90)):
        timeline += [(at, spread, u), (at + 12, forward, u), (at + 20, far, u)]
    timeline.sort(key=lambda entry: entry[0])
    last = 2 * n - 1

    @pl.when(i == 0)
    def _():
        padded[...] = jnp.zeros_like(padded)

    for at, action, u in timeline:
        if at < last:

            @pl.when(i == max(at, 0))
            def _(action=action, u=u):
                action() if u is None else action(u)

    @pl.when(i < n)
    def _():
        padded[0:width, :] = embed[...]

    @pl.when(i >= n)
    def _():
        padded[0:width, :] = table[...]
        padded[width : width + 1, :] = bias[...]

    spot = lax.rem(i, n) * chunk
    turned[pl.ds(pl.multiple_of(spot, chunk), chunk), :] = padded[...].T

    @pl.when(i == n - 1)
    def _():
        for z in range(4):

            def body(b, carry, z=z):
                for j in range(8):
                    row = item_ids[z * events + b * 8 + j]
                    item_rows[z, pl.ds(b * 8 + j, 1), :] = turned[pl.ds(row, 1), :]
                return carry

            lax.fori_loop(0, events // 8, body, 0)
            item_rows[z, events:items, :] = carried[z]
        item_keep().start()

    @pl.when(i == last)
    def _():
        def body(b, carry):
            for j in range(8):
                row = out_ids[b * 8 + j]
                out_rows[pl.ds(b * 8 + j, 1), :] = turned[pl.ds(row, 1), :]
            return carry

        lax.fori_loop(0, out_rows.shape[0] // 8, body, 0)
        for at, action, u in timeline:
            if at >= last:
                action(u)
        for u in range(6):
            close(u)
        for m in range(3):
            item_send(m).wait()
        for m in range(7):
            id_copy(m).wait()
        id_keep().wait()
        for w in range(2):
            keep(w).wait()
        item_keep().wait()


def gather_all(embed, table, bias, item_ids, out_ids, own_in, own_hid, carried, own_ids, collective_id):
    width, rows = embed.shape
    gates, block, units = own_in.shape
    piece = block // 8
    chunk = 128 * max(k for k in range(1, 9) if rows % (128 * k) == 0)
    n = rows // chunk
    items = item_ids.shape[0] // 4 + carried.shape[1]
    own_shape = (gates, 2, 2, 2, piece, units)
    all_shape = (gates, 4, 2, 2, 2, piece, units)
    smem = pl.BlockSpec(memory_space=pltpu.SMEM)
    hbm = pl.BlockSpec(memory_space=pl.ANY)
    all_in, all_hid, arrived, all_ids, out_rows = pl.pallas_call(
        functools.partial(head_kernel, chunk, width),
        out_shape=(
            jax.ShapeDtypeStruct(all_shape, f32),
            jax.ShapeDtypeStruct(all_shape, f32),
            jax.ShapeDtypeStruct((items, units), f32),
            jax.ShapeDtypeStruct((8,) + own_ids.shape, jnp.int32),
            jax.ShapeDtypeStruct((out_ids.shape[0], block), f32),
        ),
        grid=(2 * n,),
        in_specs=[
            smem,
            smem,
            pl.BlockSpec((width, chunk), lambda i: (0, jnp.minimum(i, n - 1))),
            pl.BlockSpec((width, chunk), lambda i: (0, jnp.maximum(i - n, 0))),
            pl.BlockSpec((1, chunk), lambda i: (0, jnp.maximum(i - n, 0))),
            hbm,
            hbm,
            pl.BlockSpec(carried.shape, lambda i: (0, 0, 0)),
            pl.BlockSpec(own_ids.shape, lambda i: (0, 0)),
        ],
        out_specs=(hbm, hbm, hbm, hbm, pl.BlockSpec((out_ids.shape[0], block), lambda i: (0, 0))),
        scratch_shapes=[
            pltpu.VMEM((block, chunk), f32),
            pltpu.VMEM((rows, block), f32),
            pltpu.VMEM((4, items, block), f32),
            pltpu.VMEM((2,) + own_shape, f32),
            pltpu.SemaphoreType.DMA((6,)),
            pltpu.SemaphoreType.DMA((6, 9)),
            pltpu.SemaphoreType.DMA((6, 9)),
            pltpu.SemaphoreType.DMA((3,)),
            pltpu.SemaphoreType.DMA((3,)),
            pltpu.SemaphoreType.DMA((7,)),
            pltpu.SemaphoreType.DMA((7,)),
        ],
        cost_estimate=takes(120),
        compiler_params=pltpu.CompilerParams(
            collective_id=collective_id, has_side_effects=True, vmem_limit_bytes=VMEM_BYTES
        ),
    )(item_ids, out_ids, embed, table, bias, own_in.reshape(own_shape), own_hid.reshape(own_shape), carried, own_ids)
    return (
        all_in.reshape(gates, 4 * block, units),
        all_hid.reshape(gates, 4 * block, units),
        arrived,
        all_ids,
        out_rows,
    )


def loss_kernel(width, factor, outs, targets, negs, loss, douts, neg_part, target_part, share, pairs, score):
    n_col, events, block = targets.shape
    n_dp, _, count, _ = negs.shape
    lane = lax.broadcasted_iota(jnp.int32, (events, block), 1)
    for c in range(n_col):
        value = jnp.where(lane < width, outs[:, c * block : (c + 1) * block], 0.0)
        value = jnp.where(lane == width, 1.0 / n_col, value)
        share[c] = value
        pairs[0, c], pairs[1, c] = split_two(value)

    @pl.loop(0, n_dp)
    def _(b):
        cols = pl.ds(pl.multiple_of(b * count, count), count)
        total = jnp.zeros((events, count), f32)
        for c in range(n_col):
            total = total + three_products((pairs[0, c], pairs[1, c]), split_two(negs[b, c]), ((1,), (1,)))
        score[:, cols] = total

    step = 32

    @pl.loop(0, events // step)
    def _(i):
        rows = pl.ds(pl.multiple_of(i * step, step), step)
        pos = jnp.zeros((step, 1), f32)
        for c in range(n_col):
            pos = pos + jnp.sum(share[c, rows, :] * targets[c, rows, :], axis=-1, keepdims=True)
        neg = score[rows, :]
        expd = jnp.exp(neg - jnp.max(neg, axis=-1, keepdims=True))
        weight = expd * (1.0 / jnp.sum(expd, axis=-1, keepdims=True))
        sig = jax.nn.sigmoid(pos - neg)
        slope = weight * sig
        ppos = jnp.sum(slope, axis=-1, keepdims=True)
        quad = jnp.sum(weight * neg * neg, axis=-1, keepdims=True)
        slope = jnp.sum(slope * (1.0 - sig), axis=-1, keepdims=True)
        loss[rows, :] = jnp.broadcast_to(quad - jnp.log(ppos), (step, LANES))
        score[rows, :] = factor * weight * (1.0 - sig * sig * (1.0 / ppos) + neg * neg + 2.0 * neg - quad)
        dpos = -factor * slope / ppos
        for c in range(n_col):
            target_part[c, rows, :] = dpos * share[c, rows, :]
            douts[rows, c * block : (c + 1) * block] = dpos * targets[c, rows, :]

    @pl.loop(0, n_dp)
    def _(b):
        dneg = score[:, pl.ds(pl.multiple_of(b * count, count), count)]
        across, down = split_two(dneg), split_two(dneg.T)
        for c in range(n_col):
            cols = slice(c * block, (c + 1) * block)
            douts[:, cols] = douts[:, cols] + three_products(across, split_two(negs[b, c]), ((1,), (0,)))
            neg_part[c, b] = three_products(down, (pairs[0, c], pairs[1, c]), ((1,), (0,)))

    for c in range(n_col):
        cols = slice(c * block, (c + 1) * block)
        douts[:, cols] = jnp.where(lane < width, douts[:, cols], 0.0)


def run_loss(outs, targets, negs, width, factor):
    n_col, events, block = targets.shape
    n_dp, _, count, _ = negs.shape
    return pl.pallas_call(
        functools.partial(loss_kernel, width, factor),
        out_shape=(
            jax.ShapeDtypeStruct((events, LANES), f32),
            jax.ShapeDtypeStruct(outs.shape, f32),
            jax.ShapeDtypeStruct((n_col, n_dp, count, block), f32),
            jax.ShapeDtypeStruct((n_col, events, block), f32),
        ),
        in_specs=[in_vmem()] * 3,
        out_specs=(in_vmem(),) * 4,
        scratch_shapes=[
            pltpu.VMEM((n_col, events, block), f32),
            pltpu.VMEM((2, n_col, events, block), bf16),
            pltpu.VMEM((events, n_dp * count), f32),
        ],
        cost_estimate=takes(25),
        compiler_params=params(),
    )(outs, targets, negs)


def back_kernel(
    steps,
    hidden,
    douts,
    keep,
    prevs,
    resets,
    updates,
    cands,
    inners,
    neg_part,
    target_part,
    dgates,
    dstart,
    neg_all,
    target_all,
    mine,
    core_in,
    x_in,
    y_in,
    xy_in,
    yx_in,
    z_in,
    total,
    w_high,
    w_low,
    w_flow,
    z_rows,
    flow_sem,
    load_sem,
    sum_local,
    sum_send,
    sum_recv,
    row_local,
    row_send,
    row_recv,
):
    spot = Spot()
    spot.greet_all()
    rows_per, units = dstart.shape
    jobs, piece = mine.shape[0], mine.shape[4]
    step_rows = w_flow.shape[1]
    chunks = hidden.shape[0] // step_rows
    sums = SumFlow(
        spot, mine, core_in, x_in, y_in, xy_in, yx_in, z_in, total,
        lambda j, d: neg_all.at[d, pl.ds(j * piece, piece)], sum_local, sum_send, sum_recv,
    )
    rows = RowsFlow(spot, target_part, z_rows, target_all, row_local, row_send, row_recv)

    def load(i, slot):
        part = pl.ds(pl.multiple_of(i * step_rows, step_rows), step_rows)
        return pltpu.make_async_copy(hidden.at[part], w_flow.at[slot], flow_sem.at[slot])

    load(0, 0).start()
    own = []
    for j in range(jobs):
        part = pl.ds(j * piece, piece)
        own.append(pltpu.make_async_copy(neg_part.at[:, :, :, spot.k, part], mine.at[j], load_sem.at[j]))
        own[j].start()
        sums.over_core(j, neg_part.at[:, :, :, 1 - spot.k, part])
    rows.begin()

    @pl.loop(0, chunks)
    def _(i):
        slot = lax.rem(i, 2)

        @pl.when(i + 1 < chunks)
        def _():
            load(i + 1, 1 - slot).start()

        load(i, slot).wait()
        part = pl.ds(pl.multiple_of(i * step_rows, step_rows), step_rows)
        w_high[part, :], w_low[part, :] = split_two(w_flow[slot])

    def step(i, dstate):
        t = steps - 1 - i
        now = pl.ds(pl.multiple_of(t * rows_per, rows_per), rows_per)
        reset, update, cand = resets[now, :], updates[now, :], cands[now, :]
        dh = douts[now, :] + dstate
        dcand = dh * (1.0 - update) * (1.0 - cand * cand)
        dreset = dcand * inners[now, :] * reset * (1.0 - reset)
        dupdate = dh * (prevs[now, :] - cand) * update * (1.0 - update)
        dinner = dcand * reset
        dgates[now, 0:units] = dreset
        dgates[now, units : 2 * units] = dupdate
        dgates[now, 2 * units : 3 * units] = dinner
        dgates[now, 3 * units : 4 * units] = dcand
        total_now = dh * update
        for g, part in enumerate((dreset, dupdate, dinner)):
            pair = two_part(part)
            sect = slice(g * units, (g + 1) * units)
            first = jnp.dot(pair, w_high[sect, :], preferred_element_type=f32)
            second = jnp.dot(pair, w_low[sect, :], preferred_element_type=f32)
            total_now = total_now + (first[:rows_per] + first[rows_per:] + second[:rows_per])
        return keep[now, :] * total_now

    def sums_core(j):
        own[j].wait()
        sums.core(j)

    A, B, C, Z, S = sums_core, sums.first, sums.second, sums.along, sums.share
    timeline = (
        (0.0, ((A, 0), (A, 1))),
        (0.15, ((rows.forward, 0),)),
        (0.28, ((rows.spread, 1), (B, 0))),
        (0.38, ((rows.forward, 1), (rows.far, 0))),
        (0.47, ((B, 1), (rows.spread, 2))),
        (0.56, ((C, 0), (rows.forward, 2), (rows.far, 1))),
        (0.66, ((C, 1), (rows.spread, 3))),
        (0.78, ((Z, 0), (rows.forward, 3), (rows.far, 2))),
        (0.88, ((Z, 1), (S, 0))),
    )
    state, done = jnp.zeros((rows_per, units), f32), 0
    for share_done, actions in timeline:
        until = int(share_done * steps)
        if until > done:
            state, done = lax.fori_loop(done, until, step, state), until
        for action, argument in actions:
            action(argument)
    dstart[...] = lax.fori_loop(done, steps, step, state)
    rows.far(3)
    S(1)
    sums.end(0)
    rows.close()
    sums.end(1)


def run_back(hidden, douts, keep, saved, neg_part, target_part, rows_per, steps, collective_id):
    events, units = douts.shape
    count, block = neg_part.shape[2:]
    jobs = 2
    piece = count // jobs
    hbm = pl.BlockSpec(memory_space=pl.ANY)
    step_rows = units // 4
    return pl.pallas_call(
        functools.partial(back_kernel, steps),
        out_shape=(
            jax.ShapeDtypeStruct((events, 4 * units), f32),
            jax.ShapeDtypeStruct((rows_per, units), f32),
            jax.ShapeDtypeStruct((8, count, block), f32),
            jax.ShapeDtypeStruct((8, 4, events, block), f32),
        ),
        in_specs=[hbm] + [in_vmem()] * 7 + [hbm, hbm],
        out_specs=(in_vmem(), in_vmem(), hbm, hbm),
        scratch_shapes=sum_scratch(jobs, piece, block)
        + [
            pltpu.VMEM(hidden.shape, bf16),
            pltpu.VMEM(hidden.shape, bf16),
            pltpu.VMEM((2, step_rows, units), f32),
            pltpu.VMEM((4, events, block), f32),
            pltpu.SemaphoreType.DMA((2,)),
            pltpu.SemaphoreType.DMA((jobs,)),
        ]
        + flow_sems(jobs),
        cost_estimate=takes(80),
        compiler_params=pltpu.CompilerParams(
            collective_id=collective_id, has_side_effects=True, vmem_limit_bytes=VMEM_BYTES
        ),
    )(hidden, douts, keep, *saved, neg_part.reshape(4, 2, 2, 2, count, block), target_part)


def pad_kernel(weight, bias, out):
    own, full = weight.shape[1:]
    block = out.shape[1]
    n_col = out.shape[2] // block
    part = full // n_col
    out[...] = jnp.zeros_like(out)
    for c in range(n_col):
        out[0, 0:own, c * block : c * block + part] = weight[0, :, c * part : (c + 1) * part]
    out[0, 0:own, part : part + 1] = bias[0]


def pad_units(weight, bias, n_col, block):
    gates, own, full = weight.shape
    return pl.pallas_call(
        pad_kernel,
        out_shape=jax.ShapeDtypeStruct((gates, block, n_col * block), f32),
        grid=(gates,),
        in_specs=[
            pl.BlockSpec((1, own, full), lambda g: (g, 0, 0)),
            pl.BlockSpec((1, own, 1), lambda g: (g, 0, 0)),
        ],
        out_specs=pl.BlockSpec((1, block, n_col * block), lambda g: (g, 0, 0)),
        compiler_params=params(),
    )(weight, bias[:, :, None])


def gather_weight(own, n_dp):
    gates, block, units = own.shape
    flat = own.reshape(n_dp, gates * block // n_dp, units)
    piece = lax.dynamic_index_in_dim(flat, lax.axis_index("dp"), 0, keepdims=False)
    every = lax.all_gather(piece, ("col", "dp"))
    every = every.reshape(-1, gates, block, units)
    return jnp.moveaxis(every, 0, 1).reshape(gates, -1, units)


def reduce_weight(partial, n_dp, n_col):
    gates, rows, units = partial.shape
    block = rows // n_col
    parts = jnp.moveaxis(partial.reshape(gates, n_col, block, units), 1, 0)
    parts = jnp.moveaxis(parts.reshape(n_col, n_dp, gates * block // n_dp, units), 1, 0)
    mine = lax.psum_scatter(parts, "dp", scatter_dimension=0)
    mine = lax.psum_scatter(mine, "col", scatter_dimension=0)
    return lax.all_gather(mine, "dp").reshape(gates, block, units)


def swap_col(rows, n_col):
    return lax.all_to_all(rows, "col", split_axis=0, concat_axis=0, tiled=True)


def unpad_last(value, n_col, part):
    block = value.shape[-1] // n_col
    return value.reshape(value.shape[:-1] + (n_col, block))[..., :part].reshape(value.shape[:-1] + (n_col * part,))


def local(
    n_dp,
    n_col,
    item_ids,
    target_ids,
    negative_ids,
    reset_mask,
    carry_flags,
    carried_state,
    embed_table,
    input_weight,
    hidden_weight,
    gate_bias,
    hidden_bias,
    out_table,
    out_bias,
):
    sessions, steps = item_ids.shape
    own_sessions = sessions // n_col
    rows_per = round_up(own_sessions, ROWS8)
    width = embed_table.shape[0]
    table_rows = embed_table.shape[1]
    own_rows = table_rows // n_dp
    block = round_up(width + 1, LANES)
    units = n_col * block
    events = steps * rows_per
    direct = n_dp == 8 and n_col == 4 and block % 64 == 0 and own_sessions == rows_per
    factor = 1.0 / steps
    dp_at, col_at = lax.axis_index("dp"), lax.axis_index("col")

    def by_owner(value):
        value = jnp.moveaxis(value.reshape(n_col, own_sessions, steps), 1, 2)
        value = jnp.pad(value, ((0, 0), (0, 0), (0, rows_per - own_sessions)))
        return value.reshape(-1)

    item_flat, target_flat = by_owner(item_ids), by_owner(target_ids)
    own_keep = lax.dynamic_index_in_dim(
        by_owner(1 - reset_mask).reshape(n_col, events, 1), col_at, 0, keepdims=False
    ).astype(f32)
    valid = jnp.tile(jnp.arange(rows_per) < own_sessions, steps)
    lane = jnp.arange(units) % block
    first_pad = jnp.arange(units) == width

    own_in = pad_units(input_weight, gate_bias, n_col, block)
    no_bias = jnp.zeros_like(hidden_bias)
    own_hid = pad_units(hidden_weight, jnp.stack([no_bias, no_bias, hidden_bias]), n_col, block)

    carried = (carry_flags.astype(f32)[:, None] * carried_state).reshape(n_col, own_sessions, width)
    carried = jnp.pad(carried, ((0, 0), (0, rows_per - own_sessions), (0, block - width)))
    neg_count = negative_ids.shape[0]
    own_negs = lax.dynamic_slice_in_dim(negative_ids, dp_at * (neg_count // n_dp), neg_count // n_dp)
    out_ids = jnp.concatenate([target_flat, own_negs])
    if direct:
        own_ids = jnp.concatenate([item_flat, target_flat]).reshape(-1, LANES)
        all_in, all_hid, arrived, all_ids, out_rows = gather_all(
            embed_table, out_table, out_bias[None, :], item_flat, out_ids, own_in, own_hid, carried, own_ids, 1
        )
        all_ids = all_ids.reshape(n_dp, 2, -1)
    else:
        all_hid = gather_weight(own_hid, n_dp)
        all_in = gather_weight(own_in, n_dp)
        no_row = jnp.zeros((1, table_rows), f32)
        item_rows = gather_rows(embed_table, no_row, item_flat, block).reshape(n_col, events, block)
        arrived = swap_col(jnp.concatenate([item_rows, carried], axis=1), n_col)
        arrived = jnp.moveaxis(arrived, 0, 1).reshape(events + rows_per, units)
        out_rows = gather_rows(out_table, out_bias[None, :], out_ids, block)
        all_ids = lax.all_gather(jnp.stack([item_flat, target_flat]), "dp")
    all_hid, all_in = all_hid.reshape(-1, units), all_in.reshape(-1, units)
    inputs = jnp.where(first_pad, 1.0, arrived[:events])
    start = arrived[events:]
    targets = swap_col(out_rows[: n_col * events].reshape(n_col, events, block), n_col)
    negs = lax.all_gather(out_rows[n_col * events :], ("dp", "col")).reshape(n_dp, n_col, -1, block)

    all_items, all_targets = all_ids[:, 0].reshape(-1), all_ids[:, 1].reshape(-1)
    count = all_items.shape[0]
    keys = jnp.concatenate([all_items, all_targets + table_rows, negative_ids + 2 * table_rows])
    order = jnp.concatenate([jnp.tile(lax.iota(jnp.int32, count), 2), lax.iota(jnp.int32, neg_count)])
    keys, order = lax.sort((keys, order), num_keys=1)
    low = (dp_at * own_rows).astype(jnp.int32)
    by_item = (order[:count], keys[:count])
    by_target = (order[count : 2 * count], keys[count : 2 * count] - table_rows)
    by_neg = (order[2 * count :], keys[2 * count :] - 2 * table_rows)

    prevs, resets, updates, cands, inners, outs = run_forward(
        all_hid, all_in, inputs, own_keep, start, steps, width
    )

    saved = (prevs, resets, updates, cands, inners)
    if direct:
        own_loss, douts, neg_part, target_part = run_loss(outs, targets, negs, width, factor)
        own_loss = own_loss[:, :1]
        dgates, dstart, neg_all, target_all = run_back(
            all_hid, douts, own_keep, saved, neg_part, target_part, rows_per, steps, 3
        )
        neg_all, target_all = neg_all.reshape(-1, block), target_all.reshape(-1, block)
    else:
        targets = jnp.moveaxis(targets, 0, 1).reshape(events, units)
        negs = jnp.moveaxis(negs, 1, 2).reshape(neg_count, units)
        shares = jnp.where(lane == width, 1.0 / n_col, jnp.where(lane < width, outs, 0.0))
        pos_score = jnp.sum(shares * targets, axis=-1, keepdims=True)
        neg_score = lax.dot_general(shares, negs, (((1,), (1,)), ((), ())), precision=high)
        top = jnp.max(neg_score, axis=-1, keepdims=True)
        expd = jnp.exp(neg_score - top)
        weight = expd / jnp.sum(expd, axis=-1, keepdims=True)
        sig = jax.nn.sigmoid(pos_score - neg_score)
        ppos = jnp.sum(weight * sig, axis=-1, keepdims=True)
        quad = jnp.sum(weight * neg_score * neg_score, axis=-1, keepdims=True)
        slope = jnp.sum(weight * sig * (1.0 - sig), axis=-1, keepdims=True)
        own_loss = -jnp.log(ppos) + quad
        dneg = factor * weight * (1.0 - sig * sig / ppos + neg_score * neg_score + 2.0 * neg_score - quad)
        dneg = jnp.where(valid[:, None], dneg, 0.0)
        dpos = jnp.where(valid[:, None], -factor * slope / ppos, 0.0)
        douts = jnp.dot(dneg, negs, precision=high) + dpos * targets
        douts = jnp.where(lane < width, douts, 0.0)
        neg_part = lax.dot_general(dneg, shares, (((0,), (0,)), ((), ())), precision=high)
        target_part = dpos * shares

        neg_own = lax.psum_scatter(neg_part.reshape(n_dp, -1, units), "dp", scatter_dimension=0)
        neg_own = jnp.moveaxis(neg_own.reshape(-1, n_col, block), 1, 0)
        neg_own = lax.psum_scatter(neg_own, "col", scatter_dimension=0)
        neg_all = lax.all_gather(neg_own, "dp", tiled=True)
        target_own = swap_col(jnp.moveaxis(target_part.reshape(events, n_col, block), 1, 0), n_col)
        target_all = lax.all_gather(target_own.reshape(-1, block), "dp", tiled=True)
        dgates, dstart = run_backward(all_hid, douts, own_keep, saved, rows_per, steps)
    own_loss = own_loss.reshape(steps, rows_per)[:, :own_sessions]
    loss = lax.all_gather(own_loss.T, "col", tiled=True)
    grad_out, grad_obias = scatter_rows(
        [by_target + (target_all,), by_neg + (neg_all,)],
        low,
        own_rows,
        width,
        block,
    )
    grad_obias = grad_obias[0] * n_col

    gates = input_weight.shape[0]
    if direct:
        reduced, item_all, start_all = run_tail(inputs, prevs, dgates, dstart, all_in, 2)
        grad_in, grad_hid = reduced[0], reduced[1]
        item_all = item_all.reshape(-1, block)
    else:
        dx = jnp.concatenate([dgates[:, : 2 * units], dgates[:, 3 * units :]], axis=1)
        dh = dgates[:, : 3 * units]
        hid_part = lax.dot_general(dh, prevs, (((0,), (0,)), ((), ())), precision=high)
        in_part = lax.dot_general(dx, inputs, (((0,), (0,)), ((), ())), precision=high)
        dinputs = jnp.dot(dx, all_in, precision=high)
        back = jnp.concatenate([dinputs, dstart], axis=0).reshape(events + rows_per, n_col, block)
        back = swap_col(jnp.moveaxis(back, 1, 0), n_col)
        item_all = lax.all_gather(back[:, :events].reshape(-1, block), "dp", tiled=True)
        start_all = back[:, events:]
        grad_in = reduce_weight(in_part.reshape(gates, units, units), n_dp, n_col)
        grad_hid = reduce_weight(hid_part.reshape(gates, units, units), n_dp, n_col)
    grad_carried = start_all[:, :own_sessions, :width].reshape(sessions, width)
    grad_carried = carry_flags.astype(f32)[:, None] * grad_carried
    grad_embed, _ = scatter_rows([by_item + (item_all,)], low, own_rows, width, block)
    grad_in, grad_hid = grad_in[:, :width], grad_hid[:, :width]
    return (
        loss,
        grad_embed,
        unpad_last(grad_in, n_col, width),
        unpad_last(grad_hid, n_col, width),
        grad_in[:, :, width],
        grad_hid[gates - 1, :, width],
        grad_out,
        grad_obias,
        grad_carried,
    )


def solution(mesh):
    in_specs = (
        P("dp", None),
        P("dp", None),
        P(),
        P("dp", None),
        P("dp"),
        P("dp", "col"),
        P("col", None),
        P(None, "col", None),
        P(None, "col", None),
        P(None, "col"),
        P("col"),
        P("col", None),
        P(),
    )
    out_specs = (
        P("dp", None),
        P("col", "dp"),
        P(None, "col", None),
        P(None, "col", None),
        P(None, "col"),
        P("col"),
        P("col", "dp"),
        P("dp"),
        P("dp", "col"),
    )
    body = functools.partial(local, mesh.shape["dp"], mesh.shape["col"])
    return jax.shard_map(body, mesh=mesh, in_specs=in_specs, out_specs=out_specs, check_vma=False)
```

```python
import functools

import jax
import jax.numpy as jnp
from jax import lax
from jax.experimental import pallas as pl
from jax.experimental.pallas import tpu as pltpu
from jax.sharding import PartitionSpec as P

LANES = 128
ROWS8 = 8
VMEM_BYTES = 60 << 20
f32 = jnp.float32
bf16 = jnp.bfloat16
high = lax.Precision.HIGH
MESH = pl.DeviceIdType.MESH


def round_up(value, unit):
    return -(-value // unit) * unit


def params():
    return pltpu.CompilerParams(vmem_limit_bytes=VMEM_BYTES)


def takes(micros):
    return pl.CostEstimate(flops=int(micros * 1.1e9), bytes_accessed=1 << 20, transcendentals=0)


def in_vmem():
    return pl.BlockSpec(memory_space=pltpu.VMEM)


def in_smem():
    return pl.BlockSpec(memory_space=pltpu.SMEM)


def gather_kernel(chunk, count, width, ids, table, bias, out, padded, turned):
    step = pl.program_id(0)

    @pl.when(step == 0)
    def _():
        padded[...] = jnp.zeros_like(padded)

    padded[0:width, :] = table[...]
    padded[width : width + 1, :] = bias[...]
    turned[pl.ds(pl.multiple_of(step * chunk, chunk), chunk), :] = padded[...].T

    @pl.when(step == pl.num_programs(0) - 1)
    def _():
        def body(block, carry):
            for j in range(ROWS8):
                row = ids[block * ROWS8 + j]
                out[pl.ds(block * ROWS8 + j, 1), :] = turned[pl.ds(row, 1), :]
            return carry

        lax.fori_loop(0, count // ROWS8, body, 0)


def gather_rows(table, bias, ids, block):
    width, rows = table.shape
    count = ids.shape[0]
    chunk = LANES * max(k for k in range(1, 9) if rows % (LANES * k) == 0)
    return pl.pallas_call(
        functools.partial(gather_kernel, chunk, count, width),
        out_shape=jax.ShapeDtypeStruct((count, block), f32),
        grid_spec=pltpu.PrefetchScalarGridSpec(
            num_scalar_prefetch=1,
            grid=(rows // chunk,),
            in_specs=[
                pl.BlockSpec((width, chunk), lambda i, ids: (0, i)),
                pl.BlockSpec((1, chunk), lambda i, ids: (0, i)),
            ],
            out_specs=pl.BlockSpec((count, block), lambda i, ids: (0, 0)),
            scratch_shapes=[pltpu.VMEM((block, chunk), f32), pltpu.VMEM((rows, block), f32)],
        ),
        compiler_params=params(),
    )(ids, table, bias)


def scatter_kernel(width, n_lists, *refs):
    bounds = refs[0]
    lists = refs[1 : 1 + 3 * n_lists]
    out, bias_out, acc = refs[1 + 3 * n_lists :]
    acc[...] = jnp.zeros_like(acc)
    low = bounds[0]
    for k in range(n_lists):
        rows_of, ids, data = lists[3 * k : 3 * k + 3]

        def body(i, carry):
            spot = pl.ds(ids[i] - low, 1)
            acc[spot, :] = acc[spot, :] + data[pl.ds(rows_of[i], 1), :]
            return carry

        lax.fori_loop(bounds[1 + 2 * k], bounds[2 + 2 * k], body, 0)
    for j in range(acc.shape[0] // LANES):
        cols = slice(j * LANES, (j + 1) * LANES)
        turned = acc[cols, :].T
        out[:, cols] = turned[:width]
        bias_out[:, cols] = turned[width : width + 1]


def scatter_rows(lists, low, own_rows, width, block):
    ends = [low]
    operands, specs = [], []
    for order, ids, data in lists:
        ends += [jnp.sum(ids < low, dtype=jnp.int32), jnp.sum(ids < low + own_rows, dtype=jnp.int32)]
        operands += [order, ids, data]
        specs += [in_smem(), in_smem(), in_vmem()]
    return pl.pallas_call(
        functools.partial(scatter_kernel, width, len(lists)),
        out_shape=(
            jax.ShapeDtypeStruct((width, own_rows), f32),
            jax.ShapeDtypeStruct((1, own_rows), f32),
        ),
        in_specs=[in_smem()] + specs,
        out_specs=(in_vmem(), in_vmem()),
        scratch_shapes=[pltpu.VMEM((own_rows, block), f32)],
        cost_estimate=takes(20),
        compiler_params=params(),
    )(jnp.stack(ends), *operands)


def split_weight(weight, high_part, low_part):
    step = 128

    @pl.loop(0, weight.shape[0] // step)
    def _(i):
        rows = pl.ds(pl.multiple_of(i * step, step), step)
        value = weight[rows, :]
        top = value.astype(bf16)
        high_part[rows, :] = top
        low_part[rows, :] = (value - top.astype(f32)).astype(bf16)


def two_part(value):
    top = value.astype(bf16).astype(f32)
    return jnp.concatenate([top, value - top], axis=0).astype(bf16)


def forward_kernel(
    steps,
    width,
    hidden,
    entering,
    inputs,
    keep,
    start,
    prevs,
    resets,
    updates,
    cands,
    inners,
    outs,
    w_high,
    w_low,
    x_gates,
    hid_buf,
    in_buf,
    pair_buf,
    sem,
    travel=None,
):
    rows_per, units = start.shape
    step_rows = hid_buf.shape[1]
    chunks = hidden.shape[0] // step_rows

    def load(i, slot):
        rows = pl.ds(pl.multiple_of(i * step_rows, step_rows), step_rows)
        return (
            pltpu.make_async_copy(hidden.at[rows], hid_buf.at[slot], sem.at[0, slot]),
            pltpu.make_async_copy(entering.at[rows], in_buf.at[slot], sem.at[1, slot]),
        )

    for copy in load(0, 0):
        copy.start()
    timeline = travel() if travel else ()
    top = inputs[...].astype(bf16)
    pair_buf[0] = top
    pair_buf[1] = (inputs[...] - top.astype(f32)).astype(bf16)

    @pl.loop(0, chunks)
    def _(i):
        slot = lax.rem(i, 2)

        @pl.when(i + 1 < chunks)
        def _():
            for copy in load(i + 1, 1 - slot):
                copy.start()

        for copy in load(i, slot):
            copy.wait()
        cols = pl.ds(pl.multiple_of(i * step_rows, step_rows), step_rows)
        turned = hid_buf[slot].T
        first = turned.astype(bf16)
        w_high[:, cols] = first
        w_low[:, cols] = (turned - first.astype(f32)).astype(bf16)
        value = in_buf[slot]
        first = value.astype(bf16)
        second = (value - first.astype(f32)).astype(bf16)
        over = (((1,), (1,)), ((), ()))
        x_gates[:, cols] = (
            lax.dot_general(pair_buf[0], first, over, preferred_element_type=f32)
            + lax.dot_general(pair_buf[1], first, over, preferred_element_type=f32)
            + lax.dot_general(pair_buf[0], second, over, preferred_element_type=f32)
        )

    lane = lax.broadcasted_iota(jnp.int32, (rows_per, units), 1)

    def step(t, state):
        rows = pl.ds(pl.multiple_of(t * rows_per, rows_per), rows_per)
        prev = jnp.where(lane == width, 1.0, keep[rows, :] * state)
        pair = two_part(prev)

        def gate(g):
            cols = slice(g * units, (g + 1) * units)
            first = jnp.dot(pair, w_high[:, cols], preferred_element_type=f32)
            second = jnp.dot(pair, w_low[:, cols], preferred_element_type=f32)
            return first[:rows_per] + first[rows_per:] + second[:rows_per], cols

        h_reset, cols = gate(0)
        reset = jax.nn.sigmoid(x_gates[rows, cols] + h_reset)
        h_update, cols = gate(1)
        update = jax.nn.sigmoid(x_gates[rows, cols] + h_update)
        inner, cols = gate(2)
        cand = jnp.tanh(x_gates[rows, cols] + reset * inner)
        new = (1.0 - update) * cand + update * prev
        prevs[rows, :] = prev
        resets[rows, :] = reset
        updates[rows, :] = update
        cands[rows, :] = cand
        inners[rows, :] = inner
        outs[rows, :] = new
        return new

    state, done = start[...], 0
    for share_done, actions in timeline:
        until = int(share_done * steps)
        if until > done:
            state, done = lax.fori_loop(done, until, step, state), until
        for action, argument in actions:
            action(argument)
    lax.fori_loop(done, steps, step, state)


def forward_travel_kernel(steps, width, hidden, entering, inputs, keep, start, neg_own, target_own, *refs):
    saved, (neg_all, targets), scratch = refs[:6], refs[6:8], refs[8:]
    z_rows, target_send, target_recv, target_local, row_local, row_send, row_recv = scratch[7:]
    spot = Spot()
    rows = RowsFlow(spot, neg_own, z_rows, neg_all, row_local, row_send, row_recv, same=True)
    copies = []

    def begin_targets(_):
        keep_own = pltpu.make_async_copy(target_own.at[spot.c], targets.at[spot.c], target_local.at[0])
        keep_own.start()
        copies.append(keep_own)
        for m, z in enumerate(spot.z_to):
            copies.append(
                remote(target_own.at[z], targets.at[spot.c], target_send.at[m], target_recv.at[m], (spot.d, z))
            )

    def travel():
        spot.greet_all()
        rows.begin()
        return (
            (0.0, ((rows.forward, 0),)),
            (0.1, ((rows.spread, 1),)),
            (0.2, ((rows.far, 0),)),
            (0.3, ((rows.forward, 1), (rows.spread, 2), (begin_targets, None))),
            (0.4, ((rows.far, 1),)),
            (0.5, ((rows.forward, 2), (rows.spread, 3))),
            (0.6, ((rows.far, 2),)),
            (0.7, ((rows.forward, 3),)),
            (0.85, ((rows.far, 3),)),
        )

    forward_kernel(steps, width, hidden, entering, inputs, keep, start, *saved, *scratch[:7], travel=travel)
    rows.close()
    for copy in copies:
        copy.wait()


def forward_scratch(hidden, inputs):
    events, units = inputs.shape
    step_rows = units // 4
    return [
        pltpu.VMEM(hidden.shape[::-1], bf16),
        pltpu.VMEM(hidden.shape[::-1], bf16),
        pltpu.VMEM((events, hidden.shape[0]), f32),
        pltpu.VMEM((2, step_rows, units), f32),
        pltpu.VMEM((2, step_rows, units), f32),
        pltpu.VMEM((2, events, units), bf16),
        pltpu.SemaphoreType.DMA((2, 2)),
    ]


def run_forward(hidden, entering, inputs, keep, start, steps, width):
    saved = jax.ShapeDtypeStruct(inputs.shape, f32)
    hbm = pl.BlockSpec(memory_space=pl.ANY)
    return pl.pallas_call(
        functools.partial(forward_kernel, steps, width),
        out_shape=(saved,) * 6,
        in_specs=[hbm, hbm] + [in_vmem()] * 3,
        out_specs=(in_vmem(),) * 6,
        scratch_shapes=forward_scratch(hidden, inputs),
        cost_estimate=takes(75),
        compiler_params=params(),
    )(hidden, entering, inputs, keep, start)


def run_forward_travel(hidden, entering, inputs, keep, start, neg_own, target_own, steps, width, collective_id):
    saved = jax.ShapeDtypeStruct(inputs.shape, f32)
    hbm = pl.BlockSpec(memory_space=pl.ANY)
    dma = pltpu.SemaphoreType.DMA
    return pl.pallas_call(
        functools.partial(forward_travel_kernel, steps, width),
        out_shape=(saved,) * 6
        + (jax.ShapeDtypeStruct((8, 4) + neg_own.shape, f32), jax.ShapeDtypeStruct(target_own.shape, f32)),
        in_specs=[hbm, hbm] + [in_vmem()] * 3 + [hbm, hbm],
        out_specs=(in_vmem(),) * 6 + (hbm, hbm),
        scratch_shapes=forward_scratch(hidden, inputs)
        + [pltpu.VMEM((4,) + neg_own.shape, f32), dma((3,)), dma((3,)), dma((1,)), dma((4,)), dma((4, 9)), dma((4, 9))],
        cost_estimate=takes(75),
        compiler_params=pltpu.CompilerParams(
            collective_id=collective_id, has_side_effects=True, vmem_limit_bytes=VMEM_BYTES
        ),
    )(hidden, entering, inputs, keep, start, neg_own, target_own)


def backward_kernel(
    steps, weight, douts, keep, prevs, resets, updates, cands, inners, dgates, dstart, w_high, w_low
):
    rows_per, units = dstart.shape
    split_weight(weight, w_high, w_low)

    def step(i, dstate):
        t = steps - 1 - i
        rows = pl.ds(pl.multiple_of(t * rows_per, rows_per), rows_per)
        reset, update, cand = resets[rows, :], updates[rows, :], cands[rows, :]
        dh = douts[rows, :] + dstate
        dcand = dh * (1.0 - update) * (1.0 - cand * cand)
        dreset = dcand * inners[rows, :] * reset * (1.0 - reset)
        dupdate = dh * (prevs[rows, :] - cand) * update * (1.0 - update)
        dinner = dcand * reset
        dgates[rows, 0:units] = dreset
        dgates[rows, units : 2 * units] = dupdate
        dgates[rows, 2 * units : 3 * units] = dinner
        dgates[rows, 3 * units : 4 * units] = dcand
        total = dh * update
        for g, part in enumerate((dreset, dupdate, dinner)):
            pair = two_part(part)
            sect = slice(g * units, (g + 1) * units)
            first = jnp.dot(pair, w_high[sect, :], preferred_element_type=f32)
            second = jnp.dot(pair, w_low[sect, :], preferred_element_type=f32)
            total = total + (first[:rows_per] + first[rows_per:] + second[:rows_per])
        return keep[rows, :] * total

    dstart[...] = lax.fori_loop(0, steps, step, jnp.zeros((rows_per, units), f32))


def run_backward(weight, douts, keep, saved, rows_per, steps):
    events, units = douts.shape
    return pl.pallas_call(
        functools.partial(backward_kernel, steps),
        out_shape=(
            jax.ShapeDtypeStruct((events, 4 * units), f32),
            jax.ShapeDtypeStruct((rows_per, units), f32),
        ),
        in_specs=[in_vmem()] * 8,
        out_specs=(in_vmem(),) * 2,
        scratch_shapes=[pltpu.VMEM(weight.shape, bf16)] * 2,
        cost_estimate=takes(67),
        compiler_params=params(),
    )(weight, douts, keep, *saved)


def place():
    d = lax.axis_index("dp")
    c = lax.axis_index("col")
    return d // 4, (d // 2) % 2, d % 2, c, d


def greet(partners):
    barrier = pltpu.get_barrier_semaphore()
    for partner in partners:
        pl.semaphore_signal(barrier, inc=1, device_id=partner, device_id_type=MESH)
    pl.semaphore_wait(barrier, len(partners))


class Spot:
    def __init__(self):
        self.y, self.x, self.k, self.c, self.d = place()
        y, x, k, c, d = self.y, self.x, self.k, self.c, self.d
        self.x_d, self.y_d, self.core_d = d + 2 - 4 * x, d + 4 - 8 * y, d + 1 - 2 * k
        self.far_d = d + 6 - 4 * x - 8 * y
        self.core_to, self.x_to, self.y_to, self.far_to = (self.core_d, c), (self.x_d, c), (self.y_d, c), (self.far_d, c)
        self.z_to = (c + 1 - 2 * lax.rem(c, 2), lax.rem(c + 2, 4), 3 - c)

    def greet_all(self):
        greet([self.core_to, self.x_to, self.y_to, self.far_to] + [(self.d, z) for z in self.z_to])


def remote(source, target, send, recv, to):
    copy = pltpu.make_async_remote_copy(
        src_ref=source, dst_ref=target, send_sem=send, recv_sem=recv, device_id=to, device_id_type=MESH
    )
    copy.start()
    return copy


class RowsFlow:
    def __init__(self, spot, outgoing, z_rows, every, local_sem, send_sem, recv_sem, same=False):
        self.spot, self.outgoing, self.z_rows, self.every = spot, outgoing, z_rows, every
        self.local_sem, self.send_sem, self.recv_sem = local_sem, send_sem, recv_sem
        self.started = {}
        self.rows = every.shape[2]
        self.sources = (spot.c,) + spot.z_to
        self.same = same

    def send(self, u, slot, source, target, to):
        return remote(source, target, self.send_sem.at[u, slot], self.recv_sem.at[u, slot], to)

    def begin(self):
        spot = self.spot
        for m in range(3):
            z = spot.z_to[m]
            source = self.outgoing if self.same else self.outgoing.at[z]
            self.started["z", m] = self.send(1 + m, 0, source, self.z_rows.at[spot.c], (spot.d, z))
        self.spread(0)

    def spread(self, u):
        spot, src = self.spot, self.sources[u]
        if u > 0:
            self.started["z", u - 1].wait_recv()
            source = self.z_rows.at[src, 0 : self.rows]
        else:
            source = self.outgoing if self.same else self.outgoing.at[src, 0 : self.rows]
        target = self.every.at[spot.d, src]
        keep = pltpu.make_async_copy(source, target, self.local_sem.at[u])
        keep.start()
        self.started["keep", u] = keep
        for slot, (name, to) in enumerate((("x", spot.x_to), ("y", spot.y_to), ("c", spot.core_to))):
            self.started[name, u] = self.send(u, 1 + slot, source, target, to)

    def forward(self, u):
        spot, src, mid = self.spot, self.sources[u], self.rows // 2
        self.started["x", u].wait_recv()
        piece = self.every.at[spot.x_d, src, 0:mid]
        self.started["xy", u] = self.send(u, 4, piece, piece, spot.y_to)
        piece = self.every.at[spot.x_d, src]
        self.started["xc", u] = self.send(u, 5, piece, piece, spot.core_to)
        self.started["y", u].wait_recv()
        piece = self.every.at[spot.y_d, src, mid : self.rows]
        self.started["yx", u] = self.send(u, 6, piece, piece, spot.x_to)
        piece = self.every.at[spot.y_d, src]
        self.started["yc", u] = self.send(u, 7, piece, piece, spot.core_to)

    def far(self, u):
        spot, src = self.spot, self.sources[u]
        self.started["xy", u].wait_recv()
        self.started["yx", u].wait_recv()
        piece = self.every.at[spot.far_d, src]
        self.started["fc", u] = self.send(u, 8, piece, piece, spot.core_to)

    def close(self):
        for u in range(4):
            for name in ("c", "xc", "yc", "fc"):
                self.started[name, u].wait_recv()
            self.started["keep", u].wait()
        for (name, _), copy in self.started.items():
            if name != "keep":
                copy.wait_send()


class SumFlow:
    def __init__(self, spot, mine, core_in, x_in, y_in, xy_in, yx_in, z_in, total, out_at, local_sem, send_sem, recv_sem):
        self.spot, self.mine, self.core_in, self.out_at = spot, mine, core_in, out_at
        self.x_in, self.y_in, self.xy_in, self.yx_in, self.z_in, self.total = x_in, y_in, xy_in, yx_in, z_in, total
        self.local_sem, self.send_sem, self.recv_sem = local_sem, send_sem, recv_sem
        self.started = [{} for _ in range(mine.shape[0])]
        self.half = mine.shape[4] // 2

    def send(self, j, slot, source, target, to):
        return remote(source, target, self.send_sem.at[j, slot], self.recv_sem.at[j, slot], to)

    def over_core(self, j, source):
        self.started[j]["core"] = self.send(j, 0, source, self.core_in.at[j], self.spot.core_to)

    def core(self, j):
        spot, mine, half, started = self.spot, self.mine, self.half, self.started[j]
        started["core"].wait_recv()

        @pl.loop(0, 4)
        def _(a):
            for b in range(2):
                for e in range(2):
                    mine[j, a, b, e] = mine[j, a, b, e] + self.core_in[j, a, b, e]

        started["x"] = self.send(j, 1, mine.at[j, :, :, 1 - spot.x, 0:half], self.x_in.at[j], spot.x_to)
        started["y"] = self.send(j, 2, mine.at[j, :, 1 - spot.y, :, half : 2 * half], self.y_in.at[j], spot.y_to)

    def first(self, j):
        spot, mine, half, started = self.spot, self.mine, self.half, self.started[j]
        x, y = spot.x, spot.y
        started["x"].wait_recv()
        for a in range(4):
            for b in range(2):
                mine[j, a, b, x, 0:half] = mine[j, a, b, x, 0:half] + self.x_in[j, a, b]
        started["xy"] = self.send(j, 3, mine.at[j, :, 1 - y, x, 0:half], self.xy_in.at[j], spot.y_to)
        started["y"].wait_recv()
        for a in range(4):
            for e in range(2):
                mine[j, a, y, e, half : 2 * half] = mine[j, a, y, e, half : 2 * half] + self.y_in[j, a, e]
        started["yx"] = self.send(j, 4, mine.at[j, :, y, 1 - x, half : 2 * half], self.yx_in.at[j], spot.x_to)

    def second(self, j):
        spot, mine, half, started = self.spot, self.mine, self.half, self.started[j]
        x, y = spot.x, spot.y
        started["xy"].wait_recv()
        started["yx"].wait_recv()
        for a in range(4):
            mine[j, a, y, x, 0:half] = mine[j, a, y, x, 0:half] + self.xy_in[j, a]
            mine[j, a, y, x, half : 2 * half] = mine[j, a, y, x, half : 2 * half] + self.yx_in[j, a]
        for m in range(3):
            z = spot.z_to[m]
            started["z", m] = self.send(j, 5 + m, mine.at[j, z, y, x], self.z_in.at[j, m], (spot.d, z))

    def along(self, j):
        spot, started, total = self.spot, self.started[j], self.total
        for m in range(3):
            started["z", m].wait_recv()
        own = self.mine[j, spot.c, spot.y, spot.x]
        total[j] = ((own + self.z_in[j, 0]) + self.z_in[j, 1]) + self.z_in[j, 2]
        target = self.out_at(j, spot.d)
        started["keep"] = pltpu.make_async_copy(total.at[j], target, self.local_sem.at[j])
        started["keep"].start()
        pairs = (("gx", spot.x_to), ("gy", spot.y_to), ("gf", spot.far_to), ("gc", spot.core_to))
        for slot, (name, to) in enumerate(pairs):
            started[name] = self.send(j, 8 + slot, total.at[j], target, to)

    def share(self, j):
        spot, started = self.spot, self.started[j]
        for slot, (name, to) in enumerate((("gx", spot.x_to), ("gy", spot.y_to), ("gf", spot.far_to))):
            started[name].wait_recv()
            piece = self.out_at(j, to[0])
            started["c" + name] = self.send(j, 12 + slot, piece, piece, spot.core_to)

    def end(self, j, core_sent=False):
        started = self.started[j]
        for name in ("gc", "cgx", "cgy", "cgf"):
            started[name].wait_recv()
        for name, copy in started.items():
            if name == "keep":
                copy.wait()
            elif not (name == "core" and core_sent):
                copy.wait_send()


def sum_scratch(jobs, piece, lanes):
    half = piece // 2
    return [
        pltpu.VMEM((jobs, 4, 2, 2, piece, lanes), f32),
        pltpu.VMEM((jobs, 4, 2, 2, piece, lanes), f32),
        pltpu.VMEM((jobs, 4, 2, half, lanes), f32),
        pltpu.VMEM((jobs, 4, 2, half, lanes), f32),
        pltpu.VMEM((jobs, 4, half, lanes), f32),
        pltpu.VMEM((jobs, 4, half, lanes), f32),
        pltpu.VMEM((jobs, 3, piece, lanes), f32),
        pltpu.VMEM((jobs, piece, lanes), f32),
    ]


def flow_sems(jobs):
    dma = pltpu.SemaphoreType.DMA
    return [dma((jobs,)), dma((jobs, 15)), dma((jobs, 15)), dma((4,)), dma((4, 9)), dma((4, 9))]


GATE_OF = ((0, 1, 3), (0, 1, 2))


def split_two(value):
    top = value.astype(bf16)
    return top, (value - top.astype(f32)).astype(bf16)


def three_products(first, second, over):
    def product(a, b):
        return lax.dot_general(a, b, (over, ((), ())), preferred_element_type=f32)

    return product(first[0], second[0]) + product(first[1], second[0]) + product(first[0], second[1])


def tail_kernel(
    inputs,
    prevs,
    dgates,
    dstart,
    entering,
    out,
    item_all,
    start_all,
    mine,
    core_in,
    x_in,
    y_in,
    xy_in,
    yx_in,
    z_in,
    total,
    core_out,
    turned,
    acts,
    flow,
    w_flow,
    din,
    z_rows,
    flow_sem,
    start_sem,
    sum_local,
    sum_send,
    sum_recv,
    row_local,
    row_send,
    row_recv,
):
    spot = Spot()
    spot.greet_all()
    c, k = spot.c, spot.k
    jobs, _, _, _, piece, units = mine.shape
    block = din.shape[2]
    events = acts.shape[2]
    gates = jobs // 2
    sums = SumFlow(
        spot, mine, core_in, x_in, y_in, xy_in, yx_in, z_in, total,
        lambda j, d: out.at[j // gates, j % gates, d], sum_local, sum_send, sum_recv,
    )
    rows = RowsFlow(spot, din, z_rows, item_all, row_local, row_send, row_recv)

    def gate_cols(g):
        return dgates.at[:, pl.ds(g * units, units)]

    queue = [inputs, gate_cols(0), gate_cols(1), gate_cols(3), prevs, gate_cols(2)]

    def flow_copy(n):
        return pltpu.make_async_copy(queue[n], flow.at[n % 2], flow_sem.at[n % 2])

    def w_copy(n, slot):
        rows = pl.ds(pl.multiple_of(n * block, block), block)
        return pltpu.make_async_copy(entering.at[rows], w_flow.at[slot], flow_sem.at[2 + slot])

    flow_copy(0).start()
    flow_copy(1).start()
    w_copy(0, 0).start()

    def next_flow(n):
        if n + 2 < len(queue):
            flow_copy(n + 2).start()

    def take_act(n, w):
        flow_copy(n).wait()
        acts[w, 0], acts[w, 1] = split_two(flow[n % 2])
        next_flow(n)

    def take_gate(n, g, at):
        flow_copy(n).wait()

        @pl.loop(0, 4)
        def _(b):
            cols = pl.ds(pl.multiple_of(b * block, block), block)
            value = flow[n % 2, :, cols]
            turned[g, 0, b], turned[g, 1, b] = split_two(value.T)
            if at is not None:
                chunk = 4 * at + b
                slot = lax.rem(b, 2)

                @pl.when(chunk + 1 < 12)
                def _():
                    w_copy(chunk + 1, 1 - slot).start()

                w_copy(chunk, slot).wait()
                share = three_products(split_two(value), split_two(w_flow[slot]), ((1,), (0,)))
                for e in range(4):
                    part = share[:, e * block : (e + 1) * block]
                    if at == 0:
                        before = jnp.where(b == 0, 0.0, din[e, 0:events, :])
                    else:
                        before = din[e, 0:events, :]
                    din[e, 0:events, :] = before + part

        next_flow(n)

    def rows_begin():
        for e in range(4):
            din[e, events:, :] = dstart[:, e * block : (e + 1) * block]
        rows.begin()

    def rows_end():
        keeps = [
            pltpu.make_async_copy(din.at[c, events:], start_all.at[c], start_sem.at[0]),
        ] + [
            pltpu.make_async_copy(z_rows.at[z, events:], start_all.at[z], start_sem.at[1 + m])
            for m, z in enumerate(spot.z_to)
        ]
        for keep in keeps:
            keep.start()
        rows.close()
        for keep in keeps:
            keep.wait()

    def partial(j):
        w, g = j // gates, GATE_OF[j // gates][j % gates]
        slot = j % 2
        if j >= 2:
            sums.started[j - 2]["core"].wait_send()

        @pl.loop(0, 4)
        def _(b):
            value = three_products(
                (turned[g, 0, b], turned[g, 1, b]), (acts[w, 0], acts[w, 1]), ((1,), (0,))
            ).reshape(2, 2, 2, piece, units)
            for p in range(2):
                for q in range(2):
                    mine[j, b, p, q] = jnp.where(k == 0, value[p, q, 0], value[p, q, 1])
                    core_out[slot, b, p, q] = jnp.where(k == 0, value[p, q, 1], value[p, q, 0])

        sums.over_core(j, core_out.at[slot])

    A, B, C, Z, S = sums.core, sums.first, sums.second, sums.along, sums.share

    def E(j):
        sums.end(j, core_sent=j < jobs - 2)

    take_act(0, 0)
    take_gate(1, 0, 0)
    partial(0)
    take_gate(2, 1, 1)
    partial(1)
    A(0)
    take_gate(3, 3, 2)
    rows_begin()
    partial(2)
    A(1)
    take_act(4, 1)
    partial(3)
    A(2), B(0), rows.spread(1), rows.forward(0)
    partial(4)
    A(3), B(1), C(0), rows.spread(2), rows.forward(1), rows.far(0)
    take_gate(5, 2, None)
    partial(5)
    A(4), B(2), C(1), Z(0), rows.spread(3), rows.forward(2), rows.far(1)
    A(5), B(3), C(2), Z(1), S(0), rows.forward(3), rows.far(2)
    B(4), C(3), Z(2), S(1), E(0), rows.far(3)
    B(5), C(4), Z(3), S(2), E(1)
    C(5), Z(4), S(3), E(2)
    rows_end()
    Z(5), S(4), E(3)
    S(5), E(4), E(5)


def run_tail(inputs, prevs, dgates, dstart, entering, collective_id):
    events, units = inputs.shape
    gates, block = 3, units // 4
    piece = block // 8
    jobs = 2 * gates
    start_rows = dstart.shape[0]
    hbm = pl.BlockSpec(memory_space=pl.ANY)
    grads, item_all, start_all = pl.pallas_call(
        tail_kernel,
        out_shape=(
            jax.ShapeDtypeStruct((2, gates, 8, piece, units), f32),
            jax.ShapeDtypeStruct((8, 4, events, block), f32),
            jax.ShapeDtypeStruct((4, start_rows, block), f32),
        ),
        in_specs=[hbm, hbm, hbm, pl.BlockSpec(memory_space=pltpu.VMEM), hbm],
        out_specs=(hbm, hbm, hbm),
        scratch_shapes=sum_scratch(jobs, piece, units)
        + [
            pltpu.VMEM((2, 4, 2, 2, piece, units), f32),
            pltpu.VMEM((4, 2, 4, block, events), bf16),
            pltpu.VMEM((2, 2, events, units), bf16),
            pltpu.VMEM((2, events, units), f32),
            pltpu.VMEM((2, block, units), f32),
            pltpu.VMEM((4, events + start_rows, block), f32),
            pltpu.VMEM((4, events + start_rows, block), f32),
            pltpu.SemaphoreType.DMA((4,)),
            pltpu.SemaphoreType.DMA((4,)),
        ]
        + flow_sems(jobs),
        cost_estimate=takes(190),
        compiler_params=pltpu.CompilerParams(
            collective_id=collective_id, has_side_effects=True, vmem_limit_bytes=VMEM_BYTES
        ),
    )(inputs, prevs, dgates, dstart, entering)
    return grads.reshape(2, gates, 8 * piece, units), item_all, start_all


UNITS = ((0, 0), (0, 1), (1, 0), (0, 2), (1, 1), (1, 2))


def head_kernel(
    chunk,
    width,
    item_ids,
    out_ids,
    embed,
    table,
    bias,
    own_in,
    own_hid,
    carried,
    own_ids,
    all_in,
    all_hid,
    arrived,
    all_ids,
    out_rows,
    padded,
    turned,
    item_rows,
    held,
    local_sem,
    send_sem,
    recv_sem,
    row_send,
    row_recv,
    id_send,
    id_recv,
):
    y, x, k, c, d = place()
    i = pl.program_id(0)
    n = pl.num_programs(0) // 2
    core_to, x_to, y_to = (d + 1 - 2 * k, c), (d + 2 - 4 * x, c), (d + 4 - 8 * y, c)
    z_all = (c + 1 - 2 * lax.rem(c, 2), lax.rem(c + 2, 4), 3 - c)
    owns, alls = (own_in, own_hid), (all_in, all_hid)
    piece = own_in.shape[4]
    half = piece // 2
    block = item_rows.shape[2]
    items = item_rows.shape[1]
    carried_rows = carried.shape[1]
    events = items - carried_rows

    def send(u, slot):
        w, m = UNITS[u]
        z = z_all[m]
        every = alls[w]
        if slot == 0:
            source, target, to = owns[w].at[:, y, x, k], every.at[:, c, y, x, k], (d, z)
        elif slot in (4, 6):
            spot = (
                every.at[:, z, y, 1 - x, k, 0:half] if slot == 4 else every.at[:, z, 1 - y, x, k, half : 2 * half]
            )
            source, target, to = spot, spot, (y_to if slot == 4 else x_to)
        else:
            py, px, to = {
                1: (y, x, x_to),
                2: (y, x, y_to),
                3: (y, x, core_to),
                5: (y, 1 - x, core_to),
                7: (1 - y, x, core_to),
                8: (1 - y, 1 - x, core_to),
            }[slot]
            spot = every.at[:, z, py, px, k]
            source, target = spot, spot
        return pltpu.make_async_remote_copy(
            src_ref=source,
            dst_ref=target,
            send_sem=send_sem.at[u, slot],
            recv_sem=recv_sem.at[u, slot],
            device_id=to,
            device_id_type=MESH,
        )

    def load(w):
        return pltpu.make_async_copy(owns[w], held.at[w], local_sem.at[w])

    def keep(w):
        return pltpu.make_async_copy(held.at[w], alls[w].at[:, c], local_sem.at[2 + w])

    def keep_own(_):
        for w in range(2):
            load(w).wait()
            keep(w).start()

    def item_send(m):
        return pltpu.make_async_remote_copy(
            src_ref=item_rows.at[z_all[m]],
            dst_ref=arrived.at[:, pl.ds(pl.multiple_of(c * block, block), block)],
            send_sem=row_send.at[m],
            recv_sem=row_recv.at[m],
            device_id=(d, z_all[m]),
            device_id_type=MESH,
        )

    def begin_items(_):
        for m in range(3):
            item_send(m).start()

    def item_keep():
        return pltpu.make_async_copy(
            item_rows.at[c], arrived.at[:, pl.ds(pl.multiple_of(c * block, block), block)], local_sem.at[4]
        )

    def id_copy(m):
        to = lax.rem(d + 1 + m, 8)
        return pltpu.make_async_remote_copy(
            src_ref=own_ids,
            dst_ref=all_ids.at[d],
            send_sem=id_send.at[m],
            recv_sem=id_recv.at[m],
            device_id=(to, c),
            device_id_type=MESH,
        )

    def id_keep():
        return pltpu.make_async_copy(own_ids, all_ids.at[d], local_sem.at[5])

    def begin():
        greet([(lax.rem(d + 1 + m, 8), c) for m in range(7)] + [(d, z) for z in z_all])
        id_keep().start()
        for m in range(7):
            id_copy(m).start()
        begin_z(0)
        begin_z(1)
        load(0).start()
        load(1).start()

    def begin_z(u):
        send(u, 0).start()

    def spread(u):
        send(u, 0).wait_recv()
        for slot in (1, 2, 3):
            send(u, slot).start()

    def forward(u):
        send(u, 1).wait_recv()
        send(u, 4).start()
        send(u, 5).start()
        send(u, 2).wait_recv()
        send(u, 6).start()
        send(u, 7).start()

    def far(u):
        send(u, 4).wait_recv()
        send(u, 6).wait_recv()
        send(u, 8).start()

    def close(u):
        for slot in (3, 5, 7, 8):
            send(u, slot).wait_recv()
        for slot in range(9):
            send(u, slot).wait_send()

    timeline = [(-1, begin, None), (4, keep_own, 0), (64, begin_items, 0)]
    timeline += [(at, begin_z, 2 + j) for j, at in enumerate((10, 18, 34, 50))]
    for u, at in enumerate((11, 23, 34, 46, 58, 90)):
        timeline += [(at, spread, u), (at + 12, forward, u), (at + 20, far, u)]
    timeline.sort(key=lambda entry: entry[0])
    last = 2 * n - 1

    @pl.when(i == 0)
    def _():
        padded[...] = jnp.zeros_like(padded)

    for at, action, u in timeline:
        if at < last:

            @pl.when(i == max(at, 0))
            def _(action=action, u=u):
                action() if u is None else action(u)

    @pl.when(i < n)
    def _():
        padded[0:width, :] = embed[...]

    @pl.when(i >= n)
    def _():
        padded[0:width, :] = table[...]
        padded[width : width + 1, :] = bias[...]

    spot = lax.rem(i, n) * chunk
    turned[pl.ds(pl.multiple_of(spot, chunk), chunk), :] = padded[...].T

    @pl.when(i == n - 1)
    def _():
        for z in range(4):

            def body(b, carry, z=z):
                for j in range(8):
                    row = item_ids[z * events + b * 8 + j]
                    item_rows[z, pl.ds(b * 8 + j, 1), :] = turned[pl.ds(row, 1), :]
                return carry

            lax.fori_loop(0, events // 8, body, 0)
            item_rows[z, events:items, :] = carried[z]
        item_keep().start()

    @pl.when(i == last)
    def _():
        def body(b, carry):
            for j in range(8):
                row = out_ids[b * 8 + j]
                out_rows[pl.ds(b * 8 + j, 1), :] = turned[pl.ds(row, 1), :]
            return carry

        lax.fori_loop(0, out_rows.shape[0] // 8, body, 0)
        for at, action, u in timeline:
            if at >= last:
                action(u)
        for u in range(6):
            close(u)
        for m in range(3):
            item_send(m).wait()
        for m in range(7):
            id_copy(m).wait()
        id_keep().wait()
        for w in range(2):
            keep(w).wait()
        item_keep().wait()


def gather_all(embed, table, bias, item_ids, out_ids, own_in, own_hid, carried, own_ids, collective_id):
    width, rows = embed.shape
    gates, block, units = own_in.shape
    piece = block // 8
    chunk = 128 * max(k for k in range(1, 9) if rows % (128 * k) == 0)
    n = rows // chunk
    items = item_ids.shape[0] // 4 + carried.shape[1]
    own_shape = (gates, 2, 2, 2, piece, units)
    all_shape = (gates, 4, 2, 2, 2, piece, units)
    smem = pl.BlockSpec(memory_space=pltpu.SMEM)
    hbm = pl.BlockSpec(memory_space=pl.ANY)
    all_in, all_hid, arrived, all_ids, out_rows = pl.pallas_call(
        functools.partial(head_kernel, chunk, width),
        out_shape=(
            jax.ShapeDtypeStruct(all_shape, f32),
            jax.ShapeDtypeStruct(all_shape, f32),
            jax.ShapeDtypeStruct((items, units), f32),
            jax.ShapeDtypeStruct((8,) + own_ids.shape, jnp.int32),
            jax.ShapeDtypeStruct((out_ids.shape[0], block), f32),
        ),
        grid=(2 * n,),
        in_specs=[
            smem,
            smem,
            pl.BlockSpec((width, chunk), lambda i: (0, jnp.minimum(i, n - 1))),
            pl.BlockSpec((width, chunk), lambda i: (0, jnp.maximum(i - n, 0))),
            pl.BlockSpec((1, chunk), lambda i: (0, jnp.maximum(i - n, 0))),
            hbm,
            hbm,
            pl.BlockSpec(carried.shape, lambda i: (0, 0, 0)),
            pl.BlockSpec(own_ids.shape, lambda i: (0, 0)),
        ],
        out_specs=(hbm, hbm, hbm, hbm, pl.BlockSpec((out_ids.shape[0], block), lambda i: (0, 0))),
        scratch_shapes=[
            pltpu.VMEM((block, chunk), f32),
            pltpu.VMEM((rows, block), f32),
            pltpu.VMEM((4, items, block), f32),
            pltpu.VMEM((2,) + own_shape, f32),
            pltpu.SemaphoreType.DMA((6,)),
            pltpu.SemaphoreType.DMA((6, 9)),
            pltpu.SemaphoreType.DMA((6, 9)),
            pltpu.SemaphoreType.DMA((3,)),
            pltpu.SemaphoreType.DMA((3,)),
            pltpu.SemaphoreType.DMA((7,)),
            pltpu.SemaphoreType.DMA((7,)),
        ],
        cost_estimate=takes(120),
        compiler_params=pltpu.CompilerParams(
            collective_id=collective_id, has_side_effects=True, vmem_limit_bytes=VMEM_BYTES
        ),
    )(item_ids, out_ids, embed, table, bias, own_in.reshape(own_shape), own_hid.reshape(own_shape), carried, own_ids)
    return (
        all_in.reshape(gates, 4 * block, units),
        all_hid.reshape(gates, 4 * block, units),
        arrived,
        all_ids,
        out_rows,
    )


def loss_kernel(width, factor, outs, targets, negs, loss, douts, neg_part, target_part, share, pairs, score):
    n_col, events, block = targets.shape
    n_dp, _, count, _ = negs.shape
    lane = lax.broadcasted_iota(jnp.int32, (events, block), 1)
    for c in range(n_col):
        value = jnp.where(lane < width, outs[:, c * block : (c + 1) * block], 0.0)
        value = jnp.where(lane == width, 1.0 / n_col, value)
        share[c] = value
        pairs[0, c], pairs[1, c] = split_two(value)

    @pl.loop(0, n_dp)
    def _(b):
        cols = pl.ds(pl.multiple_of(b * count, count), count)
        total = jnp.zeros((events, count), f32)
        for c in range(n_col):
            total = total + three_products((pairs[0, c], pairs[1, c]), split_two(negs[b, c]), ((1,), (1,)))
        score[:, cols] = total

    step = 32

    @pl.loop(0, events // step)
    def _(i):
        rows = pl.ds(pl.multiple_of(i * step, step), step)
        pos = jnp.zeros((step, 1), f32)
        for c in range(n_col):
            pos = pos + jnp.sum(share[c, rows, :] * targets[c, rows, :], axis=-1, keepdims=True)
        neg = score[rows, :]
        expd = jnp.exp(neg - jnp.max(neg, axis=-1, keepdims=True))
        weight = expd * (1.0 / jnp.sum(expd, axis=-1, keepdims=True))
        sig = jax.nn.sigmoid(pos - neg)
        slope = weight * sig
        ppos = jnp.sum(slope, axis=-1, keepdims=True)
        quad = jnp.sum(weight * neg * neg, axis=-1, keepdims=True)
        slope = jnp.sum(slope * (1.0 - sig), axis=-1, keepdims=True)
        loss[rows, :] = jnp.broadcast_to(quad - jnp.log(ppos), (step, LANES))
        score[rows, :] = factor * weight * (1.0 - sig * sig * (1.0 / ppos) + neg * neg + 2.0 * neg - quad)
        dpos = -factor * slope / ppos
        for c in range(n_col):
            target_part[c, rows, :] = dpos * share[c, rows, :]
            douts[rows, c * block : (c + 1) * block] = dpos * targets[c, rows, :]

    @pl.loop(0, n_dp)
    def _(b):
        dneg = score[:, pl.ds(pl.multiple_of(b * count, count), count)]
        across, down = split_two(dneg), split_two(dneg.T)
        for c in range(n_col):
            cols = slice(c * block, (c + 1) * block)
            douts[:, cols] = douts[:, cols] + three_products(across, split_two(negs[b, c]), ((1,), (0,)))
            neg_part[c, b] = three_products(down, (pairs[0, c], pairs[1, c]), ((1,), (0,)))

    for c in range(n_col):
        cols = slice(c * block, (c + 1) * block)
        douts[:, cols] = jnp.where(lane < width, douts[:, cols], 0.0)


def run_loss(outs, targets, negs, width, factor):
    n_col, events, block = targets.shape
    n_dp, _, count, _ = negs.shape
    return pl.pallas_call(
        functools.partial(loss_kernel, width, factor),
        out_shape=(
            jax.ShapeDtypeStruct((events, LANES), f32),
            jax.ShapeDtypeStruct(outs.shape, f32),
            jax.ShapeDtypeStruct((n_col, n_dp, count, block), f32),
            jax.ShapeDtypeStruct((n_col, events, block), f32),
        ),
        in_specs=[in_vmem()] * 3,
        out_specs=(in_vmem(),) * 4,
        scratch_shapes=[
            pltpu.VMEM((n_col, events, block), f32),
            pltpu.VMEM((2, n_col, events, block), bf16),
            pltpu.VMEM((events, n_dp * count), f32),
        ],
        cost_estimate=takes(25),
        compiler_params=params(),
    )(outs, targets, negs)


def back_kernel(
    steps,
    hidden,
    douts,
    keep,
    prevs,
    resets,
    updates,
    cands,
    inners,
    neg_part,
    target_part,
    own_loss,
    dgates,
    dstart,
    neg_all,
    target_all,
    loss_all,
    mine,
    core_in,
    x_in,
    y_in,
    xy_in,
    yx_in,
    z_in,
    total,
    w_high,
    w_low,
    w_flow,
    z_rows,
    flow_sem,
    load_sem,
    loss_send,
    loss_recv,
    sum_local,
    sum_send,
    sum_recv,
    row_local,
    row_send,
    row_recv,
):
    spot = Spot()
    spot.greet_all()
    rows_per, units = dstart.shape
    jobs, piece = mine.shape[0], mine.shape[4]
    step_rows = w_flow.shape[1]
    chunks = hidden.shape[0] // step_rows
    sums = SumFlow(
        spot, mine, core_in, x_in, y_in, xy_in, yx_in, z_in, total,
        lambda j, d: neg_all.at[d, pl.ds(j * piece, piece)], sum_local, sum_send, sum_recv,
    )
    rows = RowsFlow(spot, target_part, z_rows, target_all, row_local, row_send, row_recv)

    def load(i, slot):
        part = pl.ds(pl.multiple_of(i * step_rows, step_rows), step_rows)
        return pltpu.make_async_copy(hidden.at[part], w_flow.at[slot], flow_sem.at[slot])

    load(0, 0).start()
    own = []
    for j in range(jobs):
        part = pl.ds(j * piece, piece)
        own.append(pltpu.make_async_copy(neg_part.at[:, :, :, spot.k, part], mine.at[j], load_sem.at[j]))
        own[j].start()
        sums.over_core(j, neg_part.at[:, :, :, 1 - spot.k, part])
    rows.begin()
    losses = [pltpu.make_async_copy(own_loss, loss_all.at[spot.c], load_sem.at[jobs])]
    losses[0].start()
    for m, z in enumerate(spot.z_to):
        losses.append(remote(own_loss, loss_all.at[spot.c], loss_send.at[m], loss_recv.at[m], (spot.d, z)))

    @pl.loop(0, chunks)
    def _(i):
        slot = lax.rem(i, 2)

        @pl.when(i + 1 < chunks)
        def _():
            load(i + 1, 1 - slot).start()

        load(i, slot).wait()
        part = pl.ds(pl.multiple_of(i * step_rows, step_rows), step_rows)
        w_high[part, :], w_low[part, :] = split_two(w_flow[slot])

    def step(i, dstate):
        t = steps - 1 - i
        now = pl.ds(pl.multiple_of(t * rows_per, rows_per), rows_per)
        reset, update, cand = resets[now, :], updates[now, :], cands[now, :]
        dh = douts[now, :] + dstate
        dcand = dh * (1.0 - update) * (1.0 - cand * cand)
        dreset = dcand * inners[now, :] * reset * (1.0 - reset)
        dupdate = dh * (prevs[now, :] - cand) * update * (1.0 - update)
        dinner = dcand * reset
        dgates[now, 0:units] = dreset
        dgates[now, units : 2 * units] = dupdate
        dgates[now, 2 * units : 3 * units] = dinner
        dgates[now, 3 * units : 4 * units] = dcand
        total_now = dh * update
        for g, part in enumerate((dreset, dupdate, dinner)):
            pair = two_part(part)
            sect = slice(g * units, (g + 1) * units)
            first = jnp.dot(pair, w_high[sect, :], preferred_element_type=f32)
            second = jnp.dot(pair, w_low[sect, :], preferred_element_type=f32)
            total_now = total_now + (first[:rows_per] + first[rows_per:] + second[:rows_per])
        return keep[now, :] * total_now

    def sums_core(j):
        own[j].wait()
        sums.core(j)

    A, B, C, Z, S = sums_core, sums.first, sums.second, sums.along, sums.share
    timeline = (
        (0.0, ((A, 0), (A, 1))),
        (0.15, ((rows.forward, 0),)),
        (0.28, ((rows.spread, 1), (B, 0))),
        (0.38, ((rows.forward, 1), (rows.far, 0))),
        (0.47, ((B, 1), (rows.spread, 2))),
        (0.56, ((C, 0), (rows.forward, 2), (rows.far, 1))),
        (0.66, ((C, 1), (rows.spread, 3))),
        (0.78, ((Z, 0), (rows.forward, 3), (rows.far, 2))),
        (0.88, ((Z, 1), (S, 0))),
    )
    state, done = jnp.zeros((rows_per, units), f32), 0
    for share_done, actions in timeline:
        until = int(share_done * steps)
        if until > done:
            state, done = lax.fori_loop(done, until, step, state), until
        for action, argument in actions:
            action(argument)
    dstart[...] = lax.fori_loop(done, steps, step, state)
    rows.far(3)
    S(1)
    sums.end(0)
    rows.close()
    sums.end(1)
    for copy in losses:
        copy.wait()


def run_back(hidden, douts, keep, saved, neg_part, target_part, own_loss, rows_per, steps, collective_id):
    events, units = douts.shape
    count, block = neg_part.shape[2:]
    jobs = 2
    piece = count // jobs
    hbm = pl.BlockSpec(memory_space=pl.ANY)
    step_rows = units // 4
    return pl.pallas_call(
        functools.partial(back_kernel, steps),
        out_shape=(
            jax.ShapeDtypeStruct((events, 4 * units), f32),
            jax.ShapeDtypeStruct((rows_per, units), f32),
            jax.ShapeDtypeStruct((8, count, block), f32),
            jax.ShapeDtypeStruct((8, 4, events, block), f32),
            jax.ShapeDtypeStruct((4,) + own_loss.shape, f32),
        ),
        in_specs=[hbm] + [in_vmem()] * 7 + [hbm, hbm, in_vmem()],
        out_specs=(in_vmem(), in_vmem(), hbm, hbm, hbm),
        scratch_shapes=sum_scratch(jobs, piece, block)
        + [
            pltpu.VMEM(hidden.shape, bf16),
            pltpu.VMEM(hidden.shape, bf16),
            pltpu.VMEM((2, step_rows, units), f32),
            pltpu.VMEM((4, events, block), f32),
            pltpu.SemaphoreType.DMA((2,)),
            pltpu.SemaphoreType.DMA((jobs + 1,)),
            pltpu.SemaphoreType.DMA((3,)),
            pltpu.SemaphoreType.DMA((3,)),
        ]
        + flow_sems(jobs),
        cost_estimate=takes(80),
        compiler_params=pltpu.CompilerParams(
            collective_id=collective_id, has_side_effects=True, vmem_limit_bytes=VMEM_BYTES
        ),
    )(hidden, douts, keep, *saved, neg_part.reshape(4, 2, 2, 2, count, block), target_part, own_loss)


def pad_kernel(weight, bias, out):
    own, full = weight.shape[1:]
    block = out.shape[1]
    n_col = out.shape[2] // block
    part = full // n_col
    out[...] = jnp.zeros_like(out)
    for c in range(n_col):
        out[0, 0:own, c * block : c * block + part] = weight[0, :, c * part : (c + 1) * part]
    out[0, 0:own, part : part + 1] = bias[0]


def pad_units(weight, bias, n_col, block):
    gates, own, full = weight.shape
    return pl.pallas_call(
        pad_kernel,
        out_shape=jax.ShapeDtypeStruct((gates, block, n_col * block), f32),
        grid=(gates,),
        in_specs=[
            pl.BlockSpec((1, own, full), lambda g: (g, 0, 0)),
            pl.BlockSpec((1, own, 1), lambda g: (g, 0, 0)),
        ],
        out_specs=pl.BlockSpec((1, block, n_col * block), lambda g: (g, 0, 0)),
        compiler_params=params(),
    )(weight, bias[:, :, None])


def gather_weight(own, n_dp):
    gates, block, units = own.shape
    flat = own.reshape(n_dp, gates * block // n_dp, units)
    piece = lax.dynamic_index_in_dim(flat, lax.axis_index("dp"), 0, keepdims=False)
    every = lax.all_gather(piece, ("col", "dp"))
    every = every.reshape(-1, gates, block, units)
    return jnp.moveaxis(every, 0, 1).reshape(gates, -1, units)


def reduce_weight(partial, n_dp, n_col):
    gates, rows, units = partial.shape
    block = rows // n_col
    parts = jnp.moveaxis(partial.reshape(gates, n_col, block, units), 1, 0)
    parts = jnp.moveaxis(parts.reshape(n_col, n_dp, gates * block // n_dp, units), 1, 0)
    mine = lax.psum_scatter(parts, "dp", scatter_dimension=0)
    mine = lax.psum_scatter(mine, "col", scatter_dimension=0)
    return lax.all_gather(mine, "dp").reshape(gates, block, units)


def swap_col(rows, n_col):
    return lax.all_to_all(rows, "col", split_axis=0, concat_axis=0, tiled=True)


def unpad_last(value, n_col, part):
    block = value.shape[-1] // n_col
    return value.reshape(value.shape[:-1] + (n_col, block))[..., :part].reshape(value.shape[:-1] + (n_col * part,))


def local(
    n_dp,
    n_col,
    item_ids,
    target_ids,
    negative_ids,
    reset_mask,
    carry_flags,
    carried_state,
    embed_table,
    input_weight,
    hidden_weight,
    gate_bias,
    hidden_bias,
    out_table,
    out_bias,
):
    sessions, steps = item_ids.shape
    own_sessions = sessions // n_col
    rows_per = round_up(own_sessions, ROWS8)
    width = embed_table.shape[0]
    table_rows = embed_table.shape[1]
    own_rows = table_rows // n_dp
    block = round_up(width + 1, LANES)
    units = n_col * block
    events = steps * rows_per
    direct = n_dp == 8 and n_col == 4 and block % 64 == 0 and own_sessions == rows_per
    factor = 1.0 / steps
    dp_at, col_at = lax.axis_index("dp"), lax.axis_index("col")

    def by_owner(value):
        value = jnp.moveaxis(value.reshape(n_col, own_sessions, steps), 1, 2)
        value = jnp.pad(value, ((0, 0), (0, 0), (0, rows_per - own_sessions)))
        return value.reshape(-1)

    item_flat, target_flat = by_owner(item_ids), by_owner(target_ids)
    own_keep = lax.dynamic_index_in_dim(
        by_owner(1 - reset_mask).reshape(n_col, events, 1), col_at, 0, keepdims=False
    ).astype(f32)
    valid = jnp.tile(jnp.arange(rows_per) < own_sessions, steps)
    lane = jnp.arange(units) % block
    first_pad = jnp.arange(units) == width

    own_in = pad_units(input_weight, gate_bias, n_col, block)
    no_bias = jnp.zeros_like(hidden_bias)
    own_hid = pad_units(hidden_weight, jnp.stack([no_bias, no_bias, hidden_bias]), n_col, block)

    carried = (carry_flags.astype(f32)[:, None] * carried_state).reshape(n_col, own_sessions, width)
    carried = jnp.pad(carried, ((0, 0), (0, rows_per - own_sessions), (0, block - width)))
    neg_count = negative_ids.shape[0]
    own_negs = lax.dynamic_slice_in_dim(negative_ids, dp_at * (neg_count // n_dp), neg_count // n_dp)
    out_ids = jnp.concatenate([target_flat, own_negs])
    if direct:
        own_ids = jnp.concatenate([item_flat, target_flat]).reshape(-1, LANES)
        all_in, all_hid, arrived, all_ids, out_rows = gather_all(
            embed_table, out_table, out_bias[None, :], item_flat, out_ids, own_in, own_hid, carried, own_ids, 1
        )
        all_ids = all_ids.reshape(n_dp, 2, -1)
    else:
        all_hid = gather_weight(own_hid, n_dp)
        all_in = gather_weight(own_in, n_dp)
        no_row = jnp.zeros((1, table_rows), f32)
        item_rows = gather_rows(embed_table, no_row, item_flat, block).reshape(n_col, events, block)
        arrived = swap_col(jnp.concatenate([item_rows, carried], axis=1), n_col)
        arrived = jnp.moveaxis(arrived, 0, 1).reshape(events + rows_per, units)
        out_rows = gather_rows(out_table, out_bias[None, :], out_ids, block)
        all_ids = lax.all_gather(jnp.stack([item_flat, target_flat]), "dp")
    all_hid, all_in = all_hid.reshape(-1, units), all_in.reshape(-1, units)
    inputs = jnp.where(first_pad, 1.0, arrived[:events])
    start = arrived[events:]
    all_items, all_targets = all_ids[:, 0].reshape(-1), all_ids[:, 1].reshape(-1)
    count = all_items.shape[0]
    keys = jnp.concatenate([all_items, all_targets + table_rows, negative_ids + 2 * table_rows])
    order = jnp.concatenate([jnp.tile(lax.iota(jnp.int32, count), 2), lax.iota(jnp.int32, neg_count)])
    scale = 1 << (max(count, neg_count) - 1).bit_length()
    if 3 * table_rows * scale < 2**31:
        packed = lax.sort(keys * scale + order)
        keys, order = packed // scale, packed % scale
    else:
        keys, order = lax.sort((keys, order), num_keys=1)
    low = (dp_at * own_rows).astype(jnp.int32)
    by_item = (order[:count], keys[:count])
    by_target = (order[count : 2 * count], keys[count : 2 * count] - table_rows)
    by_neg = (order[2 * count :], keys[2 * count :] - 2 * table_rows)

    out_targets = out_rows[: n_col * events].reshape(n_col, events, block)
    out_negs = out_rows[n_col * events :]
    if direct:
        *saved, outs, negs, targets = run_forward_travel(
            all_hid, all_in, inputs, own_keep, start, out_negs, out_targets, steps, width, 4
        )
    else:
        targets = swap_col(out_targets, n_col)
        negs = lax.all_gather(out_negs, ("dp", "col")).reshape(n_dp, n_col, -1, block)
        *saved, outs = run_forward(all_hid, all_in, inputs, own_keep, start, steps, width)
    prevs = saved[0]

    if direct:
        own_loss, douts, neg_part, target_part = run_loss(outs, targets, negs, width, factor)
        own_loss = jnp.pad(own_loss[:, 0].reshape(steps, rows_per).T, ((0, 0), (0, round_up(steps, LANES) - steps)))
        dgates, dstart, neg_all, target_all, loss_all = run_back(
            all_hid, douts, own_keep, saved, neg_part, target_part, own_loss, rows_per, steps, 3
        )
        loss = loss_all[:, :, :steps].reshape(sessions, steps)
        neg_all, target_all = neg_all.reshape(-1, block), target_all.reshape(-1, block)
    else:
        targets = jnp.moveaxis(targets, 0, 1).reshape(events, units)
        negs = jnp.moveaxis(negs, 1, 2).reshape(neg_count, units)
        shares = jnp.where(lane == width, 1.0 / n_col, jnp.where(lane < width, outs, 0.0))
        pos_score = jnp.sum(shares * targets, axis=-1, keepdims=True)
        neg_score = lax.dot_general(shares, negs, (((1,), (1,)), ((), ())), precision=high)
        top = jnp.max(neg_score, axis=-1, keepdims=True)
        expd = jnp.exp(neg_score - top)
        weight = expd / jnp.sum(expd, axis=-1, keepdims=True)
        sig = jax.nn.sigmoid(pos_score - neg_score)
        ppos = jnp.sum(weight * sig, axis=-1, keepdims=True)
        quad = jnp.sum(weight * neg_score * neg_score, axis=-1, keepdims=True)
        slope = jnp.sum(weight * sig * (1.0 - sig), axis=-1, keepdims=True)
        own_loss = -jnp.log(ppos) + quad
        dneg = factor * weight * (1.0 - sig * sig / ppos + neg_score * neg_score + 2.0 * neg_score - quad)
        dneg = jnp.where(valid[:, None], dneg, 0.0)
        dpos = jnp.where(valid[:, None], -factor * slope / ppos, 0.0)
        douts = jnp.dot(dneg, negs, precision=high) + dpos * targets
        douts = jnp.where(lane < width, douts, 0.0)
        neg_part = lax.dot_general(dneg, shares, (((0,), (0,)), ((), ())), precision=high)
        target_part = dpos * shares

        neg_own = lax.psum_scatter(neg_part.reshape(n_dp, -1, units), "dp", scatter_dimension=0)
        neg_own = jnp.moveaxis(neg_own.reshape(-1, n_col, block), 1, 0)
        neg_own = lax.psum_scatter(neg_own, "col", scatter_dimension=0)
        neg_all = lax.all_gather(neg_own, "dp", tiled=True)
        target_own = swap_col(jnp.moveaxis(target_part.reshape(events, n_col, block), 1, 0), n_col)
        target_all = lax.all_gather(target_own.reshape(-1, block), "dp", tiled=True)
        dgates, dstart = run_backward(all_hid, douts, own_keep, saved, rows_per, steps)
        own_loss = own_loss.reshape(steps, rows_per)[:, :own_sessions]
        loss = lax.all_gather(own_loss.T, "col", tiled=True)
    grad_out, grad_obias = scatter_rows(
        [by_target + (target_all,), by_neg + (neg_all,)],
        low,
        own_rows,
        width,
        block,
    )
    grad_obias = grad_obias[0] * n_col

    gates = input_weight.shape[0]
    if direct:
        reduced, item_all, start_all = run_tail(inputs, prevs, dgates, dstart, all_in, 2)
        grad_in, grad_hid = reduced[0], reduced[1]
        item_all = item_all.reshape(-1, block)
    else:
        dx = jnp.concatenate([dgates[:, : 2 * units], dgates[:, 3 * units :]], axis=1)
        dh = dgates[:, : 3 * units]
        hid_part = lax.dot_general(dh, prevs, (((0,), (0,)), ((), ())), precision=high)
        in_part = lax.dot_general(dx, inputs, (((0,), (0,)), ((), ())), precision=high)
        dinputs = jnp.dot(dx, all_in, precision=high)
        back = jnp.concatenate([dinputs, dstart], axis=0).reshape(events + rows_per, n_col, block)
        back = swap_col(jnp.moveaxis(back, 1, 0), n_col)
        item_all = lax.all_gather(back[:, :events].reshape(-1, block), "dp", tiled=True)
        start_all = back[:, events:]
        grad_in = reduce_weight(in_part.reshape(gates, units, units), n_dp, n_col)
        grad_hid = reduce_weight(hid_part.reshape(gates, units, units), n_dp, n_col)
    grad_carried = start_all[:, :own_sessions, :width].reshape(sessions, width)
    grad_carried = carry_flags.astype(f32)[:, None] * grad_carried
    grad_embed, _ = scatter_rows([by_item + (item_all,)], low, own_rows, width, block)
    grad_in, grad_hid = grad_in[:, :width], grad_hid[:, :width]
    return (
        loss,
        grad_embed,
        unpad_last(grad_in, n_col, width),
        unpad_last(grad_hid, n_col, width),
        grad_in[:, :, width],
        grad_hid[gates - 1, :, width],
        grad_out,
        grad_obias,
        grad_carried,
    )


def solution(mesh):
    in_specs = (
        P("dp", None),
        P("dp", None),
        P(),
        P("dp", None),
        P("dp"),
        P("dp", "col"),
        P("col", None),
        P(None, "col", None),
        P(None, "col", None),
        P(None, "col"),
        P("col"),
        P("col", None),
        P(),
    )
    out_specs = (
        P("dp", None),
        P("col", "dp"),
        P(None, "col", None),
        P(None, "col", None),
        P(None, "col"),
        P("col"),
        P("col", "dp"),
        P("dp"),
        P("dp", "col"),
    )
    body = functools.partial(local, mesh.shape["dp"], mesh.shape["col"])
    return jax.shard_map(body, mesh=mesh, in_specs=in_specs, out_specs=out_specs, check_vma=False)
```

```python
import functools

import jax
import jax.numpy as jnp
from jax import lax
from jax.experimental import pallas as pl
from jax.experimental.pallas import tpu as pltpu
from jax.sharding import PartitionSpec as P

LANES = 128
ROWS8 = 8
VMEM_BYTES = 60 << 20
f32 = jnp.float32
bf16 = jnp.bfloat16
high = lax.Precision.HIGH
MESH = pl.DeviceIdType.MESH


def round_up(value, unit):
    return -(-value // unit) * unit


def params():
    return pltpu.CompilerParams(vmem_limit_bytes=VMEM_BYTES)


def takes(micros):
    return pl.CostEstimate(flops=int(micros * 1.1e9), bytes_accessed=1 << 20, transcendentals=0)


def in_vmem():
    return pl.BlockSpec(memory_space=pltpu.VMEM)


def in_smem():
    return pl.BlockSpec(memory_space=pltpu.SMEM)


def gather_kernel(chunk, count, width, ids, table, bias, out, padded, turned):
    step = pl.program_id(0)

    @pl.when(step == 0)
    def _():
        padded[...] = jnp.zeros_like(padded)

    padded[0:width, :] = table[...]
    padded[width : width + 1, :] = bias[...]
    turned[pl.ds(pl.multiple_of(step * chunk, chunk), chunk), :] = padded[...].T

    @pl.when(step == pl.num_programs(0) - 1)
    def _():
        def body(block, carry):
            for j in range(ROWS8):
                row = ids[block * ROWS8 + j]
                out[pl.ds(block * ROWS8 + j, 1), :] = turned[pl.ds(row, 1), :]
            return carry

        lax.fori_loop(0, count // ROWS8, body, 0)


def gather_rows(table, bias, ids, block):
    width, rows = table.shape
    count = ids.shape[0]
    chunk = LANES * max(k for k in range(1, 9) if rows % (LANES * k) == 0)
    return pl.pallas_call(
        functools.partial(gather_kernel, chunk, count, width),
        out_shape=jax.ShapeDtypeStruct((count, block), f32),
        grid_spec=pltpu.PrefetchScalarGridSpec(
            num_scalar_prefetch=1,
            grid=(rows // chunk,),
            in_specs=[
                pl.BlockSpec((width, chunk), lambda i, ids: (0, i)),
                pl.BlockSpec((1, chunk), lambda i, ids: (0, i)),
            ],
            out_specs=pl.BlockSpec((count, block), lambda i, ids: (0, 0)),
            scratch_shapes=[pltpu.VMEM((block, chunk), f32), pltpu.VMEM((rows, block), f32)],
        ),
        compiler_params=params(),
    )(ids, table, bias)


def scatter_kernel(width, n_lists, *refs):
    bounds = refs[0]
    lists = refs[1 : 1 + 3 * n_lists]
    out, bias_out, acc = refs[1 + 3 * n_lists :]
    acc[...] = jnp.zeros_like(acc)
    low = bounds[0]
    for k in range(n_lists):
        rows_of, ids, data = lists[3 * k : 3 * k + 3]

        def body(i, carry):
            spot = pl.ds(ids[i] - low, 1)
            acc[spot, :] = acc[spot, :] + data[pl.ds(rows_of[i], 1), :]
            return carry

        lax.fori_loop(bounds[1 + 2 * k], bounds[2 + 2 * k], body, 0)
    for j in range(acc.shape[0] // LANES):
        cols = slice(j * LANES, (j + 1) * LANES)
        turned = acc[cols, :].T
        out[:, cols] = turned[:width]
        bias_out[:, cols] = turned[width : width + 1]


def scatter_rows(lists, low, own_rows, width, block):
    ends = [low]
    operands, specs = [], []
    for order, ids, data in lists:
        ends += [jnp.sum(ids < low, dtype=jnp.int32), jnp.sum(ids < low + own_rows, dtype=jnp.int32)]
        operands += [order, ids, data]
        specs += [in_smem(), in_smem(), in_vmem()]
    return pl.pallas_call(
        functools.partial(scatter_kernel, width, len(lists)),
        out_shape=(
            jax.ShapeDtypeStruct((width, own_rows), f32),
            jax.ShapeDtypeStruct((1, own_rows), f32),
        ),
        in_specs=[in_smem()] + specs,
        out_specs=(in_vmem(), in_vmem()),
        scratch_shapes=[pltpu.VMEM((own_rows, block), f32)],
        cost_estimate=takes(20),
        compiler_params=params(),
    )(jnp.stack(ends), *operands)


def finish_kernel(
    shift,
    table_rows,
    width,
    low,
    packed,
    items,
    targets,
    negs,
    grads,
    grad_embed,
    grad_out,
    grad_bias,
    grad_in,
    grad_hid,
    even,
    odd,
    item_buf,
    target_buf,
    neg_buf,
    grad_buf,
    embed_out,
    out_out,
    bias_out,
    weight_out,
    sem,
):
    own_rows = even.shape[0]
    events, neg_count = item_buf.shape[0], neg_buf.shape[0]
    n_col = grad_buf.shape[3] // even.shape[1]
    block = even.shape[1]
    loads = [
        pltpu.make_async_copy(source, target, sem.at[n])
        for n, (source, target) in enumerate(
            ((targets, target_buf), (negs, neg_buf), (grads, grad_buf), (items, item_buf))
        )
    ]
    for load in loads:
        load.start()
    stores = [
        pltpu.make_async_copy(source, target, sem.at[4 + n])
        for n, (source, target) in enumerate(
            (
                (out_out, grad_out),
                (bias_out, grad_bias),
                (weight_out.at[0], grad_in),
                (weight_out.at[1], grad_hid),
                (embed_out, grad_embed),
            )
        )
    ]

    def first_from(begin, count, bound):
        def halve(_, ends):
            left, right = ends
            middle = jnp.minimum((left + right) // 2, begin + count - 1)
            less = (left < right) & (packed[middle] < bound)
            return jnp.where(less, middle + 1, left), jnp.where(less | (left >= right), right, middle)

        return lax.fori_loop(0, count.bit_length() + 1, halve, (begin, begin + count))[0]

    def add(begin, count, which, data):
        base = low[0] + which * table_rows
        left = first_from(begin, count, base << shift)
        right = first_from(begin, count, (base + own_rows) << shift)

        def one(i, acc):
            key = packed[i]
            spot, row = (key >> shift) - base, key & ((1 << shift) - 1)
            acc[pl.ds(spot, 1), :] = acc[pl.ds(spot, 1), :] + data[pl.ds(row, 1), :]

        def four(i, carry):
            for n in range(4):
                one(left + 4 * i + n, (even, odd)[n % 2])
            return carry

        fours = (right - left) // 4
        lax.fori_loop(0, fours, four, 0)

        def rest(i, carry):
            one(i, even)
            return carry

        lax.fori_loop(left + 4 * fours, right, rest, 0)

    def clear():
        @pl.loop(0, own_rows // LANES)
        def _(j):
            rows = pl.ds(pl.multiple_of(j * LANES, LANES), LANES)
            even[rows, :] = jnp.zeros((LANES, block), f32)
            odd[rows, :] = jnp.zeros((LANES, block), f32)

    def turn(out, bias):
        @pl.loop(0, own_rows // LANES)
        def _(j):
            rows = pl.ds(pl.multiple_of(j * LANES, LANES), LANES)
            turned = (even[rows, :] + odd[rows, :]).T
            out[:, rows] = turned[:width]
            if bias is not None:
                bias[:, rows] = turned[width : width + 1] * n_col

    clear()
    loads[0].wait()
    add(events, events, 1, target_buf)
    loads[1].wait()
    add(2 * events, neg_count, 2, neg_buf)
    turn(out_out, bias_out)
    stores[0].start()
    stores[1].start()
    loads[2].wait()
    part = weight_out.shape[3] // n_col
    for w in range(2):
        for g in range(weight_out.shape[1]):
            for b in range(n_col):
                weight_out[w, g, :, b * part : (b + 1) * part] = grad_buf[w, g, 0:width, b * block : b * block + part]
        stores[2 + w].start()
    clear()
    loads[3].wait()
    add(0, events, 0, item_buf)
    turn(embed_out, None)
    stores[4].start()
    for store in stores:
        store.wait()


def run_finish(packed, shift, low, table_rows, own_rows, width, items, targets, negs, grads):
    events, block = items.shape
    _, gates, _, units = grads.shape
    n_col = units // block
    hbm = pl.BlockSpec(memory_space=pl.ANY)
    weight = jax.ShapeDtypeStruct((gates, width, n_col * width), f32)
    table = jax.ShapeDtypeStruct((width, own_rows), f32)
    return pl.pallas_call(
        functools.partial(finish_kernel, shift, table_rows, width),
        out_shape=(table, table, jax.ShapeDtypeStruct((1, own_rows), f32), weight, weight),
        in_specs=[in_smem(), in_smem()] + [hbm] * 4,
        out_specs=(hbm,) * 5,
        scratch_shapes=[
            pltpu.VMEM((own_rows, block), f32),
            pltpu.VMEM((own_rows, block), f32),
            pltpu.VMEM(items.shape, f32),
            pltpu.VMEM(targets.shape, f32),
            pltpu.VMEM(negs.shape, f32),
            pltpu.VMEM(grads.shape, f32),
            pltpu.VMEM((width, own_rows), f32),
            pltpu.VMEM((width, own_rows), f32),
            pltpu.VMEM((1, own_rows), f32),
            pltpu.VMEM((2,) + weight.shape, f32),
            pltpu.SemaphoreType.DMA((9,)),
        ],
        cost_estimate=takes(40),
        compiler_params=params(),
    )(low.reshape(1), packed, items, targets, negs, grads)


def split_weight(weight, high_part, low_part):
    step = 128

    @pl.loop(0, weight.shape[0] // step)
    def _(i):
        rows = pl.ds(pl.multiple_of(i * step, step), step)
        value = weight[rows, :]
        top = value.astype(bf16)
        high_part[rows, :] = top
        low_part[rows, :] = (value - top.astype(f32)).astype(bf16)


def two_part(value):
    top = value.astype(bf16).astype(f32)
    return jnp.concatenate([top, value - top], axis=0).astype(bf16)


def forward_kernel(
    steps,
    width,
    hidden,
    entering,
    inputs,
    keep,
    start,
    prevs,
    resets,
    updates,
    cands,
    inners,
    outs,
    w_high,
    w_low,
    x_gates,
    hid_buf,
    in_buf,
    pair_buf,
    sem,
    travel=None,
):
    rows_per, units = start.shape
    step_rows = hid_buf.shape[1]
    chunks = hidden.shape[0] // step_rows

    def load(i, slot):
        rows = pl.ds(pl.multiple_of(i * step_rows, step_rows), step_rows)
        return (
            pltpu.make_async_copy(hidden.at[rows], hid_buf.at[slot], sem.at[0, slot]),
            pltpu.make_async_copy(entering.at[rows], in_buf.at[slot], sem.at[1, slot]),
        )

    for copy in load(0, 0):
        copy.start()
    timeline = travel() if travel else ()
    top = inputs[...].astype(bf16)
    pair_buf[0] = top
    pair_buf[1] = (inputs[...] - top.astype(f32)).astype(bf16)

    @pl.loop(0, chunks)
    def _(i):
        slot = lax.rem(i, 2)

        @pl.when(i + 1 < chunks)
        def _():
            for copy in load(i + 1, 1 - slot):
                copy.start()

        for copy in load(i, slot):
            copy.wait()
        cols = pl.ds(pl.multiple_of(i * step_rows, step_rows), step_rows)
        turned = hid_buf[slot].T
        first = turned.astype(bf16)
        w_high[:, cols] = first
        w_low[:, cols] = (turned - first.astype(f32)).astype(bf16)
        value = in_buf[slot]
        first = value.astype(bf16)
        second = (value - first.astype(f32)).astype(bf16)
        over = (((1,), (1,)), ((), ()))
        x_gates[:, cols] = (
            lax.dot_general(pair_buf[0], first, over, preferred_element_type=f32)
            + lax.dot_general(pair_buf[1], first, over, preferred_element_type=f32)
            + lax.dot_general(pair_buf[0], second, over, preferred_element_type=f32)
        )

    lane = lax.broadcasted_iota(jnp.int32, (rows_per, units), 1)

    def step(t, state):
        rows = pl.ds(pl.multiple_of(t * rows_per, rows_per), rows_per)
        prev = jnp.where(lane == width, 1.0, keep[rows, :] * state)
        pair = two_part(prev)

        def gate(g):
            cols = slice(g * units, (g + 1) * units)
            first = jnp.dot(pair, w_high[:, cols], preferred_element_type=f32)
            second = jnp.dot(pair, w_low[:, cols], preferred_element_type=f32)
            return first[:rows_per] + first[rows_per:] + second[:rows_per], cols

        h_reset, cols = gate(0)
        reset = jax.nn.sigmoid(x_gates[rows, cols] + h_reset)
        h_update, cols = gate(1)
        update = jax.nn.sigmoid(x_gates[rows, cols] + h_update)
        inner, cols = gate(2)
        cand = jnp.tanh(x_gates[rows, cols] + reset * inner)
        new = (1.0 - update) * cand + update * prev
        prevs[rows, :] = prev
        resets[rows, :] = reset
        updates[rows, :] = update
        cands[rows, :] = cand
        inners[rows, :] = inner
        outs[rows, :] = new
        return new

    state, done = start[...], 0
    for share_done, actions in timeline:
        until = int(share_done * steps)
        if until > done:
            state, done = lax.fori_loop(done, until, step, state), until
        for action, argument in actions:
            action(argument)
    lax.fori_loop(done, steps, step, state)


def forward_travel_kernel(steps, width, hidden, entering, inputs, keep, start, neg_own, target_own, *refs):
    saved, (neg_all, targets), scratch = refs[:6], refs[6:8], refs[8:]
    z_rows, target_send, target_recv, target_local, row_local, row_send, row_recv = scratch[7:]
    spot = Spot()
    rows = RowsFlow(spot, neg_own, z_rows, neg_all, row_local, row_send, row_recv, same=True)
    copies = []

    def begin_targets(_):
        keep_own = pltpu.make_async_copy(target_own.at[spot.c], targets.at[spot.c], target_local.at[0])
        keep_own.start()
        copies.append(keep_own)
        for m, z in enumerate(spot.z_to):
            copies.append(
                remote(target_own.at[z], targets.at[spot.c], target_send.at[m], target_recv.at[m], (spot.d, z))
            )

    def travel():
        spot.greet_all()
        rows.begin()
        return (
            (0.0, ((rows.forward, 0),)),
            (0.1, ((rows.spread, 1),)),
            (0.2, ((rows.far, 0),)),
            (0.3, ((rows.forward, 1), (rows.spread, 2), (begin_targets, None))),
            (0.4, ((rows.far, 1),)),
            (0.5, ((rows.forward, 2), (rows.spread, 3))),
            (0.6, ((rows.far, 2),)),
            (0.7, ((rows.forward, 3),)),
            (0.85, ((rows.far, 3),)),
        )

    forward_kernel(steps, width, hidden, entering, inputs, keep, start, *saved, *scratch[:7], travel=travel)
    rows.close()
    for copy in copies:
        copy.wait()


def forward_scratch(hidden, inputs):
    events, units = inputs.shape
    step_rows = units // 4
    return [
        pltpu.VMEM(hidden.shape[::-1], bf16),
        pltpu.VMEM(hidden.shape[::-1], bf16),
        pltpu.VMEM((events, hidden.shape[0]), f32),
        pltpu.VMEM((2, step_rows, units), f32),
        pltpu.VMEM((2, step_rows, units), f32),
        pltpu.VMEM((2, events, units), bf16),
        pltpu.SemaphoreType.DMA((2, 2)),
    ]


def run_forward(hidden, entering, inputs, keep, start, steps, width):
    saved = jax.ShapeDtypeStruct(inputs.shape, f32)
    hbm = pl.BlockSpec(memory_space=pl.ANY)
    return pl.pallas_call(
        functools.partial(forward_kernel, steps, width),
        out_shape=(saved,) * 6,
        in_specs=[hbm, hbm] + [in_vmem()] * 3,
        out_specs=(in_vmem(),) * 6,
        scratch_shapes=forward_scratch(hidden, inputs),
        cost_estimate=takes(75),
        compiler_params=params(),
    )(hidden, entering, inputs, keep, start)


def run_forward_travel(hidden, entering, inputs, keep, start, neg_own, target_own, steps, width, collective_id):
    saved = jax.ShapeDtypeStruct(inputs.shape, f32)
    hbm = pl.BlockSpec(memory_space=pl.ANY)
    dma = pltpu.SemaphoreType.DMA
    return pl.pallas_call(
        functools.partial(forward_travel_kernel, steps, width),
        out_shape=(saved,) * 6
        + (jax.ShapeDtypeStruct((8, 4) + neg_own.shape, f32), jax.ShapeDtypeStruct(target_own.shape, f32)),
        in_specs=[hbm, hbm] + [in_vmem()] * 3 + [hbm, hbm],
        out_specs=(in_vmem(),) * 6 + (hbm, hbm),
        scratch_shapes=forward_scratch(hidden, inputs)
        + [pltpu.VMEM((4,) + neg_own.shape, f32), dma((3,)), dma((3,)), dma((1,)), dma((4,)), dma((4, 9)), dma((4, 9))],
        cost_estimate=takes(75),
        compiler_params=pltpu.CompilerParams(
            collective_id=collective_id, has_side_effects=True, vmem_limit_bytes=VMEM_BYTES
        ),
    )(hidden, entering, inputs, keep, start, neg_own, target_own)


def backward_kernel(
    steps, weight, douts, keep, prevs, resets, updates, cands, inners, dgates, dstart, w_high, w_low
):
    rows_per, units = dstart.shape
    split_weight(weight, w_high, w_low)

    def step(i, dstate):
        t = steps - 1 - i
        rows = pl.ds(pl.multiple_of(t * rows_per, rows_per), rows_per)
        reset, update, cand = resets[rows, :], updates[rows, :], cands[rows, :]
        dh = douts[rows, :] + dstate
        dcand = dh * (1.0 - update) * (1.0 - cand * cand)
        dreset = dcand * inners[rows, :] * reset * (1.0 - reset)
        dupdate = dh * (prevs[rows, :] - cand) * update * (1.0 - update)
        dinner = dcand * reset
        dgates[rows, 0:units] = dreset
        dgates[rows, units : 2 * units] = dupdate
        dgates[rows, 2 * units : 3 * units] = dinner
        dgates[rows, 3 * units : 4 * units] = dcand
        total = dh * update
        for g, part in enumerate((dreset, dupdate, dinner)):
            pair = two_part(part)
            sect = slice(g * units, (g + 1) * units)
            first = jnp.dot(pair, w_high[sect, :], preferred_element_type=f32)
            second = jnp.dot(pair, w_low[sect, :], preferred_element_type=f32)
            total = total + (first[:rows_per] + first[rows_per:] + second[:rows_per])
        return keep[rows, :] * total

    dstart[...] = lax.fori_loop(0, steps, step, jnp.zeros((rows_per, units), f32))


def run_backward(weight, douts, keep, saved, rows_per, steps):
    events, units = douts.shape
    return pl.pallas_call(
        functools.partial(backward_kernel, steps),
        out_shape=(
            jax.ShapeDtypeStruct((events, 4 * units), f32),
            jax.ShapeDtypeStruct((rows_per, units), f32),
        ),
        in_specs=[in_vmem()] * 8,
        out_specs=(in_vmem(),) * 2,
        scratch_shapes=[pltpu.VMEM(weight.shape, bf16)] * 2,
        cost_estimate=takes(67),
        compiler_params=params(),
    )(weight, douts, keep, *saved)


def place():
    d = lax.axis_index("dp")
    c = lax.axis_index("col")
    return d // 4, (d // 2) % 2, d % 2, c, d


def greet(partners):
    barrier = pltpu.get_barrier_semaphore()
    for partner in partners:
        pl.semaphore_signal(barrier, inc=1, device_id=partner, device_id_type=MESH)
    pl.semaphore_wait(barrier, len(partners))


class Spot:
    def __init__(self):
        self.y, self.x, self.k, self.c, self.d = place()
        y, x, k, c, d = self.y, self.x, self.k, self.c, self.d
        self.x_d, self.y_d, self.core_d = d + 2 - 4 * x, d + 4 - 8 * y, d + 1 - 2 * k
        self.far_d = d + 6 - 4 * x - 8 * y
        self.core_to, self.x_to, self.y_to, self.far_to = (self.core_d, c), (self.x_d, c), (self.y_d, c), (self.far_d, c)
        self.z_to = (c + 1 - 2 * lax.rem(c, 2), lax.rem(c + 2, 4), 3 - c)

    def greet_all(self):
        greet([self.core_to, self.x_to, self.y_to, self.far_to] + [(self.d, z) for z in self.z_to])


def remote(source, target, send, recv, to):
    copy = pltpu.make_async_remote_copy(
        src_ref=source, dst_ref=target, send_sem=send, recv_sem=recv, device_id=to, device_id_type=MESH
    )
    copy.start()
    return copy


class RowsFlow:
    def __init__(self, spot, outgoing, z_rows, every, local_sem, send_sem, recv_sem, same=False):
        self.spot, self.outgoing, self.z_rows, self.every = spot, outgoing, z_rows, every
        self.local_sem, self.send_sem, self.recv_sem = local_sem, send_sem, recv_sem
        self.started = {}
        self.rows = every.shape[2]
        self.sources = (spot.c,) + spot.z_to
        self.same = same

    def send(self, u, slot, source, target, to):
        return remote(source, target, self.send_sem.at[u, slot], self.recv_sem.at[u, slot], to)

    def begin(self):
        spot = self.spot
        for m in range(3):
            z = spot.z_to[m]
            source = self.outgoing if self.same else self.outgoing.at[z]
            self.started["z", m] = self.send(1 + m, 0, source, self.z_rows.at[spot.c], (spot.d, z))
        self.spread(0)

    def spread(self, u):
        spot, src = self.spot, self.sources[u]
        if u > 0:
            self.started["z", u - 1].wait_recv()
            source = self.z_rows.at[src, 0 : self.rows]
        else:
            source = self.outgoing if self.same else self.outgoing.at[src, 0 : self.rows]
        target = self.every.at[spot.d, src]
        keep = pltpu.make_async_copy(source, target, self.local_sem.at[u])
        keep.start()
        self.started["keep", u] = keep
        for slot, (name, to) in enumerate((("x", spot.x_to), ("y", spot.y_to), ("c", spot.core_to))):
            self.started[name, u] = self.send(u, 1 + slot, source, target, to)

    def forward(self, u):
        spot, src, mid = self.spot, self.sources[u], self.rows // 2
        self.started["x", u].wait_recv()
        piece = self.every.at[spot.x_d, src, 0:mid]
        self.started["xy", u] = self.send(u, 4, piece, piece, spot.y_to)
        piece = self.every.at[spot.x_d, src]
        self.started["xc", u] = self.send(u, 5, piece, piece, spot.core_to)
        self.started["y", u].wait_recv()
        piece = self.every.at[spot.y_d, src, mid : self.rows]
        self.started["yx", u] = self.send(u, 6, piece, piece, spot.x_to)
        piece = self.every.at[spot.y_d, src]
        self.started["yc", u] = self.send(u, 7, piece, piece, spot.core_to)

    def far(self, u):
        spot, src = self.spot, self.sources[u]
        self.started["xy", u].wait_recv()
        self.started["yx", u].wait_recv()
        piece = self.every.at[spot.far_d, src]
        self.started["fc", u] = self.send(u, 8, piece, piece, spot.core_to)

    def close(self):
        for u in range(4):
            for name in ("c", "xc", "yc", "fc"):
                self.started[name, u].wait_recv()
            self.started["keep", u].wait()
        for (name, _), copy in self.started.items():
            if name != "keep":
                copy.wait_send()


class SumFlow:
    def __init__(self, spot, mine, core_in, x_in, y_in, xy_in, yx_in, z_in, total, out_at, local_sem, send_sem, recv_sem):
        self.spot, self.mine, self.core_in, self.out_at = spot, mine, core_in, out_at
        self.x_in, self.y_in, self.xy_in, self.yx_in, self.z_in, self.total = x_in, y_in, xy_in, yx_in, z_in, total
        self.local_sem, self.send_sem, self.recv_sem = local_sem, send_sem, recv_sem
        self.started = [{} for _ in range(mine.shape[0])]
        self.half = mine.shape[4] // 2

    def send(self, j, slot, source, target, to):
        return remote(source, target, self.send_sem.at[j, slot], self.recv_sem.at[j, slot], to)

    def over_core(self, j, source):
        self.started[j]["core"] = self.send(j, 0, source, self.core_in.at[j], self.spot.core_to)

    def core(self, j):
        spot, mine, half, started = self.spot, self.mine, self.half, self.started[j]
        started["core"].wait_recv()

        @pl.loop(0, 4)
        def _(a):
            for b in range(2):
                for e in range(2):
                    mine[j, a, b, e] = mine[j, a, b, e] + self.core_in[j, a, b, e]

        started["x"] = self.send(j, 1, mine.at[j, :, :, 1 - spot.x, 0:half], self.x_in.at[j], spot.x_to)
        started["y"] = self.send(j, 2, mine.at[j, :, 1 - spot.y, :, half : 2 * half], self.y_in.at[j], spot.y_to)

    def first(self, j):
        spot, mine, half, started = self.spot, self.mine, self.half, self.started[j]
        x, y = spot.x, spot.y
        started["x"].wait_recv()
        for a in range(4):
            for b in range(2):
                mine[j, a, b, x, 0:half] = mine[j, a, b, x, 0:half] + self.x_in[j, a, b]
        started["xy"] = self.send(j, 3, mine.at[j, :, 1 - y, x, 0:half], self.xy_in.at[j], spot.y_to)
        started["y"].wait_recv()
        for a in range(4):
            for e in range(2):
                mine[j, a, y, e, half : 2 * half] = mine[j, a, y, e, half : 2 * half] + self.y_in[j, a, e]
        started["yx"] = self.send(j, 4, mine.at[j, :, y, 1 - x, half : 2 * half], self.yx_in.at[j], spot.x_to)

    def second(self, j):
        spot, mine, half, started = self.spot, self.mine, self.half, self.started[j]
        x, y = spot.x, spot.y
        started["xy"].wait_recv()
        started["yx"].wait_recv()
        for a in range(4):
            mine[j, a, y, x, 0:half] = mine[j, a, y, x, 0:half] + self.xy_in[j, a]
            mine[j, a, y, x, half : 2 * half] = mine[j, a, y, x, half : 2 * half] + self.yx_in[j, a]
        for m in range(3):
            z = spot.z_to[m]
            started["z", m] = self.send(j, 5 + m, mine.at[j, z, y, x], self.z_in.at[j, m], (spot.d, z))

    def along(self, j):
        spot, started, total = self.spot, self.started[j], self.total
        for m in range(3):
            started["z", m].wait_recv()
        own = self.mine[j, spot.c, spot.y, spot.x]
        total[j] = ((own + self.z_in[j, 0]) + self.z_in[j, 1]) + self.z_in[j, 2]
        target = self.out_at(j, spot.d)
        started["keep"] = pltpu.make_async_copy(total.at[j], target, self.local_sem.at[j])
        started["keep"].start()
        pairs = (("gx", spot.x_to), ("gy", spot.y_to), ("gf", spot.far_to), ("gc", spot.core_to))
        for slot, (name, to) in enumerate(pairs):
            started[name] = self.send(j, 8 + slot, total.at[j], target, to)

    def share(self, j):
        spot, started = self.spot, self.started[j]
        for slot, (name, to) in enumerate((("gx", spot.x_to), ("gy", spot.y_to), ("gf", spot.far_to))):
            started[name].wait_recv()
            piece = self.out_at(j, to[0])
            started["c" + name] = self.send(j, 12 + slot, piece, piece, spot.core_to)

    def end(self, j, core_sent=False):
        started = self.started[j]
        for name in ("gc", "cgx", "cgy", "cgf"):
            started[name].wait_recv()
        for name, copy in started.items():
            if name == "keep":
                copy.wait()
            elif not (name == "core" and core_sent):
                copy.wait_send()


def sum_scratch(jobs, piece, lanes):
    half = piece // 2
    return [
        pltpu.VMEM((jobs, 4, 2, 2, piece, lanes), f32),
        pltpu.VMEM((jobs, 4, 2, 2, piece, lanes), f32),
        pltpu.VMEM((jobs, 4, 2, half, lanes), f32),
        pltpu.VMEM((jobs, 4, 2, half, lanes), f32),
        pltpu.VMEM((jobs, 4, half, lanes), f32),
        pltpu.VMEM((jobs, 4, half, lanes), f32),
        pltpu.VMEM((jobs, 3, piece, lanes), f32),
        pltpu.VMEM((jobs, piece, lanes), f32),
    ]


def flow_sems(jobs):
    dma = pltpu.SemaphoreType.DMA
    return [dma((jobs,)), dma((jobs, 15)), dma((jobs, 15)), dma((4,)), dma((4, 9)), dma((4, 9))]


GATE_OF = ((0, 1, 3), (0, 1, 2))


def split_two(value):
    top = value.astype(bf16)
    return top, (value - top.astype(f32)).astype(bf16)


def three_products(first, second, over):
    def product(a, b):
        return lax.dot_general(a, b, (over, ((), ())), preferred_element_type=f32)

    return product(first[0], second[0]) + product(first[1], second[0]) + product(first[0], second[1])


def tail_kernel(
    inputs,
    prevs,
    dgates,
    dstart,
    entering,
    out,
    item_all,
    start_all,
    mine,
    core_in,
    x_in,
    y_in,
    xy_in,
    yx_in,
    z_in,
    total,
    core_out,
    turned,
    acts,
    flow,
    w_flow,
    din,
    z_rows,
    flow_sem,
    start_sem,
    sum_local,
    sum_send,
    sum_recv,
    row_local,
    row_send,
    row_recv,
):
    spot = Spot()
    spot.greet_all()
    c, k = spot.c, spot.k
    jobs, _, _, _, piece, units = mine.shape
    block = din.shape[2]
    events = acts.shape[2]
    gates = jobs // 2
    sums = SumFlow(
        spot, mine, core_in, x_in, y_in, xy_in, yx_in, z_in, total,
        lambda j, d: out.at[j // gates, j % gates, d], sum_local, sum_send, sum_recv,
    )
    rows = RowsFlow(spot, din, z_rows, item_all, row_local, row_send, row_recv)

    def gate_cols(g):
        return dgates.at[:, pl.ds(g * units, units)]

    queue = [inputs, gate_cols(0), gate_cols(1), gate_cols(3), prevs, gate_cols(2)]

    def flow_copy(n):
        return pltpu.make_async_copy(queue[n], flow.at[n % 2], flow_sem.at[n % 2])

    def w_copy(n, slot):
        rows = pl.ds(pl.multiple_of(n * block, block), block)
        return pltpu.make_async_copy(entering.at[rows], w_flow.at[slot], flow_sem.at[2 + slot])

    flow_copy(0).start()
    flow_copy(1).start()
    w_copy(0, 0).start()

    def next_flow(n):
        if n + 2 < len(queue):
            flow_copy(n + 2).start()

    def take_act(n, w):
        flow_copy(n).wait()
        acts[w, 0], acts[w, 1] = split_two(flow[n % 2])
        next_flow(n)

    def take_gate(n, g, at):
        flow_copy(n).wait()

        @pl.loop(0, 4)
        def _(b):
            cols = pl.ds(pl.multiple_of(b * block, block), block)
            value = flow[n % 2, :, cols]
            turned[g, 0, b], turned[g, 1, b] = split_two(value.T)
            if at is not None:
                chunk = 4 * at + b
                slot = lax.rem(b, 2)

                @pl.when(chunk + 1 < 12)
                def _():
                    w_copy(chunk + 1, 1 - slot).start()

                w_copy(chunk, slot).wait()
                share = three_products(split_two(value), split_two(w_flow[slot]), ((1,), (0,)))
                for e in range(4):
                    part = share[:, e * block : (e + 1) * block]
                    if at == 0:
                        before = jnp.where(b == 0, 0.0, din[e, 0:events, :])
                    else:
                        before = din[e, 0:events, :]
                    din[e, 0:events, :] = before + part

        next_flow(n)

    def rows_begin():
        for e in range(4):
            din[e, events:, :] = dstart[:, e * block : (e + 1) * block]
        rows.begin()

    def rows_end():
        keeps = [
            pltpu.make_async_copy(din.at[c, events:], start_all.at[c], start_sem.at[0]),
        ] + [
            pltpu.make_async_copy(z_rows.at[z, events:], start_all.at[z], start_sem.at[1 + m])
            for m, z in enumerate(spot.z_to)
        ]
        for keep in keeps:
            keep.start()
        rows.close()
        for keep in keeps:
            keep.wait()

    def partial(j):
        w, g = j // gates, GATE_OF[j // gates][j % gates]
        slot = j % 2
        if j >= 2:
            sums.started[j - 2]["core"].wait_send()

        @pl.loop(0, 4)
        def _(b):
            value = three_products(
                (turned[g, 0, b], turned[g, 1, b]), (acts[w, 0], acts[w, 1]), ((1,), (0,))
            ).reshape(2, 2, 2, piece, units)
            for p in range(2):
                for q in range(2):
                    mine[j, b, p, q] = jnp.where(k == 0, value[p, q, 0], value[p, q, 1])
                    core_out[slot, b, p, q] = jnp.where(k == 0, value[p, q, 1], value[p, q, 0])

        sums.over_core(j, core_out.at[slot])

    A, B, C, Z, S = sums.core, sums.first, sums.second, sums.along, sums.share

    def E(j):
        sums.end(j, core_sent=j < jobs - 2)

    take_act(0, 0)
    take_gate(1, 0, 0)
    partial(0)
    take_gate(2, 1, 1)
    partial(1)
    A(0)
    take_gate(3, 3, 2)
    rows_begin()
    partial(2)
    A(1)
    take_act(4, 1)
    partial(3)
    A(2), B(0), rows.spread(1), rows.forward(0)
    partial(4)
    A(3), B(1), C(0), rows.spread(2), rows.forward(1), rows.far(0)
    take_gate(5, 2, None)
    partial(5)
    A(4), B(2), C(1), Z(0), rows.spread(3), rows.forward(2), rows.far(1)
    A(5), B(3), C(2), Z(1), S(0), rows.forward(3), rows.far(2)
    B(4), C(3), Z(2), S(1), E(0), rows.far(3)
    B(5), C(4), Z(3), S(2), E(1)
    C(5), Z(4), S(3), E(2)
    rows_end()
    Z(5), S(4), E(3)
    S(5), E(4), E(5)


def run_tail(inputs, prevs, dgates, dstart, entering, collective_id):
    events, units = inputs.shape
    gates, block = 3, units // 4
    piece = block // 8
    jobs = 2 * gates
    start_rows = dstart.shape[0]
    hbm = pl.BlockSpec(memory_space=pl.ANY)
    grads, item_all, start_all = pl.pallas_call(
        tail_kernel,
        out_shape=(
            jax.ShapeDtypeStruct((2, gates, 8, piece, units), f32),
            jax.ShapeDtypeStruct((8, 4, events, block), f32),
            jax.ShapeDtypeStruct((4, start_rows, block), f32),
        ),
        in_specs=[hbm, hbm, hbm, pl.BlockSpec(memory_space=pltpu.VMEM), hbm],
        out_specs=(hbm, hbm, hbm),
        scratch_shapes=sum_scratch(jobs, piece, units)
        + [
            pltpu.VMEM((2, 4, 2, 2, piece, units), f32),
            pltpu.VMEM((4, 2, 4, block, events), bf16),
            pltpu.VMEM((2, 2, events, units), bf16),
            pltpu.VMEM((2, events, units), f32),
            pltpu.VMEM((2, block, units), f32),
            pltpu.VMEM((4, events + start_rows, block), f32),
            pltpu.VMEM((4, events + start_rows, block), f32),
            pltpu.SemaphoreType.DMA((4,)),
            pltpu.SemaphoreType.DMA((4,)),
        ]
        + flow_sems(jobs),
        cost_estimate=takes(190),
        compiler_params=pltpu.CompilerParams(
            collective_id=collective_id, has_side_effects=True, vmem_limit_bytes=VMEM_BYTES
        ),
    )(inputs, prevs, dgates, dstart, entering)
    return grads.reshape(2, gates, 8 * piece, units), item_all, start_all


UNITS = ((0, 0), (0, 1), (1, 0), (0, 2), (1, 1), (1, 2))


def head_kernel(
    chunk,
    width,
    item_ids,
    out_ids,
    embed,
    table,
    bias,
    own_in,
    own_hid,
    carried,
    own_ids,
    all_in,
    all_hid,
    arrived,
    all_ids,
    out_rows,
    padded,
    turned,
    item_rows,
    held,
    local_sem,
    send_sem,
    recv_sem,
    row_send,
    row_recv,
    id_send,
    id_recv,
):
    y, x, k, c, d = place()
    i = pl.program_id(0)
    n = pl.num_programs(0) // 2
    core_to, x_to, y_to = (d + 1 - 2 * k, c), (d + 2 - 4 * x, c), (d + 4 - 8 * y, c)
    z_all = (c + 1 - 2 * lax.rem(c, 2), lax.rem(c + 2, 4), 3 - c)
    owns, alls = (own_in, own_hid), (all_in, all_hid)
    piece = own_in.shape[4]
    half = piece // 2
    block = item_rows.shape[2]
    items = item_rows.shape[1]
    carried_rows = carried.shape[1]
    events = items - carried_rows

    def send(u, slot):
        w, m = UNITS[u]
        z = z_all[m]
        every = alls[w]
        if slot == 0:
            source, target, to = owns[w].at[:, y, x, k], every.at[:, c, y, x, k], (d, z)
        elif slot in (4, 6):
            spot = (
                every.at[:, z, y, 1 - x, k, 0:half] if slot == 4 else every.at[:, z, 1 - y, x, k, half : 2 * half]
            )
            source, target, to = spot, spot, (y_to if slot == 4 else x_to)
        else:
            py, px, to = {
                1: (y, x, x_to),
                2: (y, x, y_to),
                3: (y, x, core_to),
                5: (y, 1 - x, core_to),
                7: (1 - y, x, core_to),
                8: (1 - y, 1 - x, core_to),
            }[slot]
            spot = every.at[:, z, py, px, k]
            source, target = spot, spot
        return pltpu.make_async_remote_copy(
            src_ref=source,
            dst_ref=target,
            send_sem=send_sem.at[u, slot],
            recv_sem=recv_sem.at[u, slot],
            device_id=to,
            device_id_type=MESH,
        )

    def load(w):
        return pltpu.make_async_copy(owns[w], held.at[w], local_sem.at[w])

    def keep(w):
        return pltpu.make_async_copy(held.at[w], alls[w].at[:, c], local_sem.at[2 + w])

    def keep_own(_):
        for w in range(2):
            load(w).wait()
            keep(w).start()

    def item_send(m):
        return pltpu.make_async_remote_copy(
            src_ref=item_rows.at[z_all[m]],
            dst_ref=arrived.at[:, pl.ds(pl.multiple_of(c * block, block), block)],
            send_sem=row_send.at[m],
            recv_sem=row_recv.at[m],
            device_id=(d, z_all[m]),
            device_id_type=MESH,
        )

    def begin_items(_):
        for m in range(3):
            item_send(m).start()

    def item_keep():
        return pltpu.make_async_copy(
            item_rows.at[c], arrived.at[:, pl.ds(pl.multiple_of(c * block, block), block)], local_sem.at[4]
        )

    def id_copy(m):
        to = lax.rem(d + 1 + m, 8)
        return pltpu.make_async_remote_copy(
            src_ref=own_ids,
            dst_ref=all_ids.at[d],
            send_sem=id_send.at[m],
            recv_sem=id_recv.at[m],
            device_id=(to, c),
            device_id_type=MESH,
        )

    def id_keep():
        return pltpu.make_async_copy(own_ids, all_ids.at[d], local_sem.at[5])

    def begin():
        greet([(lax.rem(d + 1 + m, 8), c) for m in range(7)] + [(d, z) for z in z_all])
        id_keep().start()
        for m in range(7):
            id_copy(m).start()
        begin_z(0)
        begin_z(1)
        load(0).start()
        load(1).start()

    def begin_z(u):
        send(u, 0).start()

    def spread(u):
        send(u, 0).wait_recv()
        for slot in (1, 2, 3):
            send(u, slot).start()

    def forward(u):
        send(u, 1).wait_recv()
        send(u, 4).start()
        send(u, 5).start()
        send(u, 2).wait_recv()
        send(u, 6).start()
        send(u, 7).start()

    def far(u):
        send(u, 4).wait_recv()
        send(u, 6).wait_recv()
        send(u, 8).start()

    def close(u):
        for slot in (3, 5, 7, 8):
            send(u, slot).wait_recv()
        for slot in range(9):
            send(u, slot).wait_send()

    timeline = [(-1, begin, None), (4, keep_own, 0), (64, begin_items, 0)]
    timeline += [(at, begin_z, 2 + j) for j, at in enumerate((10, 18, 34, 50))]
    for u, at in enumerate((11, 23, 34, 46, 58, 90)):
        timeline += [(at, spread, u), (at + 12, forward, u), (at + 20, far, u)]
    timeline.sort(key=lambda entry: entry[0])
    last = 2 * n - 1

    @pl.when(i == 0)
    def _():
        padded[...] = jnp.zeros_like(padded)

    for at, action, u in timeline:
        if at < last:

            @pl.when(i == max(at, 0))
            def _(action=action, u=u):
                action() if u is None else action(u)

    @pl.when(i < n)
    def _():
        padded[0:width, :] = embed[...]

    @pl.when(i >= n)
    def _():
        padded[0:width, :] = table[...]
        padded[width : width + 1, :] = bias[...]

    spot = lax.rem(i, n) * chunk
    turned[pl.ds(pl.multiple_of(spot, chunk), chunk), :] = padded[...].T

    @pl.when(i == n - 1)
    def _():
        for z in range(4):

            def body(b, carry, z=z):
                for j in range(8):
                    row = item_ids[z * events + b * 8 + j]
                    item_rows[z, pl.ds(b * 8 + j, 1), :] = turned[pl.ds(row, 1), :]
                return carry

            lax.fori_loop(0, events // 8, body, 0)
            item_rows[z, events:items, :] = carried[z]
        item_keep().start()

    @pl.when(i == last)
    def _():
        def body(b, carry):
            for j in range(8):
                row = out_ids[b * 8 + j]
                out_rows[pl.ds(b * 8 + j, 1), :] = turned[pl.ds(row, 1), :]
            return carry

        lax.fori_loop(0, out_rows.shape[0] // 8, body, 0)
        for at, action, u in timeline:
            if at >= last:
                action(u)
        for u in range(6):
            close(u)
        for m in range(3):
            item_send(m).wait()
        for m in range(7):
            id_copy(m).wait()
        id_keep().wait()
        for w in range(2):
            keep(w).wait()
        item_keep().wait()


def gather_all(embed, table, bias, item_ids, out_ids, own_in, own_hid, carried, own_ids, collective_id):
    width, rows = embed.shape
    gates, block, units = own_in.shape
    piece = block // 8
    chunk = 128 * max(k for k in range(1, 9) if rows % (128 * k) == 0)
    n = rows // chunk
    items = item_ids.shape[0] // 4 + carried.shape[1]
    own_shape = (gates, 2, 2, 2, piece, units)
    all_shape = (gates, 4, 2, 2, 2, piece, units)
    smem = pl.BlockSpec(memory_space=pltpu.SMEM)
    hbm = pl.BlockSpec(memory_space=pl.ANY)
    all_in, all_hid, arrived, all_ids, out_rows = pl.pallas_call(
        functools.partial(head_kernel, chunk, width),
        out_shape=(
            jax.ShapeDtypeStruct(all_shape, f32),
            jax.ShapeDtypeStruct(all_shape, f32),
            jax.ShapeDtypeStruct((items, units), f32),
            jax.ShapeDtypeStruct((8,) + own_ids.shape, jnp.int32),
            jax.ShapeDtypeStruct((out_ids.shape[0], block), f32),
        ),
        grid=(2 * n,),
        in_specs=[
            smem,
            smem,
            pl.BlockSpec((width, chunk), lambda i: (0, jnp.minimum(i, n - 1))),
            pl.BlockSpec((width, chunk), lambda i: (0, jnp.maximum(i - n, 0))),
            pl.BlockSpec((1, chunk), lambda i: (0, jnp.maximum(i - n, 0))),
            hbm,
            hbm,
            pl.BlockSpec(carried.shape, lambda i: (0, 0, 0)),
            pl.BlockSpec(own_ids.shape, lambda i: (0, 0)),
        ],
        out_specs=(hbm, hbm, hbm, hbm, pl.BlockSpec((out_ids.shape[0], block), lambda i: (0, 0))),
        scratch_shapes=[
            pltpu.VMEM((block, chunk), f32),
            pltpu.VMEM((rows, block), f32),
            pltpu.VMEM((4, items, block), f32),
            pltpu.VMEM((2,) + own_shape, f32),
            pltpu.SemaphoreType.DMA((6,)),
            pltpu.SemaphoreType.DMA((6, 9)),
            pltpu.SemaphoreType.DMA((6, 9)),
            pltpu.SemaphoreType.DMA((3,)),
            pltpu.SemaphoreType.DMA((3,)),
            pltpu.SemaphoreType.DMA((7,)),
            pltpu.SemaphoreType.DMA((7,)),
        ],
        cost_estimate=takes(120),
        compiler_params=pltpu.CompilerParams(
            collective_id=collective_id, has_side_effects=True, vmem_limit_bytes=VMEM_BYTES
        ),
    )(item_ids, out_ids, embed, table, bias, own_in.reshape(own_shape), own_hid.reshape(own_shape), carried, own_ids)
    return (
        all_in.reshape(gates, 4 * block, units),
        all_hid.reshape(gates, 4 * block, units),
        arrived,
        all_ids,
        out_rows,
    )


def loss_kernel(width, factor, outs, targets, negs, loss, douts, neg_part, target_part, share, pairs, score):
    n_col, events, block = targets.shape
    n_dp, _, count, _ = negs.shape
    lane = lax.broadcasted_iota(jnp.int32, (events, block), 1)
    for c in range(n_col):
        value = jnp.where(lane < width, outs[:, c * block : (c + 1) * block], 0.0)
        value = jnp.where(lane == width, 1.0 / n_col, value)
        share[c] = value
        pairs[0, c], pairs[1, c] = split_two(value)

    @pl.loop(0, n_dp)
    def _(b):
        cols = pl.ds(pl.multiple_of(b * count, count), count)
        total = jnp.zeros((events, count), f32)
        for c in range(n_col):
            total = total + three_products((pairs[0, c], pairs[1, c]), split_two(negs[b, c]), ((1,), (1,)))
        score[:, cols] = total

    step = 32

    @pl.loop(0, events // step)
    def _(i):
        rows = pl.ds(pl.multiple_of(i * step, step), step)
        pos = jnp.zeros((step, 1), f32)
        for c in range(n_col):
            pos = pos + jnp.sum(share[c, rows, :] * targets[c, rows, :], axis=-1, keepdims=True)
        neg = score[rows, :]
        expd = jnp.exp(neg - jnp.max(neg, axis=-1, keepdims=True))
        weight = expd * (1.0 / jnp.sum(expd, axis=-1, keepdims=True))
        sig = jax.nn.sigmoid(pos - neg)
        slope = weight * sig
        ppos = jnp.sum(slope, axis=-1, keepdims=True)
        quad = jnp.sum(weight * neg * neg, axis=-1, keepdims=True)
        slope = jnp.sum(slope * (1.0 - sig), axis=-1, keepdims=True)
        loss[rows, :] = jnp.broadcast_to(quad - jnp.log(ppos), (step, LANES))
        score[rows, :] = factor * weight * (1.0 - sig * sig * (1.0 / ppos) + neg * neg + 2.0 * neg - quad)
        dpos = -factor * slope / ppos
        for c in range(n_col):
            target_part[c, rows, :] = dpos * share[c, rows, :]
            douts[rows, c * block : (c + 1) * block] = dpos * targets[c, rows, :]

    @pl.loop(0, n_dp)
    def _(b):
        dneg = score[:, pl.ds(pl.multiple_of(b * count, count), count)]
        across, down = split_two(dneg), split_two(dneg.T)
        for c in range(n_col):
            cols = slice(c * block, (c + 1) * block)
            douts[:, cols] = douts[:, cols] + three_products(across, split_two(negs[b, c]), ((1,), (0,)))
            neg_part[c, b] = three_products(down, (pairs[0, c], pairs[1, c]), ((1,), (0,)))

    for c in range(n_col):
        cols = slice(c * block, (c + 1) * block)
        douts[:, cols] = jnp.where(lane < width, douts[:, cols], 0.0)


def run_loss(outs, targets, negs, width, factor):
    n_col, events, block = targets.shape
    n_dp, _, count, _ = negs.shape
    return pl.pallas_call(
        functools.partial(loss_kernel, width, factor),
        out_shape=(
            jax.ShapeDtypeStruct((events, LANES), f32),
            jax.ShapeDtypeStruct(outs.shape, f32),
            jax.ShapeDtypeStruct((n_col, n_dp, count, block), f32),
            jax.ShapeDtypeStruct((n_col, events, block), f32),
        ),
        in_specs=[in_vmem()] * 3,
        out_specs=(in_vmem(),) * 4,
        scratch_shapes=[
            pltpu.VMEM((n_col, events, block), f32),
            pltpu.VMEM((2, n_col, events, block), bf16),
            pltpu.VMEM((events, n_dp * count), f32),
        ],
        cost_estimate=takes(25),
        compiler_params=params(),
    )(outs, targets, negs)


def back_kernel(
    steps,
    hidden,
    douts,
    keep,
    prevs,
    resets,
    updates,
    cands,
    inners,
    neg_part,
    target_part,
    own_loss,
    dgates,
    dstart,
    neg_all,
    target_all,
    loss_all,
    mine,
    core_in,
    x_in,
    y_in,
    xy_in,
    yx_in,
    z_in,
    total,
    w_high,
    w_low,
    w_flow,
    z_rows,
    flow_sem,
    load_sem,
    loss_send,
    loss_recv,
    sum_local,
    sum_send,
    sum_recv,
    row_local,
    row_send,
    row_recv,
):
    spot = Spot()
    spot.greet_all()
    rows_per, units = dstart.shape
    jobs, piece = mine.shape[0], mine.shape[4]
    step_rows = w_flow.shape[1]
    chunks = hidden.shape[0] // step_rows
    sums = SumFlow(
        spot, mine, core_in, x_in, y_in, xy_in, yx_in, z_in, total,
        lambda j, d: neg_all.at[d, pl.ds(j * piece, piece)], sum_local, sum_send, sum_recv,
    )
    rows = RowsFlow(spot, target_part, z_rows, target_all, row_local, row_send, row_recv)

    def load(i, slot):
        part = pl.ds(pl.multiple_of(i * step_rows, step_rows), step_rows)
        return pltpu.make_async_copy(hidden.at[part], w_flow.at[slot], flow_sem.at[slot])

    load(0, 0).start()
    own = []
    for j in range(jobs):
        part = pl.ds(j * piece, piece)
        own.append(pltpu.make_async_copy(neg_part.at[:, :, :, spot.k, part], mine.at[j], load_sem.at[j]))
        own[j].start()
        sums.over_core(j, neg_part.at[:, :, :, 1 - spot.k, part])
    rows.begin()
    losses = [pltpu.make_async_copy(own_loss, loss_all.at[spot.c], load_sem.at[jobs])]
    losses[0].start()
    for m, z in enumerate(spot.z_to):
        losses.append(remote(own_loss, loss_all.at[spot.c], loss_send.at[m], loss_recv.at[m], (spot.d, z)))

    @pl.loop(0, chunks)
    def _(i):
        slot = lax.rem(i, 2)

        @pl.when(i + 1 < chunks)
        def _():
            load(i + 1, 1 - slot).start()

        load(i, slot).wait()
        part = pl.ds(pl.multiple_of(i * step_rows, step_rows), step_rows)
        w_high[part, :], w_low[part, :] = split_two(w_flow[slot])

    def step(i, dstate):
        t = steps - 1 - i
        now = pl.ds(pl.multiple_of(t * rows_per, rows_per), rows_per)
        reset, update, cand = resets[now, :], updates[now, :], cands[now, :]
        dh = douts[now, :] + dstate
        dcand = dh * (1.0 - update) * (1.0 - cand * cand)
        dreset = dcand * inners[now, :] * reset * (1.0 - reset)
        dupdate = dh * (prevs[now, :] - cand) * update * (1.0 - update)
        dinner = dcand * reset
        dgates[now, 0:units] = dreset
        dgates[now, units : 2 * units] = dupdate
        dgates[now, 2 * units : 3 * units] = dinner
        dgates[now, 3 * units : 4 * units] = dcand
        total_now = dh * update
        for g, part in enumerate((dreset, dupdate, dinner)):
            pair = two_part(part)
            sect = slice(g * units, (g + 1) * units)
            first = jnp.dot(pair, w_high[sect, :], preferred_element_type=f32)
            second = jnp.dot(pair, w_low[sect, :], preferred_element_type=f32)
            total_now = total_now + (first[:rows_per] + first[rows_per:] + second[:rows_per])
        return keep[now, :] * total_now

    def sums_core(j):
        own[j].wait()
        sums.core(j)

    A, B, C, Z, S = sums_core, sums.first, sums.second, sums.along, sums.share
    timeline = (
        (0.0, ((A, 0), (A, 1))),
        (0.15, ((rows.forward, 0),)),
        (0.28, ((rows.spread, 1), (B, 0))),
        (0.38, ((rows.forward, 1), (rows.far, 0))),
        (0.47, ((B, 1), (rows.spread, 2))),
        (0.56, ((C, 0), (rows.forward, 2), (rows.far, 1))),
        (0.66, ((C, 1), (rows.spread, 3))),
        (0.78, ((Z, 0), (rows.forward, 3), (rows.far, 2))),
        (0.88, ((Z, 1), (S, 0))),
    )
    state, done = jnp.zeros((rows_per, units), f32), 0
    for share_done, actions in timeline:
        until = int(share_done * steps)
        if until > done:
            state, done = lax.fori_loop(done, until, step, state), until
        for action, argument in actions:
            action(argument)
    dstart[...] = lax.fori_loop(done, steps, step, state)
    rows.far(3)
    S(1)
    sums.end(0)
    rows.close()
    sums.end(1)
    for copy in losses:
        copy.wait()


def run_back(hidden, douts, keep, saved, neg_part, target_part, own_loss, rows_per, steps, collective_id):
    events, units = douts.shape
    count, block = neg_part.shape[2:]
    jobs = 2
    piece = count // jobs
    hbm = pl.BlockSpec(memory_space=pl.ANY)
    step_rows = units // 4
    return pl.pallas_call(
        functools.partial(back_kernel, steps),
        out_shape=(
            jax.ShapeDtypeStruct((events, 4 * units), f32),
            jax.ShapeDtypeStruct((rows_per, units), f32),
            jax.ShapeDtypeStruct((8, count, block), f32),
            jax.ShapeDtypeStruct((8, 4, events, block), f32),
            jax.ShapeDtypeStruct((4,) + own_loss.shape, f32),
        ),
        in_specs=[hbm] + [in_vmem()] * 7 + [hbm, hbm, in_vmem()],
        out_specs=(in_vmem(), in_vmem(), hbm, hbm, hbm),
        scratch_shapes=sum_scratch(jobs, piece, block)
        + [
            pltpu.VMEM(hidden.shape, bf16),
            pltpu.VMEM(hidden.shape, bf16),
            pltpu.VMEM((2, step_rows, units), f32),
            pltpu.VMEM((4, events, block), f32),
            pltpu.SemaphoreType.DMA((2,)),
            pltpu.SemaphoreType.DMA((jobs + 1,)),
            pltpu.SemaphoreType.DMA((3,)),
            pltpu.SemaphoreType.DMA((3,)),
        ]
        + flow_sems(jobs),
        cost_estimate=takes(80),
        compiler_params=pltpu.CompilerParams(
            collective_id=collective_id, has_side_effects=True, vmem_limit_bytes=VMEM_BYTES
        ),
    )(hidden, douts, keep, *saved, neg_part.reshape(4, 2, 2, 2, count, block), target_part, own_loss)


def pad_kernel(weight, bias, out):
    own, full = weight.shape[1:]
    block = out.shape[1]
    n_col = out.shape[2] // block
    part = full // n_col
    out[...] = jnp.zeros_like(out)
    for c in range(n_col):
        out[0, 0:own, c * block : c * block + part] = weight[0, :, c * part : (c + 1) * part]
    out[0, 0:own, part : part + 1] = bias[0]


def pad_units(weight, bias, n_col, block):
    gates, own, full = weight.shape
    return pl.pallas_call(
        pad_kernel,
        out_shape=jax.ShapeDtypeStruct((gates, block, n_col * block), f32),
        grid=(gates,),
        in_specs=[
            pl.BlockSpec((1, own, full), lambda g: (g, 0, 0)),
            pl.BlockSpec((1, own, 1), lambda g: (g, 0, 0)),
        ],
        out_specs=pl.BlockSpec((1, block, n_col * block), lambda g: (g, 0, 0)),
        compiler_params=params(),
    )(weight, bias[:, :, None])


def gather_weight(own, n_dp):
    gates, block, units = own.shape
    flat = own.reshape(n_dp, gates * block // n_dp, units)
    piece = lax.dynamic_index_in_dim(flat, lax.axis_index("dp"), 0, keepdims=False)
    every = lax.all_gather(piece, ("col", "dp"))
    every = every.reshape(-1, gates, block, units)
    return jnp.moveaxis(every, 0, 1).reshape(gates, -1, units)


def reduce_weight(partial, n_dp, n_col):
    gates, rows, units = partial.shape
    block = rows // n_col
    parts = jnp.moveaxis(partial.reshape(gates, n_col, block, units), 1, 0)
    parts = jnp.moveaxis(parts.reshape(n_col, n_dp, gates * block // n_dp, units), 1, 0)
    mine = lax.psum_scatter(parts, "dp", scatter_dimension=0)
    mine = lax.psum_scatter(mine, "col", scatter_dimension=0)
    return lax.all_gather(mine, "dp").reshape(gates, block, units)


def swap_col(rows, n_col):
    return lax.all_to_all(rows, "col", split_axis=0, concat_axis=0, tiled=True)


def unpad_last(value, n_col, part):
    block = value.shape[-1] // n_col
    return value.reshape(value.shape[:-1] + (n_col, block))[..., :part].reshape(value.shape[:-1] + (n_col * part,))


def local(
    n_dp,
    n_col,
    item_ids,
    target_ids,
    negative_ids,
    reset_mask,
    carry_flags,
    carried_state,
    embed_table,
    input_weight,
    hidden_weight,
    gate_bias,
    hidden_bias,
    out_table,
    out_bias,
):
    sessions, steps = item_ids.shape
    own_sessions = sessions // n_col
    rows_per = round_up(own_sessions, ROWS8)
    width = embed_table.shape[0]
    table_rows = embed_table.shape[1]
    own_rows = table_rows // n_dp
    block = round_up(width + 1, LANES)
    units = n_col * block
    events = steps * rows_per
    direct = n_dp == 8 and n_col == 4 and block % 64 == 0 and own_sessions == rows_per
    factor = 1.0 / steps
    dp_at, col_at = lax.axis_index("dp"), lax.axis_index("col")

    def by_owner(value):
        value = jnp.moveaxis(value.reshape(n_col, own_sessions, steps), 1, 2)
        value = jnp.pad(value, ((0, 0), (0, 0), (0, rows_per - own_sessions)))
        return value.reshape(-1)

    item_flat, target_flat = by_owner(item_ids), by_owner(target_ids)
    own_keep = lax.dynamic_index_in_dim(
        by_owner(1 - reset_mask).reshape(n_col, events, 1), col_at, 0, keepdims=False
    ).astype(f32)
    valid = jnp.tile(jnp.arange(rows_per) < own_sessions, steps)
    lane = jnp.arange(units) % block
    first_pad = jnp.arange(units) == width

    own_in = pad_units(input_weight, gate_bias, n_col, block)
    no_bias = jnp.zeros_like(hidden_bias)
    own_hid = pad_units(hidden_weight, jnp.stack([no_bias, no_bias, hidden_bias]), n_col, block)

    carried = (carry_flags.astype(f32)[:, None] * carried_state).reshape(n_col, own_sessions, width)
    carried = jnp.pad(carried, ((0, 0), (0, rows_per - own_sessions), (0, block - width)))
    neg_count = negative_ids.shape[0]
    own_negs = lax.dynamic_slice_in_dim(negative_ids, dp_at * (neg_count // n_dp), neg_count // n_dp)
    out_ids = jnp.concatenate([target_flat, own_negs])
    if direct:
        own_ids = jnp.concatenate([item_flat, target_flat]).reshape(-1, LANES)
        all_in, all_hid, arrived, all_ids, out_rows = gather_all(
            embed_table, out_table, out_bias[None, :], item_flat, out_ids, own_in, own_hid, carried, own_ids, 1
        )
        all_ids = all_ids.reshape(n_dp, 2, -1)
    else:
        all_hid = gather_weight(own_hid, n_dp)
        all_in = gather_weight(own_in, n_dp)
        no_row = jnp.zeros((1, table_rows), f32)
        item_rows = gather_rows(embed_table, no_row, item_flat, block).reshape(n_col, events, block)
        arrived = swap_col(jnp.concatenate([item_rows, carried], axis=1), n_col)
        arrived = jnp.moveaxis(arrived, 0, 1).reshape(events + rows_per, units)
        out_rows = gather_rows(out_table, out_bias[None, :], out_ids, block)
        all_ids = lax.all_gather(jnp.stack([item_flat, target_flat]), "dp")
    all_hid, all_in = all_hid.reshape(-1, units), all_in.reshape(-1, units)
    inputs = jnp.where(first_pad, 1.0, arrived[:events])
    start = arrived[events:]
    all_items, all_targets = all_ids[:, 0].reshape(-1), all_ids[:, 1].reshape(-1)
    count = all_items.shape[0]
    keys = jnp.concatenate([all_items, all_targets + table_rows, negative_ids + 2 * table_rows])
    order = jnp.concatenate([jnp.tile(lax.iota(jnp.int32, count), 2), lax.iota(jnp.int32, neg_count)])
    shift = (max(count, neg_count) - 1).bit_length()
    direct = direct and (3 * table_rows) << shift < 2**31
    low = (dp_at * own_rows).astype(jnp.int32)
    if direct:
        packed = lax.sort((keys << shift) | order)
    else:
        keys, order = lax.sort((keys, order), num_keys=1)
        by_item = (order[:count], keys[:count])
        by_target = (order[count : 2 * count], keys[count : 2 * count] - table_rows)
        by_neg = (order[2 * count :], keys[2 * count :] - 2 * table_rows)

    out_targets = out_rows[: n_col * events].reshape(n_col, events, block)
    out_negs = out_rows[n_col * events :]
    if direct:
        *saved, outs, negs, targets = run_forward_travel(
            all_hid, all_in, inputs, own_keep, start, out_negs, out_targets, steps, width, 4
        )
    else:
        targets = swap_col(out_targets, n_col)
        negs = lax.all_gather(out_negs, ("dp", "col")).reshape(n_dp, n_col, -1, block)
        *saved, outs = run_forward(all_hid, all_in, inputs, own_keep, start, steps, width)
    prevs = saved[0]

    if direct:
        own_loss, douts, neg_part, target_part = run_loss(outs, targets, negs, width, factor)
        own_loss = jnp.pad(own_loss[:, 0].reshape(steps, rows_per).T, ((0, 0), (0, round_up(steps, LANES) - steps)))
        dgates, dstart, neg_all, target_all, loss_all = run_back(
            all_hid, douts, own_keep, saved, neg_part, target_part, own_loss, rows_per, steps, 3
        )
        loss = loss_all[:, :, :steps].reshape(sessions, steps)
        neg_all, target_all = neg_all.reshape(-1, block), target_all.reshape(-1, block)
    else:
        targets = jnp.moveaxis(targets, 0, 1).reshape(events, units)
        negs = jnp.moveaxis(negs, 1, 2).reshape(neg_count, units)
        shares = jnp.where(lane == width, 1.0 / n_col, jnp.where(lane < width, outs, 0.0))
        pos_score = jnp.sum(shares * targets, axis=-1, keepdims=True)
        neg_score = lax.dot_general(shares, negs, (((1,), (1,)), ((), ())), precision=high)
        top = jnp.max(neg_score, axis=-1, keepdims=True)
        expd = jnp.exp(neg_score - top)
        weight = expd / jnp.sum(expd, axis=-1, keepdims=True)
        sig = jax.nn.sigmoid(pos_score - neg_score)
        ppos = jnp.sum(weight * sig, axis=-1, keepdims=True)
        quad = jnp.sum(weight * neg_score * neg_score, axis=-1, keepdims=True)
        slope = jnp.sum(weight * sig * (1.0 - sig), axis=-1, keepdims=True)
        own_loss = -jnp.log(ppos) + quad
        dneg = factor * weight * (1.0 - sig * sig / ppos + neg_score * neg_score + 2.0 * neg_score - quad)
        dneg = jnp.where(valid[:, None], dneg, 0.0)
        dpos = jnp.where(valid[:, None], -factor * slope / ppos, 0.0)
        douts = jnp.dot(dneg, negs, precision=high) + dpos * targets
        douts = jnp.where(lane < width, douts, 0.0)
        neg_part = lax.dot_general(dneg, shares, (((0,), (0,)), ((), ())), precision=high)
        target_part = dpos * shares

        neg_own = lax.psum_scatter(neg_part.reshape(n_dp, -1, units), "dp", scatter_dimension=0)
        neg_own = jnp.moveaxis(neg_own.reshape(-1, n_col, block), 1, 0)
        neg_own = lax.psum_scatter(neg_own, "col", scatter_dimension=0)
        neg_all = lax.all_gather(neg_own, "dp", tiled=True)
        target_own = swap_col(jnp.moveaxis(target_part.reshape(events, n_col, block), 1, 0), n_col)
        target_all = lax.all_gather(target_own.reshape(-1, block), "dp", tiled=True)
        dgates, dstart = run_backward(all_hid, douts, own_keep, saved, rows_per, steps)
        own_loss = own_loss.reshape(steps, rows_per)[:, :own_sessions]
        loss = lax.all_gather(own_loss.T, "col", tiled=True)
    gates = input_weight.shape[0]
    if direct:
        grads, item_all, start_all = run_tail(inputs, prevs, dgates, dstart, all_in, 2)
        grad_embed, grad_out, grad_obias, grad_in, grad_hid = run_finish(
            packed, shift, low, table_rows, own_rows, width, item_all.reshape(-1, block), target_all, neg_all, grads
        )
        grad_obias = grad_obias[0]
    else:
        dx = jnp.concatenate([dgates[:, : 2 * units], dgates[:, 3 * units :]], axis=1)
        dh = dgates[:, : 3 * units]
        hid_part = lax.dot_general(dh, prevs, (((0,), (0,)), ((), ())), precision=high)
        in_part = lax.dot_general(dx, inputs, (((0,), (0,)), ((), ())), precision=high)
        dinputs = jnp.dot(dx, all_in, precision=high)
        back = jnp.concatenate([dinputs, dstart], axis=0).reshape(events + rows_per, n_col, block)
        back = swap_col(jnp.moveaxis(back, 1, 0), n_col)
        item_all = lax.all_gather(back[:, :events].reshape(-1, block), "dp", tiled=True)
        start_all = back[:, events:]
        grad_in = reduce_weight(in_part.reshape(gates, units, units), n_dp, n_col)
        grad_hid = reduce_weight(hid_part.reshape(gates, units, units), n_dp, n_col)
        grads = jnp.stack([grad_in, grad_hid])
        grad_in, grad_hid = (unpad_last(g[:, :width], n_col, width) for g in (grad_in, grad_hid))
        grad_out, grad_obias = scatter_rows(
            [by_target + (target_all,), by_neg + (neg_all,)],
            low,
            own_rows,
            width,
            block,
        )
        grad_obias = grad_obias[0] * n_col
        grad_embed, _ = scatter_rows([by_item + (item_all,)], low, own_rows, width, block)
    grad_carried = start_all[:, :own_sessions, :width].reshape(sessions, width)
    grad_carried = carry_flags.astype(f32)[:, None] * grad_carried
    return (
        loss,
        grad_embed,
        grad_in,
        grad_hid,
        grads[0, :, :width, width],
        grads[1, gates - 1, :width, width],
        grad_out,
        grad_obias,
        grad_carried,
    )


def solution(mesh):
    in_specs = (
        P("dp", None),
        P("dp", None),
        P(),
        P("dp", None),
        P("dp"),
        P("dp", "col"),
        P("col", None),
        P(None, "col", None),
        P(None, "col", None),
        P(None, "col"),
        P("col"),
        P("col", None),
        P(),
    )
    out_specs = (
        P("dp", None),
        P("col", "dp"),
        P(None, "col", None),
        P(None, "col", None),
        P(None, "col"),
        P("col"),
        P("col", "dp"),
        P("dp"),
        P("dp", "col"),
    )
    body = functools.partial(local, mesh.shape["dp"], mesh.shape["col"])
    return jax.shard_map(body, mesh=mesh, in_specs=in_specs, out_specs=out_specs, check_vma=False)
```

```python
import functools

import jax
import jax.numpy as jnp
from jax import lax
from jax.experimental import pallas as pl
from jax.experimental.pallas import tpu as pltpu
from jax.sharding import PartitionSpec as P

LANES = 128
ROWS8 = 8
VMEM_BYTES = 60 << 20
f32 = jnp.float32
bf16 = jnp.bfloat16
high = lax.Precision.HIGH
MESH = pl.DeviceIdType.MESH


def round_up(value, unit):
    return -(-value // unit) * unit


def params():
    return pltpu.CompilerParams(vmem_limit_bytes=VMEM_BYTES)


def takes(micros):
    return pl.CostEstimate(flops=int(micros * 1.1e9), bytes_accessed=1 << 20, transcendentals=0)


def in_vmem():
    return pl.BlockSpec(memory_space=pltpu.VMEM)


def in_smem():
    return pl.BlockSpec(memory_space=pltpu.SMEM)


def gather_kernel(chunk, count, width, ids, table, bias, out, padded, turned):
    step = pl.program_id(0)

    @pl.when(step == 0)
    def _():
        padded[...] = jnp.zeros_like(padded)

    padded[0:width, :] = table[...]
    padded[width : width + 1, :] = bias[...]
    turned[pl.ds(pl.multiple_of(step * chunk, chunk), chunk), :] = padded[...].T

    @pl.when(step == pl.num_programs(0) - 1)
    def _():
        def body(block, carry):
            for j in range(ROWS8):
                row = ids[block * ROWS8 + j]
                out[pl.ds(block * ROWS8 + j, 1), :] = turned[pl.ds(row, 1), :]
            return carry

        lax.fori_loop(0, count // ROWS8, body, 0)


def gather_rows(table, bias, ids, block):
    width, rows = table.shape
    count = ids.shape[0]
    chunk = LANES * max(k for k in range(1, 9) if rows % (LANES * k) == 0)
    return pl.pallas_call(
        functools.partial(gather_kernel, chunk, count, width),
        out_shape=jax.ShapeDtypeStruct((count, block), f32),
        grid_spec=pltpu.PrefetchScalarGridSpec(
            num_scalar_prefetch=1,
            grid=(rows // chunk,),
            in_specs=[
                pl.BlockSpec((width, chunk), lambda i, ids: (0, i)),
                pl.BlockSpec((1, chunk), lambda i, ids: (0, i)),
            ],
            out_specs=pl.BlockSpec((count, block), lambda i, ids: (0, 0)),
            scratch_shapes=[pltpu.VMEM((block, chunk), f32), pltpu.VMEM((rows, block), f32)],
        ),
        compiler_params=params(),
    )(ids, table, bias)


def scatter_kernel(width, n_lists, *refs):
    bounds = refs[0]
    lists = refs[1 : 1 + 3 * n_lists]
    out, bias_out, acc = refs[1 + 3 * n_lists :]
    acc[...] = jnp.zeros_like(acc)
    low = bounds[0]
    for k in range(n_lists):
        rows_of, ids, data = lists[3 * k : 3 * k + 3]

        def body(i, carry):
            spot = pl.ds(ids[i] - low, 1)
            acc[spot, :] = acc[spot, :] + data[pl.ds(rows_of[i], 1), :]
            return carry

        lax.fori_loop(bounds[1 + 2 * k], bounds[2 + 2 * k], body, 0)
    for j in range(acc.shape[0] // LANES):
        cols = slice(j * LANES, (j + 1) * LANES)
        turned = acc[cols, :].T
        out[:, cols] = turned[:width]
        bias_out[:, cols] = turned[width : width + 1]


def scatter_rows(lists, low, own_rows, width, block):
    ends = [low]
    operands, specs = [], []
    for order, ids, data in lists:
        ends += [jnp.sum(ids < low, dtype=jnp.int32), jnp.sum(ids < low + own_rows, dtype=jnp.int32)]
        operands += [order, ids, data]
        specs += [in_smem(), in_smem(), in_vmem()]
    return pl.pallas_call(
        functools.partial(scatter_kernel, width, len(lists)),
        out_shape=(
            jax.ShapeDtypeStruct((width, own_rows), f32),
            jax.ShapeDtypeStruct((1, own_rows), f32),
        ),
        in_specs=[in_smem()] + specs,
        out_specs=(in_vmem(), in_vmem()),
        scratch_shapes=[pltpu.VMEM((own_rows, block), f32)],
        cost_estimate=takes(20),
        compiler_params=params(),
    )(jnp.stack(ends), *operands)


def finish_kernel(
    shift,
    table_rows,
    width,
    low,
    packed,
    items,
    targets,
    negs,
    grads,
    grad_embed,
    grad_out,
    grad_bias,
    grad_in,
    grad_hid,
    even,
    odd,
    item_buf,
    target_buf,
    neg_buf,
    grad_buf,
    embed_out,
    out_out,
    bias_out,
    weight_out,
    sem,
):
    own_rows = even.shape[0]
    events, neg_count = item_buf.shape[0], neg_buf.shape[0]
    block = even.shape[1]
    n_col = grad_buf.shape[2] // block
    loads = [
        pltpu.make_async_copy(source, target, sem.at[n])
        for n, (source, target) in enumerate(
            ((targets, target_buf), (negs, neg_buf), (grads, grad_buf), (items, item_buf))
        )
    ]
    for load in loads:
        load.start()
    stores = [
        pltpu.make_async_copy(source, target, sem.at[4 + n])
        for n, (source, target) in enumerate(
            (
                (out_out, grad_out),
                (bias_out, grad_bias),
                (weight_out.at[0], grad_in),
                (weight_out.at[1], grad_hid),
                (embed_out, grad_embed),
            )
        )
    ]

    def first_from(begin, count, bound):
        def halve(_, ends):
            left, right = ends
            middle = jnp.minimum((left + right) // 2, begin + count - 1)
            less = (left < right) & (packed[middle] < bound)
            return jnp.where(less, middle + 1, left), jnp.where(less | (left >= right), right, middle)

        return lax.fori_loop(0, count.bit_length() + 1, halve, (begin, begin + count))[0]

    def add(begin, count, which, data):
        base = low[0] + which * table_rows
        left = first_from(begin, count, base << shift)
        right = first_from(begin, count, (base + own_rows) << shift)

        def one(i, acc):
            key = packed[i]
            spot, row = (key >> shift) - base, key & ((1 << shift) - 1)
            acc[pl.ds(spot, 1), :] = acc[pl.ds(spot, 1), :] + data[pl.ds(row, 1), :]

        def four(i, carry):
            for n in range(4):
                one(left + 4 * i + n, (even, odd)[n % 2])
            return carry

        fours = (right - left) // 4
        lax.fori_loop(0, fours, four, 0)

        def rest(i, carry):
            one(i, even)
            return carry

        lax.fori_loop(left + 4 * fours, right, rest, 0)

    def clear():
        @pl.loop(0, own_rows // LANES)
        def _(j):
            rows = pl.ds(pl.multiple_of(j * LANES, LANES), LANES)
            even[rows, :] = jnp.zeros((LANES, block), f32)
            odd[rows, :] = jnp.zeros((LANES, block), f32)

    def turn(out, bias):
        @pl.loop(0, own_rows // LANES)
        def _(j):
            rows = pl.ds(pl.multiple_of(j * LANES, LANES), LANES)
            turned = (even[rows, :] + odd[rows, :]).T
            out[:, rows] = turned[:width]
            if bias is not None:
                bias[:, rows] = turned[width : width + 1] * n_col

    clear()
    loads[0].wait()
    add(events, events, 1, target_buf)
    loads[1].wait()
    add(2 * events, neg_count, 2, neg_buf)
    turn(out_out, bias_out)
    stores[0].start()
    stores[1].start()
    loads[2].wait()
    part = weight_out.shape[2] // n_col
    for w in range(2):
        for g in range(weight_out.shape[1]):
            for b in range(n_col):
                weight_out[w, g, b * part : (b + 1) * part, :] = grad_buf[w, g, b * block : b * block + part, 0:width]
        stores[2 + w].start()
    clear()
    loads[3].wait()
    add(0, events, 0, item_buf)
    turn(embed_out, None)
    stores[4].start()
    for store in stores:
        store.wait()


def run_finish(packed, shift, low, table_rows, own_rows, width, items, targets, negs, grads):
    events, block = items.shape
    _, gates, units, _ = grads.shape
    n_col = units // block
    hbm = pl.BlockSpec(memory_space=pl.ANY)
    weight = jax.ShapeDtypeStruct((gates, n_col * width, width), f32)
    table = jax.ShapeDtypeStruct((width, own_rows), f32)
    return pl.pallas_call(
        functools.partial(finish_kernel, shift, table_rows, width),
        out_shape=(table, table, jax.ShapeDtypeStruct((1, own_rows), f32), weight, weight),
        in_specs=[in_smem(), in_smem()] + [hbm] * 4,
        out_specs=(hbm,) * 5,
        scratch_shapes=[
            pltpu.VMEM((own_rows, block), f32),
            pltpu.VMEM((own_rows, block), f32),
            pltpu.VMEM(items.shape, f32),
            pltpu.VMEM(targets.shape, f32),
            pltpu.VMEM(negs.shape, f32),
            pltpu.VMEM(grads.shape, f32),
            pltpu.VMEM((width, own_rows), f32),
            pltpu.VMEM((width, own_rows), f32),
            pltpu.VMEM((1, own_rows), f32),
            pltpu.VMEM((2,) + weight.shape, f32),
            pltpu.SemaphoreType.DMA((9,)),
        ],
        cost_estimate=takes(40),
        compiler_params=params(),
    )(low.reshape(1), packed, items, targets, negs, grads)


def split_weight(weight, high_part, low_part):
    step = 128

    @pl.loop(0, weight.shape[0] // step)
    def _(i):
        rows = pl.ds(pl.multiple_of(i * step, step), step)
        value = weight[rows, :]
        top = value.astype(bf16)
        high_part[rows, :] = top
        low_part[rows, :] = (value - top.astype(f32)).astype(bf16)


def two_part(value):
    top = value.astype(bf16).astype(f32)
    return jnp.concatenate([top, value - top], axis=0).astype(bf16)


def forward_kernel(
    steps,
    width,
    hidden,
    entering,
    arrived,
    keep,
    prevs,
    resets,
    updates,
    cands,
    inners,
    outs,
    w_high,
    w_low,
    x_gates,
    hid_buf,
    in_buf,
    pair_buf,
    sem,
    travel=None,
):
    events, units = prevs.shape
    rows_per = arrived.shape[0] - events
    step_rows = hid_buf.shape[1]
    chunks = hidden.shape[0] // step_rows

    def load(i, slot):
        rows = pl.ds(pl.multiple_of(i * step_rows, step_rows), step_rows)
        return (
            pltpu.make_async_copy(hidden.at[rows], hid_buf.at[slot], sem.at[0, slot]),
            pltpu.make_async_copy(entering.at[rows], in_buf.at[slot], sem.at[1, slot]),
        )

    for copy in load(0, 0):
        copy.start()
    timeline = travel() if travel else ()
    pair_buf[0], pair_buf[1] = split_two(arrived[0:events, :])

    @pl.loop(0, chunks)
    def _(i):
        slot = lax.rem(i, 2)

        @pl.when(i + 1 < chunks)
        def _():
            for copy in load(i + 1, 1 - slot):
                copy.start()

        for copy in load(i, slot):
            copy.wait()
        cols = pl.ds(pl.multiple_of(i * step_rows, step_rows), step_rows)
        turned = hid_buf[slot].T
        first = turned.astype(bf16)
        w_high[:, cols] = first
        w_low[:, cols] = (turned - first.astype(f32)).astype(bf16)
        value = in_buf[slot]
        first = value.astype(bf16)
        second = (value - first.astype(f32)).astype(bf16)
        over = (((1,), (1,)), ((), ()))
        x_gates[:, cols] = (
            lax.dot_general(pair_buf[0], first, over, preferred_element_type=f32)
            + lax.dot_general(pair_buf[1], first, over, preferred_element_type=f32)
            + lax.dot_general(pair_buf[0], second, over, preferred_element_type=f32)
        )

    lane = lax.broadcasted_iota(jnp.int32, (rows_per, units), 1)

    def step(t, state):
        rows = pl.ds(pl.multiple_of(t * rows_per, rows_per), rows_per)
        prev = jnp.where(lane == width, 1.0, keep[rows, :] * state)
        pair = two_part(prev)

        def gate(g):
            cols = slice(g * units, (g + 1) * units)
            first = jnp.dot(pair, w_high[:, cols], preferred_element_type=f32)
            second = jnp.dot(pair, w_low[:, cols], preferred_element_type=f32)
            return first[:rows_per] + first[rows_per:] + second[:rows_per], cols

        h_reset, cols = gate(0)
        reset = jax.nn.sigmoid(x_gates[rows, cols] + h_reset)
        h_update, cols = gate(1)
        update = jax.nn.sigmoid(x_gates[rows, cols] + h_update)
        inner, cols = gate(2)
        cand = jnp.tanh(x_gates[rows, cols] + reset * inner)
        new = (1.0 - update) * cand + update * prev
        prevs[rows, :] = prev
        resets[rows, :] = reset
        updates[rows, :] = update
        cands[rows, :] = cand
        inners[rows, :] = inner
        outs[rows, :] = new
        return new

    state, done = arrived[events:, :], 0
    for share_done, actions in timeline:
        until = int(share_done * steps)
        if until > done:
            state, done = lax.fori_loop(done, until, step, state), until
        for action, argument in actions:
            action(argument)
    lax.fori_loop(done, steps, step, state)


def forward_travel_kernel(steps, width, hidden, entering, arrived, keep, out_rows, *refs):
    saved, (neg_all, targets), scratch = refs[:6], refs[6:8], refs[8:]
    z_rows, target_send, target_recv, target_local, row_local, row_send, row_recv = scratch[7:]
    spot = Spot()
    events = keep.shape[0]
    neg_own = out_rows.at[pl.ds(4 * events, z_rows.shape[1])]

    def target_own(z):
        return out_rows.at[pl.ds(pl.multiple_of(z * events, events), events)]

    rows = RowsFlow(spot, neg_own, z_rows, neg_all, row_local, row_send, row_recv, same=True)
    copies = []

    def begin_targets(_):
        keep_own = pltpu.make_async_copy(target_own(spot.c), targets.at[spot.c], target_local.at[0])
        keep_own.start()
        copies.append(keep_own)
        for m, z in enumerate(spot.z_to):
            copies.append(
                remote(target_own(z), targets.at[spot.c], target_send.at[m], target_recv.at[m], (spot.d, z))
            )

    def travel():
        spot.greet_all()
        rows.begin()
        return (
            (0.0, ((rows.forward, 0),)),
            (0.1, ((rows.spread, 1),)),
            (0.2, ((rows.far, 0),)),
            (0.3, ((rows.forward, 1), (rows.spread, 2), (begin_targets, None))),
            (0.4, ((rows.far, 1),)),
            (0.5, ((rows.forward, 2), (rows.spread, 3))),
            (0.6, ((rows.far, 2),)),
            (0.7, ((rows.forward, 3),)),
            (0.85, ((rows.far, 3),)),
        )

    forward_kernel(steps, width, hidden, entering, arrived, keep, *saved, *scratch[:7], travel=travel)
    rows.close()
    for copy in copies:
        copy.wait()


def forward_scratch(hidden, events):
    units = hidden.shape[1]
    step_rows = units // 4
    return [
        pltpu.VMEM(hidden.shape[::-1], bf16),
        pltpu.VMEM(hidden.shape[::-1], bf16),
        pltpu.VMEM((events, hidden.shape[0]), f32),
        pltpu.VMEM((2, step_rows, units), f32),
        pltpu.VMEM((2, step_rows, units), f32),
        pltpu.VMEM((2, events, units), bf16),
        pltpu.SemaphoreType.DMA((2, 2)),
    ]


def run_forward(hidden, entering, arrived, keep, steps, width):
    events, units = keep.shape[0], arrived.shape[1]
    saved = jax.ShapeDtypeStruct((events, units), f32)
    hbm = pl.BlockSpec(memory_space=pl.ANY)
    return pl.pallas_call(
        functools.partial(forward_kernel, steps, width),
        out_shape=(saved,) * 6,
        in_specs=[hbm, hbm] + [in_vmem()] * 2,
        out_specs=(in_vmem(),) * 6,
        scratch_shapes=forward_scratch(hidden, events),
        cost_estimate=takes(75),
        compiler_params=params(),
    )(hidden, entering, arrived, keep)


def run_forward_travel(hidden, entering, arrived, keep, out_rows, steps, width, collective_id):
    events, units = keep.shape[0], arrived.shape[1]
    block = out_rows.shape[1]
    count = out_rows.shape[0] - 4 * events
    saved = jax.ShapeDtypeStruct((events, units), f32)
    hbm = pl.BlockSpec(memory_space=pl.ANY)
    dma = pltpu.SemaphoreType.DMA
    return pl.pallas_call(
        functools.partial(forward_travel_kernel, steps, width),
        out_shape=(saved,) * 6
        + (jax.ShapeDtypeStruct((8, 4, count, block), f32), jax.ShapeDtypeStruct((4, events, block), f32)),
        in_specs=[hbm, hbm] + [in_vmem()] * 2 + [hbm],
        out_specs=(in_vmem(),) * 6 + (hbm, hbm),
        scratch_shapes=forward_scratch(hidden, events)
        + [pltpu.VMEM((4, count, block), f32), dma((3,)), dma((3,)), dma((1,)), dma((4,)), dma((4, 9)), dma((4, 9))],
        cost_estimate=takes(75),
        compiler_params=pltpu.CompilerParams(
            collective_id=collective_id, has_side_effects=True, vmem_limit_bytes=VMEM_BYTES
        ),
    )(hidden, entering, arrived, keep, out_rows)


def backward_kernel(
    steps, weight, douts, keep, prevs, resets, updates, cands, inners, dgates, dstart, w_high, w_low
):
    rows_per, units = dstart.shape
    split_weight(weight, w_high, w_low)

    def step(i, dstate):
        t = steps - 1 - i
        rows = pl.ds(pl.multiple_of(t * rows_per, rows_per), rows_per)
        reset, update, cand = resets[rows, :], updates[rows, :], cands[rows, :]
        dh = douts[rows, :] + dstate
        dcand = dh * (1.0 - update) * (1.0 - cand * cand)
        dreset = dcand * inners[rows, :] * reset * (1.0 - reset)
        dupdate = dh * (prevs[rows, :] - cand) * update * (1.0 - update)
        dinner = dcand * reset
        dgates[rows, 0:units] = dreset
        dgates[rows, units : 2 * units] = dupdate
        dgates[rows, 2 * units : 3 * units] = dinner
        dgates[rows, 3 * units : 4 * units] = dcand
        total = dh * update
        for g, part in enumerate((dreset, dupdate, dinner)):
            pair = two_part(part)
            sect = slice(g * units, (g + 1) * units)
            first = jnp.dot(pair, w_high[sect, :], preferred_element_type=f32)
            second = jnp.dot(pair, w_low[sect, :], preferred_element_type=f32)
            total = total + (first[:rows_per] + first[rows_per:] + second[:rows_per])
        return keep[rows, :] * total

    dstart[...] = lax.fori_loop(0, steps, step, jnp.zeros((rows_per, units), f32))


def run_backward(weight, douts, keep, saved, rows_per, steps):
    events, units = douts.shape
    return pl.pallas_call(
        functools.partial(backward_kernel, steps),
        out_shape=(
            jax.ShapeDtypeStruct((events, 4 * units), f32),
            jax.ShapeDtypeStruct((rows_per, units), f32),
        ),
        in_specs=[in_vmem()] * 8,
        out_specs=(in_vmem(),) * 2,
        scratch_shapes=[pltpu.VMEM(weight.shape, bf16)] * 2,
        cost_estimate=takes(67),
        compiler_params=params(),
    )(weight, douts, keep, *saved)


def place():
    d = lax.axis_index("dp")
    c = lax.axis_index("col")
    return d // 4, (d // 2) % 2, d % 2, c, d


def greet(partners):
    barrier = pltpu.get_barrier_semaphore()
    for partner in partners:
        pl.semaphore_signal(barrier, inc=1, device_id=partner, device_id_type=MESH)
    pl.semaphore_wait(barrier, len(partners))


class Spot:
    def __init__(self):
        self.y, self.x, self.k, self.c, self.d = place()
        y, x, k, c, d = self.y, self.x, self.k, self.c, self.d
        self.x_d, self.y_d, self.core_d = d + 2 - 4 * x, d + 4 - 8 * y, d + 1 - 2 * k
        self.far_d = d + 6 - 4 * x - 8 * y
        self.core_to, self.x_to, self.y_to, self.far_to = (self.core_d, c), (self.x_d, c), (self.y_d, c), (self.far_d, c)
        self.z_to = (c + 1 - 2 * lax.rem(c, 2), lax.rem(c + 2, 4), 3 - c)

    def greet_all(self):
        greet([self.core_to, self.x_to, self.y_to, self.far_to] + [(self.d, z) for z in self.z_to])


def remote(source, target, send, recv, to):
    copy = pltpu.make_async_remote_copy(
        src_ref=source, dst_ref=target, send_sem=send, recv_sem=recv, device_id=to, device_id_type=MESH
    )
    copy.start()
    return copy


class RowsFlow:
    def __init__(self, spot, outgoing, z_rows, every, local_sem, send_sem, recv_sem, same=False):
        self.spot, self.outgoing, self.z_rows, self.every = spot, outgoing, z_rows, every
        self.local_sem, self.send_sem, self.recv_sem = local_sem, send_sem, recv_sem
        self.started = {}
        self.rows = every.shape[2]
        self.sources = (spot.c,) + spot.z_to
        self.same = same

    def send(self, u, slot, source, target, to):
        return remote(source, target, self.send_sem.at[u, slot], self.recv_sem.at[u, slot], to)

    def begin(self):
        spot = self.spot
        for m in range(3):
            z = spot.z_to[m]
            source = self.outgoing if self.same else self.outgoing.at[z]
            self.started["z", m] = self.send(1 + m, 0, source, self.z_rows.at[spot.c], (spot.d, z))
        self.spread(0)

    def spread(self, u):
        spot, src = self.spot, self.sources[u]
        if u > 0:
            self.started["z", u - 1].wait_recv()
            source = self.z_rows.at[src, 0 : self.rows]
        else:
            source = self.outgoing if self.same else self.outgoing.at[src, 0 : self.rows]
        target = self.every.at[spot.d, src]
        keep = pltpu.make_async_copy(source, target, self.local_sem.at[u])
        keep.start()
        self.started["keep", u] = keep
        for slot, (name, to) in enumerate((("x", spot.x_to), ("y", spot.y_to), ("c", spot.core_to))):
            self.started[name, u] = self.send(u, 1 + slot, source, target, to)

    def forward(self, u):
        spot, src, mid = self.spot, self.sources[u], self.rows // 2
        self.started["x", u].wait_recv()
        piece = self.every.at[spot.x_d, src, 0:mid]
        self.started["xy", u] = self.send(u, 4, piece, piece, spot.y_to)
        piece = self.every.at[spot.x_d, src]
        self.started["xc", u] = self.send(u, 5, piece, piece, spot.core_to)
        self.started["y", u].wait_recv()
        piece = self.every.at[spot.y_d, src, mid : self.rows]
        self.started["yx", u] = self.send(u, 6, piece, piece, spot.x_to)
        piece = self.every.at[spot.y_d, src]
        self.started["yc", u] = self.send(u, 7, piece, piece, spot.core_to)

    def far(self, u):
        spot, src = self.spot, self.sources[u]
        self.started["xy", u].wait_recv()
        self.started["yx", u].wait_recv()
        piece = self.every.at[spot.far_d, src]
        self.started["fc", u] = self.send(u, 8, piece, piece, spot.core_to)

    def close(self):
        for u in range(4):
            for name in ("c", "xc", "yc", "fc"):
                self.started[name, u].wait_recv()
            self.started["keep", u].wait()
        for (name, _), copy in self.started.items():
            if name != "keep":
                copy.wait_send()


class SumFlow:
    def __init__(self, spot, mine, core_in, x_in, y_in, xy_in, yx_in, z_in, total, out_at, local_sem, send_sem, recv_sem):
        self.spot, self.mine, self.core_in, self.out_at = spot, mine, core_in, out_at
        self.x_in, self.y_in, self.xy_in, self.yx_in, self.z_in, self.total = x_in, y_in, xy_in, yx_in, z_in, total
        self.local_sem, self.send_sem, self.recv_sem = local_sem, send_sem, recv_sem
        self.started = [{} for _ in range(mine.shape[0])]
        self.half = mine.shape[4] // 2

    def send(self, j, slot, source, target, to):
        return remote(source, target, self.send_sem.at[j, slot], self.recv_sem.at[j, slot], to)

    def over_core(self, j, source):
        self.started[j]["core"] = self.send(j, 0, source, self.core_in.at[j], self.spot.core_to)

    def core(self, j):
        spot, mine, half, started = self.spot, self.mine, self.half, self.started[j]
        started["core"].wait_recv()

        @pl.loop(0, 4)
        def _(a):
            for b in range(2):
                for e in range(2):
                    mine[j, a, b, e] = mine[j, a, b, e] + self.core_in[j, a, b, e]

        started["x"] = self.send(j, 1, mine.at[j, :, :, 1 - spot.x, 0:half], self.x_in.at[j], spot.x_to)
        started["y"] = self.send(j, 2, mine.at[j, :, 1 - spot.y, :, half : 2 * half], self.y_in.at[j], spot.y_to)

    def first(self, j):
        spot, mine, half, started = self.spot, self.mine, self.half, self.started[j]
        x, y = spot.x, spot.y
        started["x"].wait_recv()
        for a in range(4):
            for b in range(2):
                mine[j, a, b, x, 0:half] = mine[j, a, b, x, 0:half] + self.x_in[j, a, b]
        started["xy"] = self.send(j, 3, mine.at[j, :, 1 - y, x, 0:half], self.xy_in.at[j], spot.y_to)
        started["y"].wait_recv()
        for a in range(4):
            for e in range(2):
                mine[j, a, y, e, half : 2 * half] = mine[j, a, y, e, half : 2 * half] + self.y_in[j, a, e]
        started["yx"] = self.send(j, 4, mine.at[j, :, y, 1 - x, half : 2 * half], self.yx_in.at[j], spot.x_to)

    def second(self, j):
        spot, mine, half, started = self.spot, self.mine, self.half, self.started[j]
        x, y = spot.x, spot.y
        started["xy"].wait_recv()
        started["yx"].wait_recv()
        for a in range(4):
            mine[j, a, y, x, 0:half] = mine[j, a, y, x, 0:half] + self.xy_in[j, a]
            mine[j, a, y, x, half : 2 * half] = mine[j, a, y, x, half : 2 * half] + self.yx_in[j, a]
        for m in range(3):
            z = spot.z_to[m]
            started["z", m] = self.send(j, 5 + m, mine.at[j, z, y, x], self.z_in.at[j, m], (spot.d, z))

    def along(self, j):
        spot, started, total = self.spot, self.started[j], self.total
        for m in range(3):
            started["z", m].wait_recv()
        own = self.mine[j, spot.c, spot.y, spot.x]
        total[j] = ((own + self.z_in[j, 0]) + self.z_in[j, 1]) + self.z_in[j, 2]
        target = self.out_at(j, spot.d, 0, 2 * self.half)
        started["keep"] = pltpu.make_async_copy(total.at[j], target, self.local_sem.at[j])
        started["keep"].start()
        for slot, (name, to) in enumerate((("gx", spot.x_to), ("gy", spot.y_to), ("gc", spot.core_to))):
            started[name] = self.send(j, 8 + slot, total.at[j], target, to)

    def share(self, j):
        spot, started, half = self.spot, self.started[j], self.half
        started["gx"].wait_recv()
        piece = self.out_at(j, spot.x_d, 0, half)
        started["gxy"] = self.send(j, 11, piece, piece, spot.y_to)
        piece = self.out_at(j, spot.x_d, 0, 2 * half)
        started["cgx"] = self.send(j, 12, piece, piece, spot.core_to)
        started["gy"].wait_recv()
        piece = self.out_at(j, spot.y_d, half, half)
        started["gyx"] = self.send(j, 13, piece, piece, spot.x_to)
        piece = self.out_at(j, spot.y_d, 0, 2 * half)
        started["cgy"] = self.send(j, 14, piece, piece, spot.core_to)

    def far(self, j):
        spot, started = self.spot, self.started[j]
        started["gxy"].wait_recv()
        started["gyx"].wait_recv()
        piece = self.out_at(j, spot.far_d, 0, 2 * self.half)
        started["cgf"] = self.send(j, 15, piece, piece, spot.core_to)

    def end(self, j, core_sent=False):
        started = self.started[j]
        for name in ("gc", "cgx", "cgy", "cgf"):
            started[name].wait_recv()
        for name, copy in started.items():
            if name == "keep":
                copy.wait()
            elif not (name == "core" and core_sent):
                copy.wait_send()


def sum_scratch(jobs, piece, lanes):
    half = piece // 2
    return [
        pltpu.VMEM((jobs, 4, 2, 2, piece, lanes), f32),
        pltpu.VMEM((jobs, 4, 2, 2, piece, lanes), f32),
        pltpu.VMEM((jobs, 4, 2, half, lanes), f32),
        pltpu.VMEM((jobs, 4, 2, half, lanes), f32),
        pltpu.VMEM((jobs, 4, half, lanes), f32),
        pltpu.VMEM((jobs, 4, half, lanes), f32),
        pltpu.VMEM((jobs, 3, piece, lanes), f32),
        pltpu.VMEM((jobs, piece, lanes), f32),
    ]


def flow_sems(jobs):
    dma = pltpu.SemaphoreType.DMA
    return [dma((jobs,)), dma((jobs, 16)), dma((jobs, 16)), dma((4,)), dma((4, 9)), dma((4, 9))]


GATE_OF = ((0, 1, 3), (0, 1, 2))


def split_two(value):
    top = value.astype(bf16)
    return top, (value - top.astype(f32)).astype(bf16)


def three_products(first, second, over):
    def product(a, b):
        return lax.dot_general(a, b, (over, ((), ())), preferred_element_type=f32)

    return product(first[0], second[0]) + product(first[1], second[0]) + product(first[0], second[1])


def tail_kernel(
    inputs,
    prevs,
    dgates,
    dstart,
    entering,
    out,
    item_all,
    start_all,
    mine,
    core_in,
    x_in,
    y_in,
    xy_in,
    yx_in,
    z_in,
    total,
    core_out,
    turned,
    gate_pair,
    flow,
    w_flow,
    din,
    z_rows,
    flow_sem,
    start_sem,
    sum_local,
    sum_send,
    sum_recv,
    row_local,
    row_send,
    row_recv,
):
    spot = Spot()
    spot.greet_all()
    c, k = spot.c, spot.k
    jobs, piece = mine.shape[0], mine.shape[4]
    events, units = gate_pair.shape[2:]
    block = din.shape[2]
    gates = jobs // 2
    sums = SumFlow(
        spot, mine, core_in, x_in, y_in, xy_in, yx_in, z_in, total,
        lambda j, d, at, size: out.at[j // gates, j % gates, d, pl.ds(at, size)], sum_local, sum_send, sum_recv,
    )
    rows = RowsFlow(spot, din, z_rows, item_all, row_local, row_send, row_recv)

    def gate_cols(g):
        return dgates.at[:, pl.ds(g * units, units)]

    queue = [inputs.at[pl.ds(0, events)], gate_cols(0), gate_cols(1), gate_cols(3), prevs, gate_cols(2)]

    def flow_copy(n):
        return pltpu.make_async_copy(queue[n], flow.at[n % 2], flow_sem.at[n % 2])

    def w_copy(n, slot):
        rows = pl.ds(pl.multiple_of(n * block, block), block)
        return pltpu.make_async_copy(entering.at[rows], w_flow.at[slot], flow_sem.at[2 + slot])

    flow_copy(0).start()
    flow_copy(1).start()
    w_copy(0, 0).start()

    def next_flow(n):
        if n + 2 < len(queue):
            flow_copy(n + 2).start()

    def take_act(n, w):
        flow_copy(n).wait()

        @pl.loop(0, 4)
        def _(b):
            cols = pl.ds(pl.multiple_of(b * block, block), block)
            turned[w, 0, b], turned[w, 1, b] = split_two(flow[n % 2, :, cols].T)

        next_flow(n)

    def take_gate(n, g, at):
        flow_copy(n).wait()

        @pl.loop(0, 4)
        def _(b):
            cols = pl.ds(pl.multiple_of(b * block, block), block)
            value = flow[n % 2, :, cols]
            gate_pair[g, 0, :, cols], gate_pair[g, 1, :, cols] = split_two(value)
            if at is not None:
                chunk = 4 * at + b
                slot = lax.rem(b, 2)

                @pl.when(chunk + 1 < 12)
                def _():
                    w_copy(chunk + 1, 1 - slot).start()

                w_copy(chunk, slot).wait()
                share = three_products(split_two(value), split_two(w_flow[slot]), ((1,), (0,)))
                for e in range(4):
                    part = share[:, e * block : (e + 1) * block]
                    if at == 0:
                        before = jnp.where(b == 0, 0.0, din[e, 0:events, :])
                    else:
                        before = din[e, 0:events, :]
                    din[e, 0:events, :] = before + part

        next_flow(n)

    def rows_begin():
        for e in range(4):
            din[e, events:, :] = dstart[:, e * block : (e + 1) * block]
        rows.begin()

    def rows_end():
        keeps = [
            pltpu.make_async_copy(din.at[c, events:], start_all.at[c], start_sem.at[0]),
        ] + [
            pltpu.make_async_copy(z_rows.at[z, events:], start_all.at[z], start_sem.at[1 + m])
            for m, z in enumerate(spot.z_to)
        ]
        for keep in keeps:
            keep.start()
        rows.close()
        for keep in keeps:
            keep.wait()

    def partial(j):
        w, g = j // gates, GATE_OF[j // gates][j % gates]
        slot = j % 2
        if j >= 2:
            sums.started[j - 2]["core"].wait_send()

        @pl.loop(0, 2)
        def _(p):
            for q in range(2):
                b = 2 * p + q
                value = three_products(
                    (turned[w, 0, b], turned[w, 1, b]), (gate_pair[g, 0], gate_pair[g, 1]), ((1,), (0,))
                )
                for e in range(4):
                    cols = slice(e * block, (e + 1) * block)
                    first, second = value[:piece, cols], value[piece:, cols]
                    mine[j, e, p, q] = jnp.where(k == 0, first, second)
                    core_out[slot, e, p, q] = jnp.where(k == 0, second, first)

        sums.over_core(j, core_out.at[slot])

    A, B, C, Z, S, F = sums.core, sums.first, sums.second, sums.along, sums.share, sums.far

    def E(j):
        sums.end(j, core_sent=j < jobs - 2)

    take_act(0, 0)
    take_gate(1, 0, 0)
    partial(0)
    take_gate(2, 1, 1)
    partial(1)
    A(0)
    take_gate(3, 3, 2)
    rows_begin()
    partial(2)
    A(1)
    take_act(4, 1)
    partial(3)
    A(2), B(0), rows.spread(1), rows.forward(0)
    partial(4)
    A(3), B(1), C(0), rows.spread(2), rows.forward(1), rows.far(0)
    take_gate(5, 2, None)
    partial(5)
    A(4), B(2), C(1), Z(0), rows.spread(3), rows.forward(2), rows.far(1)
    A(5), B(3), C(2), Z(1), S(0), rows.forward(3), rows.far(2)
    B(4), C(3), Z(2), S(1), F(0), rows.far(3)
    B(5), C(4), Z(3), S(2), F(1), E(0)
    C(5), Z(4), S(3), F(2), E(1)
    rows_end()
    Z(5), S(4), F(3), E(2)
    S(5), F(4), E(3)
    F(5), E(4), E(5)


def run_tail(inputs, prevs, dgates, dstart, entering, collective_id):
    events, units = prevs.shape
    gates, block = 3, units // 4
    piece = units // 8
    jobs = 2 * gates
    start_rows = dstart.shape[0]
    hbm = pl.BlockSpec(memory_space=pl.ANY)
    grads, item_all, start_all = pl.pallas_call(
        tail_kernel,
        out_shape=(
            jax.ShapeDtypeStruct((2, gates, 8, piece, block), f32),
            jax.ShapeDtypeStruct((8, 4, events, block), f32),
            jax.ShapeDtypeStruct((4, start_rows, block), f32),
        ),
        in_specs=[hbm, hbm, hbm, pl.BlockSpec(memory_space=pltpu.VMEM), hbm],
        out_specs=(hbm, hbm, hbm),
        scratch_shapes=sum_scratch(jobs, piece, block)
        + [
            pltpu.VMEM((2, 4, 2, 2, piece, block), f32),
            pltpu.VMEM((2, 2, 4, block, events), bf16),
            pltpu.VMEM((4, 2, events, units), bf16),
            pltpu.VMEM((2, events, units), f32),
            pltpu.VMEM((2, block, units), f32),
            pltpu.VMEM((4, events + start_rows, block), f32),
            pltpu.VMEM((4, events + start_rows, block), f32),
            pltpu.SemaphoreType.DMA((4,)),
            pltpu.SemaphoreType.DMA((4,)),
        ]
        + flow_sems(jobs),
        cost_estimate=takes(190),
        compiler_params=pltpu.CompilerParams(
            collective_id=collective_id, has_side_effects=True, vmem_limit_bytes=VMEM_BYTES
        ),
    )(inputs, prevs, dgates, dstart, entering)
    return grads.reshape(2, gates, units, block), item_all, start_all


HEAD_TIMES = ((8, 14, 28, 42), (10, 22, 32, 44, 56, 68), 12, 20, 58)
UNITS = ((0, 0), (0, 1), (1, 0), (0, 2), (1, 1), (1, 2))


def head_kernel(
    chunk,
    width,
    item_ids,
    out_ids,
    embed,
    table,
    bias,
    w_in,
    w_hid,
    in_bias,
    hid_bias,
    carried,
    own_ids,
    all_in,
    all_hid,
    arrived,
    all_ids,
    out_rows,
    padded,
    turned,
    item_rows,
    held,
    w_buf,
    local_sem,
    send_sem,
    recv_sem,
    row_send,
    row_recv,
    id_send,
    id_recv,
):
    y, x, k, c, d = place()
    i = pl.program_id(0)
    n = pl.num_programs(0) // 2
    core_to, x_to, y_to = (d + 1 - 2 * k, c), (d + 2 - 4 * x, c), (d + 4 - 8 * y, c)
    z_all = (c + 1 - 2 * lax.rem(c, 2), lax.rem(c + 2, 4), 3 - c)
    alls = (all_in, all_hid)
    gates, piece, units = held.shape[1], held.shape[5], held.shape[6]
    half = piece // 2
    block = item_rows.shape[2]
    items = item_rows.shape[1]
    carried_rows = carried.shape[1]
    events = items - carried_rows

    def send(u, slot):
        w, m = UNITS[u]
        z = z_all[m]
        every = alls[w]
        if slot == 0:
            source, target, to = held.at[w, :, y, x, k], every.at[:, c, y, x, k], (d, z)
        elif slot in (4, 6):
            spot = (
                every.at[:, z, y, 1 - x, k, 0:half] if slot == 4 else every.at[:, z, 1 - y, x, k, half : 2 * half]
            )
            source, target, to = spot, spot, (y_to if slot == 4 else x_to)
        else:
            py, px, to = {
                1: (y, x, x_to),
                2: (y, x, y_to),
                3: (y, x, core_to),
                5: (y, 1 - x, core_to),
                7: (1 - y, x, core_to),
                8: (1 - y, 1 - x, core_to),
            }[slot]
            spot = every.at[:, z, py, px, k]
            source, target = spot, spot
        return pltpu.make_async_remote_copy(
            src_ref=source,
            dst_ref=target,
            send_sem=send_sem.at[u, slot],
            recv_sem=recv_sem.at[u, slot],
            device_id=to,
            device_id_type=MESH,
        )

    def load(w):
        return pltpu.make_async_copy((w_in, w_hid)[w], w_buf.at[w], local_sem.at[w])

    def keep(w):
        return pltpu.make_async_copy(held.at[w], alls[w].at[:, c], local_sem.at[2 + w])

    def pad(w):
        load(w).wait()
        part, own = units // block, w_buf.shape[3]
        inner = w_buf.shape[2] // part
        for g in range(gates):
            for b in range(part):
                turned[b * block : b * block + inner, 0:own] = w_buf[w, g, b * inner : (b + 1) * inner, :]
            turned[inner : inner + 1, 0:own] = (in_bias, hid_bias)[w][g : g + 1, :]
            held[w, g] = turned[0:units, :].T.reshape(2, 2, 2, piece, units)
        keep(w).start()

    def item_send(m):
        return pltpu.make_async_remote_copy(
            src_ref=item_rows.at[z_all[m]],
            dst_ref=arrived.at[:, pl.ds(pl.multiple_of(c * block, block), block)],
            send_sem=row_send.at[m],
            recv_sem=row_recv.at[m],
            device_id=(d, z_all[m]),
            device_id_type=MESH,
        )

    def begin_items(_):
        for m in range(3):
            item_send(m).start()

    def item_keep():
        return pltpu.make_async_copy(
            item_rows.at[c], arrived.at[:, pl.ds(pl.multiple_of(c * block, block), block)], local_sem.at[4]
        )

    def id_copy(m):
        to = lax.rem(d + 1 + m, 8)
        return pltpu.make_async_remote_copy(
            src_ref=own_ids,
            dst_ref=all_ids.at[d],
            send_sem=id_send.at[m],
            recv_sem=id_recv.at[m],
            device_id=(to, c),
            device_id_type=MESH,
        )

    def id_keep():
        return pltpu.make_async_copy(own_ids, all_ids.at[d], local_sem.at[5])

    def begin():
        load(0).start()
        load(1).start()
        greet([(lax.rem(d + 1 + m, 8), c) for m in range(7)] + [(d, z) for z in z_all])
        id_keep().start()
        for m in range(7):
            id_copy(m).start()
        turned[0:units, :] = jnp.zeros((units, block), f32)
        pad(0)
        begin_z(0)
        begin_z(1)
        pad(1)

    def begin_z(u):
        send(u, 0).start()

    def spread(u):
        send(u, 0).wait_recv()
        for slot in (1, 2, 3):
            send(u, slot).start()

    def forward(u):
        send(u, 1).wait_recv()
        send(u, 4).start()
        send(u, 5).start()
        send(u, 2).wait_recv()
        send(u, 6).start()
        send(u, 7).start()

    def far(u):
        send(u, 4).wait_recv()
        send(u, 6).wait_recv()
        send(u, 8).start()

    def close(u):
        for slot in (3, 5, 7, 8):
            send(u, slot).wait_recv()
        for slot in range(9):
            send(u, slot).wait_send()

    z_at, spread_at, forward_by, far_by, items_at = HEAD_TIMES
    timeline = [(-1, begin, None), (items_at, begin_items, 0)]
    timeline += [(at, begin_z, 2 + j) for j, at in enumerate(z_at)]
    for u, at in enumerate(spread_at):
        timeline += [(at, spread, u), (at + forward_by, forward, u), (at + far_by, far, u)]
    timeline.sort(key=lambda entry: entry[0])
    last = 2 * n - 1

    @pl.when(i == 0)
    def _():
        padded[...] = jnp.zeros_like(padded)
        padded[width : width + 1, :] = jnp.full((1, chunk), jnp.where(c == 0, 1.0, 0.0), f32)

    for at, action, u in timeline:
        if at < last:

            @pl.when(i == max(at, 0))
            def _(action=action, u=u):
                action() if u is None else action(u)

    @pl.when(i < n)
    def _():
        padded[0:width, :] = embed[...]

    @pl.when(i >= n)
    def _():
        padded[0:width, :] = table[...]
        padded[width : width + 1, :] = bias[...]

    spot = lax.rem(i, n) * chunk
    turned[pl.ds(pl.multiple_of(spot, chunk), chunk), :] = padded[...].T

    @pl.when(i == n - 1)
    def _():
        for z in range(4):

            def body(b, carry, z=z):
                for j in range(8):
                    row = item_ids[z * events + b * 8 + j]
                    item_rows[z, pl.ds(b * 8 + j, 1), :] = turned[pl.ds(row, 1), :]
                return carry

            lax.fori_loop(0, events // 8, body, 0)
            item_rows[z, events:items, :] = carried[z]
        item_keep().start()

    @pl.when(i == last)
    def _():
        def body(b, carry):
            for j in range(8):
                row = out_ids[b * 8 + j]
                out_rows[pl.ds(b * 8 + j, 1), :] = turned[pl.ds(row, 1), :]
            return carry

        lax.fori_loop(0, out_rows.shape[0] // 8, body, 0)
        for at, action, u in timeline:
            if at >= last:
                action(u)
        for u in range(6):
            close(u)
        for m in range(3):
            item_send(m).wait()
        for m in range(7):
            id_copy(m).wait()
        id_keep().wait()
        for w in range(2):
            keep(w).wait()
        item_keep().wait()


def gather_all(embed, table, bias, item_ids, out_ids, w_in, w_hid, in_bias, hid_bias, carried, own_ids, collective_id):
    width, rows = embed.shape
    gates, block = w_in.shape[0], carried.shape[2]
    units = 4 * block
    piece = block // 8
    chunk = 128 * max(k for k in range(1, 9) if rows % (128 * k) == 0)
    n = rows // chunk
    items = item_ids.shape[0] // 4 + carried.shape[1]
    own_shape = (gates, 2, 2, 2, piece, units)
    all_shape = (gates, 4, 2, 2, 2, piece, units)
    smem = pl.BlockSpec(memory_space=pltpu.SMEM)
    hbm = pl.BlockSpec(memory_space=pl.ANY)
    all_in, all_hid, arrived, all_ids, out_rows = pl.pallas_call(
        functools.partial(head_kernel, chunk, width),
        out_shape=(
            jax.ShapeDtypeStruct(all_shape, f32),
            jax.ShapeDtypeStruct(all_shape, f32),
            jax.ShapeDtypeStruct((items, units), f32),
            jax.ShapeDtypeStruct((8,) + own_ids.shape, jnp.int32),
            jax.ShapeDtypeStruct((out_ids.shape[0], block), f32),
        ),
        grid=(2 * n,),
        in_specs=[
            smem,
            smem,
            pl.BlockSpec((width, chunk), lambda i: (0, jnp.minimum(i, n - 1))),
            pl.BlockSpec((width, chunk), lambda i: (0, jnp.maximum(i - n, 0))),
            pl.BlockSpec((1, chunk), lambda i: (0, jnp.maximum(i - n, 0))),
            hbm,
            hbm,
            pl.BlockSpec(in_bias.shape, lambda i: (0, 0)),
            pl.BlockSpec(hid_bias.shape, lambda i: (0, 0)),
            pl.BlockSpec(carried.shape, lambda i: (0, 0, 0)),
            pl.BlockSpec(own_ids.shape, lambda i: (0, 0)),
        ],
        out_specs=(hbm, hbm, hbm, hbm, pl.BlockSpec((out_ids.shape[0], block), lambda i: (0, 0))),
        scratch_shapes=[
            pltpu.VMEM((block, chunk), f32),
            pltpu.VMEM((rows, block), f32),
            pltpu.VMEM((4, items, block), f32),
            pltpu.VMEM((2,) + own_shape, f32),
            pltpu.VMEM((2,) + w_in.shape, f32),
            pltpu.SemaphoreType.DMA((6,)),
            pltpu.SemaphoreType.DMA((6, 9)),
            pltpu.SemaphoreType.DMA((6, 9)),
            pltpu.SemaphoreType.DMA((3,)),
            pltpu.SemaphoreType.DMA((3,)),
            pltpu.SemaphoreType.DMA((7,)),
            pltpu.SemaphoreType.DMA((7,)),
        ],
        cost_estimate=takes(120),
        compiler_params=pltpu.CompilerParams(
            collective_id=collective_id, has_side_effects=True, vmem_limit_bytes=VMEM_BYTES
        ),
    )(item_ids, out_ids, embed, table, bias, w_in, w_hid, in_bias, hid_bias, carried, own_ids)
    return (
        all_in.reshape(gates, 4 * block, units),
        all_hid.reshape(gates, 4 * block, units),
        arrived,
        all_ids,
        out_rows,
    )


def loss_kernel(width, factor, outs, targets, negs, loss, douts, neg_part, target_part, share, pairs, score):
    n_col, events, block = targets.shape
    n_dp, _, count, _ = negs.shape
    lane = lax.broadcasted_iota(jnp.int32, (events, block), 1)
    for c in range(n_col):
        value = jnp.where(lane < width, outs[:, c * block : (c + 1) * block], 0.0)
        value = jnp.where(lane == width, 1.0 / n_col, value)
        share[c] = value
        pairs[0, c], pairs[1, c] = split_two(value)

    @pl.loop(0, n_dp)
    def _(b):
        cols = pl.ds(pl.multiple_of(b * count, count), count)
        total = jnp.zeros((events, count), f32)
        for c in range(n_col):
            total = total + three_products((pairs[0, c], pairs[1, c]), split_two(negs[b, c]), ((1,), (1,)))
        score[:, cols] = total

    step = 32

    @pl.loop(0, events // step)
    def _(i):
        rows = pl.ds(pl.multiple_of(i * step, step), step)
        pos = jnp.zeros((step, 1), f32)
        for c in range(n_col):
            pos = pos + jnp.sum(share[c, rows, :] * targets[c, rows, :], axis=-1, keepdims=True)
        neg = score[rows, :]
        expd = jnp.exp(neg - jnp.max(neg, axis=-1, keepdims=True))
        weight = expd * (1.0 / jnp.sum(expd, axis=-1, keepdims=True))
        sig = jax.nn.sigmoid(pos - neg)
        slope = weight * sig
        ppos = jnp.sum(slope, axis=-1, keepdims=True)
        quad = jnp.sum(weight * neg * neg, axis=-1, keepdims=True)
        slope = jnp.sum(slope * (1.0 - sig), axis=-1, keepdims=True)
        loss[rows, :] = jnp.broadcast_to(quad - jnp.log(ppos), (step, LANES))
        score[rows, :] = factor * weight * (1.0 - sig * sig * (1.0 / ppos) + neg * neg + 2.0 * neg - quad)
        dpos = -factor * slope / ppos
        for c in range(n_col):
            target_part[c, rows, :] = dpos * share[c, rows, :]
            douts[rows, c * block : (c + 1) * block] = dpos * targets[c, rows, :]

    @pl.loop(0, n_dp)
    def _(b):
        dneg = score[:, pl.ds(pl.multiple_of(b * count, count), count)]
        across, down = split_two(dneg), split_two(dneg.T)
        for c in range(n_col):
            cols = slice(c * block, (c + 1) * block)
            douts[:, cols] = douts[:, cols] + three_products(across, split_two(negs[b, c]), ((1,), (0,)))
            neg_part[c, b] = three_products(down, (pairs[0, c], pairs[1, c]), ((1,), (0,)))

    for c in range(n_col):
        cols = slice(c * block, (c + 1) * block)
        douts[:, cols] = jnp.where(lane < width, douts[:, cols], 0.0)


def run_loss(outs, targets, negs, width, factor):
    n_col, events, block = targets.shape
    n_dp, _, count, _ = negs.shape
    return pl.pallas_call(
        functools.partial(loss_kernel, width, factor),
        out_shape=(
            jax.ShapeDtypeStruct((events, LANES), f32),
            jax.ShapeDtypeStruct(outs.shape, f32),
            jax.ShapeDtypeStruct((n_col, n_dp, count, block), f32),
            jax.ShapeDtypeStruct((n_col, events, block), f32),
        ),
        in_specs=[in_vmem()] * 3,
        out_specs=(in_vmem(),) * 4,
        scratch_shapes=[
            pltpu.VMEM((n_col, events, block), f32),
            pltpu.VMEM((2, n_col, events, block), bf16),
            pltpu.VMEM((events, n_dp * count), f32),
        ],
        cost_estimate=takes(25),
        compiler_params=params(),
    )(outs, targets, negs)


def back_kernel(
    steps,
    hidden,
    douts,
    keep,
    prevs,
    resets,
    updates,
    cands,
    inners,
    neg_part,
    target_part,
    own_loss,
    dgates,
    dstart,
    neg_all,
    target_all,
    loss_all,
    mine,
    core_in,
    x_in,
    y_in,
    xy_in,
    yx_in,
    z_in,
    total,
    w_high,
    w_low,
    w_flow,
    z_rows,
    flow_sem,
    load_sem,
    loss_send,
    loss_recv,
    sum_local,
    sum_send,
    sum_recv,
    row_local,
    row_send,
    row_recv,
):
    spot = Spot()
    spot.greet_all()
    rows_per, units = dstart.shape
    jobs, piece = mine.shape[0], mine.shape[4]
    step_rows = w_flow.shape[1]
    chunks = hidden.shape[0] // step_rows
    sums = SumFlow(
        spot, mine, core_in, x_in, y_in, xy_in, yx_in, z_in, total,
        lambda j, d, at, size: neg_all.at[d, pl.ds(j * piece + at, size)], sum_local, sum_send, sum_recv,
    )
    rows = RowsFlow(spot, target_part, z_rows, target_all, row_local, row_send, row_recv)

    def load(i, slot):
        part = pl.ds(pl.multiple_of(i * step_rows, step_rows), step_rows)
        return pltpu.make_async_copy(hidden.at[part], w_flow.at[slot], flow_sem.at[slot])

    load(0, 0).start()
    own = []
    for j in range(jobs):
        part = pl.ds(j * piece, piece)
        own.append(pltpu.make_async_copy(neg_part.at[:, :, :, spot.k, part], mine.at[j], load_sem.at[j]))
        own[j].start()
        sums.over_core(j, neg_part.at[:, :, :, 1 - spot.k, part])
    rows.begin()
    losses = [pltpu.make_async_copy(own_loss, loss_all.at[spot.c], load_sem.at[jobs])]
    losses[0].start()
    for m, z in enumerate(spot.z_to):
        losses.append(remote(own_loss, loss_all.at[spot.c], loss_send.at[m], loss_recv.at[m], (spot.d, z)))

    @pl.loop(0, chunks)
    def _(i):
        slot = lax.rem(i, 2)

        @pl.when(i + 1 < chunks)
        def _():
            load(i + 1, 1 - slot).start()

        load(i, slot).wait()
        part = pl.ds(pl.multiple_of(i * step_rows, step_rows), step_rows)
        w_high[part, :], w_low[part, :] = split_two(w_flow[slot])

    def step(i, dstate):
        t = steps - 1 - i
        now = pl.ds(pl.multiple_of(t * rows_per, rows_per), rows_per)
        reset, update, cand = resets[now, :], updates[now, :], cands[now, :]
        dh = douts[now, :] + dstate
        dcand = dh * (1.0 - update) * (1.0 - cand * cand)
        dreset = dcand * inners[now, :] * reset * (1.0 - reset)
        dupdate = dh * (prevs[now, :] - cand) * update * (1.0 - update)
        dinner = dcand * reset
        dgates[now, 0:units] = dreset
        dgates[now, units : 2 * units] = dupdate
        dgates[now, 2 * units : 3 * units] = dinner
        dgates[now, 3 * units : 4 * units] = dcand
        total_now = dh * update
        for g, part in enumerate((dreset, dupdate, dinner)):
            pair = two_part(part)
            sect = slice(g * units, (g + 1) * units)
            first = jnp.dot(pair, w_high[sect, :], preferred_element_type=f32)
            second = jnp.dot(pair, w_low[sect, :], preferred_element_type=f32)
            total_now = total_now + (first[:rows_per] + first[rows_per:] + second[:rows_per])
        return keep[now, :] * total_now

    def sums_core(j):
        own[j].wait()
        sums.core(j)

    A, B, C, Z, S, F = sums_core, sums.first, sums.second, sums.along, sums.share, sums.far
    timeline = (
        (0.0, ((A, 0), (A, 1))),
        (0.15, ((rows.forward, 0),)),
        (0.28, ((rows.spread, 1), (B, 0))),
        (0.38, ((rows.forward, 1), (rows.far, 0))),
        (0.47, ((B, 1), (rows.spread, 2))),
        (0.56, ((C, 0), (rows.forward, 2), (rows.far, 1))),
        (0.66, ((C, 1), (rows.spread, 3))),
        (0.78, ((Z, 0), (rows.forward, 3), (rows.far, 2))),
        (0.88, ((Z, 1), (S, 0))),
    )
    state, done = jnp.zeros((rows_per, units), f32), 0
    for share_done, actions in timeline:
        until = int(share_done * steps)
        if until > done:
            state, done = lax.fori_loop(done, until, step, state), until
        for action, argument in actions:
            action(argument)
    dstart[...] = lax.fori_loop(done, steps, step, state)
    rows.far(3)
    S(1), F(0), F(1)
    sums.end(0)
    rows.close()
    sums.end(1)
    for copy in losses:
        copy.wait()


def run_back(hidden, douts, keep, saved, neg_part, target_part, own_loss, rows_per, steps, collective_id):
    events, units = douts.shape
    count, block = neg_part.shape[2:]
    jobs = 2
    piece = count // jobs
    hbm = pl.BlockSpec(memory_space=pl.ANY)
    step_rows = units // 4
    return pl.pallas_call(
        functools.partial(back_kernel, steps),
        out_shape=(
            jax.ShapeDtypeStruct((events, 4 * units), f32),
            jax.ShapeDtypeStruct((rows_per, units), f32),
            jax.ShapeDtypeStruct((8, count, block), f32),
            jax.ShapeDtypeStruct((8, 4, events, block), f32),
            jax.ShapeDtypeStruct((4,) + own_loss.shape, f32),
        ),
        in_specs=[hbm] + [in_vmem()] * 7 + [hbm, hbm, in_vmem()],
        out_specs=(in_vmem(), in_vmem(), hbm, hbm, hbm),
        scratch_shapes=sum_scratch(jobs, piece, block)
        + [
            pltpu.VMEM(hidden.shape, bf16),
            pltpu.VMEM(hidden.shape, bf16),
            pltpu.VMEM((2, step_rows, units), f32),
            pltpu.VMEM((4, events, block), f32),
            pltpu.SemaphoreType.DMA((2,)),
            pltpu.SemaphoreType.DMA((jobs + 1,)),
            pltpu.SemaphoreType.DMA((3,)),
            pltpu.SemaphoreType.DMA((3,)),
        ]
        + flow_sems(jobs),
        cost_estimate=takes(80),
        compiler_params=pltpu.CompilerParams(
            collective_id=collective_id, has_side_effects=True, vmem_limit_bytes=VMEM_BYTES
        ),
    )(hidden, douts, keep, *saved, neg_part.reshape(4, 2, 2, 2, count, block), target_part, own_loss)


def pad_kernel(weight, bias, out):
    own, full = weight.shape[1:]
    block = out.shape[1]
    n_col = out.shape[2] // block
    part = full // n_col
    out[...] = jnp.zeros_like(out)
    for c in range(n_col):
        out[0, 0:own, c * block : c * block + part] = weight[0, :, c * part : (c + 1) * part]
    out[0, 0:own, part : part + 1] = bias[0]


def pad_units(weight, bias, n_col, block):
    gates, own, full = weight.shape
    return pl.pallas_call(
        pad_kernel,
        out_shape=jax.ShapeDtypeStruct((gates, block, n_col * block), f32),
        grid=(gates,),
        in_specs=[
            pl.BlockSpec((1, own, full), lambda g: (g, 0, 0)),
            pl.BlockSpec((1, own, 1), lambda g: (g, 0, 0)),
        ],
        out_specs=pl.BlockSpec((1, block, n_col * block), lambda g: (g, 0, 0)),
        compiler_params=params(),
    )(weight, bias[:, :, None])


def gather_weight(own, n_dp):
    gates, block, units = own.shape
    flat = own.reshape(n_dp, gates * block // n_dp, units)
    piece = lax.dynamic_index_in_dim(flat, lax.axis_index("dp"), 0, keepdims=False)
    every = lax.all_gather(piece, ("col", "dp"))
    every = every.reshape(-1, gates, block, units)
    return jnp.moveaxis(every, 0, 1).reshape(gates, -1, units)


def reduce_weight(partial, n_dp, n_col):
    gates, rows, units = partial.shape
    block = rows // n_col
    parts = jnp.moveaxis(partial.reshape(gates, n_col, block, units), 1, 0)
    parts = jnp.moveaxis(parts.reshape(n_col, n_dp, gates * block // n_dp, units), 1, 0)
    mine = lax.psum_scatter(parts, "dp", scatter_dimension=0)
    mine = lax.psum_scatter(mine, "col", scatter_dimension=0)
    return lax.all_gather(mine, "dp").reshape(gates, block, units)


def swap_col(rows, n_col):
    return lax.all_to_all(rows, "col", split_axis=0, concat_axis=0, tiled=True)


def unpad_last(value, n_col, part):
    block = value.shape[-1] // n_col
    return value.reshape(value.shape[:-1] + (n_col, block))[..., :part].reshape(value.shape[:-1] + (n_col * part,))


def local(
    n_dp,
    n_col,
    item_ids,
    target_ids,
    negative_ids,
    reset_mask,
    carry_flags,
    carried_state,
    embed_table,
    input_weight,
    hidden_weight,
    gate_bias,
    hidden_bias,
    out_table,
    out_bias,
):
    sessions, steps = item_ids.shape
    own_sessions = sessions // n_col
    rows_per = round_up(own_sessions, ROWS8)
    width = embed_table.shape[0]
    table_rows = embed_table.shape[1]
    own_rows = table_rows // n_dp
    block = round_up(width + 1, LANES)
    units = n_col * block
    events = steps * rows_per
    direct = n_dp == 8 and n_col == 4 and block % 64 == 0 and own_sessions == rows_per
    factor = 1.0 / steps
    dp_at, col_at = lax.axis_index("dp"), lax.axis_index("col")

    def by_owner(value):
        value = jnp.moveaxis(value.reshape(n_col, own_sessions, steps), 1, 2)
        value = jnp.pad(value, ((0, 0), (0, 0), (0, rows_per - own_sessions)))
        return value.reshape(-1)

    item_flat, target_flat = by_owner(item_ids), by_owner(target_ids)
    own_keep = lax.dynamic_index_in_dim(
        by_owner(1 - reset_mask).reshape(n_col, events, 1), col_at, 0, keepdims=False
    ).astype(f32)
    valid = jnp.tile(jnp.arange(rows_per) < own_sessions, steps)
    lane = jnp.arange(units) % block

    carried = (carry_flags.astype(f32)[:, None] * carried_state).reshape(n_col, own_sessions, width)
    carried = jnp.pad(carried, ((0, 0), (0, rows_per - own_sessions), (0, block - width)))
    neg_count = negative_ids.shape[0]
    own_negs = lax.dynamic_slice_in_dim(negative_ids, dp_at * (neg_count // n_dp), neg_count // n_dp)
    out_ids = jnp.concatenate([target_flat, own_negs])
    no_bias = jnp.zeros_like(hidden_bias)
    hid_bias = jnp.stack([no_bias, no_bias, hidden_bias])
    if direct:
        own_ids = jnp.concatenate([item_flat, target_flat]).reshape(-1, LANES)
        all_in, all_hid, arrived, all_ids, out_rows = gather_all(
            embed_table,
            out_table,
            out_bias[None, :],
            item_flat,
            out_ids,
            jnp.swapaxes(input_weight, 1, 2),
            jnp.swapaxes(hidden_weight, 1, 2),
            gate_bias,
            hid_bias,
            carried,
            own_ids,
            1,
        )
        all_ids = all_ids.reshape(n_dp, 2, -1)
    else:
        all_hid = gather_weight(pad_units(hidden_weight, hid_bias, n_col, block), n_dp)
        all_in = gather_weight(pad_units(input_weight, gate_bias, n_col, block), n_dp)
        no_row = jnp.zeros((1, table_rows), f32)
        item_rows = gather_rows(embed_table, no_row, item_flat, block).reshape(n_col, events, block)
        arrived = swap_col(jnp.concatenate([item_rows, carried], axis=1), n_col)
        arrived = jnp.moveaxis(arrived, 0, 1).reshape(events + rows_per, units)
        arrived = arrived.at[:events, width].set(1.0)
        out_rows = gather_rows(out_table, out_bias[None, :], out_ids, block)
        all_ids = lax.all_gather(jnp.stack([item_flat, target_flat]), "dp")
    all_hid, all_in = all_hid.reshape(-1, units), all_in.reshape(-1, units)

    all_items, all_targets = all_ids[:, 0].reshape(-1), all_ids[:, 1].reshape(-1)
    count = all_items.shape[0]
    keys = jnp.concatenate([all_items, all_targets + table_rows, negative_ids + 2 * table_rows])
    order = jnp.concatenate([jnp.tile(lax.iota(jnp.int32, count), 2), lax.iota(jnp.int32, neg_count)])
    shift = (max(count, neg_count) - 1).bit_length()
    direct = direct and (3 * table_rows) << shift < 2**31
    low = (dp_at * own_rows).astype(jnp.int32)
    if direct:
        packed = lax.sort((keys << shift) | order)
    else:
        keys, order = lax.sort((keys, order), num_keys=1)
        by_item = (order[:count], keys[:count])
        by_target = (order[count : 2 * count], keys[count : 2 * count] - table_rows)
        by_neg = (order[2 * count :], keys[2 * count :] - 2 * table_rows)

    if direct:
        *saved, outs, negs, targets = run_forward_travel(
            all_hid, all_in, arrived, own_keep, out_rows, steps, width, 4
        )
    else:
        targets = swap_col(out_rows[: n_col * events].reshape(n_col, events, block), n_col)
        negs = lax.all_gather(out_rows[n_col * events :], ("dp", "col")).reshape(n_dp, n_col, -1, block)
        *saved, outs = run_forward(all_hid, all_in, arrived, own_keep, steps, width)
    prevs = saved[0]

    if direct:
        own_loss, douts, neg_part, target_part = run_loss(outs, targets, negs, width, factor)
        own_loss = jnp.pad(own_loss[:, 0].reshape(steps, rows_per).T, ((0, 0), (0, round_up(steps, LANES) - steps)))
        dgates, dstart, neg_all, target_all, loss_all = run_back(
            all_hid, douts, own_keep, saved, neg_part, target_part, own_loss, rows_per, steps, 3
        )
        loss = loss_all[:, :, :steps].reshape(sessions, steps)
        neg_all, target_all = neg_all.reshape(-1, block), target_all.reshape(-1, block)
    else:
        targets = jnp.moveaxis(targets, 0, 1).reshape(events, units)
        negs = jnp.moveaxis(negs, 1, 2).reshape(neg_count, units)
        shares = jnp.where(lane == width, 1.0 / n_col, jnp.where(lane < width, outs, 0.0))
        pos_score = jnp.sum(shares * targets, axis=-1, keepdims=True)
        neg_score = lax.dot_general(shares, negs, (((1,), (1,)), ((), ())), precision=high)
        top = jnp.max(neg_score, axis=-1, keepdims=True)
        expd = jnp.exp(neg_score - top)
        weight = expd / jnp.sum(expd, axis=-1, keepdims=True)
        sig = jax.nn.sigmoid(pos_score - neg_score)
        ppos = jnp.sum(weight * sig, axis=-1, keepdims=True)
        quad = jnp.sum(weight * neg_score * neg_score, axis=-1, keepdims=True)
        slope = jnp.sum(weight * sig * (1.0 - sig), axis=-1, keepdims=True)
        own_loss = -jnp.log(ppos) + quad
        dneg = factor * weight * (1.0 - sig * sig / ppos + neg_score * neg_score + 2.0 * neg_score - quad)
        dneg = jnp.where(valid[:, None], dneg, 0.0)
        dpos = jnp.where(valid[:, None], -factor * slope / ppos, 0.0)
        douts = jnp.dot(dneg, negs, precision=high) + dpos * targets
        douts = jnp.where(lane < width, douts, 0.0)
        neg_part = lax.dot_general(dneg, shares, (((0,), (0,)), ((), ())), precision=high)
        target_part = dpos * shares

        neg_own = lax.psum_scatter(neg_part.reshape(n_dp, -1, units), "dp", scatter_dimension=0)
        neg_own = jnp.moveaxis(neg_own.reshape(-1, n_col, block), 1, 0)
        neg_own = lax.psum_scatter(neg_own, "col", scatter_dimension=0)
        neg_all = lax.all_gather(neg_own, "dp", tiled=True)
        target_own = swap_col(jnp.moveaxis(target_part.reshape(events, n_col, block), 1, 0), n_col)
        target_all = lax.all_gather(target_own.reshape(-1, block), "dp", tiled=True)
        dgates, dstart = run_backward(all_hid, douts, own_keep, saved, rows_per, steps)
        own_loss = own_loss.reshape(steps, rows_per)[:, :own_sessions]
        loss = lax.all_gather(own_loss.T, "col", tiled=True)
    gates = input_weight.shape[0]
    if direct:
        grads, item_all, start_all = run_tail(arrived, prevs, dgates, dstart, all_in, 2)
        grad_embed, grad_out, grad_obias, grad_in, grad_hid = run_finish(
            packed, shift, low, table_rows, own_rows, width, item_all.reshape(-1, block), target_all, neg_all, grads
        )
        grad_obias = grad_obias[0]
        grad_in, grad_hid = jnp.swapaxes(grad_in, 1, 2), jnp.swapaxes(grad_hid, 1, 2)
        grad_gate, grad_hbias = grads[0, :, width, :width], grads[1, gates - 1, width, :width]
    else:
        dx = jnp.concatenate([dgates[:, : 2 * units], dgates[:, 3 * units :]], axis=1)
        dh = dgates[:, : 3 * units]
        hid_part = lax.dot_general(dh, prevs, (((0,), (0,)), ((), ())), precision=high)
        in_part = lax.dot_general(dx, arrived[:events], (((0,), (0,)), ((), ())), precision=high)
        dinputs = jnp.dot(dx, all_in, precision=high)
        back = jnp.concatenate([dinputs, dstart], axis=0).reshape(events + rows_per, n_col, block)
        back = swap_col(jnp.moveaxis(back, 1, 0), n_col)
        item_all = lax.all_gather(back[:, :events].reshape(-1, block), "dp", tiled=True)
        start_all = back[:, events:]
        grad_in = reduce_weight(in_part.reshape(gates, units, units), n_dp, n_col)
        grad_hid = reduce_weight(hid_part.reshape(gates, units, units), n_dp, n_col)
        grad_gate, grad_hbias = grad_in[:, :width, width], grad_hid[gates - 1, :width, width]
        grad_in, grad_hid = (unpad_last(g[:, :width], n_col, width) for g in (grad_in, grad_hid))
        grad_out, grad_obias = scatter_rows(
            [by_target + (target_all,), by_neg + (neg_all,)],
            low,
            own_rows,
            width,
            block,
        )
        grad_obias = grad_obias[0] * n_col
        grad_embed, _ = scatter_rows([by_item + (item_all,)], low, own_rows, width, block)
    grad_carried = start_all[:, :own_sessions, :width].reshape(sessions, width)
    grad_carried = carry_flags.astype(f32)[:, None] * grad_carried
    return (
        loss,
        grad_embed,
        grad_in,
        grad_hid,
        grad_gate,
        grad_hbias,
        grad_out,
        grad_obias,
        grad_carried,
    )


def solution(mesh):
    in_specs = (
        P("dp", None),
        P("dp", None),
        P(),
        P("dp", None),
        P("dp"),
        P("dp", "col"),
        P("col", None),
        P(None, "col", None),
        P(None, "col", None),
        P(None, "col"),
        P("col"),
        P("col", None),
        P(),
    )
    out_specs = (
        P("dp", None),
        P("col", "dp"),
        P(None, "col", None),
        P(None, "col", None),
        P(None, "col"),
        P("col"),
        P("col", "dp"),
        P("dp"),
        P("dp", "col"),
    )
    body = functools.partial(local, mesh.shape["dp"], mesh.shape["col"])
    return jax.shard_map(body, mesh=mesh, in_specs=in_specs, out_specs=out_specs, check_vma=False)
```

```python
import functools

import jax
import jax.numpy as jnp
from jax import lax
from jax.experimental import pallas as pl
from jax.experimental.pallas import tpu as pltpu
from jax.sharding import PartitionSpec as P

LANES = 128
ROWS8 = 8
VMEM_BYTES = 60 << 20
f32 = jnp.float32
bf16 = jnp.bfloat16
high = lax.Precision.HIGH
MESH = pl.DeviceIdType.MESH


def round_up(value, unit):
    return -(-value // unit) * unit


def params():
    return pltpu.CompilerParams(vmem_limit_bytes=VMEM_BYTES)


def takes(micros):
    return pl.CostEstimate(flops=int(micros * 1.1e9), bytes_accessed=1 << 20, transcendentals=0)


def in_vmem():
    return pl.BlockSpec(memory_space=pltpu.VMEM)


def in_smem():
    return pl.BlockSpec(memory_space=pltpu.SMEM)


def gather_kernel(chunk, count, width, ids, table, bias, out, padded, turned):
    step = pl.program_id(0)

    @pl.when(step == 0)
    def _():
        padded[...] = jnp.zeros_like(padded)

    padded[0:width, :] = table[...]
    padded[width : width + 1, :] = bias[...]
    turned[pl.ds(pl.multiple_of(step * chunk, chunk), chunk), :] = padded[...].T

    @pl.when(step == pl.num_programs(0) - 1)
    def _():
        def body(block, carry):
            for j in range(ROWS8):
                row = ids[block * ROWS8 + j]
                out[pl.ds(block * ROWS8 + j, 1), :] = turned[pl.ds(row, 1), :]
            return carry

        lax.fori_loop(0, count // ROWS8, body, 0)


def gather_rows(table, bias, ids, block):
    width, rows = table.shape
    count = ids.shape[0]
    chunk = LANES * max(k for k in range(1, 9) if rows % (LANES * k) == 0)
    return pl.pallas_call(
        functools.partial(gather_kernel, chunk, count, width),
        out_shape=jax.ShapeDtypeStruct((count, block), f32),
        grid_spec=pltpu.PrefetchScalarGridSpec(
            num_scalar_prefetch=1,
            grid=(rows // chunk,),
            in_specs=[
                pl.BlockSpec((width, chunk), lambda i, ids: (0, i)),
                pl.BlockSpec((1, chunk), lambda i, ids: (0, i)),
            ],
            out_specs=pl.BlockSpec((count, block), lambda i, ids: (0, 0)),
            scratch_shapes=[pltpu.VMEM((block, chunk), f32), pltpu.VMEM((rows, block), f32)],
        ),
        compiler_params=params(),
    )(ids, table, bias)


def scatter_kernel(width, n_lists, *refs):
    bounds = refs[0]
    lists = refs[1 : 1 + 3 * n_lists]
    out, bias_out, acc = refs[1 + 3 * n_lists :]
    acc[...] = jnp.zeros_like(acc)
    low = bounds[0]
    for k in range(n_lists):
        rows_of, ids, data = lists[3 * k : 3 * k + 3]

        def body(i, carry):
            spot = pl.ds(ids[i] - low, 1)
            acc[spot, :] = acc[spot, :] + data[pl.ds(rows_of[i], 1), :]
            return carry

        lax.fori_loop(bounds[1 + 2 * k], bounds[2 + 2 * k], body, 0)
    for j in range(acc.shape[0] // LANES):
        cols = slice(j * LANES, (j + 1) * LANES)
        turned = acc[cols, :].T
        out[:, cols] = turned[:width]
        bias_out[:, cols] = turned[width : width + 1]


def scatter_rows(lists, low, own_rows, width, block):
    ends = [low]
    operands, specs = [], []
    for order, ids, data in lists:
        ends += [jnp.sum(ids < low, dtype=jnp.int32), jnp.sum(ids < low + own_rows, dtype=jnp.int32)]
        operands += [order, ids, data]
        specs += [in_smem(), in_smem(), in_vmem()]
    return pl.pallas_call(
        functools.partial(scatter_kernel, width, len(lists)),
        out_shape=(
            jax.ShapeDtypeStruct((width, own_rows), f32),
            jax.ShapeDtypeStruct((1, own_rows), f32),
        ),
        in_specs=[in_smem()] + specs,
        out_specs=(in_vmem(), in_vmem()),
        scratch_shapes=[pltpu.VMEM((own_rows, block), f32)],
        cost_estimate=takes(20),
        compiler_params=params(),
    )(jnp.stack(ends), *operands)


def finish_kernel(
    shift,
    table_rows,
    width,
    low,
    packed,
    items,
    targets,
    negs,
    grads,
    grad_embed,
    grad_out,
    grad_bias,
    grad_in,
    grad_hid,
    even,
    odd,
    item_buf,
    target_buf,
    neg_buf,
    grad_buf,
    embed_out,
    out_out,
    bias_out,
    weight_out,
    sem,
):
    own_rows = even.shape[0]
    events, neg_count = item_buf.shape[0], neg_buf.shape[0]
    block = even.shape[1]
    n_col = grad_buf.shape[2] // block
    loads = [
        pltpu.make_async_copy(source, target, sem.at[n])
        for n, (source, target) in enumerate(
            ((targets, target_buf), (negs, neg_buf), (grads, grad_buf), (items, item_buf))
        )
    ]
    for load in loads:
        load.start()
    stores = [
        pltpu.make_async_copy(source, target, sem.at[4 + n])
        for n, (source, target) in enumerate(
            (
                (out_out, grad_out),
                (bias_out, grad_bias),
                (weight_out.at[0], grad_in),
                (weight_out.at[1], grad_hid),
                (embed_out, grad_embed),
            )
        )
    ]

    def first_from(begin, count, bound):
        def halve(_, ends):
            left, right = ends
            middle = jnp.minimum((left + right) // 2, begin + count - 1)
            less = (left < right) & (packed[middle] < bound)
            return jnp.where(less, middle + 1, left), jnp.where(less | (left >= right), right, middle)

        return lax.fori_loop(0, count.bit_length() + 1, halve, (begin, begin + count))[0]

    def add(begin, count, which, data):
        base = low[0] + which * table_rows
        left = first_from(begin, count, base << shift)
        right = first_from(begin, count, (base + own_rows) << shift)

        def one(i, acc):
            key = packed[i]
            spot, row = (key >> shift) - base, key & ((1 << shift) - 1)
            acc[pl.ds(spot, 1), :] = acc[pl.ds(spot, 1), :] + data[pl.ds(row, 1), :]

        def four(i, carry):
            for n in range(4):
                one(left + 4 * i + n, (even, odd)[n % 2])
            return carry

        fours = (right - left) // 4
        lax.fori_loop(0, fours, four, 0)

        def rest(i, carry):
            one(i, even)
            return carry

        lax.fori_loop(left + 4 * fours, right, rest, 0)

    def clear():
        @pl.loop(0, own_rows // LANES)
        def _(j):
            rows = pl.ds(pl.multiple_of(j * LANES, LANES), LANES)
            even[rows, :] = jnp.zeros((LANES, block), f32)
            odd[rows, :] = jnp.zeros((LANES, block), f32)

    def turn(out, bias):
        @pl.loop(0, own_rows // LANES)
        def _(j):
            rows = pl.ds(pl.multiple_of(j * LANES, LANES), LANES)
            turned = (even[rows, :] + odd[rows, :]).T
            out[:, rows] = turned[:width]
            if bias is not None:
                bias[:, rows] = turned[width : width + 1] * n_col

    clear()
    loads[0].wait()
    add(events, events, 1, target_buf)
    loads[1].wait()
    add(2 * events, neg_count, 2, neg_buf)
    turn(out_out, bias_out)
    stores[0].start()
    stores[1].start()
    loads[2].wait()
    part = weight_out.shape[2] // n_col
    for w in range(2):
        for g in range(weight_out.shape[1]):
            for b in range(n_col):
                weight_out[w, g, b * part : (b + 1) * part, :] = grad_buf[w, g, b * block : b * block + part, 0:width]
        stores[2 + w].start()
    clear()
    loads[3].wait()
    add(0, events, 0, item_buf)
    turn(embed_out, None)
    stores[4].start()
    for store in stores:
        store.wait()


def run_finish(packed, shift, low, table_rows, own_rows, width, items, targets, negs, grads):
    events, block = items.shape
    _, gates, units, _ = grads.shape
    n_col = units // block
    hbm = pl.BlockSpec(memory_space=pl.ANY)
    weight = jax.ShapeDtypeStruct((gates, n_col * width, width), f32)
    table = jax.ShapeDtypeStruct((width, own_rows), f32)
    return pl.pallas_call(
        functools.partial(finish_kernel, shift, table_rows, width),
        out_shape=(table, table, jax.ShapeDtypeStruct((1, own_rows), f32), weight, weight),
        in_specs=[in_smem(), in_smem()] + [hbm] * 4,
        out_specs=(hbm,) * 5,
        scratch_shapes=[
            pltpu.VMEM((own_rows, block), f32),
            pltpu.VMEM((own_rows, block), f32),
            pltpu.VMEM(items.shape, f32),
            pltpu.VMEM(targets.shape, f32),
            pltpu.VMEM(negs.shape, f32),
            pltpu.VMEM(grads.shape, f32),
            pltpu.VMEM((width, own_rows), f32),
            pltpu.VMEM((width, own_rows), f32),
            pltpu.VMEM((1, own_rows), f32),
            pltpu.VMEM((2,) + weight.shape, f32),
            pltpu.SemaphoreType.DMA((9,)),
        ],
        cost_estimate=takes(40),
        compiler_params=params(),
    )(low.reshape(1), packed, items, targets, negs, grads)


def split_weight(weight, high_part, low_part):
    step = 128

    @pl.loop(0, weight.shape[0] // step)
    def _(i):
        rows = pl.ds(pl.multiple_of(i * step, step), step)
        value = weight[rows, :]
        top = value.astype(bf16)
        high_part[rows, :] = top
        low_part[rows, :] = (value - top.astype(f32)).astype(bf16)


def two_part(value):
    top = value.astype(bf16).astype(f32)
    return jnp.concatenate([top, value - top], axis=0).astype(bf16)


def forward_kernel(
    steps,
    width,
    hidden,
    entering,
    arrived,
    keep,
    prevs,
    resets,
    updates,
    cands,
    inners,
    outs,
    w_high,
    w_low,
    x_gates,
    hid_buf,
    in_buf,
    pair_buf,
    sem,
    travel=None,
):
    events, units = prevs.shape
    rows_per = arrived.shape[0] - events
    step_rows = hid_buf.shape[1]
    chunks = hidden.shape[0] // step_rows

    def load(i, slot):
        rows = pl.ds(pl.multiple_of(i * step_rows, step_rows), step_rows)
        return (
            pltpu.make_async_copy(hidden.at[rows], hid_buf.at[slot], sem.at[0, slot]),
            pltpu.make_async_copy(entering.at[rows], in_buf.at[slot], sem.at[1, slot]),
        )

    for copy in load(0, 0):
        copy.start()
    timeline = travel() if travel else ()
    pair_buf[0], pair_buf[1] = split_two(arrived[0:events, :])

    @pl.loop(0, chunks)
    def _(i):
        slot = lax.rem(i, 2)

        @pl.when(i + 1 < chunks)
        def _():
            for copy in load(i + 1, 1 - slot):
                copy.start()

        for copy in load(i, slot):
            copy.wait()
        cols = pl.ds(pl.multiple_of(i * step_rows, step_rows), step_rows)
        turned = hid_buf[slot].T
        first = turned.astype(bf16)
        w_high[:, cols] = first
        w_low[:, cols] = (turned - first.astype(f32)).astype(bf16)
        value = in_buf[slot]
        first = value.astype(bf16)
        second = (value - first.astype(f32)).astype(bf16)
        over = (((1,), (1,)), ((), ()))
        x_gates[:, cols] = (
            lax.dot_general(pair_buf[0], first, over, preferred_element_type=f32)
            + lax.dot_general(pair_buf[1], first, over, preferred_element_type=f32)
            + lax.dot_general(pair_buf[0], second, over, preferred_element_type=f32)
        )

    lane = lax.broadcasted_iota(jnp.int32, (rows_per, units), 1)

    def step(t, state):
        rows = pl.ds(pl.multiple_of(t * rows_per, rows_per), rows_per)
        prev = jnp.where(lane == width, 1.0, keep[rows, :] * state)
        pair = two_part(prev)

        def gate(g):
            cols = slice(g * units, (g + 1) * units)
            first = jnp.dot(pair, w_high[:, cols], preferred_element_type=f32)
            second = jnp.dot(pair, w_low[:, cols], preferred_element_type=f32)
            return first[:rows_per] + first[rows_per:] + second[:rows_per], cols

        h_reset, cols = gate(0)
        reset = jax.nn.sigmoid(x_gates[rows, cols] + h_reset)
        h_update, cols = gate(1)
        update = jax.nn.sigmoid(x_gates[rows, cols] + h_update)
        inner, cols = gate(2)
        cand = jnp.tanh(x_gates[rows, cols] + reset * inner)
        new = (1.0 - update) * cand + update * prev
        prevs[rows, :] = prev
        resets[rows, :] = reset
        updates[rows, :] = update
        cands[rows, :] = cand
        inners[rows, :] = inner
        outs[rows, :] = new
        return new

    state, done = arrived[events:, :], 0
    for share_done, actions in timeline:
        until = int(share_done * steps)
        if until > done:
            state, done = lax.fori_loop(done, until, step, state), until
        for action, argument in actions:
            action(argument)
    lax.fori_loop(done, steps, step, state)


def forward_travel_kernel(steps, width, hidden, entering, arrived, keep, out_rows, *refs):
    saved, (neg_all, targets), scratch = refs[:6], refs[6:8], refs[8:]
    z_rows, target_send, target_recv, target_local, row_local, row_send, row_recv = scratch[7:]
    spot = Spot()
    events = keep.shape[0]
    neg_own = out_rows.at[pl.ds(4 * events, z_rows.shape[1])]

    def target_own(z):
        return out_rows.at[pl.ds(pl.multiple_of(z * events, events), events)]

    rows = RowsFlow(spot, neg_own, z_rows, neg_all, row_local, row_send, row_recv, same=True)
    copies = []

    def begin_targets(_):
        keep_own = pltpu.make_async_copy(target_own(spot.c), targets.at[spot.c], target_local.at[0])
        keep_own.start()
        copies.append(keep_own)
        for m, z in enumerate(spot.z_to):
            copies.append(
                remote(target_own(z), targets.at[spot.c], target_send.at[m], target_recv.at[m], (spot.d, z))
            )

    def travel():
        spot.greet_all()
        rows.begin()
        return (
            (0.0, ((rows.forward, 0),)),
            (0.1, ((rows.spread, 1),)),
            (0.2, ((rows.far, 0),)),
            (0.3, ((rows.forward, 1), (rows.spread, 2), (begin_targets, None))),
            (0.4, ((rows.far, 1),)),
            (0.5, ((rows.forward, 2), (rows.spread, 3))),
            (0.6, ((rows.far, 2),)),
            (0.7, ((rows.forward, 3),)),
            (0.85, ((rows.far, 3),)),
        )

    forward_kernel(steps, width, hidden, entering, arrived, keep, *saved, *scratch[:7], travel=travel)
    rows.close()
    for copy in copies:
        copy.wait()


def forward_scratch(hidden, events):
    units = hidden.shape[1]
    step_rows = units // 4
    return [
        pltpu.VMEM(hidden.shape[::-1], bf16),
        pltpu.VMEM(hidden.shape[::-1], bf16),
        pltpu.VMEM((events, hidden.shape[0]), f32),
        pltpu.VMEM((2, step_rows, units), f32),
        pltpu.VMEM((2, step_rows, units), f32),
        pltpu.VMEM((2, events, units), bf16),
        pltpu.SemaphoreType.DMA((2, 2)),
    ]


def run_forward(hidden, entering, arrived, keep, steps, width):
    events, units = keep.shape[0], arrived.shape[1]
    saved = jax.ShapeDtypeStruct((events, units), f32)
    hbm = pl.BlockSpec(memory_space=pl.ANY)
    return pl.pallas_call(
        functools.partial(forward_kernel, steps, width),
        out_shape=(saved,) * 6,
        in_specs=[hbm, hbm] + [in_vmem()] * 2,
        out_specs=(in_vmem(),) * 6,
        scratch_shapes=forward_scratch(hidden, events),
        cost_estimate=takes(75),
        compiler_params=params(),
    )(hidden, entering, arrived, keep)


def run_forward_travel(hidden, entering, arrived, keep, out_rows, steps, width, collective_id):
    events, units = keep.shape[0], arrived.shape[1]
    block = out_rows.shape[1]
    count = out_rows.shape[0] - 4 * events
    saved = jax.ShapeDtypeStruct((events, units), f32)
    hbm = pl.BlockSpec(memory_space=pl.ANY)
    dma = pltpu.SemaphoreType.DMA
    return pl.pallas_call(
        functools.partial(forward_travel_kernel, steps, width),
        out_shape=(saved,) * 6
        + (jax.ShapeDtypeStruct((8, 4, count, block), f32), jax.ShapeDtypeStruct((4, events, block), f32)),
        in_specs=[hbm, hbm] + [in_vmem()] * 2 + [hbm],
        out_specs=(in_vmem(),) * 6 + (hbm, hbm),
        scratch_shapes=forward_scratch(hidden, events)
        + [pltpu.VMEM((4, count, block), f32), dma((3,)), dma((3,)), dma((1,)), dma((4,)), dma((4, 9)), dma((4, 9))],
        cost_estimate=takes(75),
        compiler_params=pltpu.CompilerParams(
            collective_id=collective_id, has_side_effects=True, vmem_limit_bytes=VMEM_BYTES
        ),
    )(hidden, entering, arrived, keep, out_rows)


def backward_kernel(
    steps, weight, douts, keep, prevs, resets, updates, cands, inners, dgates, dstart, w_high, w_low
):
    rows_per, units = dstart.shape
    split_weight(weight, w_high, w_low)

    def step(i, dstate):
        t = steps - 1 - i
        rows = pl.ds(pl.multiple_of(t * rows_per, rows_per), rows_per)
        reset, update, cand = resets[rows, :], updates[rows, :], cands[rows, :]
        dh = douts[rows, :] + dstate
        dcand = dh * (1.0 - update) * (1.0 - cand * cand)
        dreset = dcand * inners[rows, :] * reset * (1.0 - reset)
        dupdate = dh * (prevs[rows, :] - cand) * update * (1.0 - update)
        dinner = dcand * reset
        dgates[rows, 0:units] = dreset
        dgates[rows, units : 2 * units] = dupdate
        dgates[rows, 2 * units : 3 * units] = dinner
        dgates[rows, 3 * units : 4 * units] = dcand
        total = dh * update
        for g, part in enumerate((dreset, dupdate, dinner)):
            pair = two_part(part)
            sect = slice(g * units, (g + 1) * units)
            first = jnp.dot(pair, w_high[sect, :], preferred_element_type=f32)
            second = jnp.dot(pair, w_low[sect, :], preferred_element_type=f32)
            total = total + (first[:rows_per] + first[rows_per:] + second[:rows_per])
        return keep[rows, :] * total

    dstart[...] = lax.fori_loop(0, steps, step, jnp.zeros((rows_per, units), f32))


def run_backward(weight, douts, keep, saved, rows_per, steps):
    events, units = douts.shape
    return pl.pallas_call(
        functools.partial(backward_kernel, steps),
        out_shape=(
            jax.ShapeDtypeStruct((events, 4 * units), f32),
            jax.ShapeDtypeStruct((rows_per, units), f32),
        ),
        in_specs=[in_vmem()] * 8,
        out_specs=(in_vmem(),) * 2,
        scratch_shapes=[pltpu.VMEM(weight.shape, bf16)] * 2,
        cost_estimate=takes(67),
        compiler_params=params(),
    )(weight, douts, keep, *saved)


def place():
    d = lax.axis_index("dp")
    c = lax.axis_index("col")
    return d // 4, (d // 2) % 2, d % 2, c, d


def greet(partners):
    barrier = pltpu.get_barrier_semaphore()
    for partner in partners:
        pl.semaphore_signal(barrier, inc=1, device_id=partner, device_id_type=MESH)
    pl.semaphore_wait(barrier, len(partners))


class Spot:
    def __init__(self):
        self.y, self.x, self.k, self.c, self.d = place()
        y, x, k, c, d = self.y, self.x, self.k, self.c, self.d
        self.x_d, self.y_d, self.core_d = d + 2 - 4 * x, d + 4 - 8 * y, d + 1 - 2 * k
        self.far_d = d + 6 - 4 * x - 8 * y
        self.core_to, self.x_to, self.y_to, self.far_to = (self.core_d, c), (self.x_d, c), (self.y_d, c), (self.far_d, c)
        self.z_to = (c + 1 - 2 * lax.rem(c, 2), lax.rem(c + 2, 4), 3 - c)

    def greet_all(self):
        greet([self.core_to, self.x_to, self.y_to, self.far_to] + [(self.d, z) for z in self.z_to])


def remote(source, target, send, recv, to):
    copy = pltpu.make_async_remote_copy(
        src_ref=source, dst_ref=target, send_sem=send, recv_sem=recv, device_id=to, device_id_type=MESH
    )
    copy.start()
    return copy


class RowsFlow:
    def __init__(self, spot, outgoing, z_rows, every, local_sem, send_sem, recv_sem, same=False):
        self.spot, self.outgoing, self.z_rows, self.every = spot, outgoing, z_rows, every
        self.local_sem, self.send_sem, self.recv_sem = local_sem, send_sem, recv_sem
        self.started = {}
        self.rows = every.shape[2]
        self.sources = (spot.c,) + spot.z_to
        self.same = same

    def send(self, u, slot, source, target, to):
        return remote(source, target, self.send_sem.at[u, slot], self.recv_sem.at[u, slot], to)

    def begin(self):
        spot = self.spot
        for m in range(3):
            z = spot.z_to[m]
            source = self.outgoing if self.same else self.outgoing.at[z]
            self.started["z", m] = self.send(1 + m, 0, source, self.z_rows.at[spot.c], (spot.d, z))
        self.spread(0)

    def spread(self, u):
        spot, src = self.spot, self.sources[u]
        if u > 0:
            self.started["z", u - 1].wait_recv()
            source = self.z_rows.at[src, 0 : self.rows]
        else:
            source = self.outgoing if self.same else self.outgoing.at[src, 0 : self.rows]
        target = self.every.at[spot.d, src]
        keep = pltpu.make_async_copy(source, target, self.local_sem.at[u])
        keep.start()
        self.started["keep", u] = keep
        for slot, (name, to) in enumerate((("x", spot.x_to), ("y", spot.y_to), ("c", spot.core_to))):
            self.started[name, u] = self.send(u, 1 + slot, source, target, to)

    def forward(self, u):
        spot, src, mid = self.spot, self.sources[u], self.rows // 2
        self.started["x", u].wait_recv()
        piece = self.every.at[spot.x_d, src, 0:mid]
        self.started["xy", u] = self.send(u, 4, piece, piece, spot.y_to)
        piece = self.every.at[spot.x_d, src]
        self.started["xc", u] = self.send(u, 5, piece, piece, spot.core_to)
        self.started["y", u].wait_recv()
        piece = self.every.at[spot.y_d, src, mid : self.rows]
        self.started["yx", u] = self.send(u, 6, piece, piece, spot.x_to)
        piece = self.every.at[spot.y_d, src]
        self.started["yc", u] = self.send(u, 7, piece, piece, spot.core_to)

    def far(self, u):
        spot, src = self.spot, self.sources[u]
        self.started["xy", u].wait_recv()
        self.started["yx", u].wait_recv()
        piece = self.every.at[spot.far_d, src]
        self.started["fc", u] = self.send(u, 8, piece, piece, spot.core_to)

    def close(self):
        for u in range(4):
            for name in ("c", "xc", "yc", "fc"):
                self.started[name, u].wait_recv()
            self.started["keep", u].wait()
        for (name, _), copy in self.started.items():
            if name != "keep":
                copy.wait_send()


class SumFlow:
    def __init__(self, spot, mine, core_in, x_in, y_in, xy_in, yx_in, z_in, total, out_at, local_sem, send_sem, recv_sem):
        self.spot, self.mine, self.core_in, self.out_at = spot, mine, core_in, out_at
        self.x_in, self.y_in, self.xy_in, self.yx_in, self.z_in, self.total = x_in, y_in, xy_in, yx_in, z_in, total
        self.local_sem, self.send_sem, self.recv_sem = local_sem, send_sem, recv_sem
        self.started = [{} for _ in range(mine.shape[0])]
        self.half = mine.shape[4] // 2

    def send(self, j, slot, source, target, to):
        return remote(source, target, self.send_sem.at[j, slot], self.recv_sem.at[j, slot], to)

    def over_core(self, j, source):
        self.started[j]["core"] = self.send(j, 0, source, self.core_in.at[j], self.spot.core_to)

    def core(self, j):
        spot, mine, half, started = self.spot, self.mine, self.half, self.started[j]
        started["core"].wait_recv()

        @pl.loop(0, 4)
        def _(a):
            for b in range(2):
                for e in range(2):
                    mine[j, a, b, e] = mine[j, a, b, e] + self.core_in[j, a, b, e]

        started["x"] = self.send(j, 1, mine.at[j, :, :, 1 - spot.x, 0:half], self.x_in.at[j], spot.x_to)
        started["y"] = self.send(j, 2, mine.at[j, :, 1 - spot.y, :, half : 2 * half], self.y_in.at[j], spot.y_to)

    def first(self, j):
        spot, mine, half, started = self.spot, self.mine, self.half, self.started[j]
        x, y = spot.x, spot.y
        started["x"].wait_recv()
        for a in range(4):
            for b in range(2):
                mine[j, a, b, x, 0:half] = mine[j, a, b, x, 0:half] + self.x_in[j, a, b]
        started["xy"] = self.send(j, 3, mine.at[j, :, 1 - y, x, 0:half], self.xy_in.at[j], spot.y_to)
        started["y"].wait_recv()
        for a in range(4):
            for e in range(2):
                mine[j, a, y, e, half : 2 * half] = mine[j, a, y, e, half : 2 * half] + self.y_in[j, a, e]
        started["yx"] = self.send(j, 4, mine.at[j, :, y, 1 - x, half : 2 * half], self.yx_in.at[j], spot.x_to)

    def second(self, j):
        spot, mine, half, started = self.spot, self.mine, self.half, self.started[j]
        x, y = spot.x, spot.y
        started["xy"].wait_recv()
        started["yx"].wait_recv()
        for a in range(4):
            mine[j, a, y, x, 0:half] = mine[j, a, y, x, 0:half] + self.xy_in[j, a]
            mine[j, a, y, x, half : 2 * half] = mine[j, a, y, x, half : 2 * half] + self.yx_in[j, a]
        for m in range(3):
            z = spot.z_to[m]
            started["z", m] = self.send(j, 5 + m, mine.at[j, z, y, x], self.z_in.at[j, m], (spot.d, z))

    def along(self, j):
        spot, started, total = self.spot, self.started[j], self.total
        for m in range(3):
            started["z", m].wait_recv()
        own = self.mine[j, spot.c, spot.y, spot.x]
        total[j] = ((own + self.z_in[j, 0]) + self.z_in[j, 1]) + self.z_in[j, 2]
        target = self.out_at(j, spot.d, 0, 2 * self.half)
        started["keep"] = pltpu.make_async_copy(total.at[j], target, self.local_sem.at[j])
        started["keep"].start()
        for slot, (name, to) in enumerate((("gx", spot.x_to), ("gy", spot.y_to), ("gc", spot.core_to))):
            started[name] = self.send(j, 8 + slot, total.at[j], target, to)

    def share(self, j):
        spot, started, half = self.spot, self.started[j], self.half
        started["gx"].wait_recv()
        piece = self.out_at(j, spot.x_d, 0, half)
        started["gxy"] = self.send(j, 11, piece, piece, spot.y_to)
        piece = self.out_at(j, spot.x_d, 0, 2 * half)
        started["cgx"] = self.send(j, 12, piece, piece, spot.core_to)
        started["gy"].wait_recv()
        piece = self.out_at(j, spot.y_d, half, half)
        started["gyx"] = self.send(j, 13, piece, piece, spot.x_to)
        piece = self.out_at(j, spot.y_d, 0, 2 * half)
        started["cgy"] = self.send(j, 14, piece, piece, spot.core_to)

    def far(self, j):
        spot, started = self.spot, self.started[j]
        started["gxy"].wait_recv()
        started["gyx"].wait_recv()
        piece = self.out_at(j, spot.far_d, 0, 2 * self.half)
        started["cgf"] = self.send(j, 15, piece, piece, spot.core_to)

    def end(self, j, core_sent=False):
        started = self.started[j]
        for name in ("gc", "cgx", "cgy", "cgf"):
            started[name].wait_recv()
        for name, copy in started.items():
            if name == "keep":
                copy.wait()
            elif not (name == "core" and core_sent):
                copy.wait_send()


def sum_scratch(jobs, piece, lanes):
    half = piece // 2
    return [
        pltpu.VMEM((jobs, 4, 2, 2, piece, lanes), f32),
        pltpu.VMEM((jobs, 4, 2, 2, piece, lanes), f32),
        pltpu.VMEM((jobs, 4, 2, half, lanes), f32),
        pltpu.VMEM((jobs, 4, 2, half, lanes), f32),
        pltpu.VMEM((jobs, 4, half, lanes), f32),
        pltpu.VMEM((jobs, 4, half, lanes), f32),
        pltpu.VMEM((jobs, 3, piece, lanes), f32),
        pltpu.VMEM((jobs, piece, lanes), f32),
    ]


def flow_sems(jobs):
    dma = pltpu.SemaphoreType.DMA
    return [dma((jobs,)), dma((jobs, 16)), dma((jobs, 16)), dma((4,)), dma((4, 9)), dma((4, 9))]


GATE_OF = ((0, 1, 3), (0, 1, 2))


def split_two(value):
    top = value.astype(bf16)
    return top, (value - top.astype(f32)).astype(bf16)


def three_products(first, second, over):
    def product(a, b):
        return lax.dot_general(a, b, (over, ((), ())), preferred_element_type=f32)

    return product(first[0], second[0]) + product(first[1], second[0]) + product(first[0], second[1])


def tail_kernel(
    inputs,
    prevs,
    dgates,
    dstart,
    entering,
    out,
    item_all,
    start_all,
    mine,
    core_in,
    x_in,
    y_in,
    xy_in,
    yx_in,
    z_in,
    total,
    core_out,
    turned,
    gate_pair,
    flow,
    w_flow,
    din,
    z_rows,
    flow_sem,
    start_sem,
    sum_local,
    sum_send,
    sum_recv,
    row_local,
    row_send,
    row_recv,
):
    spot = Spot()
    spot.greet_all()
    c, k = spot.c, spot.k
    jobs, piece = mine.shape[0], mine.shape[4]
    events, units = gate_pair.shape[2:]
    block = din.shape[2]
    gates = jobs // 2
    sums = SumFlow(
        spot, mine, core_in, x_in, y_in, xy_in, yx_in, z_in, total,
        lambda j, d, at, size: out.at[j // gates, j % gates, d, pl.ds(at, size)], sum_local, sum_send, sum_recv,
    )
    rows = RowsFlow(spot, din, z_rows, item_all, row_local, row_send, row_recv)

    def gate_cols(g):
        return dgates.at[:, pl.ds(g * units, units)]

    queue = [inputs.at[pl.ds(0, events)], gate_cols(0), gate_cols(1), gate_cols(3), prevs, gate_cols(2)]

    def flow_copy(n):
        return pltpu.make_async_copy(queue[n], flow.at[n % 2], flow_sem.at[n % 2])

    def w_copy(n, slot):
        rows = pl.ds(pl.multiple_of(n * block, block), block)
        return pltpu.make_async_copy(entering.at[rows], w_flow.at[slot], flow_sem.at[2 + slot])

    flow_copy(0).start()
    flow_copy(1).start()
    w_copy(0, 0).start()

    def next_flow(n):
        if n + 2 < len(queue):
            flow_copy(n + 2).start()

    def take_act(n, w):
        flow_copy(n).wait()

        @pl.loop(0, 4)
        def _(b):
            cols = pl.ds(pl.multiple_of(b * block, block), block)
            turned[w, 0, b], turned[w, 1, b] = split_two(flow[n % 2, :, cols].T)

        next_flow(n)

    def take_gate(n, g, at):
        flow_copy(n).wait()

        @pl.loop(0, 4)
        def _(b):
            cols = pl.ds(pl.multiple_of(b * block, block), block)
            value = flow[n % 2, :, cols]
            gate_pair[g, 0, :, cols], gate_pair[g, 1, :, cols] = split_two(value)
            if at is not None:
                chunk = 4 * at + b
                slot = lax.rem(b, 2)

                @pl.when(chunk + 1 < 12)
                def _():
                    w_copy(chunk + 1, 1 - slot).start()

                w_copy(chunk, slot).wait()
                share = three_products(split_two(value), split_two(w_flow[slot]), ((1,), (0,)))
                for e in range(4):
                    part = share[:, e * block : (e + 1) * block]
                    if at == 0:
                        before = jnp.where(b == 0, 0.0, din[e, 0:events, :])
                    else:
                        before = din[e, 0:events, :]
                    din[e, 0:events, :] = before + part

        next_flow(n)

    def rows_begin():
        for e in range(4):
            din[e, events:, :] = dstart[:, e * block : (e + 1) * block]
        rows.begin()

    def rows_end():
        keeps = [
            pltpu.make_async_copy(din.at[c, events:], start_all.at[c], start_sem.at[0]),
        ] + [
            pltpu.make_async_copy(z_rows.at[z, events:], start_all.at[z], start_sem.at[1 + m])
            for m, z in enumerate(spot.z_to)
        ]
        for keep in keeps:
            keep.start()
        rows.close()
        for keep in keeps:
            keep.wait()

    def partial(j):
        w, g = j // gates, GATE_OF[j // gates][j % gates]
        slot = j % 2
        if j >= 2:
            sums.started[j - 2]["core"].wait_send()

        @pl.loop(0, 2)
        def _(p):
            for q in range(2):
                b = 2 * p + q
                value = three_products(
                    (turned[w, 0, b], turned[w, 1, b]), (gate_pair[g, 0], gate_pair[g, 1]), ((1,), (0,))
                )
                for e in range(4):
                    cols = slice(e * block, (e + 1) * block)
                    first, second = value[:piece, cols], value[piece:, cols]
                    mine[j, e, p, q] = jnp.where(k == 0, first, second)
                    core_out[slot, e, p, q] = jnp.where(k == 0, second, first)

        sums.over_core(j, core_out.at[slot])

    A, B, C, Z, S, F = sums.core, sums.first, sums.second, sums.along, sums.share, sums.far

    def E(j):
        sums.end(j, core_sent=j < jobs - 2)

    take_act(0, 0)
    take_gate(1, 0, 0)
    partial(0)
    take_gate(2, 1, 1)
    partial(1)
    A(0)
    take_gate(3, 3, 2)
    rows_begin()
    partial(2)
    A(1)
    take_act(4, 1)
    partial(3)
    A(2), B(0), rows.spread(1), rows.forward(0)
    partial(4)
    A(3), B(1), C(0), rows.spread(2), rows.forward(1), rows.far(0)
    take_gate(5, 2, None)
    partial(5)
    A(4), B(2), C(1), Z(0), rows.spread(3), rows.forward(2), rows.far(1)
    A(5), B(3), C(2), Z(1), S(0), rows.forward(3), rows.far(2)
    B(4), C(3), Z(2), S(1), F(0), rows.far(3)
    B(5), C(4), Z(3), S(2), F(1), E(0)
    C(5), Z(4), S(3), F(2), E(1)
    rows_end()
    Z(5), S(4), F(3), E(2)
    S(5), F(4), E(3)
    F(5), E(4), E(5)


def run_tail(inputs, prevs, dgates, dstart, entering, collective_id):
    events, units = prevs.shape
    gates, block = 3, units // 4
    piece = units // 8
    jobs = 2 * gates
    start_rows = dstart.shape[0]
    hbm = pl.BlockSpec(memory_space=pl.ANY)
    grads, item_all, start_all = pl.pallas_call(
        tail_kernel,
        out_shape=(
            jax.ShapeDtypeStruct((2, gates, 8, piece, block), f32),
            jax.ShapeDtypeStruct((8, 4, events, block), f32),
            jax.ShapeDtypeStruct((4, start_rows, block), f32),
        ),
        in_specs=[hbm, hbm, hbm, pl.BlockSpec(memory_space=pltpu.VMEM), hbm],
        out_specs=(hbm, hbm, hbm),
        scratch_shapes=sum_scratch(jobs, piece, block)
        + [
            pltpu.VMEM((2, 4, 2, 2, piece, block), f32),
            pltpu.VMEM((2, 2, 4, block, events), bf16),
            pltpu.VMEM((4, 2, events, units), bf16),
            pltpu.VMEM((2, events, units), f32),
            pltpu.VMEM((2, block, units), f32),
            pltpu.VMEM((4, events + start_rows, block), f32),
            pltpu.VMEM((4, events + start_rows, block), f32),
            pltpu.SemaphoreType.DMA((4,)),
            pltpu.SemaphoreType.DMA((4,)),
        ]
        + flow_sems(jobs),
        cost_estimate=takes(190),
        compiler_params=pltpu.CompilerParams(
            collective_id=collective_id, has_side_effects=True, vmem_limit_bytes=VMEM_BYTES
        ),
    )(inputs, prevs, dgates, dstart, entering)
    return grads.reshape(2, gates, units, block), item_all, start_all


HEAD_TIMES = ((8, 14, 28, 42), (10, 22, 32, 44, 56, 68), 12, 20, 58)
UNITS = ((0, 0), (0, 1), (1, 0), (0, 2), (1, 1), (1, 2))


def head_kernel(
    chunk,
    width,
    item_ids,
    out_ids,
    embed,
    table,
    bias,
    w_in,
    w_hid,
    in_bias,
    hid_bias,
    carried,
    own_ids,
    all_in,
    all_hid,
    arrived,
    all_ids,
    out_rows,
    padded,
    turned,
    item_rows,
    held,
    w_buf,
    local_sem,
    send_sem,
    recv_sem,
    row_send,
    row_recv,
    id_send,
    id_recv,
):
    y, x, k, c, d = place()
    i = pl.program_id(0)
    n = pl.num_programs(0) // 2
    core_to, x_to, y_to = (d + 1 - 2 * k, c), (d + 2 - 4 * x, c), (d + 4 - 8 * y, c)
    z_all = (c + 1 - 2 * lax.rem(c, 2), lax.rem(c + 2, 4), 3 - c)
    alls = (all_in, all_hid)
    gates, piece, units = held.shape[1], held.shape[5], held.shape[6]
    half = piece // 2
    block = item_rows.shape[2]
    items = item_rows.shape[1]
    carried_rows = carried.shape[1]
    events = items - carried_rows

    def send(u, slot):
        w, m = UNITS[u]
        z = z_all[m]
        every = alls[w]
        if slot == 0:
            source, target, to = held.at[w, :, y, x, k], every.at[:, c, y, x, k], (d, z)
        elif slot in (4, 6):
            spot = (
                every.at[:, z, y, 1 - x, k, 0:half] if slot == 4 else every.at[:, z, 1 - y, x, k, half : 2 * half]
            )
            source, target, to = spot, spot, (y_to if slot == 4 else x_to)
        else:
            py, px, to = {
                1: (y, x, x_to),
                2: (y, x, y_to),
                3: (y, x, core_to),
                5: (y, 1 - x, core_to),
                7: (1 - y, x, core_to),
                8: (1 - y, 1 - x, core_to),
            }[slot]
            spot = every.at[:, z, py, px, k]
            source, target = spot, spot
        return pltpu.make_async_remote_copy(
            src_ref=source,
            dst_ref=target,
            send_sem=send_sem.at[u, slot],
            recv_sem=recv_sem.at[u, slot],
            device_id=to,
            device_id_type=MESH,
        )

    def load(w):
        return pltpu.make_async_copy((w_in, w_hid)[w], w_buf.at[w], local_sem.at[w])

    def keep(w):
        return pltpu.make_async_copy(held.at[w], alls[w].at[:, c], local_sem.at[2 + w])

    def pad(w):
        load(w).wait()
        part, own = units // block, w_buf.shape[3]
        inner = w_buf.shape[2] // part
        for g in range(gates):
            for b in range(part):
                turned[b * block : b * block + inner, 0:own] = w_buf[w, g, b * inner : (b + 1) * inner, :]
            turned[inner : inner + 1, 0:own] = (in_bias, hid_bias)[w][g : g + 1, :]
            held[w, g] = turned[0:units, :].T.reshape(2, 2, 2, piece, units)
        keep(w).start()

    def item_send(m):
        return pltpu.make_async_remote_copy(
            src_ref=item_rows.at[z_all[m]],
            dst_ref=arrived.at[:, pl.ds(pl.multiple_of(c * block, block), block)],
            send_sem=row_send.at[m],
            recv_sem=row_recv.at[m],
            device_id=(d, z_all[m]),
            device_id_type=MESH,
        )

    def begin_items(_):
        for m in range(3):
            item_send(m).start()

    def item_keep():
        return pltpu.make_async_copy(
            item_rows.at[c], arrived.at[:, pl.ds(pl.multiple_of(c * block, block), block)], local_sem.at[4]
        )

    def id_copy(m):
        to = lax.rem(d + 1 + m, 8)
        return pltpu.make_async_remote_copy(
            src_ref=own_ids,
            dst_ref=all_ids.at[d],
            send_sem=id_send.at[m],
            recv_sem=id_recv.at[m],
            device_id=(to, c),
            device_id_type=MESH,
        )

    def id_keep():
        return pltpu.make_async_copy(own_ids, all_ids.at[d], local_sem.at[5])

    def begin():
        load(0).start()
        load(1).start()
        greet([(lax.rem(d + 1 + m, 8), c) for m in range(7)] + [(d, z) for z in z_all])
        id_keep().start()
        for m in range(7):
            id_copy(m).start()
        turned[0:units, :] = jnp.zeros((units, block), f32)
        pad(0)
        begin_z(0)
        begin_z(1)
        pad(1)

    def begin_z(u):
        send(u, 0).start()

    def spread(u):
        send(u, 0).wait_recv()
        for slot in (1, 2, 3):
            send(u, slot).start()

    def forward(u):
        send(u, 1).wait_recv()
        send(u, 4).start()
        send(u, 5).start()
        send(u, 2).wait_recv()
        send(u, 6).start()
        send(u, 7).start()

    def far(u):
        send(u, 4).wait_recv()
        send(u, 6).wait_recv()
        send(u, 8).start()

    def close(u):
        for slot in (3, 5, 7, 8):
            send(u, slot).wait_recv()
        for slot in range(9):
            send(u, slot).wait_send()

    z_at, spread_at, forward_by, far_by, items_at = HEAD_TIMES
    timeline = [(-1, begin, None), (items_at, begin_items, 0)]
    timeline += [(at, begin_z, 2 + j) for j, at in enumerate(z_at)]
    for u, at in enumerate(spread_at):
        timeline += [(at, spread, u), (at + forward_by, forward, u), (at + far_by, far, u)]
    timeline.sort(key=lambda entry: entry[0])
    last = 2 * n - 1

    @pl.when(i == 0)
    def _():
        padded[...] = jnp.zeros_like(padded)
        padded[width : width + 1, :] = jnp.full((1, chunk), jnp.where(c == 0, 1.0, 0.0), f32)

    for at, action, u in timeline:
        if at < last:

            @pl.when(i == max(at, 0))
            def _(action=action, u=u):
                action() if u is None else action(u)

    @pl.when(i < n)
    def _():
        padded[0:width, :] = embed[...]

    @pl.when(i >= n)
    def _():
        padded[0:width, :] = table[...]
        padded[width : width + 1, :] = bias[...]

    spot = lax.rem(i, n) * chunk
    turned[pl.ds(pl.multiple_of(spot, chunk), chunk), :] = padded[...].T

    @pl.when(i == n - 1)
    def _():
        for z in range(4):

            def body(b, carry, z=z):
                for j in range(8):
                    row = item_ids[z * events + b * 8 + j]
                    item_rows[z, pl.ds(b * 8 + j, 1), :] = turned[pl.ds(row, 1), :]
                return carry

            lax.fori_loop(0, events // 8, body, 0)
            item_rows[z, events:items, :] = carried[z]
        item_keep().start()

    @pl.when(i == last)
    def _():
        def body(b, carry):
            for j in range(8):
                row = out_ids[b * 8 + j]
                out_rows[pl.ds(b * 8 + j, 1), :] = turned[pl.ds(row, 1), :]
            return carry

        lax.fori_loop(0, out_rows.shape[0] // 8, body, 0)
        for at, action, u in timeline:
            if at >= last:
                action(u)
        for u in range(6):
            close(u)
        for m in range(3):
            item_send(m).wait()
        for m in range(7):
            id_copy(m).wait()
        id_keep().wait()
        for w in range(2):
            keep(w).wait()
        item_keep().wait()


def gather_all(embed, table, bias, item_ids, out_ids, w_in, w_hid, in_bias, hid_bias, carried, own_ids, collective_id):
    width, rows = embed.shape
    gates, block = w_in.shape[0], carried.shape[2]
    units = 4 * block
    piece = block // 8
    chunk = 128 * max(k for k in range(1, 9) if rows % (128 * k) == 0)
    n = rows // chunk
    items = item_ids.shape[0] // 4 + carried.shape[1]
    own_shape = (gates, 2, 2, 2, piece, units)
    all_shape = (gates, 4, 2, 2, 2, piece, units)
    smem = pl.BlockSpec(memory_space=pltpu.SMEM)
    hbm = pl.BlockSpec(memory_space=pl.ANY)
    all_in, all_hid, arrived, all_ids, out_rows = pl.pallas_call(
        functools.partial(head_kernel, chunk, width),
        out_shape=(
            jax.ShapeDtypeStruct(all_shape, f32),
            jax.ShapeDtypeStruct(all_shape, f32),
            jax.ShapeDtypeStruct((items, units), f32),
            jax.ShapeDtypeStruct((8,) + own_ids.shape, jnp.int32),
            jax.ShapeDtypeStruct((out_ids.shape[0], block), f32),
        ),
        grid=(2 * n,),
        in_specs=[
            smem,
            smem,
            pl.BlockSpec((width, chunk), lambda i: (0, jnp.minimum(i, n - 1))),
            pl.BlockSpec((width, chunk), lambda i: (0, jnp.maximum(i - n, 0))),
            pl.BlockSpec((1, chunk), lambda i: (0, jnp.maximum(i - n, 0))),
            hbm,
            hbm,
            pl.BlockSpec(in_bias.shape, lambda i: (0, 0)),
            pl.BlockSpec(hid_bias.shape, lambda i: (0, 0)),
            pl.BlockSpec(carried.shape, lambda i: (0, 0, 0)),
            pl.BlockSpec(own_ids.shape, lambda i: (0, 0)),
        ],
        out_specs=(hbm, hbm, hbm, hbm, pl.BlockSpec((out_ids.shape[0], block), lambda i: (0, 0))),
        scratch_shapes=[
            pltpu.VMEM((block, chunk), f32),
            pltpu.VMEM((rows, block), f32),
            pltpu.VMEM((4, items, block), f32),
            pltpu.VMEM((2,) + own_shape, f32),
            pltpu.VMEM((2,) + w_in.shape, f32),
            pltpu.SemaphoreType.DMA((6,)),
            pltpu.SemaphoreType.DMA((6, 9)),
            pltpu.SemaphoreType.DMA((6, 9)),
            pltpu.SemaphoreType.DMA((3,)),
            pltpu.SemaphoreType.DMA((3,)),
            pltpu.SemaphoreType.DMA((7,)),
            pltpu.SemaphoreType.DMA((7,)),
        ],
        cost_estimate=takes(120),
        compiler_params=pltpu.CompilerParams(
            collective_id=collective_id, has_side_effects=True, vmem_limit_bytes=VMEM_BYTES
        ),
    )(item_ids, out_ids, embed, table, bias, w_in, w_hid, in_bias, hid_bias, carried, own_ids)
    return (
        all_in.reshape(gates, 4 * block, units),
        all_hid.reshape(gates, 4 * block, units),
        arrived,
        all_ids,
        out_rows,
    )


def back_kernel(
    steps,
    width,
    factor,
    hidden,
    outs,
    targets,
    negs,
    keep,
    prevs,
    resets,
    updates,
    cands,
    inners,
    dgates,
    dstart,
    neg_all,
    target_all,
    loss_all,
    halves,
    core_in,
    x_in,
    y_in,
    xy_in,
    yx_in,
    z_in,
    total,
    w_high,
    w_low,
    w_flow,
    z_rows,
    share,
    pairs,
    score,
    neg_flow,
    target_part,
    douts,
    own_loss,
    flow_sem,
    neg_sem,
    loss_sem,
    loss_send,
    loss_recv,
    sum_local,
    sum_send,
    sum_recv,
    row_local,
    row_send,
    row_recv,
):
    spot = Spot()
    spot.greet_all()
    rows_per, units = dstart.shape
    mine, core_out = halves.at[0], halves.at[1]
    jobs, piece = halves.shape[1], halves.shape[5]
    step_rows = w_flow.shape[1]
    chunks = hidden.shape[0] // step_rows
    n_col, events, block = targets.shape
    n_dp, _, count, _ = negs.shape
    sums = SumFlow(
        spot, mine, core_in, x_in, y_in, xy_in, yx_in, z_in, total,
        lambda j, d, at, size: neg_all.at[d, pl.ds(j * piece + at, size)], sum_local, sum_send, sum_recv,
    )
    rows = RowsFlow(spot, target_part, z_rows, target_all, row_local, row_send, row_recv)

    def load(i, slot):
        part = pl.ds(pl.multiple_of(i * step_rows, step_rows), step_rows)
        return pltpu.make_async_copy(hidden.at[part], w_flow.at[slot], flow_sem.at[slot])

    def split_chunk(i):
        slot = lax.rem(i, 2)

        @pl.when(i + 1 < chunks)
        def _():
            load(i + 1, 1 - slot).start()

        load(i, slot).wait()
        part = pl.ds(pl.multiple_of(i * step_rows, step_rows), step_rows)
        w_high[part, :], w_low[part, :] = split_two(w_flow[slot])

    def load_neg(b, slot):
        return pltpu.make_async_copy(negs.at[b], neg_flow.at[slot], neg_sem.at[slot])

    load_neg(0, 0).start()
    load(0, 0).start()
    lane = lax.broadcasted_iota(jnp.int32, (events, block), 1)
    for c in range(n_col):
        value = jnp.where(lane < width, outs[:, c * block : (c + 1) * block], 0.0)
        value = jnp.where(lane == width, 1.0 / n_col, value)
        share[c] = value
        pairs[0, c], pairs[1, c] = split_two(value)

    @pl.loop(0, n_dp)
    def _(b):
        slot = lax.rem(b, 2)
        load_neg(lax.rem(b + 1, n_dp), 1 - slot).start()
        load_neg(b, slot).wait()
        value = jnp.zeros((events, count), f32)
        for c in range(n_col):
            value = value + three_products((pairs[0, c], pairs[1, c]), split_two(neg_flow[slot, c]), ((1,), (1,)))
        score[:, pl.ds(pl.multiple_of(b * count, count), count)] = value
        split_chunk(b)

    part_steps = 4
    step_lane = lax.broadcasted_iota(jnp.int32, (rows_per, LANES), 1)

    def events_part(i, losses):
        size = part_steps * rows_per
        now = pl.ds(pl.multiple_of(i * size, size), size)
        pos = jnp.zeros((size, 1), f32)
        for c in range(n_col):
            pos = pos + jnp.sum(share[c, now, :] * targets[c, now, :], axis=-1, keepdims=True)
        neg = score[now, :]
        expd = jnp.exp(neg - jnp.max(neg, axis=-1, keepdims=True))
        weight = expd * (1.0 / jnp.sum(expd, axis=-1, keepdims=True))
        sig = jax.nn.sigmoid(pos - neg)
        slope = weight * sig
        ppos = jnp.sum(slope, axis=-1, keepdims=True)
        quad = jnp.sum(weight * neg * neg, axis=-1, keepdims=True)
        slope = jnp.sum(slope * (1.0 - sig), axis=-1, keepdims=True)
        value = quad - jnp.log(ppos)
        for q in range(part_steps):
            losses = jnp.where(step_lane == part_steps * i + q, value[q * rows_per : (q + 1) * rows_per], losses)
        score[now, :] = factor * weight * (1.0 - sig * sig * (1.0 / ppos) + neg * neg + 2.0 * neg - quad)
        dpos = -factor * slope / ppos
        for c in range(n_col):
            target_part[c, now, :] = dpos * share[c, now, :]
            douts[now, c * block : (c + 1) * block] = dpos * targets[c, now, :]
        return losses

    own_loss[...] = lax.fori_loop(0, steps // part_steps, events_part, jnp.zeros((rows_per, LANES), f32))
    rows.begin()
    losses = [pltpu.make_async_copy(own_loss, loss_all.at[spot.c], loss_sem.at[0])]
    losses[0].start()
    for m, z in enumerate(spot.z_to):
        losses.append(remote(own_loss, loss_all.at[spot.c], loss_send.at[m], loss_recv.at[m], (spot.d, z)))

    def neg_block(p, q, core, j):
        b = 4 * p + 2 * q + core
        dneg = score[:, pl.ds(pl.multiple_of(b * count, count), count)]
        down = split_two(dneg[:, j * piece : (j + 1) * piece].T)
        which = lax.rem(core + spot.k, 2)
        for c in range(n_col):
            halves[which, j, c, p, q] = three_products(down, (pairs[0, c], pairs[1, c]), ((1,), (0,)))
        return b, dneg

    @pl.loop(0, 2)
    def _(p):
        for q in range(2):
            for core in range(2):
                neg_block(p, q, core, 0)
            split_chunk(n_dp + 2 * p + q)

    sums.over_core(0, core_out.at[0])

    @pl.loop(0, 2)
    def _(p):
        for q in range(2):
            for core in range(2):
                b, dneg = neg_block(p, q, core, 1)
                if q == 1 and core == 1:

                    @pl.when(p == 0)
                    def _():
                        load_neg(b + 1, 0).start()

                else:
                    load_neg(b + 1, 1 - core).start()
                load_neg(b, core).wait()
                across = split_two(dneg)
                for c in range(n_col):
                    cols = slice(c * block, (c + 1) * block)
                    douts[:, cols] = douts[:, cols] + three_products(across, split_two(neg_flow[core, c]), ((1,), (0,)))

    sums.over_core(1, core_out.at[1])
    for c in range(n_col):
        cols = slice(c * block, (c + 1) * block)
        douts[:, cols] = jnp.where(lane < width, douts[:, cols], 0.0)

    def step(i, dstate):
        t = steps - 1 - i
        now = pl.ds(pl.multiple_of(t * rows_per, rows_per), rows_per)
        reset, update, cand = resets[now, :], updates[now, :], cands[now, :]
        dh = douts[now, :] + dstate
        dcand = dh * (1.0 - update) * (1.0 - cand * cand)
        dreset = dcand * inners[now, :] * reset * (1.0 - reset)
        dupdate = dh * (prevs[now, :] - cand) * update * (1.0 - update)
        dinner = dcand * reset
        dgates[now, 0:units] = dreset
        dgates[now, units : 2 * units] = dupdate
        dgates[now, 2 * units : 3 * units] = dinner
        dgates[now, 3 * units : 4 * units] = dcand
        total_now = dh * update
        for g, part in enumerate((dreset, dupdate, dinner)):
            pair = two_part(part)
            sect = slice(g * units, (g + 1) * units)
            first = jnp.dot(pair, w_high[sect, :], preferred_element_type=f32)
            second = jnp.dot(pair, w_low[sect, :], preferred_element_type=f32)
            total_now = total_now + (first[:rows_per] + first[rows_per:] + second[:rows_per])
        return keep[now, :] * total_now

    A, B, C, Z, S, F = sums.core, sums.first, sums.second, sums.along, sums.share, sums.far
    timeline = (
        (0.0, ((A, 0),)),
        (0.1, ((A, 1), (rows.forward, 0),)),
        (0.3, ((B, 0), (rows.spread, 1), (rows.far, 0),)),
        (0.44, ((B, 1), (rows.forward, 1), (rows.spread, 2),)),
        (0.56, ((C, 0), (rows.far, 1),)),
        (0.66, ((C, 1), (rows.forward, 2), (rows.spread, 3),)),
        (0.78, ((Z, 0), (rows.far, 2),)),
        (0.9, ((Z, 1), (S, 0), (rows.forward, 3),)),
        (1.0, ((S, 1), (F, 0),)),
    )
    state, done = jnp.zeros((rows_per, units), f32), 0
    for share_done, actions in timeline:
        until = int(share_done * steps)
        if until > done:
            state, done = lax.fori_loop(done, until, step, state), until
        for action, argument in actions:
            action(argument)
    dstart[...] = lax.fori_loop(done, steps, step, state)
    F(1), rows.far(3)
    sums.end(0)
    rows.close()
    sums.end(1)
    for copy in losses:
        copy.wait()


def run_back(hidden, outs, targets, negs, keep, saved, rows_per, steps, width, factor, collective_id):
    events, units = outs.shape
    n_dp, n_col, count, block = negs.shape
    jobs = 2
    piece = count // jobs
    hbm = pl.BlockSpec(memory_space=pl.ANY)
    step_rows = units // 4
    dma = pltpu.SemaphoreType.DMA
    return pl.pallas_call(
        functools.partial(back_kernel, steps, width, factor),
        out_shape=(
            jax.ShapeDtypeStruct((events, 4 * units), f32),
            jax.ShapeDtypeStruct((rows_per, units), f32),
            jax.ShapeDtypeStruct((8, count, block), f32),
            jax.ShapeDtypeStruct((8, 4, events, block), f32),
            jax.ShapeDtypeStruct((4, rows_per, LANES), f32),
        ),
        in_specs=[hbm, in_vmem(), in_vmem(), hbm] + [in_vmem()] * 6,
        out_specs=(in_vmem(), in_vmem(), hbm, hbm, hbm),
        scratch_shapes=[pltpu.VMEM((2, jobs, 4, 2, 2, piece, block), f32)]
        + sum_scratch(jobs, piece, block)[1:]
        + [
            pltpu.VMEM(hidden.shape, bf16),
            pltpu.VMEM(hidden.shape, bf16),
            pltpu.VMEM((2, step_rows, units), f32),
            pltpu.VMEM((4, events, block), f32),
            pltpu.VMEM((n_col, events, block), f32),
            pltpu.VMEM((2, n_col, events, block), bf16),
            pltpu.VMEM((events, n_dp * count), f32),
            pltpu.VMEM((2, n_col, count, block), f32),
            pltpu.VMEM((n_col, events, block), f32),
            pltpu.VMEM((events, units), f32),
            pltpu.VMEM((rows_per, LANES), f32),
            dma((2,)),
            dma((2,)),
            dma((1,)),
            dma((3,)),
            dma((3,)),
        ]
        + flow_sems(jobs),
        cost_estimate=takes(110),
        compiler_params=pltpu.CompilerParams(
            collective_id=collective_id, has_side_effects=True, vmem_limit_bytes=VMEM_BYTES
        ),
    )(hidden, outs, targets, negs, keep, *saved)


def pad_kernel(weight, bias, out):
    own, full = weight.shape[1:]
    block = out.shape[1]
    n_col = out.shape[2] // block
    part = full // n_col
    out[...] = jnp.zeros_like(out)
    for c in range(n_col):
        out[0, 0:own, c * block : c * block + part] = weight[0, :, c * part : (c + 1) * part]
    out[0, 0:own, part : part + 1] = bias[0]


def pad_units(weight, bias, n_col, block):
    gates, own, full = weight.shape
    return pl.pallas_call(
        pad_kernel,
        out_shape=jax.ShapeDtypeStruct((gates, block, n_col * block), f32),
        grid=(gates,),
        in_specs=[
            pl.BlockSpec((1, own, full), lambda g: (g, 0, 0)),
            pl.BlockSpec((1, own, 1), lambda g: (g, 0, 0)),
        ],
        out_specs=pl.BlockSpec((1, block, n_col * block), lambda g: (g, 0, 0)),
        compiler_params=params(),
    )(weight, bias[:, :, None])


def gather_weight(own, n_dp):
    gates, block, units = own.shape
    flat = own.reshape(n_dp, gates * block // n_dp, units)
    piece = lax.dynamic_index_in_dim(flat, lax.axis_index("dp"), 0, keepdims=False)
    every = lax.all_gather(piece, ("col", "dp"))
    every = every.reshape(-1, gates, block, units)
    return jnp.moveaxis(every, 0, 1).reshape(gates, -1, units)


def reduce_weight(partial, n_dp, n_col):
    gates, rows, units = partial.shape
    block = rows // n_col
    parts = jnp.moveaxis(partial.reshape(gates, n_col, block, units), 1, 0)
    parts = jnp.moveaxis(parts.reshape(n_col, n_dp, gates * block // n_dp, units), 1, 0)
    mine = lax.psum_scatter(parts, "dp", scatter_dimension=0)
    mine = lax.psum_scatter(mine, "col", scatter_dimension=0)
    return lax.all_gather(mine, "dp").reshape(gates, block, units)


def swap_col(rows, n_col):
    return lax.all_to_all(rows, "col", split_axis=0, concat_axis=0, tiled=True)


def unpad_last(value, n_col, part):
    block = value.shape[-1] // n_col
    return value.reshape(value.shape[:-1] + (n_col, block))[..., :part].reshape(value.shape[:-1] + (n_col * part,))


def local(
    n_dp,
    n_col,
    item_ids,
    target_ids,
    negative_ids,
    reset_mask,
    carry_flags,
    carried_state,
    embed_table,
    input_weight,
    hidden_weight,
    gate_bias,
    hidden_bias,
    out_table,
    out_bias,
):
    sessions, steps = item_ids.shape
    own_sessions = sessions // n_col
    rows_per = round_up(own_sessions, ROWS8)
    width = embed_table.shape[0]
    table_rows = embed_table.shape[1]
    own_rows = table_rows // n_dp
    block = round_up(width + 1, LANES)
    units = n_col * block
    events = steps * rows_per
    direct = n_dp == 8 and n_col == 4 and block % 64 == 0 and own_sessions == rows_per and steps % 4 == 0 and steps <= LANES
    factor = 1.0 / steps
    dp_at, col_at = lax.axis_index("dp"), lax.axis_index("col")

    def by_owner(value):
        value = jnp.moveaxis(value.reshape(n_col, own_sessions, steps), 1, 2)
        value = jnp.pad(value, ((0, 0), (0, 0), (0, rows_per - own_sessions)))
        return value.reshape(-1)

    item_flat, target_flat = by_owner(item_ids), by_owner(target_ids)
    own_keep = lax.dynamic_index_in_dim(
        by_owner(1 - reset_mask).reshape(n_col, events, 1), col_at, 0, keepdims=False
    ).astype(f32)
    valid = jnp.tile(jnp.arange(rows_per) < own_sessions, steps)
    lane = jnp.arange(units) % block

    carried = (carry_flags.astype(f32)[:, None] * carried_state).reshape(n_col, own_sessions, width)
    carried = jnp.pad(carried, ((0, 0), (0, rows_per - own_sessions), (0, block - width)))
    neg_count = negative_ids.shape[0]
    own_negs = lax.dynamic_slice_in_dim(negative_ids, dp_at * (neg_count // n_dp), neg_count // n_dp)
    out_ids = jnp.concatenate([target_flat, own_negs])
    no_bias = jnp.zeros_like(hidden_bias)
    hid_bias = jnp.stack([no_bias, no_bias, hidden_bias])
    if direct:
        own_ids = jnp.concatenate([item_flat, target_flat]).reshape(-1, LANES)
        all_in, all_hid, arrived, all_ids, out_rows = gather_all(
            embed_table,
            out_table,
            out_bias[None, :],
            item_flat,
            out_ids,
            jnp.swapaxes(input_weight, 1, 2),
            jnp.swapaxes(hidden_weight, 1, 2),
            gate_bias,
            hid_bias,
            carried,
            own_ids,
            1,
        )
        all_ids = all_ids.reshape(n_dp, 2, -1)
    else:
        all_hid = gather_weight(pad_units(hidden_weight, hid_bias, n_col, block), n_dp)
        all_in = gather_weight(pad_units(input_weight, gate_bias, n_col, block), n_dp)
        no_row = jnp.zeros((1, table_rows), f32)
        item_rows = gather_rows(embed_table, no_row, item_flat, block).reshape(n_col, events, block)
        arrived = swap_col(jnp.concatenate([item_rows, carried], axis=1), n_col)
        arrived = jnp.moveaxis(arrived, 0, 1).reshape(events + rows_per, units)
        arrived = arrived.at[:events, width].set(1.0)
        out_rows = gather_rows(out_table, out_bias[None, :], out_ids, block)
        all_ids = lax.all_gather(jnp.stack([item_flat, target_flat]), "dp")
    all_hid, all_in = all_hid.reshape(-1, units), all_in.reshape(-1, units)

    all_items, all_targets = all_ids[:, 0].reshape(-1), all_ids[:, 1].reshape(-1)
    count = all_items.shape[0]
    keys = jnp.concatenate([all_items, all_targets + table_rows, negative_ids + 2 * table_rows])
    order = jnp.concatenate([jnp.tile(lax.iota(jnp.int32, count), 2), lax.iota(jnp.int32, neg_count)])
    shift = (max(count, neg_count) - 1).bit_length()
    direct = direct and (3 * table_rows) << shift < 2**31
    low = (dp_at * own_rows).astype(jnp.int32)
    if direct:
        packed = lax.sort((keys << shift) | order)
    else:
        keys, order = lax.sort((keys, order), num_keys=1)
        by_item = (order[:count], keys[:count])
        by_target = (order[count : 2 * count], keys[count : 2 * count] - table_rows)
        by_neg = (order[2 * count :], keys[2 * count :] - 2 * table_rows)

    if direct:
        *saved, outs, negs, targets = run_forward_travel(
            all_hid, all_in, arrived, own_keep, out_rows, steps, width, 4
        )
    else:
        targets = swap_col(out_rows[: n_col * events].reshape(n_col, events, block), n_col)
        negs = lax.all_gather(out_rows[n_col * events :], ("dp", "col")).reshape(n_dp, n_col, -1, block)
        *saved, outs = run_forward(all_hid, all_in, arrived, own_keep, steps, width)
    prevs = saved[0]

    if direct:
        dgates, dstart, neg_all, target_all, loss_all = run_back(
            all_hid, outs, targets, negs, own_keep, saved, rows_per, steps, width, factor, 3
        )
        loss = loss_all[:, :, :steps].reshape(sessions, steps)
        neg_all, target_all = neg_all.reshape(-1, block), target_all.reshape(-1, block)
    else:
        targets = jnp.moveaxis(targets, 0, 1).reshape(events, units)
        negs = jnp.moveaxis(negs, 1, 2).reshape(neg_count, units)
        shares = jnp.where(lane == width, 1.0 / n_col, jnp.where(lane < width, outs, 0.0))
        pos_score = jnp.sum(shares * targets, axis=-1, keepdims=True)
        neg_score = lax.dot_general(shares, negs, (((1,), (1,)), ((), ())), precision=high)
        top = jnp.max(neg_score, axis=-1, keepdims=True)
        expd = jnp.exp(neg_score - top)
        weight = expd / jnp.sum(expd, axis=-1, keepdims=True)
        sig = jax.nn.sigmoid(pos_score - neg_score)
        ppos = jnp.sum(weight * sig, axis=-1, keepdims=True)
        quad = jnp.sum(weight * neg_score * neg_score, axis=-1, keepdims=True)
        slope = jnp.sum(weight * sig * (1.0 - sig), axis=-1, keepdims=True)
        own_loss = -jnp.log(ppos) + quad
        dneg = factor * weight * (1.0 - sig * sig / ppos + neg_score * neg_score + 2.0 * neg_score - quad)
        dneg = jnp.where(valid[:, None], dneg, 0.0)
        dpos = jnp.where(valid[:, None], -factor * slope / ppos, 0.0)
        douts = jnp.dot(dneg, negs, precision=high) + dpos * targets
        douts = jnp.where(lane < width, douts, 0.0)
        neg_part = lax.dot_general(dneg, shares, (((0,), (0,)), ((), ())), precision=high)
        target_part = dpos * shares

        neg_own = lax.psum_scatter(neg_part.reshape(n_dp, -1, units), "dp", scatter_dimension=0)
        neg_own = jnp.moveaxis(neg_own.reshape(-1, n_col, block), 1, 0)
        neg_own = lax.psum_scatter(neg_own, "col", scatter_dimension=0)
        neg_all = lax.all_gather(neg_own, "dp", tiled=True)
        target_own = swap_col(jnp.moveaxis(target_part.reshape(events, n_col, block), 1, 0), n_col)
        target_all = lax.all_gather(target_own.reshape(-1, block), "dp", tiled=True)
        dgates, dstart = run_backward(all_hid, douts, own_keep, saved, rows_per, steps)
        own_loss = own_loss.reshape(steps, rows_per)[:, :own_sessions]
        loss = lax.all_gather(own_loss.T, "col", tiled=True)
    gates = input_weight.shape[0]
    if direct:
        grads, item_all, start_all = run_tail(arrived, prevs, dgates, dstart, all_in, 2)
        grad_embed, grad_out, grad_obias, grad_in, grad_hid = run_finish(
            packed, shift, low, table_rows, own_rows, width, item_all.reshape(-1, block), target_all, neg_all, grads
        )
        grad_obias = grad_obias[0]
        grad_in, grad_hid = jnp.swapaxes(grad_in, 1, 2), jnp.swapaxes(grad_hid, 1, 2)
        grad_gate, grad_hbias = grads[0, :, width, :width], grads[1, gates - 1, width, :width]
    else:
        dx = jnp.concatenate([dgates[:, : 2 * units], dgates[:, 3 * units :]], axis=1)
        dh = dgates[:, : 3 * units]
        hid_part = lax.dot_general(dh, prevs, (((0,), (0,)), ((), ())), precision=high)
        in_part = lax.dot_general(dx, arrived[:events], (((0,), (0,)), ((), ())), precision=high)
        dinputs = jnp.dot(dx, all_in, precision=high)
        back = jnp.concatenate([dinputs, dstart], axis=0).reshape(events + rows_per, n_col, block)
        back = swap_col(jnp.moveaxis(back, 1, 0), n_col)
        item_all = lax.all_gather(back[:, :events].reshape(-1, block), "dp", tiled=True)
        start_all = back[:, events:]
        grad_in = reduce_weight(in_part.reshape(gates, units, units), n_dp, n_col)
        grad_hid = reduce_weight(hid_part.reshape(gates, units, units), n_dp, n_col)
        grad_gate, grad_hbias = grad_in[:, :width, width], grad_hid[gates - 1, :width, width]
        grad_in, grad_hid = (unpad_last(g[:, :width], n_col, width) for g in (grad_in, grad_hid))
        grad_out, grad_obias = scatter_rows(
            [by_target + (target_all,), by_neg + (neg_all,)],
            low,
            own_rows,
            width,
            block,
        )
        grad_obias = grad_obias[0] * n_col
        grad_embed, _ = scatter_rows([by_item + (item_all,)], low, own_rows, width, block)
    grad_carried = start_all[:, :own_sessions, :width].reshape(sessions, width)
    grad_carried = carry_flags.astype(f32)[:, None] * grad_carried
    return (
        loss,
        grad_embed,
        grad_in,
        grad_hid,
        grad_gate,
        grad_hbias,
        grad_out,
        grad_obias,
        grad_carried,
    )


def solution(mesh):
    in_specs = (
        P("dp", None),
        P("dp", None),
        P(),
        P("dp", None),
        P("dp"),
        P("dp", "col"),
        P("col", None),
        P(None, "col", None),
        P(None, "col", None),
        P(None, "col"),
        P("col"),
        P("col", None),
        P(),
    )
    out_specs = (
        P("dp", None),
        P("col", "dp"),
        P(None, "col", None),
        P(None, "col", None),
        P(None, "col"),
        P("col"),
        P("col", "dp"),
        P("dp"),
        P("dp", "col"),
    )
    body = functools.partial(local, mesh.shape["dp"], mesh.shape["col"])
    return jax.shard_map(body, mesh=mesh, in_specs=in_specs, out_specs=out_specs, check_vma=False)
```

```python
import functools

import jax
import jax.numpy as jnp
from jax import lax
from jax.experimental import pallas as pl
from jax.experimental.pallas import tpu as pltpu
from jax.sharding import PartitionSpec as P

LANES = 128
ROWS8 = 8
VMEM_BYTES = 60 << 20
f32 = jnp.float32
bf16 = jnp.bfloat16
high = lax.Precision.HIGH
MESH = pl.DeviceIdType.MESH


def round_up(value, unit):
    return -(-value // unit) * unit


def params():
    return pltpu.CompilerParams(vmem_limit_bytes=VMEM_BYTES)


def takes(micros):
    return pl.CostEstimate(flops=int(micros * 1.1e9), bytes_accessed=1 << 20, transcendentals=0)


def in_vmem():
    return pl.BlockSpec(memory_space=pltpu.VMEM)


def in_smem():
    return pl.BlockSpec(memory_space=pltpu.SMEM)


def gather_kernel(chunk, count, width, ids, table, bias, out, padded, turned):
    step = pl.program_id(0)

    @pl.when(step == 0)
    def _():
        padded[...] = jnp.zeros_like(padded)

    padded[0:width, :] = table[...]
    padded[width : width + 1, :] = bias[...]
    turned[pl.ds(pl.multiple_of(step * chunk, chunk), chunk), :] = padded[...].T

    @pl.when(step == pl.num_programs(0) - 1)
    def _():
        def body(block, carry):
            for j in range(ROWS8):
                row = ids[block * ROWS8 + j]
                out[pl.ds(block * ROWS8 + j, 1), :] = turned[pl.ds(row, 1), :]
            return carry

        lax.fori_loop(0, count // ROWS8, body, 0)


def gather_rows(table, bias, ids, block):
    width, rows = table.shape
    count = ids.shape[0]
    chunk = LANES * max(k for k in range(1, 9) if rows % (LANES * k) == 0)
    return pl.pallas_call(
        functools.partial(gather_kernel, chunk, count, width),
        out_shape=jax.ShapeDtypeStruct((count, block), f32),
        grid_spec=pltpu.PrefetchScalarGridSpec(
            num_scalar_prefetch=1,
            grid=(rows // chunk,),
            in_specs=[
                pl.BlockSpec((width, chunk), lambda i, ids: (0, i)),
                pl.BlockSpec((1, chunk), lambda i, ids: (0, i)),
            ],
            out_specs=pl.BlockSpec((count, block), lambda i, ids: (0, 0)),
            scratch_shapes=[pltpu.VMEM((block, chunk), f32), pltpu.VMEM((rows, block), f32)],
        ),
        compiler_params=params(),
    )(ids, table, bias)


def scatter_kernel(width, n_lists, *refs):
    bounds = refs[0]
    lists = refs[1 : 1 + 3 * n_lists]
    out, bias_out, acc = refs[1 + 3 * n_lists :]
    acc[...] = jnp.zeros_like(acc)
    low = bounds[0]
    for k in range(n_lists):
        rows_of, ids, data = lists[3 * k : 3 * k + 3]

        def body(i, carry):
            spot = pl.ds(ids[i] - low, 1)
            acc[spot, :] = acc[spot, :] + data[pl.ds(rows_of[i], 1), :]
            return carry

        lax.fori_loop(bounds[1 + 2 * k], bounds[2 + 2 * k], body, 0)
    for j in range(acc.shape[0] // LANES):
        cols = slice(j * LANES, (j + 1) * LANES)
        turned = acc[cols, :].T
        out[:, cols] = turned[:width]
        bias_out[:, cols] = turned[width : width + 1]


def scatter_rows(lists, low, own_rows, width, block):
    ends = [low]
    operands, specs = [], []
    for order, ids, data in lists:
        ends += [jnp.sum(ids < low, dtype=jnp.int32), jnp.sum(ids < low + own_rows, dtype=jnp.int32)]
        operands += [order, ids, data]
        specs += [in_smem(), in_smem(), in_vmem()]
    return pl.pallas_call(
        functools.partial(scatter_kernel, width, len(lists)),
        out_shape=(
            jax.ShapeDtypeStruct((width, own_rows), f32),
            jax.ShapeDtypeStruct((1, own_rows), f32),
        ),
        in_specs=[in_smem()] + specs,
        out_specs=(in_vmem(), in_vmem()),
        scratch_shapes=[pltpu.VMEM((own_rows, block), f32)],
        cost_estimate=takes(20),
        compiler_params=params(),
    )(jnp.stack(ends), *operands)


def finish_kernel(
    shift,
    table_rows,
    width,
    low,
    packed,
    items,
    targets,
    negs,
    grads,
    grad_embed,
    grad_out,
    grad_bias,
    grad_in,
    grad_hid,
    even,
    odd,
    item_buf,
    target_buf,
    neg_buf,
    grad_buf,
    embed_out,
    out_out,
    bias_out,
    weight_out,
    sem,
):
    own_rows = even.shape[0]
    events, neg_count = item_buf.shape[0], neg_buf.shape[0]
    block = even.shape[1]
    n_col = grad_buf.shape[2] // block
    loads = [
        pltpu.make_async_copy(source, target, sem.at[n])
        for n, (source, target) in enumerate(
            ((targets, target_buf), (negs, neg_buf), (grads, grad_buf), (items, item_buf))
        )
    ]
    for load in loads:
        load.start()
    stores = [
        pltpu.make_async_copy(source, target, sem.at[4 + n])
        for n, (source, target) in enumerate(
            (
                (out_out, grad_out),
                (bias_out, grad_bias),
                (weight_out.at[0], grad_in),
                (weight_out.at[1], grad_hid),
                (embed_out, grad_embed),
            )
        )
    ]

    def first_from(begin, count, bound):
        def halve(_, ends):
            left, right = ends
            middle = jnp.minimum((left + right) // 2, begin + count - 1)
            less = (left < right) & (packed[middle] < bound)
            return jnp.where(less, middle + 1, left), jnp.where(less | (left >= right), right, middle)

        return lax.fori_loop(0, count.bit_length() + 1, halve, (begin, begin + count))[0]

    def add(begin, count, which, data):
        base = low[0] + which * table_rows
        left = first_from(begin, count, base << shift)
        right = first_from(begin, count, (base + own_rows) << shift)

        def one(i, acc):
            key = packed[i]
            spot, row = (key >> shift) - base, key & ((1 << shift) - 1)
            acc[pl.ds(spot, 1), :] = acc[pl.ds(spot, 1), :] + data[pl.ds(row, 1), :]

        def four(i, carry):
            for n in range(4):
                one(left + 4 * i + n, (even, odd)[n % 2])
            return carry

        fours = (right - left) // 4
        lax.fori_loop(0, fours, four, 0)

        def rest(i, carry):
            one(i, even)
            return carry

        lax.fori_loop(left + 4 * fours, right, rest, 0)

    def clear():
        @pl.loop(0, own_rows // LANES)
        def _(j):
            rows = pl.ds(pl.multiple_of(j * LANES, LANES), LANES)
            even[rows, :] = jnp.zeros((LANES, block), f32)
            odd[rows, :] = jnp.zeros((LANES, block), f32)

    def turn(out, bias):
        @pl.loop(0, own_rows // LANES)
        def _(j):
            rows = pl.ds(pl.multiple_of(j * LANES, LANES), LANES)
            turned = (even[rows, :] + odd[rows, :]).T
            out[:, rows] = turned[:width]
            if bias is not None:
                bias[:, rows] = turned[width : width + 1] * n_col

    clear()
    loads[0].wait()
    add(events, events, 1, target_buf)
    loads[1].wait()
    add(2 * events, neg_count, 2, neg_buf)
    turn(out_out, bias_out)
    stores[0].start()
    stores[1].start()
    loads[2].wait()
    part = weight_out.shape[2] // n_col
    for w in range(2):
        for g in range(weight_out.shape[1]):
            for b in range(n_col):
                weight_out[w, g, b * part : (b + 1) * part, :] = grad_buf[w, g, b * block : b * block + part, 0:width]
        stores[2 + w].start()
    clear()
    loads[3].wait()
    add(0, events, 0, item_buf)
    turn(embed_out, None)
    stores[4].start()
    for store in stores:
        store.wait()


def run_finish(packed, shift, low, table_rows, own_rows, width, items, targets, negs, grads):
    events, block = items.shape
    _, gates, units, _ = grads.shape
    n_col = units // block
    hbm = pl.BlockSpec(memory_space=pl.ANY)
    weight = jax.ShapeDtypeStruct((gates, n_col * width, width), f32)
    table = jax.ShapeDtypeStruct((width, own_rows), f32)
    return pl.pallas_call(
        functools.partial(finish_kernel, shift, table_rows, width),
        out_shape=(table, table, jax.ShapeDtypeStruct((1, own_rows), f32), weight, weight),
        in_specs=[in_smem(), in_smem()] + [hbm] * 4,
        out_specs=(hbm,) * 5,
        scratch_shapes=[
            pltpu.VMEM((own_rows, block), f32),
            pltpu.VMEM((own_rows, block), f32),
            pltpu.VMEM(items.shape, f32),
            pltpu.VMEM(targets.shape, f32),
            pltpu.VMEM(negs.shape, f32),
            pltpu.VMEM(grads.shape, f32),
            pltpu.VMEM((width, own_rows), f32),
            pltpu.VMEM((width, own_rows), f32),
            pltpu.VMEM((1, own_rows), f32),
            pltpu.VMEM((2,) + weight.shape, f32),
            pltpu.SemaphoreType.DMA((9,)),
        ],
        cost_estimate=takes(40),
        compiler_params=params(),
    )(low.reshape(1), packed, items, targets, negs, grads)


def split_weight(weight, high_part, low_part):
    step = 128

    @pl.loop(0, weight.shape[0] // step)
    def _(i):
        rows = pl.ds(pl.multiple_of(i * step, step), step)
        value = weight[rows, :]
        top = value.astype(bf16)
        high_part[rows, :] = top
        low_part[rows, :] = (value - top.astype(f32)).astype(bf16)


def two_part(value):
    top = value.astype(bf16).astype(f32)
    return jnp.concatenate([top, value - top], axis=0).astype(bf16)


def forward_kernel(
    steps,
    width,
    hidden,
    entering,
    arrived,
    keep,
    prevs,
    resets,
    updates,
    cands,
    inners,
    outs,
    w_high,
    w_low,
    x_gates,
    hid_buf,
    in_buf,
    pair_buf,
    sem,
    travel=None,
):
    events, units = prevs.shape
    rows_per = arrived.shape[0] - events
    step_rows = hid_buf.shape[1]
    chunks = hidden.shape[0] // step_rows

    def load(i, slot):
        rows = pl.ds(pl.multiple_of(i * step_rows, step_rows), step_rows)
        return (
            pltpu.make_async_copy(hidden.at[rows], hid_buf.at[slot], sem.at[0, slot]),
            pltpu.make_async_copy(entering.at[rows], in_buf.at[slot], sem.at[1, slot]),
        )

    for copy in load(0, 0):
        copy.start()
    timeline = travel() if travel else ()
    pair_buf[0], pair_buf[1] = split_two(arrived[0:events, :])

    @pl.loop(0, chunks)
    def _(i):
        slot = lax.rem(i, 2)

        @pl.when(i + 1 < chunks)
        def _():
            for copy in load(i + 1, 1 - slot):
                copy.start()

        for copy in load(i, slot):
            copy.wait()
        cols = pl.ds(pl.multiple_of(i * step_rows, step_rows), step_rows)
        turned = hid_buf[slot].T
        first = turned.astype(bf16)
        w_high[:, cols] = first
        w_low[:, cols] = (turned - first.astype(f32)).astype(bf16)
        value = in_buf[slot]
        first = value.astype(bf16)
        second = (value - first.astype(f32)).astype(bf16)
        over = (((1,), (1,)), ((), ()))
        x_gates[:, cols] = (
            lax.dot_general(pair_buf[0], first, over, preferred_element_type=f32)
            + lax.dot_general(pair_buf[1], first, over, preferred_element_type=f32)
            + lax.dot_general(pair_buf[0], second, over, preferred_element_type=f32)
        )

    lane = lax.broadcasted_iota(jnp.int32, (rows_per, units), 1)

    def step(t, state):
        rows = pl.ds(pl.multiple_of(t * rows_per, rows_per), rows_per)
        prev = jnp.where(lane == width, 1.0, keep[rows, :] * state)
        pair = two_part(prev)

        def gate(g):
            cols = slice(g * units, (g + 1) * units)
            first = jnp.dot(pair, w_high[:, cols], preferred_element_type=f32)
            second = jnp.dot(pair, w_low[:, cols], preferred_element_type=f32)
            return first[:rows_per] + first[rows_per:] + second[:rows_per], cols

        h_reset, cols = gate(0)
        reset = jax.nn.sigmoid(x_gates[rows, cols] + h_reset)
        h_update, cols = gate(1)
        update = jax.nn.sigmoid(x_gates[rows, cols] + h_update)
        inner, cols = gate(2)
        cand = jnp.tanh(x_gates[rows, cols] + reset * inner)
        new = (1.0 - update) * cand + update * prev
        prevs[rows, :] = prev
        resets[rows, :] = reset
        updates[rows, :] = update
        cands[rows, :] = cand
        inners[rows, :] = inner
        outs[rows, :] = new
        return new

    state, done = arrived[events:, :], 0
    for share_done, actions in timeline:
        until = int(share_done * steps)
        if until > done:
            state, done = lax.fori_loop(done, until, step, state), until
        for action, argument in actions:
            action(argument)
    lax.fori_loop(done, steps, step, state)


def forward_travel_kernel(steps, width, hidden, entering, arrived, keep, out_rows, *refs):
    saved, (neg_all, targets), scratch = refs[:6], refs[6:8], refs[8:]
    z_rows, target_send, target_recv, target_local, row_local, row_send, row_recv = scratch[7:]
    spot = Spot()
    events = keep.shape[0]
    neg_own = out_rows.at[pl.ds(4 * events, z_rows.shape[1])]

    def target_own(z):
        return out_rows.at[pl.ds(pl.multiple_of(z * events, events), events)]

    rows = RowsFlow(spot, neg_own, z_rows, neg_all, row_local, row_send, row_recv, same=True)
    copies = []

    def begin_targets(_):
        keep_own = pltpu.make_async_copy(target_own(spot.c), targets.at[spot.c], target_local.at[0])
        keep_own.start()
        copies.append(keep_own)
        for m, z in enumerate(spot.z_to):
            copies.append(
                remote(target_own(z), targets.at[spot.c], target_send.at[m], target_recv.at[m], (spot.d, z))
            )

    def travel():
        spot.greet_all()
        rows.begin()
        return (
            (0.0, ((rows.forward, 0),)),
            (0.1, ((rows.spread, 1),)),
            (0.2, ((rows.far, 0),)),
            (0.3, ((rows.forward, 1), (rows.spread, 2), (begin_targets, None))),
            (0.4, ((rows.far, 1),)),
            (0.5, ((rows.forward, 2), (rows.spread, 3))),
            (0.6, ((rows.far, 2),)),
            (0.7, ((rows.forward, 3),)),
            (0.85, ((rows.far, 3),)),
        )

    forward_kernel(steps, width, hidden, entering, arrived, keep, *saved, *scratch[:7], travel=travel)
    rows.close()
    for copy in copies:
        copy.wait()


def forward_scratch(hidden, events):
    units = hidden.shape[1]
    step_rows = units // 4
    return [
        pltpu.VMEM(hidden.shape[::-1], bf16),
        pltpu.VMEM(hidden.shape[::-1], bf16),
        pltpu.VMEM((events, hidden.shape[0]), f32),
        pltpu.VMEM((2, step_rows, units), f32),
        pltpu.VMEM((2, step_rows, units), f32),
        pltpu.VMEM((2, events, units), bf16),
        pltpu.SemaphoreType.DMA((2, 2)),
    ]


def run_forward(hidden, entering, arrived, keep, steps, width):
    events, units = keep.shape[0], arrived.shape[1]
    saved = jax.ShapeDtypeStruct((events, units), f32)
    hbm = pl.BlockSpec(memory_space=pl.ANY)
    return pl.pallas_call(
        functools.partial(forward_kernel, steps, width),
        out_shape=(saved,) * 6,
        in_specs=[hbm, hbm] + [in_vmem()] * 2,
        out_specs=(in_vmem(),) * 6,
        scratch_shapes=forward_scratch(hidden, events),
        cost_estimate=takes(75),
        compiler_params=params(),
    )(hidden, entering, arrived, keep)


def run_forward_travel(hidden, entering, arrived, keep, out_rows, steps, width, collective_id):
    events, units = keep.shape[0], arrived.shape[1]
    block = out_rows.shape[1]
    count = out_rows.shape[0] - 4 * events
    saved = jax.ShapeDtypeStruct((events, units), f32)
    hbm = pl.BlockSpec(memory_space=pl.ANY)
    dma = pltpu.SemaphoreType.DMA
    return pl.pallas_call(
        functools.partial(forward_travel_kernel, steps, width),
        out_shape=(saved,) * 6
        + (jax.ShapeDtypeStruct((8, 4, count, block), f32), jax.ShapeDtypeStruct((4, events, block), f32)),
        in_specs=[hbm, hbm] + [in_vmem()] * 2 + [hbm],
        out_specs=(in_vmem(),) * 6 + (hbm, hbm),
        scratch_shapes=forward_scratch(hidden, events)
        + [pltpu.VMEM((4, count, block), f32), dma((3,)), dma((3,)), dma((1,)), dma((4,)), dma((4, 9)), dma((4, 9))],
        cost_estimate=takes(75),
        compiler_params=pltpu.CompilerParams(
            collective_id=collective_id, has_side_effects=True, vmem_limit_bytes=VMEM_BYTES
        ),
    )(hidden, entering, arrived, keep, out_rows)


def backward_kernel(
    steps, weight, douts, keep, prevs, resets, updates, cands, inners, dgates, dstart, w_high, w_low
):
    rows_per, units = dstart.shape
    split_weight(weight, w_high, w_low)

    def step(i, dstate):
        t = steps - 1 - i
        rows = pl.ds(pl.multiple_of(t * rows_per, rows_per), rows_per)
        reset, update, cand = resets[rows, :], updates[rows, :], cands[rows, :]
        dh = douts[rows, :] + dstate
        dcand = dh * (1.0 - update) * (1.0 - cand * cand)
        dreset = dcand * inners[rows, :] * reset * (1.0 - reset)
        dupdate = dh * (prevs[rows, :] - cand) * update * (1.0 - update)
        dinner = dcand * reset
        dgates[rows, 0:units] = dreset
        dgates[rows, units : 2 * units] = dupdate
        dgates[rows, 2 * units : 3 * units] = dinner
        dgates[rows, 3 * units : 4 * units] = dcand
        total = dh * update
        for g, part in enumerate((dreset, dupdate, dinner)):
            pair = two_part(part)
            sect = slice(g * units, (g + 1) * units)
            first = jnp.dot(pair, w_high[sect, :], preferred_element_type=f32)
            second = jnp.dot(pair, w_low[sect, :], preferred_element_type=f32)
            total = total + (first[:rows_per] + first[rows_per:] + second[:rows_per])
        return keep[rows, :] * total

    dstart[...] = lax.fori_loop(0, steps, step, jnp.zeros((rows_per, units), f32))


def run_backward(weight, douts, keep, saved, rows_per, steps):
    events, units = douts.shape
    return pl.pallas_call(
        functools.partial(backward_kernel, steps),
        out_shape=(
            jax.ShapeDtypeStruct((events, 4 * units), f32),
            jax.ShapeDtypeStruct((rows_per, units), f32),
        ),
        in_specs=[in_vmem()] * 8,
        out_specs=(in_vmem(),) * 2,
        scratch_shapes=[pltpu.VMEM(weight.shape, bf16)] * 2,
        cost_estimate=takes(67),
        compiler_params=params(),
    )(weight, douts, keep, *saved)


def place():
    d = lax.axis_index("dp")
    c = lax.axis_index("col")
    return d // 4, (d // 2) % 2, d % 2, c, d


def greet(partners):
    barrier = pltpu.get_barrier_semaphore()
    for partner in partners:
        pl.semaphore_signal(barrier, inc=1, device_id=partner, device_id_type=MESH)
    pl.semaphore_wait(barrier, len(partners))


class Spot:
    def __init__(self):
        self.y, self.x, self.k, self.c, self.d = place()
        y, x, k, c, d = self.y, self.x, self.k, self.c, self.d
        self.x_d, self.y_d, self.core_d = d + 2 - 4 * x, d + 4 - 8 * y, d + 1 - 2 * k
        self.far_d = d + 6 - 4 * x - 8 * y
        self.core_to, self.x_to, self.y_to, self.far_to = (self.core_d, c), (self.x_d, c), (self.y_d, c), (self.far_d, c)
        self.z_to = (c + 1 - 2 * lax.rem(c, 2), lax.rem(c + 2, 4), 3 - c)

    def greet_all(self):
        greet([self.core_to, self.x_to, self.y_to, self.far_to] + [(self.d, z) for z in self.z_to])


def remote(source, target, send, recv, to):
    copy = pltpu.make_async_remote_copy(
        src_ref=source, dst_ref=target, send_sem=send, recv_sem=recv, device_id=to, device_id_type=MESH
    )
    copy.start()
    return copy


class RowsFlow:
    def __init__(self, spot, outgoing, z_rows, every, local_sem, send_sem, recv_sem, same=False):
        self.spot, self.outgoing, self.z_rows, self.every = spot, outgoing, z_rows, every
        self.local_sem, self.send_sem, self.recv_sem = local_sem, send_sem, recv_sem
        self.started = {}
        self.rows = every.shape[2]
        self.sources = (spot.c,) + spot.z_to
        self.same = same

    def send(self, u, slot, source, target, to):
        return remote(source, target, self.send_sem.at[u, slot], self.recv_sem.at[u, slot], to)

    def begin(self):
        spot = self.spot
        for m in range(3):
            z = spot.z_to[m]
            source = self.outgoing if self.same else self.outgoing.at[z]
            self.started["z", m] = self.send(1 + m, 0, source, self.z_rows.at[spot.c], (spot.d, z))
        self.spread(0)

    def spread(self, u):
        spot, src = self.spot, self.sources[u]
        if u > 0:
            self.started["z", u - 1].wait_recv()
            source = self.z_rows.at[src, 0 : self.rows]
        else:
            source = self.outgoing if self.same else self.outgoing.at[src, 0 : self.rows]
        target = self.every.at[spot.d, src]
        keep = pltpu.make_async_copy(source, target, self.local_sem.at[u])
        keep.start()
        self.started["keep", u] = keep
        for slot, (name, to) in enumerate((("x", spot.x_to), ("y", spot.y_to), ("c", spot.core_to))):
            self.started[name, u] = self.send(u, 1 + slot, source, target, to)

    def forward(self, u):
        spot, src, mid = self.spot, self.sources[u], self.rows // 2
        self.started["x", u].wait_recv()
        piece = self.every.at[spot.x_d, src, 0:mid]
        self.started["xy", u] = self.send(u, 4, piece, piece, spot.y_to)
        piece = self.every.at[spot.x_d, src]
        self.started["xc", u] = self.send(u, 5, piece, piece, spot.core_to)
        self.started["y", u].wait_recv()
        piece = self.every.at[spot.y_d, src, mid : self.rows]
        self.started["yx", u] = self.send(u, 6, piece, piece, spot.x_to)
        piece = self.every.at[spot.y_d, src]
        self.started["yc", u] = self.send(u, 7, piece, piece, spot.core_to)

    def far(self, u):
        spot, src = self.spot, self.sources[u]
        self.started["xy", u].wait_recv()
        self.started["yx", u].wait_recv()
        piece = self.every.at[spot.far_d, src]
        self.started["fc", u] = self.send(u, 8, piece, piece, spot.core_to)

    def close(self):
        for u in range(4):
            for name in ("c", "xc", "yc", "fc"):
                self.started[name, u].wait_recv()
            self.started["keep", u].wait()
        for (name, _), copy in self.started.items():
            if name != "keep":
                copy.wait_send()


class SumFlow:
    def __init__(self, spot, mine, core_in, x_in, y_in, xy_in, yx_in, z_in, total, out_at, local_sem, send_sem, recv_sem):
        self.spot, self.mine, self.core_in, self.out_at = spot, mine, core_in, out_at
        self.x_in, self.y_in, self.xy_in, self.yx_in, self.z_in, self.total = x_in, y_in, xy_in, yx_in, z_in, total
        self.local_sem, self.send_sem, self.recv_sem = local_sem, send_sem, recv_sem
        self.started = [{} for _ in range(mine.shape[0])]
        self.half = mine.shape[4] // 2

    def send(self, j, slot, source, target, to):
        return remote(source, target, self.send_sem.at[j, slot], self.recv_sem.at[j, slot], to)

    def over_core(self, j, source):
        self.started[j]["core"] = self.send(j, 0, source, self.core_in.at[j], self.spot.core_to)

    def core(self, j):
        spot, mine, half, started = self.spot, self.mine, self.half, self.started[j]
        started["core"].wait_recv()

        @pl.loop(0, 4)
        def _(a):
            for b in range(2):
                for e in range(2):
                    mine[j, a, b, e] = mine[j, a, b, e] + self.core_in[j, a, b, e]

        started["x"] = self.send(j, 1, mine.at[j, :, :, 1 - spot.x, 0:half], self.x_in.at[j], spot.x_to)
        started["y"] = self.send(j, 2, mine.at[j, :, 1 - spot.y, :, half : 2 * half], self.y_in.at[j], spot.y_to)

    def first(self, j):
        spot, mine, half, started = self.spot, self.mine, self.half, self.started[j]
        x, y = spot.x, spot.y
        started["x"].wait_recv()
        for a in range(4):
            for b in range(2):
                mine[j, a, b, x, 0:half] = mine[j, a, b, x, 0:half] + self.x_in[j, a, b]
        started["xy"] = self.send(j, 3, mine.at[j, :, 1 - y, x, 0:half], self.xy_in.at[j], spot.y_to)
        started["y"].wait_recv()
        for a in range(4):
            for e in range(2):
                mine[j, a, y, e, half : 2 * half] = mine[j, a, y, e, half : 2 * half] + self.y_in[j, a, e]
        started["yx"] = self.send(j, 4, mine.at[j, :, y, 1 - x, half : 2 * half], self.yx_in.at[j], spot.x_to)

    def second(self, j):
        spot, mine, half, started = self.spot, self.mine, self.half, self.started[j]
        x, y = spot.x, spot.y
        started["xy"].wait_recv()
        started["yx"].wait_recv()
        for a in range(4):
            mine[j, a, y, x, 0:half] = mine[j, a, y, x, 0:half] + self.xy_in[j, a]
            mine[j, a, y, x, half : 2 * half] = mine[j, a, y, x, half : 2 * half] + self.yx_in[j, a]
        for m in range(3):
            z = spot.z_to[m]
            started["z", m] = self.send(j, 5 + m, mine.at[j, z, y, x], self.z_in.at[j, m], (spot.d, z))

    def along(self, j):
        spot, started, total = self.spot, self.started[j], self.total
        for m in range(3):
            started["z", m].wait_recv()
        own = self.mine[j, spot.c, spot.y, spot.x]
        total[j] = ((own + self.z_in[j, 0]) + self.z_in[j, 1]) + self.z_in[j, 2]
        target = self.out_at(j, spot.d, 0, 2 * self.half)
        started["keep"] = pltpu.make_async_copy(total.at[j], target, self.local_sem.at[j])
        started["keep"].start()
        for slot, (name, to) in enumerate((("gx", spot.x_to), ("gy", spot.y_to), ("gc", spot.core_to))):
            started[name] = self.send(j, 8 + slot, total.at[j], target, to)

    def share(self, j):
        spot, started, half = self.spot, self.started[j], self.half
        started["gx"].wait_recv()
        piece = self.out_at(j, spot.x_d, 0, half)
        started["gxy"] = self.send(j, 11, piece, piece, spot.y_to)
        piece = self.out_at(j, spot.x_d, 0, 2 * half)
        started["cgx"] = self.send(j, 12, piece, piece, spot.core_to)
        started["gy"].wait_recv()
        piece = self.out_at(j, spot.y_d, half, half)
        started["gyx"] = self.send(j, 13, piece, piece, spot.x_to)
        piece = self.out_at(j, spot.y_d, 0, 2 * half)
        started["cgy"] = self.send(j, 14, piece, piece, spot.core_to)

    def far(self, j):
        spot, started = self.spot, self.started[j]
        started["gxy"].wait_recv()
        started["gyx"].wait_recv()
        piece = self.out_at(j, spot.far_d, 0, 2 * self.half)
        started["cgf"] = self.send(j, 15, piece, piece, spot.core_to)

    def end(self, j, core_sent=False):
        started = self.started[j]
        for name in ("gc", "cgx", "cgy", "cgf"):
            started[name].wait_recv()
        for name, copy in started.items():
            if name == "keep":
                copy.wait()
            elif not (name == "core" and core_sent):
                copy.wait_send()


def sum_scratch(jobs, piece, lanes):
    half = piece // 2
    return [
        pltpu.VMEM((jobs, 4, 2, 2, piece, lanes), f32),
        pltpu.VMEM((jobs, 4, 2, 2, piece, lanes), f32),
        pltpu.VMEM((jobs, 4, 2, half, lanes), f32),
        pltpu.VMEM((jobs, 4, 2, half, lanes), f32),
        pltpu.VMEM((jobs, 4, half, lanes), f32),
        pltpu.VMEM((jobs, 4, half, lanes), f32),
        pltpu.VMEM((jobs, 3, piece, lanes), f32),
        pltpu.VMEM((jobs, piece, lanes), f32),
    ]


def flow_sems(jobs):
    dma = pltpu.SemaphoreType.DMA
    return [dma((jobs,)), dma((jobs, 16)), dma((jobs, 16)), dma((4,)), dma((4, 9)), dma((4, 9))]


GATE_OF = ((0, 1, 3), (0, 1, 2))


def split_two(value):
    top = value.astype(bf16)
    return top, (value - top.astype(f32)).astype(bf16)


def three_products(first, second, over):
    def product(a, b):
        return lax.dot_general(a, b, (over, ((), ())), preferred_element_type=f32)

    return product(first[0], second[0]) + product(first[1], second[0]) + product(first[0], second[1])


def tail_kernel(
    inputs,
    prevs,
    dgates,
    dstart,
    entering,
    out,
    item_all,
    start_all,
    mine,
    core_in,
    x_in,
    y_in,
    xy_in,
    yx_in,
    z_in,
    total,
    core_out,
    turned,
    gate_pair,
    flow,
    w_flow,
    din,
    z_rows,
    flow_sem,
    start_sem,
    sum_local,
    sum_send,
    sum_recv,
    row_local,
    row_send,
    row_recv,
):
    spot = Spot()
    spot.greet_all()
    c, k = spot.c, spot.k
    jobs, piece = mine.shape[0], mine.shape[4]
    events, units = gate_pair.shape[2:]
    block = din.shape[2]
    gates = jobs // 2
    sums = SumFlow(
        spot, mine, core_in, x_in, y_in, xy_in, yx_in, z_in, total,
        lambda j, d, at, size: out.at[j // gates, j % gates, d, pl.ds(at, size)], sum_local, sum_send, sum_recv,
    )
    rows = RowsFlow(spot, din, z_rows, item_all, row_local, row_send, row_recv)

    def gate_cols(g):
        return dgates.at[:, pl.ds(g * units, units)]

    queue = [inputs.at[pl.ds(0, events)], gate_cols(0), gate_cols(1), gate_cols(3), prevs, gate_cols(2)]

    def flow_copy(n):
        return pltpu.make_async_copy(queue[n], flow.at[n % 2], flow_sem.at[n % 2])

    def w_copy(n, slot):
        rows = pl.ds(pl.multiple_of(n * block, block), block)
        return pltpu.make_async_copy(entering.at[rows], w_flow.at[slot], flow_sem.at[2 + slot])

    flow_copy(0).start()
    flow_copy(1).start()
    w_copy(0, 0).start()

    def next_flow(n):
        if n + 2 < len(queue):
            flow_copy(n + 2).start()

    def take_act(n, w):
        flow_copy(n).wait()

        @pl.loop(0, 4)
        def _(b):
            cols = pl.ds(pl.multiple_of(b * block, block), block)
            turned[w, 0, b], turned[w, 1, b] = split_two(flow[n % 2, :, cols].T)

        next_flow(n)

    def take_gate(n, g, at):
        flow_copy(n).wait()

        @pl.loop(0, 4)
        def _(b):
            cols = pl.ds(pl.multiple_of(b * block, block), block)
            value = flow[n % 2, :, cols]
            gate_pair[g, 0, :, cols], gate_pair[g, 1, :, cols] = split_two(value)
            if at is not None:
                chunk = 4 * at + b
                slot = lax.rem(b, 2)

                @pl.when(chunk + 1 < 12)
                def _():
                    w_copy(chunk + 1, 1 - slot).start()

                w_copy(chunk, slot).wait()
                share = three_products(split_two(value), split_two(w_flow[slot]), ((1,), (0,)))
                for e in range(4):
                    part = share[:, e * block : (e + 1) * block]
                    if at == 0:
                        before = jnp.where(b == 0, 0.0, din[e, 0:events, :])
                    else:
                        before = din[e, 0:events, :]
                    din[e, 0:events, :] = before + part

        next_flow(n)

    def rows_begin():
        for e in range(4):
            din[e, events:, :] = dstart[:, e * block : (e + 1) * block]
        rows.begin()

    def rows_end():
        keeps = [
            pltpu.make_async_copy(din.at[c, events:], start_all.at[c], start_sem.at[0]),
        ] + [
            pltpu.make_async_copy(z_rows.at[z, events:], start_all.at[z], start_sem.at[1 + m])
            for m, z in enumerate(spot.z_to)
        ]
        for keep in keeps:
            keep.start()
        rows.close()
        for keep in keeps:
            keep.wait()

    def partial(j):
        w, g = j // gates, GATE_OF[j // gates][j % gates]
        slot = j % 2
        if j >= 2:
            sums.started[j - 2]["core"].wait_send()

        @pl.loop(0, 2)
        def _(p):
            for q in range(2):
                b = 2 * p + q
                value = three_products(
                    (turned[w, 0, b], turned[w, 1, b]), (gate_pair[g, 0], gate_pair[g, 1]), ((1,), (0,))
                )
                for e in range(4):
                    cols = slice(e * block, (e + 1) * block)
                    first, second = value[:piece, cols], value[piece:, cols]
                    mine[j, e, p, q] = jnp.where(k == 0, first, second)
                    core_out[slot, e, p, q] = jnp.where(k == 0, second, first)

        sums.over_core(j, core_out.at[slot])

    A, B, C, Z, S, F = sums.core, sums.first, sums.second, sums.along, sums.share, sums.far

    def E(j):
        sums.end(j, core_sent=j < jobs - 2)

    take_act(0, 0)
    take_gate(1, 0, 0)
    partial(0)
    take_gate(2, 1, 1)
    partial(1)
    A(0)
    take_gate(3, 3, 2)
    rows_begin()
    partial(2)
    A(1)
    take_act(4, 1)
    partial(3)
    A(2), B(0), rows.spread(1), rows.forward(0)
    partial(4)
    A(3), B(1), C(0), rows.spread(2), rows.forward(1), rows.far(0)
    take_gate(5, 2, None)
    partial(5)
    A(4), B(2), C(1), Z(0), rows.spread(3), rows.forward(2), rows.far(1)
    A(5), B(3), C(2), Z(1), S(0), rows.forward(3), rows.far(2)
    B(4), C(3), Z(2), S(1), F(0), rows.far(3)
    B(5), C(4), Z(3), S(2), F(1), E(0)
    C(5), Z(4), S(3), F(2), E(1)
    rows_end()
    Z(5), S(4), F(3), E(2)
    S(5), F(4), E(3)
    F(5), E(4), E(5)


def run_tail(inputs, prevs, dgates, dstart, entering, collective_id):
    events, units = prevs.shape
    gates, block = 3, units // 4
    piece = units // 8
    jobs = 2 * gates
    start_rows = dstart.shape[0]
    hbm = pl.BlockSpec(memory_space=pl.ANY)
    grads, item_all, start_all = pl.pallas_call(
        tail_kernel,
        out_shape=(
            jax.ShapeDtypeStruct((2, gates, 8, piece, block), f32),
            jax.ShapeDtypeStruct((8, 4, events, block), f32),
            jax.ShapeDtypeStruct((4, start_rows, block), f32),
        ),
        in_specs=[hbm, hbm, hbm, pl.BlockSpec(memory_space=pltpu.VMEM), hbm],
        out_specs=(hbm, hbm, hbm),
        scratch_shapes=sum_scratch(jobs, piece, block)
        + [
            pltpu.VMEM((2, 4, 2, 2, piece, block), f32),
            pltpu.VMEM((2, 2, 4, block, events), bf16),
            pltpu.VMEM((4, 2, events, units), bf16),
            pltpu.VMEM((2, events, units), f32),
            pltpu.VMEM((2, block, units), f32),
            pltpu.VMEM((4, events + start_rows, block), f32),
            pltpu.VMEM((4, events + start_rows, block), f32),
            pltpu.SemaphoreType.DMA((4,)),
            pltpu.SemaphoreType.DMA((4,)),
        ]
        + flow_sems(jobs),
        cost_estimate=takes(190),
        compiler_params=pltpu.CompilerParams(
            collective_id=collective_id, has_side_effects=True, vmem_limit_bytes=VMEM_BYTES
        ),
    )(inputs, prevs, dgates, dstart, entering)
    return grads.reshape(2, gates, units, block), item_all, start_all


HEAD_TIMES = ((8, 14, 28, 42), (10, 22, 32, 44, 56, 68), 12, 20, 58)
UNITS = ((0, 0), (0, 1), (1, 0), (0, 2), (1, 1), (1, 2))


def head_kernel(
    chunk,
    width,
    flat_ids,
    negative_ids,
    embed,
    table,
    bias,
    w_in,
    w_hid,
    in_bias,
    hid_bias,
    carried,
    own_ids,
    all_in,
    all_hid,
    arrived,
    all_ids,
    out_rows,
    padded,
    turned,
    item_rows,
    held,
    w_buf,
    local_sem,
    send_sem,
    recv_sem,
    row_send,
    row_recv,
    id_send,
    id_recv,
):
    y, x, k, c, d = place()
    i = pl.program_id(0)
    n = pl.num_programs(0) // 2
    core_to, x_to, y_to = (d + 1 - 2 * k, c), (d + 2 - 4 * x, c), (d + 4 - 8 * y, c)
    z_all = (c + 1 - 2 * lax.rem(c, 2), lax.rem(c + 2, 4), 3 - c)
    alls = (all_in, all_hid)
    gates, piece, units = held.shape[1], held.shape[5], held.shape[6]
    half = piece // 2
    block = item_rows.shape[2]
    items = item_rows.shape[1]
    carried_rows = carried.shape[1]
    events = items - carried_rows

    def send(u, slot):
        w, m = UNITS[u]
        z = z_all[m]
        every = alls[w]
        if slot == 0:
            source, target, to = held.at[w, :, y, x, k], every.at[:, c, y, x, k], (d, z)
        elif slot in (4, 6):
            spot = (
                every.at[:, z, y, 1 - x, k, 0:half] if slot == 4 else every.at[:, z, 1 - y, x, k, half : 2 * half]
            )
            source, target, to = spot, spot, (y_to if slot == 4 else x_to)
        else:
            py, px, to = {
                1: (y, x, x_to),
                2: (y, x, y_to),
                3: (y, x, core_to),
                5: (y, 1 - x, core_to),
                7: (1 - y, x, core_to),
                8: (1 - y, 1 - x, core_to),
            }[slot]
            spot = every.at[:, z, py, px, k]
            source, target = spot, spot
        return pltpu.make_async_remote_copy(
            src_ref=source,
            dst_ref=target,
            send_sem=send_sem.at[u, slot],
            recv_sem=recv_sem.at[u, slot],
            device_id=to,
            device_id_type=MESH,
        )

    def load(w):
        return pltpu.make_async_copy((w_in, w_hid)[w], w_buf.at[w], local_sem.at[w])

    def keep(w):
        return pltpu.make_async_copy(held.at[w], alls[w].at[:, c], local_sem.at[2 + w])

    def pad(w):
        load(w).wait()
        part, own = units // block, w_buf.shape[3]
        inner = w_buf.shape[2] // part
        for g in range(gates):
            for b in range(part):
                turned[b * block : b * block + inner, 0:own] = w_buf[w, g, b * inner : (b + 1) * inner, :]
            turned[inner : inner + 1, 0:own] = (in_bias, hid_bias)[w][g : g + 1, :]
            held[w, g] = turned[0:units, :].T.reshape(2, 2, 2, piece, units)
        keep(w).start()

    def item_send(m):
        return pltpu.make_async_remote_copy(
            src_ref=item_rows.at[z_all[m]],
            dst_ref=arrived.at[:, pl.ds(pl.multiple_of(c * block, block), block)],
            send_sem=row_send.at[m],
            recv_sem=row_recv.at[m],
            device_id=(d, z_all[m]),
            device_id_type=MESH,
        )

    def begin_items(_):
        for m in range(3):
            item_send(m).start()

    def item_keep():
        return pltpu.make_async_copy(
            item_rows.at[c], arrived.at[:, pl.ds(pl.multiple_of(c * block, block), block)], local_sem.at[4]
        )

    def id_copy(m):
        to = lax.rem(d + 1 + m, 8)
        return pltpu.make_async_remote_copy(
            src_ref=own_ids,
            dst_ref=all_ids.at[d],
            send_sem=id_send.at[m],
            recv_sem=id_recv.at[m],
            device_id=(to, c),
            device_id_type=MESH,
        )

    def id_keep():
        return pltpu.make_async_copy(own_ids, all_ids.at[d], local_sem.at[5])

    def begin():
        load(0).start()
        load(1).start()
        greet([(lax.rem(d + 1 + m, 8), c) for m in range(7)] + [(d, z) for z in z_all])
        id_keep().start()
        for m in range(7):
            id_copy(m).start()
        turned[0:units, :] = jnp.zeros((units, block), f32)
        pad(0)
        begin_z(0)
        begin_z(1)
        pad(1)

    def begin_z(u):
        send(u, 0).start()

    def spread(u):
        send(u, 0).wait_recv()
        for slot in (1, 2, 3):
            send(u, slot).start()

    def forward(u):
        send(u, 1).wait_recv()
        send(u, 4).start()
        send(u, 5).start()
        send(u, 2).wait_recv()
        send(u, 6).start()
        send(u, 7).start()

    def far(u):
        send(u, 4).wait_recv()
        send(u, 6).wait_recv()
        send(u, 8).start()

    def close(u):
        for slot in (3, 5, 7, 8):
            send(u, slot).wait_recv()
        for slot in range(9):
            send(u, slot).wait_send()

    z_at, spread_at, forward_by, far_by, items_at = HEAD_TIMES
    timeline = [(-1, begin, None), (items_at, begin_items, 0)]
    timeline += [(at, begin_z, 2 + j) for j, at in enumerate(z_at)]
    for u, at in enumerate(spread_at):
        timeline += [(at, spread, u), (at + forward_by, forward, u), (at + far_by, far, u)]
    timeline.sort(key=lambda entry: entry[0])
    last = 2 * n - 1

    @pl.when(i == 0)
    def _():
        padded[...] = jnp.zeros_like(padded)
        padded[width : width + 1, :] = jnp.full((1, chunk), jnp.where(c == 0, 1.0, 0.0), f32)

    for at, action, u in timeline:
        if at < last:

            @pl.when(i == max(at, 0))
            def _(action=action, u=u):
                action() if u is None else action(u)

    @pl.when(i < n)
    def _():
        padded[0:width, :] = embed[...]

    @pl.when(i >= n)
    def _():
        padded[0:width, :] = table[...]
        padded[width : width + 1, :] = bias[...]

    spot = lax.rem(i, n) * chunk
    turned[pl.ds(pl.multiple_of(spot, chunk), chunk), :] = padded[...].T

    @pl.when(i == n - 1)
    def _():
        for z in range(4):

            def body(b, carry, z=z):
                for j in range(8):
                    row = flat_ids[z * events + b * 8 + j]
                    item_rows[z, pl.ds(b * 8 + j, 1), :] = turned[pl.ds(row, 1), :]
                return carry

            lax.fori_loop(0, events // 8, body, 0)
            item_rows[z, events:items, :] = carried[z]
        item_keep().start()

    @pl.when(i == last)
    def _():
        targets = 4 * events
        count = out_rows.shape[0] - targets

        def target_body(b, carry):
            for j in range(8):
                row = flat_ids[targets + b * 8 + j]
                out_rows[pl.ds(b * 8 + j, 1), :] = turned[pl.ds(row, 1), :]
            return carry

        def neg_body(b, carry):
            for j in range(8):
                row = negative_ids[d * count + b * 8 + j]
                out_rows[pl.ds(targets + b * 8 + j, 1), :] = turned[pl.ds(row, 1), :]
            return carry

        lax.fori_loop(0, targets // 8, target_body, 0)
        lax.fori_loop(0, count // 8, neg_body, 0)
        for at, action, u in timeline:
            if at >= last:
                action(u)
        for u in range(6):
            close(u)
        for m in range(3):
            item_send(m).wait()
        for m in range(7):
            id_copy(m).wait()
        id_keep().wait()
        for w in range(2):
            keep(w).wait()
        item_keep().wait()


def gather_all(embed, table, bias, flat_ids, negative_ids, w_in, w_hid, in_bias, hid_bias, carried, own_ids, collective_id):
    width, rows = embed.shape
    gates, block = w_in.shape[0], carried.shape[2]
    units = 4 * block
    piece = block // 8
    chunk = 128 * max(k for k in range(1, 9) if rows % (128 * k) == 0)
    n = rows // chunk
    items = flat_ids.shape[0] // 8 + carried.shape[1]
    out_count = flat_ids.shape[0] // 2 + negative_ids.shape[0] // 8
    own_shape = (gates, 2, 2, 2, piece, units)
    all_shape = (gates, 4, 2, 2, 2, piece, units)
    smem = pl.BlockSpec(memory_space=pltpu.SMEM)
    hbm = pl.BlockSpec(memory_space=pl.ANY)
    all_in, all_hid, arrived, all_ids, out_rows = pl.pallas_call(
        functools.partial(head_kernel, chunk, width),
        out_shape=(
            jax.ShapeDtypeStruct(all_shape, f32),
            jax.ShapeDtypeStruct(all_shape, f32),
            jax.ShapeDtypeStruct((items, units), f32),
            jax.ShapeDtypeStruct((8,) + own_ids.shape, jnp.int32),
            jax.ShapeDtypeStruct((out_count, block), f32),
        ),
        grid=(2 * n,),
        in_specs=[
            smem,
            smem,
            pl.BlockSpec((width, chunk), lambda i: (0, jnp.minimum(i, n - 1))),
            pl.BlockSpec((width, chunk), lambda i: (0, jnp.maximum(i - n, 0))),
            pl.BlockSpec((1, chunk), lambda i: (0, jnp.maximum(i - n, 0))),
            hbm,
            hbm,
            pl.BlockSpec(in_bias.shape, lambda i: (0, 0)),
            pl.BlockSpec(hid_bias.shape, lambda i: (0, 0)),
            pl.BlockSpec(carried.shape, lambda i: (0, 0, 0)),
            pl.BlockSpec(own_ids.shape, lambda i: (0, 0)),
        ],
        out_specs=(hbm, hbm, hbm, hbm, pl.BlockSpec((out_count, block), lambda i: (0, 0))),
        scratch_shapes=[
            pltpu.VMEM((block, chunk), f32),
            pltpu.VMEM((rows, block), f32),
            pltpu.VMEM((4, items, block), f32),
            pltpu.VMEM((2,) + own_shape, f32),
            pltpu.VMEM((2,) + w_in.shape, f32),
            pltpu.SemaphoreType.DMA((6,)),
            pltpu.SemaphoreType.DMA((6, 9)),
            pltpu.SemaphoreType.DMA((6, 9)),
            pltpu.SemaphoreType.DMA((3,)),
            pltpu.SemaphoreType.DMA((3,)),
            pltpu.SemaphoreType.DMA((7,)),
            pltpu.SemaphoreType.DMA((7,)),
        ],
        cost_estimate=takes(120),
        compiler_params=pltpu.CompilerParams(
            collective_id=collective_id, has_side_effects=True, vmem_limit_bytes=VMEM_BYTES
        ),
    )(flat_ids, negative_ids, embed, table, bias, w_in, w_hid, in_bias, hid_bias, carried, own_ids)
    return (
        all_in.reshape(gates, 4 * block, units),
        all_hid.reshape(gates, 4 * block, units),
        arrived,
        all_ids,
        out_rows,
    )


def back_kernel(
    steps,
    width,
    factor,
    hidden,
    outs,
    targets,
    negs,
    keep,
    prevs,
    resets,
    updates,
    cands,
    inners,
    dgates,
    dstart,
    neg_all,
    target_all,
    loss_all,
    halves,
    core_in,
    x_in,
    y_in,
    xy_in,
    yx_in,
    z_in,
    total,
    w_high,
    w_low,
    w_flow,
    z_rows,
    share,
    pairs,
    score,
    neg_flow,
    target_part,
    douts,
    own_loss,
    flow_sem,
    neg_sem,
    loss_sem,
    loss_send,
    loss_recv,
    sum_local,
    sum_send,
    sum_recv,
    row_local,
    row_send,
    row_recv,
):
    spot = Spot()
    spot.greet_all()
    rows_per, units = dstart.shape
    mine, core_out = halves.at[0], halves.at[1]
    jobs, piece = halves.shape[1], halves.shape[5]
    step_rows = w_flow.shape[1]
    chunks = hidden.shape[0] // step_rows
    n_col, events, block = targets.shape
    n_dp, _, count, _ = negs.shape
    sums = SumFlow(
        spot, mine, core_in, x_in, y_in, xy_in, yx_in, z_in, total,
        lambda j, d, at, size: neg_all.at[d, pl.ds(j * piece + at, size)], sum_local, sum_send, sum_recv,
    )
    rows = RowsFlow(spot, target_part, z_rows, target_all, row_local, row_send, row_recv)

    def load(i, slot):
        part = pl.ds(pl.multiple_of(i * step_rows, step_rows), step_rows)
        return pltpu.make_async_copy(hidden.at[part], w_flow.at[slot], flow_sem.at[slot])

    def split_chunk(i):
        slot = lax.rem(i, 2)

        @pl.when(i + 1 < chunks)
        def _():
            load(i + 1, 1 - slot).start()

        load(i, slot).wait()
        part = pl.ds(pl.multiple_of(i * step_rows, step_rows), step_rows)
        w_high[part, :], w_low[part, :] = split_two(w_flow[slot])

    def load_neg(b, slot):
        return pltpu.make_async_copy(negs.at[b], neg_flow.at[slot], neg_sem.at[slot])

    load_neg(0, 0).start()
    load(0, 0).start()
    lane = lax.broadcasted_iota(jnp.int32, (events, block), 1)
    for c in range(n_col):
        value = jnp.where(lane < width, outs[:, c * block : (c + 1) * block], 0.0)
        value = jnp.where(lane == width, 1.0 / n_col, value)
        share[c] = value
        pairs[0, c], pairs[1, c] = split_two(value)

    @pl.loop(0, n_dp)
    def _(b):
        slot = lax.rem(b, 2)
        load_neg(lax.rem(b + 1, n_dp), 1 - slot).start()
        load_neg(b, slot).wait()
        value = jnp.zeros((events, count), f32)
        for c in range(n_col):
            value = value + three_products((pairs[0, c], pairs[1, c]), split_two(neg_flow[slot, c]), ((1,), (1,)))
        score[:, pl.ds(pl.multiple_of(b * count, count), count)] = value
        split_chunk(b)

    part_steps = 4
    step_lane = lax.broadcasted_iota(jnp.int32, (rows_per, LANES), 1)

    def events_part(i, losses):
        size = part_steps * rows_per
        now = pl.ds(pl.multiple_of(i * size, size), size)
        pos = jnp.zeros((size, 1), f32)
        for c in range(n_col):
            pos = pos + jnp.sum(share[c, now, :] * targets[c, now, :], axis=-1, keepdims=True)
        neg = score[now, :]
        expd = jnp.exp(neg - jnp.max(neg, axis=-1, keepdims=True))
        weight = expd * (1.0 / jnp.sum(expd, axis=-1, keepdims=True))
        sig = jax.nn.sigmoid(pos - neg)
        slope = weight * sig
        ppos = jnp.sum(slope, axis=-1, keepdims=True)
        quad = jnp.sum(weight * neg * neg, axis=-1, keepdims=True)
        slope = jnp.sum(slope * (1.0 - sig), axis=-1, keepdims=True)
        value = quad - jnp.log(ppos)
        for q in range(part_steps):
            losses = jnp.where(step_lane == part_steps * i + q, value[q * rows_per : (q + 1) * rows_per], losses)
        score[now, :] = factor * weight * (1.0 - sig * sig * (1.0 / ppos) + neg * neg + 2.0 * neg - quad)
        dpos = -factor * slope / ppos
        for c in range(n_col):
            target_part[c, now, :] = dpos * share[c, now, :]
            douts[now, c * block : (c + 1) * block] = dpos * targets[c, now, :]
        return losses

    own_loss[...] = lax.fori_loop(0, steps // part_steps, events_part, jnp.zeros((rows_per, LANES), f32))
    rows.begin()
    losses = [pltpu.make_async_copy(own_loss, loss_all.at[spot.c], loss_sem.at[0])]
    losses[0].start()
    for m, z in enumerate(spot.z_to):
        losses.append(remote(own_loss, loss_all.at[spot.c], loss_send.at[m], loss_recv.at[m], (spot.d, z)))

    def neg_block(p, q, core, j):
        b = 4 * p + 2 * q + core
        dneg = score[:, pl.ds(pl.multiple_of(b * count, count), count)]
        down = split_two(dneg[:, j * piece : (j + 1) * piece].T)
        which = lax.rem(core + spot.k, 2)
        for c in range(n_col):
            halves[which, j, c, p, q] = three_products(down, (pairs[0, c], pairs[1, c]), ((1,), (0,)))
        return b, dneg

    @pl.loop(0, 2)
    def _(p):
        for q in range(2):
            for core in range(2):
                neg_block(p, q, core, 0)
            split_chunk(n_dp + 2 * p + q)

    sums.over_core(0, core_out.at[0])

    @pl.loop(0, 2)
    def _(p):
        for q in range(2):
            for core in range(2):
                b, dneg = neg_block(p, q, core, 1)
                if q == 1 and core == 1:

                    @pl.when(p == 0)
                    def _():
                        load_neg(b + 1, 0).start()

                else:
                    load_neg(b + 1, 1 - core).start()
                load_neg(b, core).wait()
                across = split_two(dneg)
                for c in range(n_col):
                    cols = slice(c * block, (c + 1) * block)
                    douts[:, cols] = douts[:, cols] + three_products(across, split_two(neg_flow[core, c]), ((1,), (0,)))

    sums.over_core(1, core_out.at[1])
    for c in range(n_col):
        cols = slice(c * block, (c + 1) * block)
        douts[:, cols] = jnp.where(lane < width, douts[:, cols], 0.0)

    def step(i, dstate):
        t = steps - 1 - i
        now = pl.ds(pl.multiple_of(t * rows_per, rows_per), rows_per)
        reset, update, cand = resets[now, :], updates[now, :], cands[now, :]
        dh = douts[now, :] + dstate
        dcand = dh * (1.0 - update) * (1.0 - cand * cand)
        dreset = dcand * inners[now, :] * reset * (1.0 - reset)
        dupdate = dh * (prevs[now, :] - cand) * update * (1.0 - update)
        dinner = dcand * reset
        dgates[now, 0:units] = dreset
        dgates[now, units : 2 * units] = dupdate
        dgates[now, 2 * units : 3 * units] = dinner
        dgates[now, 3 * units : 4 * units] = dcand
        total_now = dh * update
        for g, part in enumerate((dreset, dupdate, dinner)):
            pair = two_part(part)
            sect = slice(g * units, (g + 1) * units)
            first = jnp.dot(pair, w_high[sect, :], preferred_element_type=f32)
            second = jnp.dot(pair, w_low[sect, :], preferred_element_type=f32)
            total_now = total_now + (first[:rows_per] + first[rows_per:] + second[:rows_per])
        return keep[now, :] * total_now

    A, B, C, Z, S, F = sums.core, sums.first, sums.second, sums.along, sums.share, sums.far
    timeline = (
        (0.0, ((A, 0),)),
        (0.1, ((A, 1), (rows.forward, 0),)),
        (0.3, ((B, 0), (rows.spread, 1), (rows.far, 0),)),
        (0.44, ((B, 1), (rows.forward, 1), (rows.spread, 2),)),
        (0.56, ((C, 0), (rows.far, 1),)),
        (0.66, ((C, 1), (rows.forward, 2), (rows.spread, 3),)),
        (0.78, ((Z, 0), (rows.far, 2),)),
        (0.9, ((Z, 1), (S, 0), (rows.forward, 3),)),
        (1.0, ((S, 1), (F, 0),)),
    )
    state, done = jnp.zeros((rows_per, units), f32), 0
    for share_done, actions in timeline:
        until = int(share_done * steps)
        if until > done:
            state, done = lax.fori_loop(done, until, step, state), until
        for action, argument in actions:
            action(argument)
    dstart[...] = lax.fori_loop(done, steps, step, state)
    F(1), rows.far(3)
    sums.end(0)
    rows.close()
    sums.end(1)
    for copy in losses:
        copy.wait()


def run_back(hidden, outs, targets, negs, keep, saved, rows_per, steps, width, factor, collective_id):
    events, units = outs.shape
    n_dp, n_col, count, block = negs.shape
    jobs = 2
    piece = count // jobs
    hbm = pl.BlockSpec(memory_space=pl.ANY)
    step_rows = units // 4
    dma = pltpu.SemaphoreType.DMA
    return pl.pallas_call(
        functools.partial(back_kernel, steps, width, factor),
        out_shape=(
            jax.ShapeDtypeStruct((events, 4 * units), f32),
            jax.ShapeDtypeStruct((rows_per, units), f32),
            jax.ShapeDtypeStruct((8, count, block), f32),
            jax.ShapeDtypeStruct((8, 4, events, block), f32),
            jax.ShapeDtypeStruct((4, rows_per, LANES), f32),
        ),
        in_specs=[hbm, in_vmem(), in_vmem(), hbm] + [in_vmem()] * 6,
        out_specs=(in_vmem(), in_vmem(), hbm, hbm, hbm),
        scratch_shapes=[pltpu.VMEM((2, jobs, 4, 2, 2, piece, block), f32)]
        + sum_scratch(jobs, piece, block)[1:]
        + [
            pltpu.VMEM(hidden.shape, bf16),
            pltpu.VMEM(hidden.shape, bf16),
            pltpu.VMEM((2, step_rows, units), f32),
            pltpu.VMEM((4, events, block), f32),
            pltpu.VMEM((n_col, events, block), f32),
            pltpu.VMEM((2, n_col, events, block), bf16),
            pltpu.VMEM((events, n_dp * count), f32),
            pltpu.VMEM((2, n_col, count, block), f32),
            pltpu.VMEM((n_col, events, block), f32),
            pltpu.VMEM((events, units), f32),
            pltpu.VMEM((rows_per, LANES), f32),
            dma((2,)),
            dma((2,)),
            dma((1,)),
            dma((3,)),
            dma((3,)),
        ]
        + flow_sems(jobs),
        cost_estimate=takes(110),
        compiler_params=pltpu.CompilerParams(
            collective_id=collective_id, has_side_effects=True, vmem_limit_bytes=VMEM_BYTES
        ),
    )(hidden, outs, targets, negs, keep, *saved)


def pad_kernel(weight, bias, out):
    own, full = weight.shape[1:]
    block = out.shape[1]
    n_col = out.shape[2] // block
    part = full // n_col
    out[...] = jnp.zeros_like(out)
    for c in range(n_col):
        out[0, 0:own, c * block : c * block + part] = weight[0, :, c * part : (c + 1) * part]
    out[0, 0:own, part : part + 1] = bias[0]


def pad_units(weight, bias, n_col, block):
    gates, own, full = weight.shape
    return pl.pallas_call(
        pad_kernel,
        out_shape=jax.ShapeDtypeStruct((gates, block, n_col * block), f32),
        grid=(gates,),
        in_specs=[
            pl.BlockSpec((1, own, full), lambda g: (g, 0, 0)),
            pl.BlockSpec((1, own, 1), lambda g: (g, 0, 0)),
        ],
        out_specs=pl.BlockSpec((1, block, n_col * block), lambda g: (g, 0, 0)),
        compiler_params=params(),
    )(weight, bias[:, :, None])


def gather_weight(own, n_dp):
    gates, block, units = own.shape
    flat = own.reshape(n_dp, gates * block // n_dp, units)
    piece = lax.dynamic_index_in_dim(flat, lax.axis_index("dp"), 0, keepdims=False)
    every = lax.all_gather(piece, ("col", "dp"))
    every = every.reshape(-1, gates, block, units)
    return jnp.moveaxis(every, 0, 1).reshape(gates, -1, units)


def reduce_weight(partial, n_dp, n_col):
    gates, rows, units = partial.shape
    block = rows // n_col
    parts = jnp.moveaxis(partial.reshape(gates, n_col, block, units), 1, 0)
    parts = jnp.moveaxis(parts.reshape(n_col, n_dp, gates * block // n_dp, units), 1, 0)
    mine = lax.psum_scatter(parts, "dp", scatter_dimension=0)
    mine = lax.psum_scatter(mine, "col", scatter_dimension=0)
    return lax.all_gather(mine, "dp").reshape(gates, block, units)


def swap_col(rows, n_col):
    return lax.all_to_all(rows, "col", split_axis=0, concat_axis=0, tiled=True)


def unpad_last(value, n_col, part):
    block = value.shape[-1] // n_col
    return value.reshape(value.shape[:-1] + (n_col, block))[..., :part].reshape(value.shape[:-1] + (n_col * part,))


def local(
    n_dp,
    n_col,
    item_ids,
    target_ids,
    negative_ids,
    reset_mask,
    carry_flags,
    carried_state,
    embed_table,
    input_weight,
    hidden_weight,
    gate_bias,
    hidden_bias,
    out_table,
    out_bias,
):
    sessions, steps = item_ids.shape
    own_sessions = sessions // n_col
    rows_per = round_up(own_sessions, ROWS8)
    width = embed_table.shape[0]
    table_rows = embed_table.shape[1]
    own_rows = table_rows // n_dp
    block = round_up(width + 1, LANES)
    units = n_col * block
    events = steps * rows_per
    direct = n_dp == 8 and n_col == 4 and block % 64 == 0 and own_sessions == rows_per and steps % 4 == 0 and steps <= LANES
    factor = 1.0 / steps
    dp_at, col_at = lax.axis_index("dp"), lax.axis_index("col")

    def by_owner(value):
        value = jnp.moveaxis(value.reshape(n_col, own_sessions, steps), 1, 2)
        value = jnp.pad(value, ((0, 0), (0, 0), (0, rows_per - own_sessions)))
        return value.reshape(-1)

    both_ids = jnp.stack([item_ids, target_ids]).reshape(2, n_col, own_sessions, steps)
    both_ids = jnp.pad(jnp.moveaxis(both_ids, 2, 3), ((0, 0), (0, 0), (0, 0), (0, rows_per - own_sessions)))
    item_flat, target_flat = both_ids[0].reshape(-1), both_ids[1].reshape(-1)
    own_keep = lax.dynamic_index_in_dim(
        by_owner(1 - reset_mask).reshape(n_col, events, 1), col_at, 0, keepdims=False
    ).astype(f32)
    valid = jnp.tile(jnp.arange(rows_per) < own_sessions, steps)
    lane = jnp.arange(units) % block

    carried = (carry_flags.astype(f32)[:, None] * carried_state).reshape(n_col, own_sessions, width)
    carried = jnp.pad(carried, ((0, 0), (0, rows_per - own_sessions), (0, block - width)))
    neg_count = negative_ids.shape[0]
    own_negs = lax.dynamic_slice_in_dim(negative_ids, dp_at * (neg_count // n_dp), neg_count // n_dp)
    out_ids = jnp.concatenate([target_flat, own_negs])
    no_bias = jnp.zeros_like(hidden_bias)
    hid_bias = jnp.stack([no_bias, no_bias, hidden_bias])
    if direct:
        flat_ids = both_ids.reshape(-1)
        own_ids = both_ids.reshape(-1, LANES)
        all_in, all_hid, arrived, all_ids, out_rows = gather_all(
            embed_table,
            out_table,
            out_bias[None, :],
            flat_ids,
            negative_ids,
            jnp.swapaxes(input_weight, 1, 2),
            jnp.swapaxes(hidden_weight, 1, 2),
            gate_bias,
            hid_bias,
            carried,
            own_ids,
            1,
        )
        all_ids = all_ids.reshape(n_dp, 2, -1)
    else:
        all_hid = gather_weight(pad_units(hidden_weight, hid_bias, n_col, block), n_dp)
        all_in = gather_weight(pad_units(input_weight, gate_bias, n_col, block), n_dp)
        no_row = jnp.zeros((1, table_rows), f32)
        item_rows = gather_rows(embed_table, no_row, item_flat, block).reshape(n_col, events, block)
        arrived = swap_col(jnp.concatenate([item_rows, carried], axis=1), n_col)
        arrived = jnp.moveaxis(arrived, 0, 1).reshape(events + rows_per, units)
        arrived = arrived.at[:events, width].set(1.0)
        out_rows = gather_rows(out_table, out_bias[None, :], out_ids, block)
        all_ids = lax.all_gather(jnp.stack([item_flat, target_flat]), "dp")
    all_hid, all_in = all_hid.reshape(-1, units), all_in.reshape(-1, units)

    all_items, all_targets = all_ids[:, 0].reshape(-1), all_ids[:, 1].reshape(-1)
    count = all_items.shape[0]
    keys = jnp.concatenate([all_items, all_targets + table_rows, negative_ids + 2 * table_rows])
    order = jnp.concatenate([jnp.tile(lax.iota(jnp.int32, count), 2), lax.iota(jnp.int32, neg_count)])
    shift = (max(count, neg_count) - 1).bit_length()
    direct = direct and (3 * table_rows) << shift < 2**31
    low = (dp_at * own_rows).astype(jnp.int32)
    if direct:
        packed = lax.sort((keys << shift) | order)
    else:
        keys, order = lax.sort((keys, order), num_keys=1)
        by_item = (order[:count], keys[:count])
        by_target = (order[count : 2 * count], keys[count : 2 * count] - table_rows)
        by_neg = (order[2 * count :], keys[2 * count :] - 2 * table_rows)

    if direct:
        *saved, outs, negs, targets = run_forward_travel(
            all_hid, all_in, arrived, own_keep, out_rows, steps, width, 4
        )
    else:
        targets = swap_col(out_rows[: n_col * events].reshape(n_col, events, block), n_col)
        negs = lax.all_gather(out_rows[n_col * events :], ("dp", "col")).reshape(n_dp, n_col, -1, block)
        *saved, outs = run_forward(all_hid, all_in, arrived, own_keep, steps, width)
    prevs = saved[0]

    if direct:
        dgates, dstart, neg_all, target_all, loss_all = run_back(
            all_hid, outs, targets, negs, own_keep, saved, rows_per, steps, width, factor, 3
        )
        loss = loss_all[:, :, :steps].reshape(sessions, steps)
        neg_all, target_all = neg_all.reshape(-1, block), target_all.reshape(-1, block)
    else:
        targets = jnp.moveaxis(targets, 0, 1).reshape(events, units)
        negs = jnp.moveaxis(negs, 1, 2).reshape(neg_count, units)
        shares = jnp.where(lane == width, 1.0 / n_col, jnp.where(lane < width, outs, 0.0))
        pos_score = jnp.sum(shares * targets, axis=-1, keepdims=True)
        neg_score = lax.dot_general(shares, negs, (((1,), (1,)), ((), ())), precision=high)
        top = jnp.max(neg_score, axis=-1, keepdims=True)
        expd = jnp.exp(neg_score - top)
        weight = expd / jnp.sum(expd, axis=-1, keepdims=True)
        sig = jax.nn.sigmoid(pos_score - neg_score)
        ppos = jnp.sum(weight * sig, axis=-1, keepdims=True)
        quad = jnp.sum(weight * neg_score * neg_score, axis=-1, keepdims=True)
        slope = jnp.sum(weight * sig * (1.0 - sig), axis=-1, keepdims=True)
        own_loss = -jnp.log(ppos) + quad
        dneg = factor * weight * (1.0 - sig * sig / ppos + neg_score * neg_score + 2.0 * neg_score - quad)
        dneg = jnp.where(valid[:, None], dneg, 0.0)
        dpos = jnp.where(valid[:, None], -factor * slope / ppos, 0.0)
        douts = jnp.dot(dneg, negs, precision=high) + dpos * targets
        douts = jnp.where(lane < width, douts, 0.0)
        neg_part = lax.dot_general(dneg, shares, (((0,), (0,)), ((), ())), precision=high)
        target_part = dpos * shares

        neg_own = lax.psum_scatter(neg_part.reshape(n_dp, -1, units), "dp", scatter_dimension=0)
        neg_own = jnp.moveaxis(neg_own.reshape(-1, n_col, block), 1, 0)
        neg_own = lax.psum_scatter(neg_own, "col", scatter_dimension=0)
        neg_all = lax.all_gather(neg_own, "dp", tiled=True)
        target_own = swap_col(jnp.moveaxis(target_part.reshape(events, n_col, block), 1, 0), n_col)
        target_all = lax.all_gather(target_own.reshape(-1, block), "dp", tiled=True)
        dgates, dstart = run_backward(all_hid, douts, own_keep, saved, rows_per, steps)
        own_loss = own_loss.reshape(steps, rows_per)[:, :own_sessions]
        loss = lax.all_gather(own_loss.T, "col", tiled=True)
    gates = input_weight.shape[0]
    if direct:
        grads, item_all, start_all = run_tail(arrived, prevs, dgates, dstart, all_in, 2)
        grad_embed, grad_out, grad_obias, grad_in, grad_hid = run_finish(
            packed, shift, low, table_rows, own_rows, width, item_all.reshape(-1, block), target_all, neg_all, grads
        )
        grad_obias = grad_obias[0]
        grad_in, grad_hid = jnp.swapaxes(grad_in, 1, 2), jnp.swapaxes(grad_hid, 1, 2)
        grad_gate, grad_hbias = grads[0, :, width, :width], grads[1, gates - 1, width, :width]
    else:
        dx = jnp.concatenate([dgates[:, : 2 * units], dgates[:, 3 * units :]], axis=1)
        dh = dgates[:, : 3 * units]
        hid_part = lax.dot_general(dh, prevs, (((0,), (0,)), ((), ())), precision=high)
        in_part = lax.dot_general(dx, arrived[:events], (((0,), (0,)), ((), ())), precision=high)
        dinputs = jnp.dot(dx, all_in, precision=high)
        back = jnp.concatenate([dinputs, dstart], axis=0).reshape(events + rows_per, n_col, block)
        back = swap_col(jnp.moveaxis(back, 1, 0), n_col)
        item_all = lax.all_gather(back[:, :events].reshape(-1, block), "dp", tiled=True)
        start_all = back[:, events:]
        grad_in = reduce_weight(in_part.reshape(gates, units, units), n_dp, n_col)
        grad_hid = reduce_weight(hid_part.reshape(gates, units, units), n_dp, n_col)
        grad_gate, grad_hbias = grad_in[:, :width, width], grad_hid[gates - 1, :width, width]
        grad_in, grad_hid = (unpad_last(g[:, :width], n_col, width) for g in (grad_in, grad_hid))
        grad_out, grad_obias = scatter_rows(
            [by_target + (target_all,), by_neg + (neg_all,)],
            low,
            own_rows,
            width,
            block,
        )
        grad_obias = grad_obias[0] * n_col
        grad_embed, _ = scatter_rows([by_item + (item_all,)], low, own_rows, width, block)
    grad_carried = start_all[:, :own_sessions, :width].reshape(sessions, width)
    grad_carried = carry_flags.astype(f32)[:, None] * grad_carried
    return (
        loss,
        grad_embed,
        grad_in,
        grad_hid,
        grad_gate,
        grad_hbias,
        grad_out,
        grad_obias,
        grad_carried,
    )


def solution(mesh):
    in_specs = (
        P("dp", None),
        P("dp", None),
        P(),
        P("dp", None),
        P("dp"),
        P("dp", "col"),
        P("col", None),
        P(None, "col", None),
        P(None, "col", None),
        P(None, "col"),
        P("col"),
        P("col", None),
        P(),
    )
    out_specs = (
        P("dp", None),
        P("col", "dp"),
        P(None, "col", None),
        P(None, "col", None),
        P(None, "col"),
        P("col"),
        P("col", "dp"),
        P("dp"),
        P("dp", "col"),
    )
    body = functools.partial(local, mesh.shape["dp"], mesh.shape["col"])
    return jax.shard_map(body, mesh=mesh, in_specs=in_specs, out_specs=out_specs, check_vma=False)
```

```python
import functools

import jax
import jax.numpy as jnp
from jax import lax
from jax.experimental import pallas as pl
from jax.experimental.pallas import tpu as pltpu
from jax.sharding import PartitionSpec as P

LANES = 128
ROWS8 = 8
VMEM_BYTES = 60 << 20
f32 = jnp.float32
bf16 = jnp.bfloat16
high = lax.Precision.HIGH
MESH = pl.DeviceIdType.MESH


def round_up(value, unit):
    return -(-value // unit) * unit


def params():
    return pltpu.CompilerParams(vmem_limit_bytes=VMEM_BYTES)


def takes(micros):
    return pl.CostEstimate(flops=int(micros * 1.1e9), bytes_accessed=1 << 20, transcendentals=0)


def in_vmem():
    return pl.BlockSpec(memory_space=pltpu.VMEM)


def in_smem():
    return pl.BlockSpec(memory_space=pltpu.SMEM)


def gather_kernel(chunk, count, width, ids, table, bias, out, padded, turned):
    step = pl.program_id(0)

    @pl.when(step == 0)
    def _():
        padded[...] = jnp.zeros_like(padded)

    padded[0:width, :] = table[...]
    padded[width : width + 1, :] = bias[...]
    turned[pl.ds(pl.multiple_of(step * chunk, chunk), chunk), :] = padded[...].T

    @pl.when(step == pl.num_programs(0) - 1)
    def _():
        def body(block, carry):
            for j in range(ROWS8):
                row = ids[block * ROWS8 + j]
                out[pl.ds(block * ROWS8 + j, 1), :] = turned[pl.ds(row, 1), :]
            return carry

        lax.fori_loop(0, count // ROWS8, body, 0)


def gather_rows(table, bias, ids, block):
    width, rows = table.shape
    count = ids.shape[0]
    chunk = LANES * max(k for k in range(1, 9) if rows % (LANES * k) == 0)
    return pl.pallas_call(
        functools.partial(gather_kernel, chunk, count, width),
        out_shape=jax.ShapeDtypeStruct((count, block), f32),
        grid_spec=pltpu.PrefetchScalarGridSpec(
            num_scalar_prefetch=1,
            grid=(rows // chunk,),
            in_specs=[
                pl.BlockSpec((width, chunk), lambda i, ids: (0, i)),
                pl.BlockSpec((1, chunk), lambda i, ids: (0, i)),
            ],
            out_specs=pl.BlockSpec((count, block), lambda i, ids: (0, 0)),
            scratch_shapes=[pltpu.VMEM((block, chunk), f32), pltpu.VMEM((rows, block), f32)],
        ),
        compiler_params=params(),
    )(ids, table, bias)


def scatter_kernel(width, n_lists, *refs):
    bounds = refs[0]
    lists = refs[1 : 1 + 3 * n_lists]
    out, bias_out, acc = refs[1 + 3 * n_lists :]
    acc[...] = jnp.zeros_like(acc)
    low = bounds[0]
    for k in range(n_lists):
        rows_of, ids, data = lists[3 * k : 3 * k + 3]

        def body(i, carry):
            spot = pl.ds(ids[i] - low, 1)
            acc[spot, :] = acc[spot, :] + data[pl.ds(rows_of[i], 1), :]
            return carry

        lax.fori_loop(bounds[1 + 2 * k], bounds[2 + 2 * k], body, 0)
    for j in range(acc.shape[0] // LANES):
        cols = slice(j * LANES, (j + 1) * LANES)
        turned = acc[cols, :].T
        out[:, cols] = turned[:width]
        bias_out[:, cols] = turned[width : width + 1]


def scatter_rows(lists, low, own_rows, width, block):
    ends = [low]
    operands, specs = [], []
    for order, ids, data in lists:
        ends += [jnp.sum(ids < low, dtype=jnp.int32), jnp.sum(ids < low + own_rows, dtype=jnp.int32)]
        operands += [order, ids, data]
        specs += [in_smem(), in_smem(), in_vmem()]
    return pl.pallas_call(
        functools.partial(scatter_kernel, width, len(lists)),
        out_shape=(
            jax.ShapeDtypeStruct((width, own_rows), f32),
            jax.ShapeDtypeStruct((1, own_rows), f32),
        ),
        in_specs=[in_smem()] + specs,
        out_specs=(in_vmem(), in_vmem()),
        scratch_shapes=[pltpu.VMEM((own_rows, block), f32)],
        cost_estimate=takes(20),
        compiler_params=params(),
    )(jnp.stack(ends), *operands)


def finish_kernel(
    shift,
    table_rows,
    width,
    low,
    packed,
    items,
    targets,
    negs,
    grads,
    grad_embed,
    grad_out,
    grad_bias,
    grad_in,
    grad_hid,
    even,
    odd,
    item_buf,
    target_buf,
    neg_buf,
    grad_buf,
    embed_out,
    out_out,
    bias_out,
    weight_out,
    sem,
):
    own_rows = even.shape[0]
    events, neg_count = item_buf.shape[0], neg_buf.shape[0]
    block = even.shape[1]
    n_col = grad_buf.shape[2] // block
    loads = [
        pltpu.make_async_copy(source, target, sem.at[n])
        for n, (source, target) in enumerate(
            ((targets, target_buf), (negs, neg_buf), (grads, grad_buf), (items, item_buf))
        )
    ]
    for load in loads:
        load.start()
    stores = [
        pltpu.make_async_copy(source, target, sem.at[4 + n])
        for n, (source, target) in enumerate(
            (
                (out_out, grad_out),
                (bias_out, grad_bias),
                (weight_out.at[0], grad_in),
                (weight_out.at[1], grad_hid),
                (embed_out, grad_embed),
            )
        )
    ]

    def first_from(begin, count, bound):
        def halve(_, ends):
            left, right = ends
            middle = jnp.minimum((left + right) // 2, begin + count - 1)
            less = (left < right) & (packed[middle] < bound)
            return jnp.where(less, middle + 1, left), jnp.where(less | (left >= right), right, middle)

        return lax.fori_loop(0, count.bit_length() + 1, halve, (begin, begin + count))[0]

    def add(begin, count, which, data):
        base = low[0] + which * table_rows
        left = first_from(begin, count, base << shift)
        right = first_from(begin, count, (base + own_rows) << shift)

        def one(i, acc):
            key = packed[i]
            spot, row = (key >> shift) - base, key & ((1 << shift) - 1)
            acc[pl.ds(spot, 1), :] = acc[pl.ds(spot, 1), :] + data[pl.ds(row, 1), :]

        def eight(i, carry):
            for n in range(8):
                one(left + 8 * i + n, (even, odd)[n % 2])
            return carry

        eights = (right - left) // 8
        lax.fori_loop(0, eights, eight, 0)

        def rest(i, carry):
            one(i, even)
            return carry

        lax.fori_loop(left + 8 * eights, right, rest, 0)

    def clear():
        @pl.loop(0, own_rows // LANES)
        def _(j):
            rows = pl.ds(pl.multiple_of(j * LANES, LANES), LANES)
            even[rows, :] = jnp.zeros((LANES, block), f32)
            odd[rows, :] = jnp.zeros((LANES, block), f32)

    def turn(out, bias):
        @pl.loop(0, own_rows // LANES)
        def _(j):
            rows = pl.ds(pl.multiple_of(j * LANES, LANES), LANES)
            turned = (even[rows, :] + odd[rows, :]).T
            out[:, rows] = turned[:width]
            if bias is not None:
                bias[:, rows] = turned[width : width + 1] * n_col

    clear()
    loads[0].wait()
    add(events, events, 1, target_buf)
    loads[1].wait()
    add(2 * events, neg_count, 2, neg_buf)
    turn(out_out, bias_out)
    stores[0].start()
    stores[1].start()
    loads[2].wait()
    part = weight_out.shape[2] // n_col
    for w in range(2):
        for g in range(weight_out.shape[1]):
            for b in range(n_col):
                weight_out[w, g, b * part : (b + 1) * part, :] = grad_buf[w, g, b * block : b * block + part, 0:width]
        stores[2 + w].start()
    clear()
    loads[3].wait()
    add(0, events, 0, item_buf)
    turn(embed_out, None)
    stores[4].start()
    for store in stores:
        store.wait()


def run_finish(packed, shift, low, table_rows, own_rows, width, items, targets, negs, grads):
    events, block = items.shape
    _, gates, units, _ = grads.shape
    n_col = units // block
    hbm = pl.BlockSpec(memory_space=pl.ANY)
    weight = jax.ShapeDtypeStruct((gates, n_col * width, width), f32)
    table = jax.ShapeDtypeStruct((width, own_rows), f32)
    return pl.pallas_call(
        functools.partial(finish_kernel, shift, table_rows, width),
        out_shape=(table, table, jax.ShapeDtypeStruct((1, own_rows), f32), weight, weight),
        in_specs=[in_smem(), in_smem()] + [hbm] * 4,
        out_specs=(hbm,) * 5,
        scratch_shapes=[
            pltpu.VMEM((own_rows, block), f32),
            pltpu.VMEM((own_rows, block), f32),
            pltpu.VMEM(items.shape, f32),
            pltpu.VMEM(targets.shape, f32),
            pltpu.VMEM(negs.shape, f32),
            pltpu.VMEM(grads.shape, f32),
            pltpu.VMEM((width, own_rows), f32),
            pltpu.VMEM((width, own_rows), f32),
            pltpu.VMEM((1, own_rows), f32),
            pltpu.VMEM((2,) + weight.shape, f32),
            pltpu.SemaphoreType.DMA((9,)),
        ],
        cost_estimate=takes(40),
        compiler_params=params(),
    )(low.reshape(1), packed, items, targets, negs, grads)


def split_weight(weight, high_part, low_part):
    step = 128

    @pl.loop(0, weight.shape[0] // step)
    def _(i):
        rows = pl.ds(pl.multiple_of(i * step, step), step)
        value = weight[rows, :]
        top = value.astype(bf16)
        high_part[rows, :] = top
        low_part[rows, :] = (value - top.astype(f32)).astype(bf16)


def two_part(value):
    top = value.astype(bf16).astype(f32)
    return jnp.concatenate([top, value - top], axis=0).astype(bf16)


def forward_kernel(
    steps,
    width,
    hidden,
    entering,
    arrived,
    keep,
    prevs,
    resets,
    updates,
    cands,
    inners,
    outs,
    w_high,
    w_low,
    x_gates,
    hid_buf,
    in_buf,
    pair_buf,
    sem,
    travel=None,
):
    events, units = prevs.shape
    rows_per = arrived.shape[0] - events
    step_rows = hid_buf.shape[1]
    chunks = hidden.shape[0] // step_rows

    def load(i, slot):
        rows = pl.ds(pl.multiple_of(i * step_rows, step_rows), step_rows)
        return (
            pltpu.make_async_copy(hidden.at[rows], hid_buf.at[slot], sem.at[0, slot]),
            pltpu.make_async_copy(entering.at[rows], in_buf.at[slot], sem.at[1, slot]),
        )

    for copy in load(0, 0):
        copy.start()
    timeline = travel() if travel else ()
    pair_buf[0], pair_buf[1] = split_two(arrived[0:events, :])

    @pl.loop(0, chunks)
    def _(i):
        slot = lax.rem(i, 2)

        @pl.when(i + 1 < chunks)
        def _():
            for copy in load(i + 1, 1 - slot):
                copy.start()

        for copy in load(i, slot):
            copy.wait()
        cols = pl.ds(pl.multiple_of(i * step_rows, step_rows), step_rows)
        turned = hid_buf[slot].T
        first = turned.astype(bf16)
        w_high[:, cols] = first
        w_low[:, cols] = (turned - first.astype(f32)).astype(bf16)
        value = in_buf[slot]
        first = value.astype(bf16)
        second = (value - first.astype(f32)).astype(bf16)
        over = (((1,), (1,)), ((), ()))
        x_gates[:, cols] = (
            lax.dot_general(pair_buf[0], first, over, preferred_element_type=f32)
            + lax.dot_general(pair_buf[1], first, over, preferred_element_type=f32)
            + lax.dot_general(pair_buf[0], second, over, preferred_element_type=f32)
        )

    lane = lax.broadcasted_iota(jnp.int32, (rows_per, units), 1)

    def step(t, state):
        rows = pl.ds(pl.multiple_of(t * rows_per, rows_per), rows_per)
        prev = jnp.where(lane == width, 1.0, keep[rows, :] * state)
        pair = two_part(prev)

        def gate(g):
            cols = slice(g * units, (g + 1) * units)
            first = jnp.dot(pair, w_high[:, cols], preferred_element_type=f32)
            second = jnp.dot(pair, w_low[:, cols], preferred_element_type=f32)
            return first[:rows_per] + first[rows_per:] + second[:rows_per], cols

        h_reset, cols = gate(0)
        reset = jax.nn.sigmoid(x_gates[rows, cols] + h_reset)
        h_update, cols = gate(1)
        update = jax.nn.sigmoid(x_gates[rows, cols] + h_update)
        inner, cols = gate(2)
        cand = jnp.tanh(x_gates[rows, cols] + reset * inner)
        new = (1.0 - update) * cand + update * prev
        prevs[rows, :] = prev
        resets[rows, :] = reset
        updates[rows, :] = update
        cands[rows, :] = cand
        inners[rows, :] = inner
        outs[rows, :] = new
        return new

    state, done = arrived[events:, :], 0
    for share_done, actions in timeline:
        until = int(share_done * steps)
        if until > done:
            state, done = lax.fori_loop(done, until, step, state), until
        for action, argument in actions:
            action(argument)
    lax.fori_loop(done, steps, step, state)


def forward_travel_kernel(steps, width, hidden, entering, arrived, keep, out_rows, *refs):
    saved, (neg_all, targets), scratch = refs[:6], refs[6:8], refs[8:]
    z_rows, target_send, target_recv, target_local, row_local, row_send, row_recv = scratch[7:]
    spot = Spot()
    events = keep.shape[0]
    neg_own = out_rows.at[pl.ds(4 * events, z_rows.shape[1])]

    def target_own(z):
        return out_rows.at[pl.ds(pl.multiple_of(z * events, events), events)]

    rows = RowsFlow(spot, neg_own, z_rows, neg_all, row_local, row_send, row_recv, same=True)
    copies = []

    def begin_targets(_):
        keep_own = pltpu.make_async_copy(target_own(spot.c), targets.at[spot.c], target_local.at[0])
        keep_own.start()
        copies.append(keep_own)
        for m, z in enumerate(spot.z_to):
            copies.append(
                remote(target_own(z), targets.at[spot.c], target_send.at[m], target_recv.at[m], (spot.d, z))
            )

    def travel():
        spot.greet_all()
        rows.begin()
        return (
            (0.0, ((rows.forward, 0),)),
            (0.1, ((rows.spread, 1),)),
            (0.2, ((rows.far, 0),)),
            (0.3, ((rows.forward, 1), (rows.spread, 2), (begin_targets, None))),
            (0.4, ((rows.far, 1),)),
            (0.5, ((rows.forward, 2), (rows.spread, 3))),
            (0.6, ((rows.far, 2),)),
            (0.7, ((rows.forward, 3),)),
            (0.85, ((rows.far, 3),)),
        )

    forward_kernel(steps, width, hidden, entering, arrived, keep, *saved, *scratch[:7], travel=travel)
    rows.close()
    for copy in copies:
        copy.wait()


def forward_scratch(hidden, events):
    units = hidden.shape[1]
    step_rows = units // 4
    return [
        pltpu.VMEM(hidden.shape[::-1], bf16),
        pltpu.VMEM(hidden.shape[::-1], bf16),
        pltpu.VMEM((events, hidden.shape[0]), f32),
        pltpu.VMEM((2, step_rows, units), f32),
        pltpu.VMEM((2, step_rows, units), f32),
        pltpu.VMEM((2, events, units), bf16),
        pltpu.SemaphoreType.DMA((2, 2)),
    ]


def run_forward(hidden, entering, arrived, keep, steps, width):
    events, units = keep.shape[0], arrived.shape[1]
    saved = jax.ShapeDtypeStruct((events, units), f32)
    hbm = pl.BlockSpec(memory_space=pl.ANY)
    return pl.pallas_call(
        functools.partial(forward_kernel, steps, width),
        out_shape=(saved,) * 6,
        in_specs=[hbm, hbm] + [in_vmem()] * 2,
        out_specs=(in_vmem(),) * 6,
        scratch_shapes=forward_scratch(hidden, events),
        cost_estimate=takes(75),
        compiler_params=params(),
    )(hidden, entering, arrived, keep)


def run_forward_travel(hidden, entering, arrived, keep, out_rows, steps, width, collective_id):
    events, units = keep.shape[0], arrived.shape[1]
    block = out_rows.shape[1]
    count = out_rows.shape[0] - 4 * events
    saved = jax.ShapeDtypeStruct((events, units), f32)
    hbm = pl.BlockSpec(memory_space=pl.ANY)
    dma = pltpu.SemaphoreType.DMA
    return pl.pallas_call(
        functools.partial(forward_travel_kernel, steps, width),
        out_shape=(saved,) * 6
        + (jax.ShapeDtypeStruct((8, 4, count, block), f32), jax.ShapeDtypeStruct((4, events, block), f32)),
        in_specs=[hbm, hbm] + [in_vmem()] * 2 + [hbm],
        out_specs=(in_vmem(),) * 6 + (hbm, hbm),
        scratch_shapes=forward_scratch(hidden, events)
        + [pltpu.VMEM((4, count, block), f32), dma((3,)), dma((3,)), dma((1,)), dma((4,)), dma((4, 9)), dma((4, 9))],
        cost_estimate=takes(75),
        compiler_params=pltpu.CompilerParams(
            collective_id=collective_id, has_side_effects=True, vmem_limit_bytes=VMEM_BYTES
        ),
    )(hidden, entering, arrived, keep, out_rows)


def backward_kernel(
    steps, weight, douts, keep, prevs, resets, updates, cands, inners, dgates, dstart, w_high, w_low
):
    rows_per, units = dstart.shape
    split_weight(weight, w_high, w_low)

    def step(i, dstate):
        t = steps - 1 - i
        rows = pl.ds(pl.multiple_of(t * rows_per, rows_per), rows_per)
        reset, update, cand = resets[rows, :], updates[rows, :], cands[rows, :]
        dh = douts[rows, :] + dstate
        dcand = dh * (1.0 - update) * (1.0 - cand * cand)
        dreset = dcand * inners[rows, :] * reset * (1.0 - reset)
        dupdate = dh * (prevs[rows, :] - cand) * update * (1.0 - update)
        dinner = dcand * reset
        dgates[rows, 0:units] = dreset
        dgates[rows, units : 2 * units] = dupdate
        dgates[rows, 2 * units : 3 * units] = dinner
        dgates[rows, 3 * units : 4 * units] = dcand
        total = dh * update
        for g, part in enumerate((dreset, dupdate, dinner)):
            pair = two_part(part)
            sect = slice(g * units, (g + 1) * units)
            first = jnp.dot(pair, w_high[sect, :], preferred_element_type=f32)
            second = jnp.dot(pair, w_low[sect, :], preferred_element_type=f32)
            total = total + (first[:rows_per] + first[rows_per:] + second[:rows_per])
        return keep[rows, :] * total

    dstart[...] = lax.fori_loop(0, steps, step, jnp.zeros((rows_per, units), f32))


def run_backward(weight, douts, keep, saved, rows_per, steps):
    events, units = douts.shape
    return pl.pallas_call(
        functools.partial(backward_kernel, steps),
        out_shape=(
            jax.ShapeDtypeStruct((events, 4 * units), f32),
            jax.ShapeDtypeStruct((rows_per, units), f32),
        ),
        in_specs=[in_vmem()] * 8,
        out_specs=(in_vmem(),) * 2,
        scratch_shapes=[pltpu.VMEM(weight.shape, bf16)] * 2,
        cost_estimate=takes(67),
        compiler_params=params(),
    )(weight, douts, keep, *saved)


def place():
    d = lax.axis_index("dp")
    c = lax.axis_index("col")
    return d // 4, (d // 2) % 2, d % 2, c, d


def greet(partners):
    barrier = pltpu.get_barrier_semaphore()
    for partner in partners:
        pl.semaphore_signal(barrier, inc=1, device_id=partner, device_id_type=MESH)
    pl.semaphore_wait(barrier, len(partners))


class Spot:
    def __init__(self):
        self.y, self.x, self.k, self.c, self.d = place()
        y, x, k, c, d = self.y, self.x, self.k, self.c, self.d
        self.x_d, self.y_d, self.core_d = d + 2 - 4 * x, d + 4 - 8 * y, d + 1 - 2 * k
        self.far_d = d + 6 - 4 * x - 8 * y
        self.core_to, self.x_to, self.y_to, self.far_to = (self.core_d, c), (self.x_d, c), (self.y_d, c), (self.far_d, c)
        self.z_to = (c + 1 - 2 * lax.rem(c, 2), lax.rem(c + 2, 4), 3 - c)

    def greet_all(self):
        greet([self.core_to, self.x_to, self.y_to, self.far_to] + [(self.d, z) for z in self.z_to])


def remote(source, target, send, recv, to):
    copy = pltpu.make_async_remote_copy(
        src_ref=source, dst_ref=target, send_sem=send, recv_sem=recv, device_id=to, device_id_type=MESH
    )
    copy.start()
    return copy


class RowsFlow:
    def __init__(self, spot, outgoing, z_rows, every, local_sem, send_sem, recv_sem, same=False):
        self.spot, self.outgoing, self.z_rows, self.every = spot, outgoing, z_rows, every
        self.local_sem, self.send_sem, self.recv_sem = local_sem, send_sem, recv_sem
        self.started = {}
        self.rows = every.shape[2]
        self.sources = (spot.c,) + spot.z_to
        self.same = same

    def send(self, u, slot, source, target, to):
        return remote(source, target, self.send_sem.at[u, slot], self.recv_sem.at[u, slot], to)

    def begin(self):
        spot = self.spot
        for m in range(3):
            z = spot.z_to[m]
            source = self.outgoing if self.same else self.outgoing.at[z]
            self.started["z", m] = self.send(1 + m, 0, source, self.z_rows.at[spot.c], (spot.d, z))
        self.spread(0)

    def spread(self, u):
        spot, src = self.spot, self.sources[u]
        if u > 0:
            self.started["z", u - 1].wait_recv()
            source = self.z_rows.at[src, 0 : self.rows]
        else:
            source = self.outgoing if self.same else self.outgoing.at[src, 0 : self.rows]
        target = self.every.at[spot.d, src]
        keep = pltpu.make_async_copy(source, target, self.local_sem.at[u])
        keep.start()
        self.started["keep", u] = keep
        for slot, (name, to) in enumerate((("x", spot.x_to), ("y", spot.y_to), ("c", spot.core_to))):
            self.started[name, u] = self.send(u, 1 + slot, source, target, to)

    def forward(self, u):
        spot, src, mid = self.spot, self.sources[u], self.rows // 2
        self.started["x", u].wait_recv()
        piece = self.every.at[spot.x_d, src, 0:mid]
        self.started["xy", u] = self.send(u, 4, piece, piece, spot.y_to)
        piece = self.every.at[spot.x_d, src]
        self.started["xc", u] = self.send(u, 5, piece, piece, spot.core_to)
        self.started["y", u].wait_recv()
        piece = self.every.at[spot.y_d, src, mid : self.rows]
        self.started["yx", u] = self.send(u, 6, piece, piece, spot.x_to)
        piece = self.every.at[spot.y_d, src]
        self.started["yc", u] = self.send(u, 7, piece, piece, spot.core_to)

    def far(self, u):
        spot, src = self.spot, self.sources[u]
        self.started["xy", u].wait_recv()
        self.started["yx", u].wait_recv()
        piece = self.every.at[spot.far_d, src]
        self.started["fc", u] = self.send(u, 8, piece, piece, spot.core_to)

    def close(self):
        for u in range(4):
            for name in ("c", "xc", "yc", "fc"):
                self.started[name, u].wait_recv()
            self.started["keep", u].wait()
        for (name, _), copy in self.started.items():
            if name != "keep":
                copy.wait_send()


class SumFlow:
    def __init__(self, spot, mine, core_in, x_in, y_in, xy_in, yx_in, z_in, total, out_at, local_sem, send_sem, recv_sem):
        self.spot, self.mine, self.core_in, self.out_at = spot, mine, core_in, out_at
        self.x_in, self.y_in, self.xy_in, self.yx_in, self.z_in, self.total = x_in, y_in, xy_in, yx_in, z_in, total
        self.local_sem, self.send_sem, self.recv_sem = local_sem, send_sem, recv_sem
        self.started = [{} for _ in range(mine.shape[0])]
        self.half = mine.shape[4] // 2

    def send(self, j, slot, source, target, to):
        return remote(source, target, self.send_sem.at[j, slot], self.recv_sem.at[j, slot], to)

    def over_core(self, j, source):
        self.started[j]["core"] = self.send(j, 0, source, self.core_in.at[j], self.spot.core_to)

    def core(self, j):
        spot, mine, half, started = self.spot, self.mine, self.half, self.started[j]
        started["core"].wait_recv()

        @pl.loop(0, 4)
        def _(a):
            for b in range(2):
                for e in range(2):
                    mine[j, a, b, e] = mine[j, a, b, e] + self.core_in[j, a, b, e]

        started["x"] = self.send(j, 1, mine.at[j, :, :, 1 - spot.x, 0:half], self.x_in.at[j], spot.x_to)
        started["y"] = self.send(j, 2, mine.at[j, :, 1 - spot.y, :, half : 2 * half], self.y_in.at[j], spot.y_to)

    def first(self, j):
        spot, mine, half, started = self.spot, self.mine, self.half, self.started[j]
        x, y = spot.x, spot.y
        started["x"].wait_recv()
        for a in range(4):
            for b in range(2):
                mine[j, a, b, x, 0:half] = mine[j, a, b, x, 0:half] + self.x_in[j, a, b]
        started["xy"] = self.send(j, 3, mine.at[j, :, 1 - y, x, 0:half], self.xy_in.at[j], spot.y_to)
        started["y"].wait_recv()
        for a in range(4):
            for e in range(2):
                mine[j, a, y, e, half : 2 * half] = mine[j, a, y, e, half : 2 * half] + self.y_in[j, a, e]
        started["yx"] = self.send(j, 4, mine.at[j, :, y, 1 - x, half : 2 * half], self.yx_in.at[j], spot.x_to)

    def second(self, j):
        spot, mine, half, started = self.spot, self.mine, self.half, self.started[j]
        x, y = spot.x, spot.y
        started["xy"].wait_recv()
        started["yx"].wait_recv()
        for a in range(4):
            mine[j, a, y, x, 0:half] = mine[j, a, y, x, 0:half] + self.xy_in[j, a]
            mine[j, a, y, x, half : 2 * half] = mine[j, a, y, x, half : 2 * half] + self.yx_in[j, a]
        for m in range(3):
            z = spot.z_to[m]
            started["z", m] = self.send(j, 5 + m, mine.at[j, z, y, x], self.z_in.at[j, m], (spot.d, z))

    def along(self, j):
        spot, started, total = self.spot, self.started[j], self.total
        for m in range(3):
            started["z", m].wait_recv()
        own = self.mine[j, spot.c, spot.y, spot.x]
        total[j] = ((own + self.z_in[j, 0]) + self.z_in[j, 1]) + self.z_in[j, 2]
        target = self.out_at(j, spot.d, 0, 2 * self.half)
        started["keep"] = pltpu.make_async_copy(total.at[j], target, self.local_sem.at[j])
        started["keep"].start()
        for slot, (name, to) in enumerate((("gx", spot.x_to), ("gy", spot.y_to), ("gc", spot.core_to))):
            started[name] = self.send(j, 8 + slot, total.at[j], target, to)

    def share(self, j):
        spot, started, half = self.spot, self.started[j], self.half
        started["gx"].wait_recv()
        piece = self.out_at(j, spot.x_d, 0, half)
        started["gxy"] = self.send(j, 11, piece, piece, spot.y_to)
        piece = self.out_at(j, spot.x_d, 0, 2 * half)
        started["cgx"] = self.send(j, 12, piece, piece, spot.core_to)
        started["gy"].wait_recv()
        piece = self.out_at(j, spot.y_d, half, half)
        started["gyx"] = self.send(j, 13, piece, piece, spot.x_to)
        piece = self.out_at(j, spot.y_d, 0, 2 * half)
        started["cgy"] = self.send(j, 14, piece, piece, spot.core_to)

    def far(self, j):
        spot, started = self.spot, self.started[j]
        started["gxy"].wait_recv()
        started["gyx"].wait_recv()
        piece = self.out_at(j, spot.far_d, 0, 2 * self.half)
        started["cgf"] = self.send(j, 15, piece, piece, spot.core_to)

    def end(self, j, core_sent=False):
        started = self.started[j]
        for name in ("gc", "cgx", "cgy", "cgf"):
            started[name].wait_recv()
        for name, copy in started.items():
            if name == "keep":
                copy.wait()
            elif not (name == "core" and core_sent):
                copy.wait_send()


def sum_scratch(jobs, piece, lanes):
    half = piece // 2
    return [
        pltpu.VMEM((jobs, 4, 2, 2, piece, lanes), f32),
        pltpu.VMEM((jobs, 4, 2, 2, piece, lanes), f32),
        pltpu.VMEM((jobs, 4, 2, half, lanes), f32),
        pltpu.VMEM((jobs, 4, 2, half, lanes), f32),
        pltpu.VMEM((jobs, 4, half, lanes), f32),
        pltpu.VMEM((jobs, 4, half, lanes), f32),
        pltpu.VMEM((jobs, 3, piece, lanes), f32),
        pltpu.VMEM((jobs, piece, lanes), f32),
    ]


def flow_sems(jobs):
    dma = pltpu.SemaphoreType.DMA
    return [dma((jobs,)), dma((jobs, 16)), dma((jobs, 16)), dma((4,)), dma((4, 9)), dma((4, 9))]


GATE_OF = ((0, 1, 3), (0, 1, 2))


def split_two(value):
    top = value.astype(bf16)
    return top, (value - top.astype(f32)).astype(bf16)


def three_products(first, second, over):
    def product(a, b):
        return lax.dot_general(a, b, (over, ((), ())), preferred_element_type=f32)

    return product(first[0], second[0]) + product(first[1], second[0]) + product(first[0], second[1])


def tail_kernel(
    inputs,
    prevs,
    dgates,
    dstart,
    entering,
    out,
    item_all,
    start_all,
    mine,
    core_in,
    x_in,
    y_in,
    xy_in,
    yx_in,
    z_in,
    total,
    core_out,
    turned,
    gate_pair,
    flow,
    w_flow,
    din,
    z_rows,
    flow_sem,
    start_sem,
    sum_local,
    sum_send,
    sum_recv,
    row_local,
    row_send,
    row_recv,
):
    spot = Spot()
    spot.greet_all()
    c, k = spot.c, spot.k
    jobs, piece = mine.shape[0], mine.shape[4]
    events, units = gate_pair.shape[2:]
    block = din.shape[2]
    gates = jobs // 2
    sums = SumFlow(
        spot, mine, core_in, x_in, y_in, xy_in, yx_in, z_in, total,
        lambda j, d, at, size: out.at[j // gates, j % gates, d, pl.ds(at, size)], sum_local, sum_send, sum_recv,
    )
    rows = RowsFlow(spot, din, z_rows, item_all, row_local, row_send, row_recv)

    def gate_cols(g):
        return dgates.at[:, pl.ds(g * units, units)]

    queue = [inputs.at[pl.ds(0, events)], gate_cols(0), gate_cols(1), gate_cols(3), prevs, gate_cols(2)]

    def flow_copy(n):
        return pltpu.make_async_copy(queue[n], flow.at[n % 2], flow_sem.at[n % 2])

    def w_copy(n, slot):
        rows = pl.ds(pl.multiple_of(n * block, block), block)
        return pltpu.make_async_copy(entering.at[rows], w_flow.at[slot], flow_sem.at[2 + slot])

    flow_copy(0).start()
    flow_copy(1).start()
    w_copy(0, 0).start()

    def next_flow(n):
        if n + 2 < len(queue):
            flow_copy(n + 2).start()

    def take_act(n, w):
        flow_copy(n).wait()

        @pl.loop(0, 4)
        def _(b):
            cols = pl.ds(pl.multiple_of(b * block, block), block)
            turned[w, 0, b], turned[w, 1, b] = split_two(flow[n % 2, :, cols].T)

        next_flow(n)

    def take_gate(n, g, at):
        flow_copy(n).wait()

        @pl.loop(0, 4)
        def _(b):
            cols = pl.ds(pl.multiple_of(b * block, block), block)
            value = flow[n % 2, :, cols]
            gate_pair[g, 0, :, cols], gate_pair[g, 1, :, cols] = split_two(value)
            if at is not None:
                chunk = 4 * at + b
                slot = lax.rem(b, 2)

                @pl.when(chunk + 1 < 12)
                def _():
                    w_copy(chunk + 1, 1 - slot).start()

                w_copy(chunk, slot).wait()
                share = three_products(split_two(value), split_two(w_flow[slot]), ((1,), (0,)))
                for e in range(4):
                    part = share[:, e * block : (e + 1) * block]
                    if at == 0:
                        before = jnp.where(b == 0, 0.0, din[e, 0:events, :])
                    else:
                        before = din[e, 0:events, :]
                    din[e, 0:events, :] = before + part

        next_flow(n)

    def rows_begin():
        for e in range(4):
            din[e, events:, :] = dstart[:, e * block : (e + 1) * block]
        rows.begin()

    def rows_end():
        keeps = [
            pltpu.make_async_copy(din.at[c, events:], start_all.at[c], start_sem.at[0]),
        ] + [
            pltpu.make_async_copy(z_rows.at[z, events:], start_all.at[z], start_sem.at[1 + m])
            for m, z in enumerate(spot.z_to)
        ]
        for keep in keeps:
            keep.start()
        rows.close()
        for keep in keeps:
            keep.wait()

    def partial(j):
        w, g = j // gates, GATE_OF[j // gates][j % gates]
        slot = j % 2
        if j >= 2:
            sums.started[j - 2]["core"].wait_send()

        @pl.loop(0, 2)
        def _(p):
            for q in range(2):
                b = 2 * p + q
                value = three_products(
                    (turned[w, 0, b], turned[w, 1, b]), (gate_pair[g, 0], gate_pair[g, 1]), ((1,), (0,))
                )
                for e in range(4):
                    cols = slice(e * block, (e + 1) * block)
                    first, second = value[:piece, cols], value[piece:, cols]
                    mine[j, e, p, q] = jnp.where(k == 0, first, second)
                    core_out[slot, e, p, q] = jnp.where(k == 0, second, first)

        sums.over_core(j, core_out.at[slot])

    A, B, C, Z, S, F = sums.core, sums.first, sums.second, sums.along, sums.share, sums.far

    def E(j):
        sums.end(j, core_sent=j < jobs - 2)

    take_act(0, 0)
    take_gate(1, 0, 0)
    partial(0)
    take_gate(2, 1, 1)
    partial(1)
    A(0)
    take_gate(3, 3, 2)
    rows_begin()
    partial(2)
    A(1)
    take_act(4, 1)
    partial(3)
    A(2), B(0), rows.spread(1), rows.forward(0)
    partial(4)
    A(3), B(1), C(0), rows.spread(2), rows.forward(1), rows.far(0)
    take_gate(5, 2, None)
    partial(5)
    A(4), B(2), C(1), Z(0), rows.spread(3), rows.forward(2), rows.far(1)
    A(5), B(3), C(2), Z(1), S(0), rows.forward(3), rows.far(2)
    B(4), C(3), Z(2), S(1), F(0), rows.far(3)
    B(5), C(4), Z(3), S(2), F(1), E(0)
    C(5), Z(4), S(3), F(2), E(1)
    rows_end()
    Z(5), S(4), F(3), E(2)
    S(5), F(4), E(3)
    F(5), E(4), E(5)


def run_tail(inputs, prevs, dgates, dstart, entering, collective_id):
    events, units = prevs.shape
    gates, block = 3, units // 4
    piece = units // 8
    jobs = 2 * gates
    start_rows = dstart.shape[0]
    hbm = pl.BlockSpec(memory_space=pl.ANY)
    grads, item_all, start_all = pl.pallas_call(
        tail_kernel,
        out_shape=(
            jax.ShapeDtypeStruct((2, gates, 8, piece, block), f32),
            jax.ShapeDtypeStruct((8, 4, events, block), f32),
            jax.ShapeDtypeStruct((4, start_rows, block), f32),
        ),
        in_specs=[hbm, hbm, hbm, pl.BlockSpec(memory_space=pltpu.VMEM), hbm],
        out_specs=(hbm, hbm, hbm),
        scratch_shapes=sum_scratch(jobs, piece, block)
        + [
            pltpu.VMEM((2, 4, 2, 2, piece, block), f32),
            pltpu.VMEM((2, 2, 4, block, events), bf16),
            pltpu.VMEM((4, 2, events, units), bf16),
            pltpu.VMEM((2, events, units), f32),
            pltpu.VMEM((2, block, units), f32),
            pltpu.VMEM((4, events + start_rows, block), f32),
            pltpu.VMEM((4, events + start_rows, block), f32),
            pltpu.SemaphoreType.DMA((4,)),
            pltpu.SemaphoreType.DMA((4,)),
        ]
        + flow_sems(jobs),
        cost_estimate=takes(190),
        compiler_params=pltpu.CompilerParams(
            collective_id=collective_id, has_side_effects=True, vmem_limit_bytes=VMEM_BYTES
        ),
    )(inputs, prevs, dgates, dstart, entering)
    return grads.reshape(2, gates, units, block), item_all, start_all


HEAD_TIMES = ((8, 14, 28, 42), (10, 22, 32, 44, 56, 68), 12, 20, 58)
UNITS = ((0, 0), (0, 1), (1, 0), (0, 2), (1, 1), (1, 2))


def head_kernel(
    chunk,
    width,
    flat_ids,
    negative_ids,
    embed,
    table,
    bias,
    w_in,
    w_hid,
    in_bias,
    hid_bias,
    carried,
    own_ids,
    all_in,
    all_hid,
    arrived,
    all_ids,
    out_rows,
    padded,
    turned,
    item_rows,
    held,
    w_buf,
    local_sem,
    send_sem,
    recv_sem,
    row_send,
    row_recv,
    id_send,
    id_recv,
):
    y, x, k, c, d = place()
    i = pl.program_id(0)
    n = pl.num_programs(0) // 2
    core_to, x_to, y_to = (d + 1 - 2 * k, c), (d + 2 - 4 * x, c), (d + 4 - 8 * y, c)
    z_all = (c + 1 - 2 * lax.rem(c, 2), lax.rem(c + 2, 4), 3 - c)
    alls = (all_in, all_hid)
    gates, piece, units = held.shape[1], held.shape[5], held.shape[6]
    half = piece // 2
    block = item_rows.shape[2]
    items = item_rows.shape[1]
    carried_rows = carried.shape[1]
    events = items - carried_rows

    def send(u, slot):
        w, m = UNITS[u]
        z = z_all[m]
        every = alls[w]
        if slot == 0:
            source, target, to = held.at[w, :, y, x, k], every.at[:, c, y, x, k], (d, z)
        elif slot in (4, 6):
            spot = (
                every.at[:, z, y, 1 - x, k, 0:half] if slot == 4 else every.at[:, z, 1 - y, x, k, half : 2 * half]
            )
            source, target, to = spot, spot, (y_to if slot == 4 else x_to)
        else:
            py, px, to = {
                1: (y, x, x_to),
                2: (y, x, y_to),
                3: (y, x, core_to),
                5: (y, 1 - x, core_to),
                7: (1 - y, x, core_to),
                8: (1 - y, 1 - x, core_to),
            }[slot]
            spot = every.at[:, z, py, px, k]
            source, target = spot, spot
        return pltpu.make_async_remote_copy(
            src_ref=source,
            dst_ref=target,
            send_sem=send_sem.at[u, slot],
            recv_sem=recv_sem.at[u, slot],
            device_id=to,
            device_id_type=MESH,
        )

    def load(w):
        return pltpu.make_async_copy((w_in, w_hid)[w], w_buf.at[w], local_sem.at[w])

    def keep(w):
        return pltpu.make_async_copy(held.at[w], alls[w].at[:, c], local_sem.at[2 + w])

    def pad(w):
        load(w).wait()
        part, own = units // block, w_buf.shape[3]
        inner = w_buf.shape[2] // part
        for g in range(gates):
            for b in range(part):
                turned[b * block : b * block + inner, 0:own] = w_buf[w, g, b * inner : (b + 1) * inner, :]
            turned[inner : inner + 1, 0:own] = (in_bias, hid_bias)[w][g : g + 1, :]
            held[w, g] = turned[0:units, :].T.reshape(2, 2, 2, piece, units)
        keep(w).start()

    def item_send(m):
        return pltpu.make_async_remote_copy(
            src_ref=item_rows.at[z_all[m]],
            dst_ref=arrived.at[:, pl.ds(pl.multiple_of(c * block, block), block)],
            send_sem=row_send.at[m],
            recv_sem=row_recv.at[m],
            device_id=(d, z_all[m]),
            device_id_type=MESH,
        )

    def begin_items(_):
        for m in range(3):
            item_send(m).start()

    def item_keep():
        return pltpu.make_async_copy(
            item_rows.at[c], arrived.at[:, pl.ds(pl.multiple_of(c * block, block), block)], local_sem.at[4]
        )

    def id_copy(m):
        to = lax.rem(d + 1 + m, 8)
        return pltpu.make_async_remote_copy(
            src_ref=own_ids,
            dst_ref=all_ids.at[d],
            send_sem=id_send.at[m],
            recv_sem=id_recv.at[m],
            device_id=(to, c),
            device_id_type=MESH,
        )

    def id_keep():
        return pltpu.make_async_copy(own_ids, all_ids.at[d], local_sem.at[5])

    def begin():
        load(0).start()
        load(1).start()
        greet([(lax.rem(d + 1 + m, 8), c) for m in range(7)] + [(d, z) for z in z_all])
        id_keep().start()
        for m in range(7):
            id_copy(m).start()
        turned[0:units, :] = jnp.zeros((units, block), f32)
        pad(0)
        begin_z(0)
        begin_z(1)
        pad(1)

    def begin_z(u):
        send(u, 0).start()

    def spread(u):
        send(u, 0).wait_recv()
        for slot in (1, 2, 3):
            send(u, slot).start()

    def forward(u):
        send(u, 1).wait_recv()
        send(u, 4).start()
        send(u, 5).start()
        send(u, 2).wait_recv()
        send(u, 6).start()
        send(u, 7).start()

    def far(u):
        send(u, 4).wait_recv()
        send(u, 6).wait_recv()
        send(u, 8).start()

    def close(u):
        for slot in (3, 5, 7, 8):
            send(u, slot).wait_recv()
        for slot in range(9):
            send(u, slot).wait_send()

    z_at, spread_at, forward_by, far_by, items_at = HEAD_TIMES
    timeline = [(-1, begin, None), (items_at, begin_items, 0)]
    timeline += [(at, begin_z, 2 + j) for j, at in enumerate(z_at)]
    for u, at in enumerate(spread_at):
        timeline += [(at, spread, u), (at + forward_by, forward, u), (at + far_by, far, u)]
    timeline.sort(key=lambda entry: entry[0])
    last = 2 * n - 1

    @pl.when(i == 0)
    def _():
        padded[...] = jnp.zeros_like(padded)
        padded[width : width + 1, :] = jnp.full((1, chunk), jnp.where(c == 0, 1.0, 0.0), f32)

    for at, action, u in timeline:
        if at < last:

            @pl.when(i == max(at, 0))
            def _(action=action, u=u):
                action() if u is None else action(u)

    @pl.when(i < n)
    def _():
        padded[0:width, :] = embed[...]

    @pl.when(i >= n)
    def _():
        padded[0:width, :] = table[...]
        padded[width : width + 1, :] = bias[...]

    spot = lax.rem(i, n) * chunk
    turned[pl.ds(pl.multiple_of(spot, chunk), chunk), :] = padded[...].T

    @pl.when(i == n - 1)
    def _():
        for z in range(4):

            def body(b, carry, z=z):
                for j in range(8):
                    row = flat_ids[z * events + b * 8 + j]
                    item_rows[z, pl.ds(b * 8 + j, 1), :] = turned[pl.ds(row, 1), :]
                return carry

            lax.fori_loop(0, events // 8, body, 0)
            item_rows[z, events:items, :] = carried[z]
        item_keep().start()

    @pl.when(i == last)
    def _():
        targets = 4 * events
        count = out_rows.shape[0] - targets

        def target_body(b, carry):
            for j in range(8):
                row = flat_ids[targets + b * 8 + j]
                out_rows[pl.ds(b * 8 + j, 1), :] = turned[pl.ds(row, 1), :]
            return carry

        def neg_body(b, carry):
            for j in range(8):
                row = negative_ids[d * count + b * 8 + j]
                out_rows[pl.ds(targets + b * 8 + j, 1), :] = turned[pl.ds(row, 1), :]
            return carry

        lax.fori_loop(0, targets // 8, target_body, 0)
        lax.fori_loop(0, count // 8, neg_body, 0)
        for at, action, u in timeline:
            if at >= last:
                action(u)
        for u in range(6):
            close(u)
        for m in range(3):
            item_send(m).wait()
        for m in range(7):
            id_copy(m).wait()
        id_keep().wait()
        for w in range(2):
            keep(w).wait()
        item_keep().wait()


def gather_all(embed, table, bias, flat_ids, negative_ids, w_in, w_hid, in_bias, hid_bias, carried, own_ids, collective_id):
    width, rows = embed.shape
    gates, block = w_in.shape[0], carried.shape[2]
    units = 4 * block
    piece = block // 8
    chunk = 128 * max(k for k in range(1, 9) if rows % (128 * k) == 0)
    n = rows // chunk
    items = flat_ids.shape[0] // 8 + carried.shape[1]
    out_count = flat_ids.shape[0] // 2 + negative_ids.shape[0] // 8
    own_shape = (gates, 2, 2, 2, piece, units)
    all_shape = (gates, 4, 2, 2, 2, piece, units)
    smem = pl.BlockSpec(memory_space=pltpu.SMEM)
    hbm = pl.BlockSpec(memory_space=pl.ANY)
    all_in, all_hid, arrived, all_ids, out_rows = pl.pallas_call(
        functools.partial(head_kernel, chunk, width),
        out_shape=(
            jax.ShapeDtypeStruct(all_shape, f32),
            jax.ShapeDtypeStruct(all_shape, f32),
            jax.ShapeDtypeStruct((items, units), f32),
            jax.ShapeDtypeStruct((8,) + own_ids.shape, jnp.int32),
            jax.ShapeDtypeStruct((out_count, block), f32),
        ),
        grid=(2 * n,),
        in_specs=[
            smem,
            smem,
            pl.BlockSpec((width, chunk), lambda i: (0, jnp.minimum(i, n - 1))),
            pl.BlockSpec((width, chunk), lambda i: (0, jnp.maximum(i - n, 0))),
            pl.BlockSpec((1, chunk), lambda i: (0, jnp.maximum(i - n, 0))),
            hbm,
            hbm,
            pl.BlockSpec(in_bias.shape, lambda i: (0, 0)),
            pl.BlockSpec(hid_bias.shape, lambda i: (0, 0)),
            pl.BlockSpec(carried.shape, lambda i: (0, 0, 0)),
            pl.BlockSpec(own_ids.shape, lambda i: (0, 0)),
        ],
        out_specs=(hbm, hbm, hbm, hbm, pl.BlockSpec((out_count, block), lambda i: (0, 0))),
        scratch_shapes=[
            pltpu.VMEM((block, chunk), f32),
            pltpu.VMEM((rows, block), f32),
            pltpu.VMEM((4, items, block), f32),
            pltpu.VMEM((2,) + own_shape, f32),
            pltpu.VMEM((2,) + w_in.shape, f32),
            pltpu.SemaphoreType.DMA((6,)),
            pltpu.SemaphoreType.DMA((6, 9)),
            pltpu.SemaphoreType.DMA((6, 9)),
            pltpu.SemaphoreType.DMA((3,)),
            pltpu.SemaphoreType.DMA((3,)),
            pltpu.SemaphoreType.DMA((7,)),
            pltpu.SemaphoreType.DMA((7,)),
        ],
        cost_estimate=takes(120),
        compiler_params=pltpu.CompilerParams(
            collective_id=collective_id, has_side_effects=True, vmem_limit_bytes=VMEM_BYTES
        ),
    )(flat_ids, negative_ids, embed, table, bias, w_in, w_hid, in_bias, hid_bias, carried, own_ids)
    return (
        all_in.reshape(gates, 4 * block, units),
        all_hid.reshape(gates, 4 * block, units),
        arrived,
        all_ids,
        out_rows,
    )


def back_kernel(
    steps,
    width,
    factor,
    hidden,
    outs,
    targets,
    negs,
    keep,
    prevs,
    resets,
    updates,
    cands,
    inners,
    dgates,
    dstart,
    neg_all,
    target_all,
    loss_all,
    halves,
    core_in,
    x_in,
    y_in,
    xy_in,
    yx_in,
    z_in,
    total,
    w_high,
    w_low,
    w_flow,
    z_rows,
    share,
    pairs,
    score,
    neg_flow,
    target_part,
    douts,
    own_loss,
    flow_sem,
    neg_sem,
    loss_sem,
    loss_send,
    loss_recv,
    sum_local,
    sum_send,
    sum_recv,
    row_local,
    row_send,
    row_recv,
):
    spot = Spot()
    spot.greet_all()
    rows_per, units = dstart.shape
    mine, core_out = halves.at[0], halves.at[1]
    jobs, piece = halves.shape[1], halves.shape[5]
    step_rows = w_flow.shape[1]
    chunks = hidden.shape[0] // step_rows
    n_col, events, block = targets.shape
    n_dp, _, count, _ = negs.shape
    sums = SumFlow(
        spot, mine, core_in, x_in, y_in, xy_in, yx_in, z_in, total,
        lambda j, d, at, size: neg_all.at[d, pl.ds(j * piece + at, size)], sum_local, sum_send, sum_recv,
    )
    rows = RowsFlow(spot, target_part, z_rows, target_all, row_local, row_send, row_recv)

    def load(i, slot):
        part = pl.ds(pl.multiple_of(i * step_rows, step_rows), step_rows)
        return pltpu.make_async_copy(hidden.at[part], w_flow.at[slot], flow_sem.at[slot])

    def split_chunk(i):
        slot = lax.rem(i, 2)

        @pl.when(i + 1 < chunks)
        def _():
            load(i + 1, 1 - slot).start()

        load(i, slot).wait()
        part = pl.ds(pl.multiple_of(i * step_rows, step_rows), step_rows)
        w_high[part, :], w_low[part, :] = split_two(w_flow[slot])

    def load_neg(b, slot):
        return pltpu.make_async_copy(negs.at[b], neg_flow.at[slot], neg_sem.at[slot])

    load_neg(0, 0).start()
    load(0, 0).start()
    lane = lax.broadcasted_iota(jnp.int32, (events, block), 1)
    for c in range(n_col):
        value = jnp.where(lane < width, outs[:, c * block : (c + 1) * block], 0.0)
        value = jnp.where(lane == width, 1.0 / n_col, value)
        share[c] = value
        pairs[0, c], pairs[1, c] = split_two(value)

    @pl.loop(0, n_dp)
    def _(b):
        slot = lax.rem(b, 2)
        load_neg(lax.rem(b + 1, n_dp), 1 - slot).start()
        load_neg(b, slot).wait()
        value = jnp.zeros((events, count), f32)
        for c in range(n_col):
            value = value + three_products((pairs[0, c], pairs[1, c]), split_two(neg_flow[slot, c]), ((1,), (1,)))
        score[:, pl.ds(pl.multiple_of(b * count, count), count)] = value
        split_chunk(b)

    part_steps = 4
    step_lane = lax.broadcasted_iota(jnp.int32, (rows_per, LANES), 1)

    def events_part(i, losses):
        size = part_steps * rows_per
        now = pl.ds(pl.multiple_of(i * size, size), size)
        pos = jnp.zeros((size, 1), f32)
        for c in range(n_col):
            pos = pos + jnp.sum(share[c, now, :] * targets[c, now, :], axis=-1, keepdims=True)
        neg = score[now, :]
        expd = jnp.exp(neg - jnp.max(neg, axis=-1, keepdims=True))
        weight = expd * (1.0 / jnp.sum(expd, axis=-1, keepdims=True))
        sig = jax.nn.sigmoid(pos - neg)
        slope = weight * sig
        ppos = jnp.sum(slope, axis=-1, keepdims=True)
        quad = jnp.sum(weight * neg * neg, axis=-1, keepdims=True)
        slope = jnp.sum(slope * (1.0 - sig), axis=-1, keepdims=True)
        value = quad - jnp.log(ppos)
        for q in range(part_steps):
            losses = jnp.where(step_lane == part_steps * i + q, value[q * rows_per : (q + 1) * rows_per], losses)
        score[now, :] = factor * weight * (1.0 - sig * sig * (1.0 / ppos) + neg * neg + 2.0 * neg - quad)
        dpos = -factor * slope / ppos
        for c in range(n_col):
            target_part[c, now, :] = dpos * share[c, now, :]
            douts[now, c * block : (c + 1) * block] = dpos * targets[c, now, :]
        return losses

    own_loss[...] = lax.fori_loop(0, steps // part_steps, events_part, jnp.zeros((rows_per, LANES), f32))
    rows.begin()
    losses = [pltpu.make_async_copy(own_loss, loss_all.at[spot.c], loss_sem.at[0])]
    losses[0].start()
    for m, z in enumerate(spot.z_to):
        losses.append(remote(own_loss, loss_all.at[spot.c], loss_send.at[m], loss_recv.at[m], (spot.d, z)))

    def neg_block(p, q, core, j):
        b = 4 * p + 2 * q + core
        dneg = score[:, pl.ds(pl.multiple_of(b * count, count), count)]
        down = split_two(dneg[:, j * piece : (j + 1) * piece].T)
        which = lax.rem(core + spot.k, 2)
        for c in range(n_col):
            halves[which, j, c, p, q] = three_products(down, (pairs[0, c], pairs[1, c]), ((1,), (0,)))
        return b, dneg

    @pl.loop(0, 2)
    def _(p):
        for q in range(2):
            for core in range(2):
                neg_block(p, q, core, 0)
            split_chunk(n_dp + 2 * p + q)

    sums.over_core(0, core_out.at[0])

    @pl.loop(0, 2)
    def _(p):
        for q in range(2):
            for core in range(2):
                b, dneg = neg_block(p, q, core, 1)
                if q == 1 and core == 1:

                    @pl.when(p == 0)
                    def _():
                        load_neg(b + 1, 0).start()

                else:
                    load_neg(b + 1, 1 - core).start()
                load_neg(b, core).wait()
                across = split_two(dneg)
                for c in range(n_col):
                    cols = slice(c * block, (c + 1) * block)
                    douts[:, cols] = douts[:, cols] + three_products(across, split_two(neg_flow[core, c]), ((1,), (0,)))

    sums.over_core(1, core_out.at[1])
    for c in range(n_col):
        cols = slice(c * block, (c + 1) * block)
        douts[:, cols] = jnp.where(lane < width, douts[:, cols], 0.0)

    def step(i, dstate):
        t = steps - 1 - i
        now = pl.ds(pl.multiple_of(t * rows_per, rows_per), rows_per)
        reset, update, cand = resets[now, :], updates[now, :], cands[now, :]
        dh = douts[now, :] + dstate
        dcand = dh * (1.0 - update) * (1.0 - cand * cand)
        dreset = dcand * inners[now, :] * reset * (1.0 - reset)
        dupdate = dh * (prevs[now, :] - cand) * update * (1.0 - update)
        dinner = dcand * reset
        dgates[now, 0:units] = dreset
        dgates[now, units : 2 * units] = dupdate
        dgates[now, 2 * units : 3 * units] = dinner
        dgates[now, 3 * units : 4 * units] = dcand
        total_now = dh * update
        for g, part in enumerate((dreset, dupdate, dinner)):
            pair = two_part(part)
            sect = slice(g * units, (g + 1) * units)
            first = jnp.dot(pair, w_high[sect, :], preferred_element_type=f32)
            second = jnp.dot(pair, w_low[sect, :], preferred_element_type=f32)
            total_now = total_now + (first[:rows_per] + first[rows_per:] + second[:rows_per])
        return keep[now, :] * total_now

    A, B, C, Z, S, F = sums.core, sums.first, sums.second, sums.along, sums.share, sums.far
    timeline = (
        (0.0, ((A, 0),)),
        (0.1, ((A, 1), (rows.forward, 0),)),
        (0.3, ((B, 0), (rows.spread, 1), (rows.far, 0),)),
        (0.44, ((B, 1), (rows.forward, 1), (rows.spread, 2),)),
        (0.56, ((C, 0), (rows.far, 1),)),
        (0.66, ((C, 1), (rows.forward, 2), (rows.spread, 3),)),
        (0.78, ((Z, 0), (rows.far, 2),)),
        (0.9, ((Z, 1), (S, 0), (rows.forward, 3),)),
        (1.0, ((S, 1), (F, 0),)),
    )
    state, done = jnp.zeros((rows_per, units), f32), 0
    for share_done, actions in timeline:
        until = int(share_done * steps)
        if until > done:
            state, done = lax.fori_loop(done, until, step, state), until
        for action, argument in actions:
            action(argument)
    dstart[...] = lax.fori_loop(done, steps, step, state)
    F(1), rows.far(3)
    sums.end(0)
    rows.close()
    sums.end(1)
    for copy in losses:
        copy.wait()


def run_back(hidden, outs, targets, negs, keep, saved, rows_per, steps, width, factor, collective_id):
    events, units = outs.shape
    n_dp, n_col, count, block = negs.shape
    jobs = 2
    piece = count // jobs
    hbm = pl.BlockSpec(memory_space=pl.ANY)
    step_rows = units // 4
    dma = pltpu.SemaphoreType.DMA
    return pl.pallas_call(
        functools.partial(back_kernel, steps, width, factor),
        out_shape=(
            jax.ShapeDtypeStruct((events, 4 * units), f32),
            jax.ShapeDtypeStruct((rows_per, units), f32),
            jax.ShapeDtypeStruct((8, count, block), f32),
            jax.ShapeDtypeStruct((8, 4, events, block), f32),
            jax.ShapeDtypeStruct((4, rows_per, LANES), f32),
        ),
        in_specs=[hbm, in_vmem(), in_vmem(), hbm] + [in_vmem()] * 6,
        out_specs=(in_vmem(), in_vmem(), hbm, hbm, hbm),
        scratch_shapes=[pltpu.VMEM((2, jobs, 4, 2, 2, piece, block), f32)]
        + sum_scratch(jobs, piece, block)[1:]
        + [
            pltpu.VMEM(hidden.shape, bf16),
            pltpu.VMEM(hidden.shape, bf16),
            pltpu.VMEM((2, step_rows, units), f32),
            pltpu.VMEM((4, events, block), f32),
            pltpu.VMEM((n_col, events, block), f32),
            pltpu.VMEM((2, n_col, events, block), bf16),
            pltpu.VMEM((events, n_dp * count), f32),
            pltpu.VMEM((2, n_col, count, block), f32),
            pltpu.VMEM((n_col, events, block), f32),
            pltpu.VMEM((events, units), f32),
            pltpu.VMEM((rows_per, LANES), f32),
            dma((2,)),
            dma((2,)),
            dma((1,)),
            dma((3,)),
            dma((3,)),
        ]
        + flow_sems(jobs),
        cost_estimate=takes(110),
        compiler_params=pltpu.CompilerParams(
            collective_id=collective_id, has_side_effects=True, vmem_limit_bytes=VMEM_BYTES
        ),
    )(hidden, outs, targets, negs, keep, *saved)


def pad_kernel(weight, bias, out):
    own, full = weight.shape[1:]
    block = out.shape[1]
    n_col = out.shape[2] // block
    part = full // n_col
    out[...] = jnp.zeros_like(out)
    for c in range(n_col):
        out[0, 0:own, c * block : c * block + part] = weight[0, :, c * part : (c + 1) * part]
    out[0, 0:own, part : part + 1] = bias[0]


def pad_units(weight, bias, n_col, block):
    gates, own, full = weight.shape
    return pl.pallas_call(
        pad_kernel,
        out_shape=jax.ShapeDtypeStruct((gates, block, n_col * block), f32),
        grid=(gates,),
        in_specs=[
            pl.BlockSpec((1, own, full), lambda g: (g, 0, 0)),
            pl.BlockSpec((1, own, 1), lambda g: (g, 0, 0)),
        ],
        out_specs=pl.BlockSpec((1, block, n_col * block), lambda g: (g, 0, 0)),
        compiler_params=params(),
    )(weight, bias[:, :, None])


def gather_weight(own, n_dp):
    gates, block, units = own.shape
    flat = own.reshape(n_dp, gates * block // n_dp, units)
    piece = lax.dynamic_index_in_dim(flat, lax.axis_index("dp"), 0, keepdims=False)
    every = lax.all_gather(piece, ("col", "dp"))
    every = every.reshape(-1, gates, block, units)
    return jnp.moveaxis(every, 0, 1).reshape(gates, -1, units)


def reduce_weight(partial, n_dp, n_col):
    gates, rows, units = partial.shape
    block = rows // n_col
    parts = jnp.moveaxis(partial.reshape(gates, n_col, block, units), 1, 0)
    parts = jnp.moveaxis(parts.reshape(n_col, n_dp, gates * block // n_dp, units), 1, 0)
    mine = lax.psum_scatter(parts, "dp", scatter_dimension=0)
    mine = lax.psum_scatter(mine, "col", scatter_dimension=0)
    return lax.all_gather(mine, "dp").reshape(gates, block, units)


def swap_col(rows, n_col):
    return lax.all_to_all(rows, "col", split_axis=0, concat_axis=0, tiled=True)


def unpad_last(value, n_col, part):
    block = value.shape[-1] // n_col
    return value.reshape(value.shape[:-1] + (n_col, block))[..., :part].reshape(value.shape[:-1] + (n_col * part,))


def local(
    n_dp,
    n_col,
    item_ids,
    target_ids,
    negative_ids,
    reset_mask,
    carry_flags,
    carried_state,
    embed_table,
    input_weight,
    hidden_weight,
    gate_bias,
    hidden_bias,
    out_table,
    out_bias,
):
    sessions, steps = item_ids.shape
    own_sessions = sessions // n_col
    rows_per = round_up(own_sessions, ROWS8)
    width = embed_table.shape[0]
    table_rows = embed_table.shape[1]
    own_rows = table_rows // n_dp
    block = round_up(width + 1, LANES)
    units = n_col * block
    events = steps * rows_per
    direct = n_dp == 8 and n_col == 4 and block % 64 == 0 and own_sessions == rows_per and steps % 4 == 0 and steps <= LANES
    factor = 1.0 / steps
    dp_at, col_at = lax.axis_index("dp"), lax.axis_index("col")

    def by_owner(value):
        value = jnp.moveaxis(value.reshape(n_col, own_sessions, steps), 1, 2)
        value = jnp.pad(value, ((0, 0), (0, 0), (0, rows_per - own_sessions)))
        return value.reshape(-1)

    both_ids = jnp.stack([item_ids, target_ids]).reshape(2, n_col, own_sessions, steps)
    both_ids = jnp.pad(jnp.moveaxis(both_ids, 2, 3), ((0, 0), (0, 0), (0, 0), (0, rows_per - own_sessions)))
    item_flat, target_flat = both_ids[0].reshape(-1), both_ids[1].reshape(-1)
    own_keep = lax.dynamic_index_in_dim(
        by_owner(1 - reset_mask).reshape(n_col, events, 1), col_at, 0, keepdims=False
    ).astype(f32)
    valid = jnp.tile(jnp.arange(rows_per) < own_sessions, steps)
    lane = jnp.arange(units) % block

    carried = (carry_flags.astype(f32)[:, None] * carried_state).reshape(n_col, own_sessions, width)
    carried = jnp.pad(carried, ((0, 0), (0, rows_per - own_sessions), (0, block - width)))
    neg_count = negative_ids.shape[0]
    own_negs = lax.dynamic_slice_in_dim(negative_ids, dp_at * (neg_count // n_dp), neg_count // n_dp)
    out_ids = jnp.concatenate([target_flat, own_negs])
    no_bias = jnp.zeros_like(hidden_bias)
    hid_bias = jnp.stack([no_bias, no_bias, hidden_bias])
    if direct:
        flat_ids = both_ids.reshape(-1)
        own_ids = both_ids.reshape(-1, LANES)
        all_in, all_hid, arrived, all_ids, out_rows = gather_all(
            embed_table,
            out_table,
            out_bias[None, :],
            flat_ids,
            negative_ids,
            jnp.swapaxes(input_weight, 1, 2),
            jnp.swapaxes(hidden_weight, 1, 2),
            gate_bias,
            hid_bias,
            carried,
            own_ids,
            1,
        )
        all_ids = all_ids.reshape(n_dp, 2, -1)
    else:
        all_hid = gather_weight(pad_units(hidden_weight, hid_bias, n_col, block), n_dp)
        all_in = gather_weight(pad_units(input_weight, gate_bias, n_col, block), n_dp)
        no_row = jnp.zeros((1, table_rows), f32)
        item_rows = gather_rows(embed_table, no_row, item_flat, block).reshape(n_col, events, block)
        arrived = swap_col(jnp.concatenate([item_rows, carried], axis=1), n_col)
        arrived = jnp.moveaxis(arrived, 0, 1).reshape(events + rows_per, units)
        arrived = arrived.at[:events, width].set(1.0)
        out_rows = gather_rows(out_table, out_bias[None, :], out_ids, block)
        all_ids = lax.all_gather(jnp.stack([item_flat, target_flat]), "dp")
    all_hid, all_in = all_hid.reshape(-1, units), all_in.reshape(-1, units)

    all_items, all_targets = all_ids[:, 0].reshape(-1), all_ids[:, 1].reshape(-1)
    count = all_items.shape[0]
    keys = jnp.concatenate([all_items, all_targets + table_rows, negative_ids + 2 * table_rows])
    order = jnp.concatenate([jnp.tile(lax.iota(jnp.int32, count), 2), lax.iota(jnp.int32, neg_count)])
    shift = (max(count, neg_count) - 1).bit_length()
    direct = direct and (3 * table_rows) << shift < 2**31
    low = (dp_at * own_rows).astype(jnp.int32)
    if direct:
        packed = lax.sort((keys << shift) | order)
    else:
        keys, order = lax.sort((keys, order), num_keys=1)
        by_item = (order[:count], keys[:count])
        by_target = (order[count : 2 * count], keys[count : 2 * count] - table_rows)
        by_neg = (order[2 * count :], keys[2 * count :] - 2 * table_rows)

    if direct:
        *saved, outs, negs, targets = run_forward_travel(
            all_hid, all_in, arrived, own_keep, out_rows, steps, width, 4
        )
    else:
        targets = swap_col(out_rows[: n_col * events].reshape(n_col, events, block), n_col)
        negs = lax.all_gather(out_rows[n_col * events :], ("dp", "col")).reshape(n_dp, n_col, -1, block)
        *saved, outs = run_forward(all_hid, all_in, arrived, own_keep, steps, width)
    prevs = saved[0]

    if direct:
        dgates, dstart, neg_all, target_all, loss_all = run_back(
            all_hid, outs, targets, negs, own_keep, saved, rows_per, steps, width, factor, 3
        )
        loss = loss_all[:, :, :steps].reshape(sessions, steps)
        neg_all, target_all = neg_all.reshape(-1, block), target_all.reshape(-1, block)
    else:
        targets = jnp.moveaxis(targets, 0, 1).reshape(events, units)
        negs = jnp.moveaxis(negs, 1, 2).reshape(neg_count, units)
        shares = jnp.where(lane == width, 1.0 / n_col, jnp.where(lane < width, outs, 0.0))
        pos_score = jnp.sum(shares * targets, axis=-1, keepdims=True)
        neg_score = lax.dot_general(shares, negs, (((1,), (1,)), ((), ())), precision=high)
        top = jnp.max(neg_score, axis=-1, keepdims=True)
        expd = jnp.exp(neg_score - top)
        weight = expd / jnp.sum(expd, axis=-1, keepdims=True)
        sig = jax.nn.sigmoid(pos_score - neg_score)
        ppos = jnp.sum(weight * sig, axis=-1, keepdims=True)
        quad = jnp.sum(weight * neg_score * neg_score, axis=-1, keepdims=True)
        slope = jnp.sum(weight * sig * (1.0 - sig), axis=-1, keepdims=True)
        own_loss = -jnp.log(ppos) + quad
        dneg = factor * weight * (1.0 - sig * sig / ppos + neg_score * neg_score + 2.0 * neg_score - quad)
        dneg = jnp.where(valid[:, None], dneg, 0.0)
        dpos = jnp.where(valid[:, None], -factor * slope / ppos, 0.0)
        douts = jnp.dot(dneg, negs, precision=high) + dpos * targets
        douts = jnp.where(lane < width, douts, 0.0)
        neg_part = lax.dot_general(dneg, shares, (((0,), (0,)), ((), ())), precision=high)
        target_part = dpos * shares

        neg_own = lax.psum_scatter(neg_part.reshape(n_dp, -1, units), "dp", scatter_dimension=0)
        neg_own = jnp.moveaxis(neg_own.reshape(-1, n_col, block), 1, 0)
        neg_own = lax.psum_scatter(neg_own, "col", scatter_dimension=0)
        neg_all = lax.all_gather(neg_own, "dp", tiled=True)
        target_own = swap_col(jnp.moveaxis(target_part.reshape(events, n_col, block), 1, 0), n_col)
        target_all = lax.all_gather(target_own.reshape(-1, block), "dp", tiled=True)
        dgates, dstart = run_backward(all_hid, douts, own_keep, saved, rows_per, steps)
        own_loss = own_loss.reshape(steps, rows_per)[:, :own_sessions]
        loss = lax.all_gather(own_loss.T, "col", tiled=True)
    gates = input_weight.shape[0]
    if direct:
        grads, item_all, start_all = run_tail(arrived, prevs, dgates, dstart, all_in, 2)
        grad_embed, grad_out, grad_obias, grad_in, grad_hid = run_finish(
            packed, shift, low, table_rows, own_rows, width, item_all.reshape(-1, block), target_all, neg_all, grads
        )
        grad_obias = grad_obias[0]
        grad_in, grad_hid = jnp.swapaxes(grad_in, 1, 2), jnp.swapaxes(grad_hid, 1, 2)
        grad_gate, grad_hbias = grads[0, :, width, :width], grads[1, gates - 1, width, :width]
    else:
        dx = jnp.concatenate([dgates[:, : 2 * units], dgates[:, 3 * units :]], axis=1)
        dh = dgates[:, : 3 * units]
        hid_part = lax.dot_general(dh, prevs, (((0,), (0,)), ((), ())), precision=high)
        in_part = lax.dot_general(dx, arrived[:events], (((0,), (0,)), ((), ())), precision=high)
        dinputs = jnp.dot(dx, all_in, precision=high)
        back = jnp.concatenate([dinputs, dstart], axis=0).reshape(events + rows_per, n_col, block)
        back = swap_col(jnp.moveaxis(back, 1, 0), n_col)
        item_all = lax.all_gather(back[:, :events].reshape(-1, block), "dp", tiled=True)
        start_all = back[:, events:]
        grad_in = reduce_weight(in_part.reshape(gates, units, units), n_dp, n_col)
        grad_hid = reduce_weight(hid_part.reshape(gates, units, units), n_dp, n_col)
        grad_gate, grad_hbias = grad_in[:, :width, width], grad_hid[gates - 1, :width, width]
        grad_in, grad_hid = (unpad_last(g[:, :width], n_col, width) for g in (grad_in, grad_hid))
        grad_out, grad_obias = scatter_rows(
            [by_target + (target_all,), by_neg + (neg_all,)],
            low,
            own_rows,
            width,
            block,
        )
        grad_obias = grad_obias[0] * n_col
        grad_embed, _ = scatter_rows([by_item + (item_all,)], low, own_rows, width, block)
    grad_carried = start_all[:, :own_sessions, :width].reshape(sessions, width)
    grad_carried = carry_flags.astype(f32)[:, None] * grad_carried
    return (
        loss,
        grad_embed,
        grad_in,
        grad_hid,
        grad_gate,
        grad_hbias,
        grad_out,
        grad_obias,
        grad_carried,
    )


def solution(mesh):
    in_specs = (
        P("dp", None),
        P("dp", None),
        P(),
        P("dp", None),
        P("dp"),
        P("dp", "col"),
        P("col", None),
        P(None, "col", None),
        P(None, "col", None),
        P(None, "col"),
        P("col"),
        P("col", None),
        P(),
    )
    out_specs = (
        P("dp", None),
        P("col", "dp"),
        P(None, "col", None),
        P(None, "col", None),
        P(None, "col"),
        P("col"),
        P("col", "dp"),
        P("dp"),
        P("dp", "col"),
    )
    body = functools.partial(local, mesh.shape["dp"], mesh.shape["col"])
    return jax.shard_map(body, mesh=mesh, in_specs=in_specs, out_specs=out_specs, check_vma=False)
```
